32 devices in a mesh: groups: 2 (over y), brick: 8 (over z, x), batch: 2 (over core).
Axes of the slice: x: 2, y: 2, z: 4, core: 2. Of those that a mesh axis runs over, the one named last changes fastest.
Arguments:
- features: bfloat16 [4, 2048, 128], P(('groups', 'batch'), 'brick'), parts along dimension 0, may hold values from -6 to 6
- cotangent: bfloat16 [4, 2048, 128], P(('groups', 'batch'), 'brick'), parts along dimension 0, may hold values from -6 to 6
- neighbours: int32 [27, 4096], P(None, ('groups', 'brick')), parts along dimension 1, may hold values from -1 to 2047, as said below
- timesteps: int32 [4], P(('groups', 'batch')), parts along dimension 0, may hold values from 0 to 999
- condition: bfloat16 [4, 128], P(('groups', 'batch')), parts along dimension 0, may hold values from -6 to 6
- w_time: bfloat16 [128, 128], replicated, may hold values from -0.5 to 0.5
- w_conv: bfloat16 [27, 128, 128], replicated, may hold values from -0.109375 to 0.109375
Outputs:
- conv_out: bfloat16 [4, 2048, 128], P(('groups', 'batch'), 'brick'), parts along dimension 0
- feature_grad: bfloat16 [4, 2048, 128], P(('groups', 'batch'), 'brick'), parts along dimension 0
- weight_grad: float32 [54, 128, 128], P('groups'), parts along dimension 0
The draws below stay inside these ranges and needn't reach their ends.
There are 2 independent parts, one for each index of `groups`. The reference program is written for one: setup_inputs(seed, part) draws one part's arguments, and reference() takes and returns one part's arrays. A program takes and returns all parts, laid end to end along the dimension named above; an argument that names none is the same for every part. Nothing has to cross between parts.
Inputs may be any that keep to these rules, and one draw needn't show every extreme that they name: `neighbours`: entry k, b is the voxel at offset (k // 9 - 1, k // 3 % 3 - 1, k % 3 - 1) from voxel b, or -1 if it is not occupied; entry 13 is b itself; c stands at offset k of b exactly when b stands at offset 26 - k of c. The ground is a grid of device tiles of 4 x 4 columns, 2 ** ((log2 8 + 1) // 2) tiles along the first dimension and 2 ** (log2 8 // 2) along the second, device i holding tile (i // tiles along the second, i % tiles along the second) and voxels i * 256 to (i + 1) * 256 - 1; within a device, voxel ((u * 4) + v) * 16 + l is layer l of column (u, v) of its tile. Neighbours differ by at most one column along each ground dimension.
All inputs are finite; a program needn't handle non-finite values.
Results may differ from the reference program's by a relative error of at most 0.0052.
Values may be sent and summed in bfloat16 or wider, within the bound.
No kernel may reach another device: no remote copies, remote signals or barrier semaphores. Data moves between devices by JAX's collectives and lax.ppermute only.
A program may use at most 64 MiB of HBM per device.

```python
import jax
import jax.numpy as jnp
import numpy as np
from jax import lax

C = 128
LAYERS = 16
TILE = 4
BRICK_DEV = 256
TOTAL = 2048
N_BRICK = 8


def draw_neighbours(key, part):
    key = jax.random.fold_in(key, 11)
    bits = N_BRICK.bit_length() - 1
    tiles_x = 2 ** ((bits + 1) // 2)
    tiles_y = 2 ** (bits // 2)
    side_x = tiles_x * TILE
    side_y = tiles_y * TILE
    heights = jax.random.randint(key, (side_x, side_y), 0, 2)
    ident = np.arange(TOTAL)
    owner = ident // BRICK_DEV
    inside = ident % BRICK_DEV
    column = inside // LAYERS
    layer = inside % LAYERS
    pos_x = owner // tiles_y * TILE + column // TILE
    pos_y = owner % tiles_y * TILE + column % TILE
    own_height = heights[pos_x, pos_y]
    rows = []
    for k in range(27):
        dx = k // 9 - 1
        dy = k // 3 % 3 - 1
        dz = k % 3 - 1
        nx = pos_x + dx
        ny = pos_y + dy
        ok_xy = (nx >= 0) & (nx < side_x) & (ny >= 0) & (ny < side_y)
        cx = np.clip(nx, 0, side_x - 1)
        cy = np.clip(ny, 0, side_y - 1)
        other = heights[cx, cy]
        new_layer = layer + dz + own_height - other
        ok = jnp.asarray(ok_xy) & (new_layer >= 0) & (new_layer < LAYERS)
        tile_rank = cx // TILE * tiles_y + cy // TILE
        number = tile_rank * BRICK_DEV + (cx % TILE * TILE + cy % TILE) * LAYERS + new_layer
        rows.append(jnp.where(ok, number, -1).astype(jnp.int32))
    return jnp.stack(rows)


def levels(own_key, extent, split, least, high):
    def one(position, parts):
        steps = jax.random.uniform(jax.random.fold_in(jax.random.fold_in(own_key, 6), position), (parts,), jnp.float32, least / len(split), high / len(split))
        return jnp.repeat(jnp.exp(steps), extent[position] // parts).reshape((-1,) + (1,) * (len(extent) - position - 1))

    factor_of = one(*split[0])
    for cut in split[1:]:
        factor_of = factor_of * one(*cut)
    return factor_of


def bell_draw(stream_key, dims, scale, most, pieces=(), kind=jnp.bfloat16):
    drawn = jax.random.normal(stream_key, dims, jnp.float32) * scale
    if len(pieces) > 0:
        drawn = levels(stream_key, dims, pieces, -0.22, 0.18) * drawn
    return jnp.clip(drawn, min=-most, max=most).astype(kind)


def setup_inputs(seed: int = 0, part: int = 0) -> dict:
    seeds = jax.random.split(jax.random.key(seed), 8)
    part_splits = jax.random.split(jax.random.fold_in(seeds[7], part), 8)
    return {
        "features": bell_draw(part_splits[0], (2, TOTAL, C), 1.0, 6.0, ((0, 2), (1, 8))),
        "cotangent": bell_draw(part_splits[1], (2, TOTAL, C), 1.0, 6.0, ((0, 2), (1, 8))),
        "neighbours": draw_neighbours(jax.random.fold_in(jax.random.fold_in(seeds[7], part), 71), part),
        "timesteps": jax.random.randint(part_splits[3], (2,), 0, 1000).astype(jnp.int32),
        "condition": bell_draw(part_splits[4], (2, C), 1.0, 6.0, ((0, 2),)),
        "w_time": bell_draw(seeds[5], (C, C), C ** -0.5, 0.5),
        "w_conv": bell_draw(seeds[6], (27, C, C), (27 * C) ** -0.5, 0.109375),
    }


def shifted(timesteps, condition, w_time):
    half = condition.shape[1] // 2
    freq = jnp.exp(-jnp.log(10000.0) * jnp.arange(half, dtype=jnp.float32) / half)
    angle = timesteps.astype(jnp.float32)[:, None] * freq[None, :]
    temb = jnp.concatenate([jnp.sin(angle), jnp.cos(angle)], axis=1).astype(jnp.bfloat16)
    return jnp.dot(temb, w_time, preferred_element_type=jnp.float32) + condition.astype(jnp.float32)


def reference(features, cotangent, neighbours, timesteps, condition, w_time, w_conv):
    total = features.shape[1]
    width = features.shape[2]
    shift = shifted(timesteps, condition, w_time)
    index = jnp.where(neighbours < 0, total, neighbours).astype(jnp.int32)
    zero_row = jnp.zeros((1, width), jnp.bfloat16)
    outs = []
    grads = []
    weight_grad = jnp.zeros((27, width, width), jnp.float32)
    for member in range(2):
        z_val = features[member].astype(jnp.float32) + shift[member][None, :]
        act = jax.nn.silu(z_val).astype(jnp.bfloat16)
        act_pad = jnp.concatenate([act, zero_row], axis=0)
        cot = cotangent[member]
        cot_pad = jnp.concatenate([cot, zero_row], axis=0)
        result = jnp.zeros((total, width), jnp.float32)
        back = jnp.zeros((total, width), jnp.float32)
        terms = []
        for k in range(27):
            gathered = act_pad[index[k]]
            result = result + jnp.dot(gathered, w_conv[k], preferred_element_type=jnp.float32)
            back = back + jnp.dot(cot_pad[index[26 - k]], w_conv[k].T, preferred_element_type=jnp.float32)
            terms.append(lax.dot_general(gathered, cot, (((0,), (0,)), ((), ())), preferred_element_type=jnp.float32))
        weight_grad = weight_grad + jnp.stack(terms)
        sig = jax.nn.sigmoid(z_val)
        outs.append(result.astype(jnp.bfloat16))
        grads.append((back * sig * (1.0 + z_val * (1.0 - sig))).astype(jnp.bfloat16))
    return jnp.stack(outs), jnp.stack(grads), weight_grad
```

```python
import jax
import jax.numpy as jnp
from jax import lax
from jax.sharding import PartitionSpec as P

LAYERS = 16
TILE = 4


def passed_along(block, axis, distance):
    devices = range(lax.axis_size(axis))
    route = [(i - distance, i) for i in devices if i - distance in devices]
    return lax.ppermute(block, axis, route)


def shifted(timesteps, condition, w_time):
    half = condition.shape[1] // 2
    freq = jnp.exp(-jnp.log(10000.0) * jnp.arange(half, dtype=jnp.float32) / half)
    angle = timesteps.astype(jnp.float32)[:, None] * freq[None, :]
    temb = jnp.concatenate([jnp.sin(angle), jnp.cos(angle)], axis=1).astype(jnp.bfloat16)
    return jnp.dot(temb, w_time, preferred_element_type=jnp.float32) + condition.astype(jnp.float32)


def slab_rows(block, side_recv, front_recv, width):
    widened = jnp.concatenate([side_recv[0], block, side_recv[1]], axis=1)
    slab = jnp.concatenate([front_recv[0][None], widened, front_recv[1][None]], axis=0)
    flat = slab.reshape(-1, width)
    return jnp.concatenate([flat, jnp.zeros((1, width), jnp.bfloat16)], axis=0)


def shards(features, cotangent, neighbours, timesteps, condition, w_time, w_conv):
    rows_here = features.shape[1]
    width = features.shape[2]
    peers = lax.axis_size("brick")
    bits = peers.bit_length() - 1
    tiles_y = 2 ** (bits // 2)
    here = lax.axis_index("brick")
    tile_x = here // tiles_y
    tile_y = here % tiles_y
    side = TILE
    layers = LAYERS
    wide = side + 2
    valid = neighbours >= 0
    safe = jnp.where(valid, neighbours, 0)
    owner = safe // rows_here
    inside = safe % rows_here
    column = inside // layers
    layer = inside % layers
    local_x = (owner // tiles_y - tile_x) * side + column // side + 1
    local_y = (owner % tiles_y - tile_y) * side + column % side + 1
    sentinel = wide * wide * layers
    ext_index = jnp.where(valid, (local_x * wide + local_y) * layers + layer, sentinel).T
    shift = shifted(timesteps, condition, w_time)
    z_val = features[0].astype(jnp.float32) + shift[0][None, :]
    act = jax.nn.silu(z_val).astype(jnp.bfloat16)
    cot = cotangent[0]
    act_block = act.reshape(side, side, layers, width)
    cot_block = cot.reshape(side, side, layers, width)
    w_forward = w_conv.reshape(27 * width, width)
    w_backward = jnp.transpose(w_conv[::-1], (0, 2, 1)).reshape(27 * width, width)
    side_moves = ((1, side - 1), (-1, 0))
    front_moves = ((tiles_y, side - 1), (-tiles_y, 0))
    act_list = []
    for by, edge in side_moves:
        act_list.append(passed_along(act_block[:, edge], "brick", by))
    act_side = (act_list[0][:, None], act_list[1][:, None])
    act_wide = jnp.concatenate([act_side[0], act_block, act_side[1]], axis=1)
    act_fronts = []
    for by, edge in front_moves:
        act_fronts.append(passed_along(act_wide[edge], "brick", by))
    act_front = (act_fronts[0], act_fronts[1])
    act_ext = slab_rows(act_block, act_side, act_front, width)
    gathered = act_ext[ext_index].reshape(rows_here, 27 * width)
    conv_out = jnp.dot(gathered, w_forward, preferred_element_type=jnp.float32).astype(jnp.bfloat16)
    partial_grad = lax.dot_general(
        gathered, cot, (((0,), (0,)), ((), ())), preferred_element_type=jnp.float32
    )
    both = ("brick", "batch")
    parts = peers * lax.axis_size("batch")
    rows = 27 * width
    extra = -rows % (8 * parts)
    pieces = jnp.pad(partial_grad.astype(jnp.bfloat16), ((0, extra), (0, 0))).reshape(parts, -1, width)
    arrived = lax.all_to_all(pieces, both, 0, 0)
    summed = arrived.astype(jnp.float32).sum(0).astype(jnp.bfloat16)
    whole = lax.all_gather(summed, both, axis=0, tiled=True)
    weight_grad = whole[:rows].astype(jnp.float32).reshape(27, width, width)
    cot_list = []
    for by, edge in side_moves:
        cot_list.append(passed_along(cot_block[:, edge], "brick", by))
    cot_side = (cot_list[0][:, None], cot_list[1][:, None])
    cot_wide = jnp.concatenate([cot_side[0], cot_block, cot_side[1]], axis=1)
    cot_fronts = []
    for by, edge in front_moves:
        cot_fronts.append(passed_along(cot_wide[edge], "brick", by))
    cot_front = (cot_fronts[0], cot_fronts[1])
    cot_ext = slab_rows(cot_block, cot_side, cot_front, width)
    cot_gathered = cot_ext[ext_index].reshape(rows_here, 27 * width)
    back = jnp.dot(cot_gathered, w_backward, preferred_element_type=jnp.float32)
    sig = jax.nn.sigmoid(z_val)
    feature_grad = (back * sig * (1.0 + z_val * (1.0 - sig))).astype(jnp.bfloat16)
    return (conv_out[None], feature_grad[None], weight_grad)


def solution(mesh):
    in_specs = (
        P(("groups", "batch"), "brick", None),
        P(("groups", "batch"), "brick", None),
        P(None, ("groups", "brick")),
        P(("groups", "batch")),
        P(("groups", "batch"), None),
        P(),
        P(),
    )
    out_specs = (
        P(("groups", "batch"), "brick", None),
        P(("groups", "batch"), "brick", None),
        P("groups", None, None),
    )
    return jax.shard_map(shards, mesh=mesh, in_specs=in_specs, out_specs=out_specs, check_vma=False)
```

```python
import functools

import jax
import jax.numpy as jnp
from jax import lax
from jax.experimental import pallas as pl
from jax.experimental.pallas import tpu as pltpu
from jax.sharding import PartitionSpec as P

LAYERS = 16
TILE = 4
STRIP = TILE * LAYERS
HALF = 13
CODE_ROWS = 16
VMEM_BYTES = 48 * 1024 * 1024


def time_embedding(timesteps, width):
    half = width // 2
    freq = jnp.exp(-jnp.log(10000.0) * jnp.arange(half, dtype=jnp.float32) / half)
    angle = timesteps.astype(jnp.float32)[:, None] * freq[None, :]
    return jnp.concatenate([jnp.sin(angle), jnp.cos(angle)], axis=1).astype(jnp.bfloat16)


def strip_codes(neighbours, tiles_y):
    rows_here = TILE * STRIP
    code = (neighbours // rows_here) % tiles_y * STRIP + neighbours % STRIP
    return jnp.where(neighbours < 0, -1, code).astype(jnp.float32)


def pack_kernel(tiles_y, feat_ref, cot_ref, near_ref, temb_ref, cond_ref, wt_ref, pack_ref, shift_ref):
    rows, width = feat_ref.shape
    shift = jnp.dot(temb_ref[...], wt_ref[...], preferred_element_type=jnp.float32)
    shift = shift + cond_ref[...].astype(jnp.float32)
    shift_ref[...] = shift
    z_val = feat_ref[...].astype(jnp.float32) + shift
    pack_ref[:rows, :width] = (z_val * jax.nn.sigmoid(z_val)).astype(jnp.bfloat16)
    pack_ref[:rows, width:] = cot_ref[...]
    pack_ref[rows:, :] = strip_codes(near_ref[:CODE_ROWS, :], tiles_y).astype(jnp.bfloat16)


def weight_kernel(tiles_x, tiles_y, pack_ref, own_ref, sent_ref, ground, turned, codes, gathered):
    width = own_ref.shape[2]
    rows = TILE * STRIP
    span = tiles_y * STRIP
    strips = tiles_x * TILE
    for tile_x in range(tiles_x):
        for tile_y in range(tiles_y):
            tile = tile_x * tiles_y + tile_y
            columns = pack_ref[tile, rows:, :].astype(jnp.float32).T
            for u in range(TILE):
                at = (tile_x * TILE + u) * span + tile_y * STRIP
                ground[at:at + STRIP, :] = pack_ref[tile, u * STRIP:(u + 1) * STRIP, :]
                codes[at:at + STRIP, :] = columns[u * STRIP:(u + 1) * STRIP, :]
    for strip in range(strips):
        at = strip * span
        turned[:, at:at + span] = ground[at:at + span, :].T
    place = lax.broadcasted_iota(jnp.int32, (span, span), 1).astype(jnp.float32)

    def select(strip, carry):
        at = pl.multiple_of(strip * span, span)
        before = pl.multiple_of(jnp.maximum(strip - 1, 0) * span, span)
        code = codes[pl.ds(at, span), :]
        for first, last, source in ((0, 9, before), (9, HALF, at)):
            block = ground[pl.ds(source, span), :]
            for k in range(first, last):
                pick = (code[:, k:k + 1] == place).astype(jnp.bfloat16)
                rows_k = jnp.dot(pick, block, preferred_element_type=jnp.float32)
                gathered[k, pl.ds(at, span), :] = rows_k.astype(jnp.bfloat16)
        return carry

    lax.fori_loop(0, strips, select, 0)

    def multiply(k, carry):
        low = jnp.dot(turned[width:, :], gathered[k, :, :width], preferred_element_type=jnp.float32).T
        high = jnp.dot(turned[:width, :], gathered[k, :, width:], preferred_element_type=jnp.float32)
        own_ref[k] = low
        sent_ref[k] = low.astype(jnp.bfloat16)
        own_ref[2 * HALF - k] = high
        sent_ref[2 * HALF - k] = high.astype(jnp.bfloat16)
        return carry

    lax.fori_loop(0, HALF, multiply, 0)
    centre = jnp.dot(turned[:width, :], ground[:, width:], preferred_element_type=jnp.float32)
    own_ref[HALF] = centre
    sent_ref[HALF] = centre.astype(jnp.bfloat16)


def voxel_kernel(tiles_x, tiles_y, where_ref, pack_ref, near_ref, feat_ref, shift_ref, w_ref,
                 conv_ref, grad_ref, near_act, near_cot, w_back):
    rows, width = feat_ref.shape
    span = tiles_y * STRIP
    strips = tiles_x * TILE
    first = where_ref[0] // tiles_y * TILE
    code = strip_codes(near_ref[...], tiles_y).T
    place = lax.broadcasted_iota(jnp.int32, (STRIP, span), 1).astype(jnp.float32)
    for u in range(TILE):
        here = u * STRIP
        for side in range(3):
            strip = jnp.clip(first + u + side - 1, 0, strips - 1)
            tile = strip // TILE * tiles_y
            at = pl.multiple_of(strip % TILE * STRIP, STRIP)
            block = jnp.concatenate([pack_ref[tile + i, pl.ds(at, STRIP), :] for i in range(tiles_y)], axis=0)
            for k in range(9 * side, 9 * side + 9):
                pick = (code[here:here + STRIP, k:k + 1] == place).astype(jnp.bfloat16)
                rows_k = jnp.dot(pick, block, preferred_element_type=jnp.float32).astype(jnp.bfloat16)
                near_act[here:here + STRIP, k * width:(k + 1) * width] = rows_k[:, :width]
                near_cot[here:here + STRIP, k * width:(k + 1) * width] = rows_k[:, width:]
    for k in range(27):
        w_back[:, k * width:(k + 1) * width] = w_ref[26 - k]
    conv = jnp.dot(near_act[...], w_ref[...].reshape(27 * width, width), preferred_element_type=jnp.float32)
    conv_ref[...] = conv.astype(jnp.bfloat16)
    back = lax.dot_general(near_cot[...], w_back[...], (((1,), (1,)), ((), ())), preferred_element_type=jnp.float32)
    z_val = feat_ref[...].astype(jnp.float32) + shift_ref[...]
    sig = jax.nn.sigmoid(z_val)
    grad_ref[...] = (back * sig * (1.0 + z_val * (1.0 - sig))).astype(jnp.bfloat16)


def whole_scene(features, cotangent, neighbours, timesteps, condition, w_time, w_conv, tiles_x, tiles_y):
    rows, width = features.shape[1:]
    peers = tiles_x * tiles_y
    total = peers * rows
    temb = time_embedding(timesteps, width)
    packed, shift = pl.pallas_call(
        functools.partial(pack_kernel, tiles_y),
        out_shape=(
            jax.ShapeDtypeStruct((rows + CODE_ROWS, 2 * width), jnp.bfloat16),
            jax.ShapeDtypeStruct((1, width), jnp.float32),
        ),
        name="pack_tile",
    )(features[0], cotangent[0], neighbours, temb, condition, w_time)
    scene = lax.all_gather(packed, "brick")
    own, sent = pl.pallas_call(
        functools.partial(weight_kernel, tiles_x, tiles_y),
        out_shape=(
            jax.ShapeDtypeStruct((27, width, width), jnp.float32),
            jax.ShapeDtypeStruct((27, width, width), jnp.bfloat16),
        ),
        scratch_shapes=[
            pltpu.VMEM((total, 2 * width), jnp.bfloat16),
            pltpu.VMEM((2 * width, total), jnp.bfloat16),
            pltpu.VMEM((total, CODE_ROWS), jnp.float32),
            pltpu.VMEM((HALF, total, 2 * width), jnp.bfloat16),
        ],
        compiler_params=pltpu.CompilerParams(vmem_limit_bytes=VMEM_BYTES),
        name="weight_terms",
    )(scene)
    other = lax.ppermute(sent, "batch", [(0, 1), (1, 0)])
    here = lax.axis_index("brick").astype(jnp.int32).reshape(1)
    vmem = pl.BlockSpec(memory_space=pltpu.VMEM)
    conv_out, feature_grad = pl.pallas_call(
        functools.partial(voxel_kernel, tiles_x, tiles_y),
        out_shape=(
            jax.ShapeDtypeStruct((rows, width), jnp.bfloat16),
            jax.ShapeDtypeStruct((rows, width), jnp.bfloat16),
        ),
        in_specs=[pl.BlockSpec(memory_space=pltpu.SMEM)] + [vmem] * 5,
        scratch_shapes=[
            pltpu.VMEM((rows, 27 * width), jnp.bfloat16),
            pltpu.VMEM((rows, 27 * width), jnp.bfloat16),
            pltpu.VMEM((width, 27 * width), jnp.bfloat16),
        ],
        compiler_params=pltpu.CompilerParams(vmem_limit_bytes=VMEM_BYTES),
        cost_estimate=pl.CostEstimate(flops=10**9, bytes_accessed=4 * 10**6, transcendentals=0),
        name="voxel_outputs",
    )(here, scene, neighbours, features[0], shift, w_conv)
    weight_grad = own + other.astype(jnp.float32)
    return (conv_out[None], feature_grad[None], weight_grad)


def passed_along(block, axis, distance):
    devices = range(lax.axis_size(axis))
    route = [(i - distance, i) for i in devices if i - distance in devices]
    return lax.ppermute(block, axis, route)


def slab_rows(block, side_recv, front_recv, width):
    widened = jnp.concatenate([side_recv[0], block, side_recv[1]], axis=1)
    slab = jnp.concatenate([front_recv[0][None], widened, front_recv[1][None]], axis=0)
    flat = slab.reshape(-1, width)
    return jnp.concatenate([flat, jnp.zeros((1, width), jnp.bfloat16)], axis=0)


def with_halo(block, tiles_y):
    width = block.shape[-1]
    side = TILE
    side_recv = tuple(passed_along(block[:, edge], "brick", by)[:, None] for by, edge in ((1, side - 1), (-1, 0)))
    wide = jnp.concatenate([side_recv[0], block, side_recv[1]], axis=1)
    front_recv = tuple(passed_along(wide[edge], "brick", by) for by, edge in ((tiles_y, side - 1), (-tiles_y, 0)))
    return slab_rows(block, side_recv, front_recv, width)


def halo_plan(features, cotangent, neighbours, timesteps, condition, w_time, w_conv, tiles_x, tiles_y):
    rows_here, width = features.shape[1:]
    here = lax.axis_index("brick")
    tile_x = here // tiles_y
    tile_y = here % tiles_y
    side = TILE
    layers = LAYERS
    wide = side + 2
    valid = neighbours >= 0
    safe = jnp.where(valid, neighbours, 0)
    owner = safe // rows_here
    inside = safe % rows_here
    column = inside // layers
    layer = inside % layers
    local_x = (owner // tiles_y - tile_x) * side + column // side + 1
    local_y = (owner % tiles_y - tile_y) * side + column % side + 1
    sentinel = wide * wide * layers
    ext_index = jnp.where(valid, (local_x * wide + local_y) * layers + layer, sentinel).T
    temb = time_embedding(timesteps, width)
    shift = jnp.dot(temb, w_time, preferred_element_type=jnp.float32) + condition.astype(jnp.float32)
    z_val = features[0].astype(jnp.float32) + shift[0][None, :]
    act = jax.nn.silu(z_val).astype(jnp.bfloat16)
    cot = cotangent[0]
    w_forward = w_conv.reshape(27 * width, width)
    w_backward = jnp.transpose(w_conv[::-1], (0, 2, 1)).reshape(27 * width, width)
    act_ext = with_halo(act.reshape(side, side, layers, width), tiles_y)
    gathered = act_ext[ext_index].reshape(rows_here, 27 * width)
    conv_out = jnp.dot(gathered, w_forward, preferred_element_type=jnp.float32).astype(jnp.bfloat16)
    partial_grad = lax.dot_general(
        gathered, cot, (((0,), (0,)), ((), ())), preferred_element_type=jnp.float32
    )
    both = ("brick", "batch")
    parts = tiles_x * tiles_y * lax.axis_size("batch")
    rows = 27 * width
    extra = -rows % (8 * parts)
    pieces = jnp.pad(partial_grad.astype(jnp.bfloat16), ((0, extra), (0, 0))).reshape(parts, -1, width)
    arrived = lax.all_to_all(pieces, both, 0, 0)
    summed = arrived.astype(jnp.float32).sum(0).astype(jnp.bfloat16)
    whole = lax.all_gather(summed, both, axis=0, tiled=True)
    weight_grad = whole[:rows].astype(jnp.float32).reshape(27, width, width)
    cot_ext = with_halo(cot.reshape(side, side, layers, width), tiles_y)
    cot_gathered = cot_ext[ext_index].reshape(rows_here, 27 * width)
    back = jnp.dot(cot_gathered, w_backward, preferred_element_type=jnp.float32)
    sig = jax.nn.sigmoid(z_val)
    feature_grad = (back * sig * (1.0 + z_val * (1.0 - sig))).astype(jnp.bfloat16)
    return (conv_out[None], feature_grad[None], weight_grad)


def shards(*arrays):
    peers = lax.axis_size("brick")
    bits = peers.bit_length() - 1
    tiles_x = 2 ** ((bits + 1) // 2)
    tiles_y = 2 ** (bits // 2)
    plan = whole_scene if tiles_y == 2 else halo_plan
    return plan(*arrays, tiles_x, tiles_y)


def solution(mesh):
    in_specs = (
        P(("groups", "batch"), "brick", None),
        P(("groups", "batch"), "brick", None),
        P(None, ("groups", "brick")),
        P(("groups", "batch")),
        P(("groups", "batch"), None),
        P(),
        P(),
    )
    out_specs = (
        P(("groups", "batch"), "brick", None),
        P(("groups", "batch"), "brick", None),
        P("groups", None, None),
    )
    return jax.shard_map(shards, mesh=mesh, in_specs=in_specs, out_specs=out_specs, check_vma=False)
```

```python
import functools

import jax
import jax.numpy as jnp
from jax import lax
from jax.experimental import pallas as pl
from jax.experimental.pallas import tpu as pltpu
from jax.sharding import PartitionSpec as P

LAYERS = 16
TILE = 4
STRIP = TILE * LAYERS
HALF = 13
CODE_ROWS = 16
WEIGHT_VMEM = 32 * 1024 * 1024
VOXEL_VMEM = 16 * 1024 * 1024


def time_embedding(timesteps, width):
    half = width // 2
    freq = jnp.exp(-jnp.log(10000.0) * jnp.arange(half, dtype=jnp.float32) / half)
    angle = timesteps.astype(jnp.float32)[:, None] * freq[None, :]
    return jnp.concatenate([jnp.sin(angle), jnp.cos(angle)], axis=1).astype(jnp.bfloat16)


def strip_codes(neighbours, tiles_y):
    rows_here = TILE * STRIP
    code = (neighbours // rows_here) % tiles_y * STRIP + neighbours % STRIP
    return jnp.where(neighbours < 0, -1, code).astype(jnp.float32)


def pack_kernel(tiles_y, feat_ref, near_ref, temb_ref, cond_ref, wt_ref, pack_ref, z_ref, code_ref):
    rows, width = feat_ref.shape
    shift = jnp.dot(temb_ref[...], wt_ref[...], preferred_element_type=jnp.float32)
    shift = shift + cond_ref[...].astype(jnp.float32)
    z_val = feat_ref[...].astype(jnp.float32) + shift
    z_ref[...] = z_val
    pack_ref[:rows, :] = (z_val * jax.nn.sigmoid(z_val)).astype(jnp.bfloat16)
    code = strip_codes(near_ref[...], tiles_y)
    code_ref[...] = code.T
    for half in range(rows // width):
        at = rows + half * CODE_ROWS
        piece = code[:CODE_ROWS, half * width:(half + 1) * width]
        pack_ref[at:at + CODE_ROWS, :] = piece.astype(jnp.bfloat16)


def weight_kernel(tiles_x, tiles_y, act_ref, cot_ref, own_ref, sent_ref, ground, turned, codes, near_act, near_cot):
    width = own_ref.shape[2]
    rows = TILE * STRIP
    span = tiles_y * STRIP
    strips = tiles_x * TILE
    for tile_x in range(tiles_x):
        for tile_y in range(tiles_y):
            tile = tile_x * tiles_y + tile_y
            for half in range(rows // width):
                at = rows + half * CODE_ROWS
                columns = act_ref[tile, at:at + CODE_ROWS, :].astype(jnp.float32).T
                for part in range(width // STRIP):
                    u = half * (width // STRIP) + part
                    to = (tile_x * TILE + u) * span + tile_y * STRIP
                    codes[to:to + STRIP, :] = columns[part * STRIP:(part + 1) * STRIP, :]
            for u in range(TILE):
                to = (tile_x * TILE + u) * span + tile_y * STRIP
                ground[to:to + STRIP, :width] = act_ref[tile, u * STRIP:(u + 1) * STRIP, :]
                ground[to:to + STRIP, width:] = cot_ref[tile, u * STRIP:(u + 1) * STRIP, :]
    for strip in range(strips):
        at = strip * span
        turned[:, at:at + span] = ground[at:at + span, :].T
    place = lax.broadcasted_iota(jnp.int32, (span, span), 1).astype(jnp.float32)
    last = HALF // 2
    near_act[last, :, width:] = ground[:, :width]
    near_cot[last, :, width:] = ground[:, width:]

    def select(strip, carry):
        at = pl.multiple_of(strip * span, span)
        before = pl.multiple_of(jnp.maximum(strip - 1, 0) * span, span)
        code = codes[pl.ds(at, span), :]
        for first, stop, source in ((0, 9, before), (9, HALF, at)):
            block = ground[pl.ds(source, span), :]
            picks = [(code[:, k:k + 1] == place).astype(jnp.bfloat16) for k in range(first, stop)]
            near = jnp.dot(jnp.concatenate(picks, axis=0), block, preferred_element_type=jnp.float32)
            near = near.astype(jnp.bfloat16)
            for k in range(first, stop):
                rows_k = near[(k - first) * span:(k - first + 1) * span, :]
                side = k % 2 * width
                near_act[k // 2, pl.ds(at, span), side:side + width] = rows_k[:, :width]
                near_cot[k // 2, pl.ds(at, span), side:side + width] = rows_k[:, width:]
        return carry

    lax.fori_loop(0, strips, select, 0)

    for pair in range(last + 1):
        low = jnp.dot(turned[width:, :], near_act[pair], preferred_element_type=jnp.float32)
        high = jnp.dot(turned[:width, :], near_cot[pair], preferred_element_type=jnp.float32)
        for side in range(2):
            k = 2 * pair + side
            above = high[:, side * width:(side + 1) * width]
            own_ref[2 * HALF - k] = above
            sent_ref[2 * HALF - k] = above.astype(jnp.bfloat16)
            if k < HALF:
                below = low[:, side * width:(side + 1) * width].T
                own_ref[k] = below
                sent_ref[k] = below.astype(jnp.bfloat16)


def voxel_kernel(tiles_x, tiles_y, where_ref, act_ref, cot_ref, code_ref, z_ref, w_ref,
                 conv_ref, grad_ref, near_act, near_cot, w_back):
    rows, width = z_ref.shape
    span = tiles_y * STRIP
    strips = tiles_x * TILE
    first = where_ref[0] // tiles_y * TILE
    place = lax.broadcasted_iota(jnp.int32, (STRIP, span), 1).astype(jnp.float32)
    for u in range(TILE):
        here = u * STRIP
        code = code_ref[here:here + STRIP, :]
        for side in range(3):
            strip = jnp.clip(first + u + side - 1, 0, strips - 1)
            tile = strip // TILE * tiles_y
            at = pl.multiple_of(strip % TILE * STRIP, STRIP)
            pieces = [
                jnp.concatenate([ref[tile + i, pl.ds(at, STRIP), :] for i in range(tiles_y)], axis=0)
                for ref in (act_ref, cot_ref)
            ]
            block = jnp.concatenate(pieces, axis=1)
            ks = range(9 * side, 9 * side + 9)
            picks = [(code[:, k:k + 1] == place).astype(jnp.bfloat16) for k in ks]
            near = jnp.dot(jnp.concatenate(picks, axis=0), block, preferred_element_type=jnp.float32)
            near = near.astype(jnp.bfloat16)
            for k in ks:
                rows_k = near[(k - 9 * side) * STRIP:(k - 9 * side + 1) * STRIP, :]
                near_act[here:here + STRIP, k * width:(k + 1) * width] = rows_k[:, :width]
                near_cot[here:here + STRIP, k * width:(k + 1) * width] = rows_k[:, width:]
    for k in range(27):
        w_back[:, k * width:(k + 1) * width] = w_ref[26 - k]
    conv = jnp.dot(near_act[...], w_ref[...].reshape(27 * width, width), preferred_element_type=jnp.float32)
    conv_ref[...] = conv.astype(jnp.bfloat16)
    back = lax.dot_general(near_cot[...], w_back[...], (((1,), (1,)), ((), ())), preferred_element_type=jnp.float32)
    z_val = z_ref[...]
    sig = jax.nn.sigmoid(z_val)
    grad_ref[...] = (back * sig * (1.0 + z_val * (1.0 - sig))).astype(jnp.bfloat16)


def whole_scene(features, cotangent, neighbours, timesteps, condition, w_time, w_conv, tiles_x, tiles_y):
    rows, width = features.shape[1:]
    peers = tiles_x * tiles_y
    total = peers * rows
    vmem = pl.BlockSpec(memory_space=pltpu.VMEM)
    temb = time_embedding(timesteps, width)
    packed, z_val, code = pl.pallas_call(
        functools.partial(pack_kernel, tiles_y),
        out_shape=(
            jax.ShapeDtypeStruct((rows + rows // width * CODE_ROWS, width), jnp.bfloat16),
            jax.ShapeDtypeStruct((rows, width), jnp.float32),
            jax.ShapeDtypeStruct((rows, 27), jnp.float32),
        ),
        out_specs=(vmem, vmem, vmem),
        name="pack_tile",
    )(features[0], neighbours, temb, condition, w_time)
    cot_all = lax.all_gather(cotangent[0], "brick")
    cot_all, packed = lax.optimization_barrier((cot_all, packed))
    act_all = lax.all_gather(packed, "brick")
    own, sent = pl.pallas_call(
        functools.partial(weight_kernel, tiles_x, tiles_y),
        out_shape=(
            jax.ShapeDtypeStruct((27, width, width), jnp.float32),
            jax.ShapeDtypeStruct((27, width, width), jnp.bfloat16),
        ),
        in_specs=[vmem, vmem],
        out_specs=(vmem, vmem),
        scratch_shapes=[
            pltpu.VMEM((total, 2 * width), jnp.bfloat16),
            pltpu.VMEM((2 * width, total), jnp.bfloat16),
            pltpu.VMEM((total, CODE_ROWS), jnp.float32),
            pltpu.VMEM((HALF // 2 + 1, total, 2 * width), jnp.bfloat16),
            pltpu.VMEM((HALF // 2 + 1, total, 2 * width), jnp.bfloat16),
        ],
        compiler_params=pltpu.CompilerParams(vmem_limit_bytes=WEIGHT_VMEM),
        name="weight_terms",
    )(act_all, cot_all)
    other = lax.ppermute(sent, "batch", [(0, 1), (1, 0)])
    here = lax.axis_index("brick").astype(jnp.int32).reshape(1)
    conv_out, feature_grad = pl.pallas_call(
        functools.partial(voxel_kernel, tiles_x, tiles_y),
        out_shape=(
            jax.ShapeDtypeStruct((rows, width), jnp.bfloat16),
            jax.ShapeDtypeStruct((rows, width), jnp.bfloat16),
        ),
        in_specs=[pl.BlockSpec(memory_space=pltpu.SMEM)] + [vmem] * 5,
        scratch_shapes=[
            pltpu.VMEM((rows, 27 * width), jnp.bfloat16),
            pltpu.VMEM((rows, 27 * width), jnp.bfloat16),
            pltpu.VMEM((width, 27 * width), jnp.bfloat16),
        ],
        compiler_params=pltpu.CompilerParams(vmem_limit_bytes=VOXEL_VMEM),
        cost_estimate=pl.CostEstimate(flops=10**9, bytes_accessed=4 * 10**6, transcendentals=0),
        name="voxel_outputs",
    )(here, act_all, cot_all, code, z_val, w_conv)
    weight_grad = own + other.astype(jnp.float32)
    return (conv_out[None], feature_grad[None], weight_grad)


def passed_along(block, axis, distance):
    devices = range(lax.axis_size(axis))
    route = [(i - distance, i) for i in devices if i - distance in devices]
    return lax.ppermute(block, axis, route)


def slab_rows(block, side_recv, front_recv, width):
    widened = jnp.concatenate([side_recv[0], block, side_recv[1]], axis=1)
    slab = jnp.concatenate([front_recv[0][None], widened, front_recv[1][None]], axis=0)
    flat = slab.reshape(-1, width)
    return jnp.concatenate([flat, jnp.zeros((1, width), jnp.bfloat16)], axis=0)


def with_halo(block, tiles_y):
    width = block.shape[-1]
    side = TILE
    side_recv = tuple(passed_along(block[:, edge], "brick", by)[:, None] for by, edge in ((1, side - 1), (-1, 0)))
    wide = jnp.concatenate([side_recv[0], block, side_recv[1]], axis=1)
    front_recv = tuple(passed_along(wide[edge], "brick", by) for by, edge in ((tiles_y, side - 1), (-tiles_y, 0)))
    return slab_rows(block, side_recv, front_recv, width)


def halo_plan(features, cotangent, neighbours, timesteps, condition, w_time, w_conv, tiles_x, tiles_y):
    rows_here, width = features.shape[1:]
    here = lax.axis_index("brick")
    tile_x = here // tiles_y
    tile_y = here % tiles_y
    side = TILE
    layers = LAYERS
    wide = side + 2
    valid = neighbours >= 0
    safe = jnp.where(valid, neighbours, 0)
    owner = safe // rows_here
    inside = safe % rows_here
    column = inside // layers
    layer = inside % layers
    local_x = (owner // tiles_y - tile_x) * side + column // side + 1
    local_y = (owner % tiles_y - tile_y) * side + column % side + 1
    sentinel = wide * wide * layers
    ext_index = jnp.where(valid, (local_x * wide + local_y) * layers + layer, sentinel).T
    temb = time_embedding(timesteps, width)
    shift = jnp.dot(temb, w_time, preferred_element_type=jnp.float32) + condition.astype(jnp.float32)
    z_val = features[0].astype(jnp.float32) + shift[0][None, :]
    act = jax.nn.silu(z_val).astype(jnp.bfloat16)
    cot = cotangent[0]
    w_forward = w_conv.reshape(27 * width, width)
    w_backward = jnp.transpose(w_conv[::-1], (0, 2, 1)).reshape(27 * width, width)
    act_ext = with_halo(act.reshape(side, side, layers, width), tiles_y)
    gathered = act_ext[ext_index].reshape(rows_here, 27 * width)
    conv_out = jnp.dot(gathered, w_forward, preferred_element_type=jnp.float32).astype(jnp.bfloat16)
    partial_grad = lax.dot_general(
        gathered, cot, (((0,), (0,)), ((), ())), preferred_element_type=jnp.float32
    )
    both = ("brick", "batch")
    parts = tiles_x * tiles_y * lax.axis_size("batch")
    rows = 27 * width
    extra = -rows % (8 * parts)
    pieces = jnp.pad(partial_grad.astype(jnp.bfloat16), ((0, extra), (0, 0))).reshape(parts, -1, width)
    arrived = lax.all_to_all(pieces, both, 0, 0)
    summed = arrived.astype(jnp.float32).sum(0).astype(jnp.bfloat16)
    whole = lax.all_gather(summed, both, axis=0, tiled=True)
    weight_grad = whole[:rows].astype(jnp.float32).reshape(27, width, width)
    cot_ext = with_halo(cot.reshape(side, side, layers, width), tiles_y)
    cot_gathered = cot_ext[ext_index].reshape(rows_here, 27 * width)
    back = jnp.dot(cot_gathered, w_backward, preferred_element_type=jnp.float32)
    sig = jax.nn.sigmoid(z_val)
    feature_grad = (back * sig * (1.0 + z_val * (1.0 - sig))).astype(jnp.bfloat16)
    return (conv_out[None], feature_grad[None], weight_grad)


def shards(*arrays):
    peers = lax.axis_size("brick")
    bits = peers.bit_length() - 1
    tiles_x = 2 ** ((bits + 1) // 2)
    tiles_y = 2 ** (bits // 2)
    plan = whole_scene if tiles_y == 2 else halo_plan
    return plan(*arrays, tiles_x, tiles_y)


def solution(mesh):
    in_specs = (
        P(("groups", "batch"), "brick", None),
        P(("groups", "batch"), "brick", None),
        P(None, ("groups", "brick")),
        P(("groups", "batch")),
        P(("groups", "batch"), None),
        P(),
        P(),
    )
    out_specs = (
        P(("groups", "batch"), "brick", None),
        P(("groups", "batch"), "brick", None),
        P("groups", None, None),
    )
    return jax.shard_map(shards, mesh=mesh, in_specs=in_specs, out_specs=out_specs, check_vma=False)
```

```python
import functools

import jax
import jax.numpy as jnp
from jax import lax
from jax.experimental import pallas as pl
from jax.experimental.pallas import tpu as pltpu
from jax.sharding import PartitionSpec as P

LAYERS = 16
TILE = 4
STRIP = TILE * LAYERS
HALF = 13
CODE_ROWS = 16
KERNEL_VMEM = 24 * 1024 * 1024


def time_embedding(timesteps, width):
    half = width // 2
    freq = jnp.exp(-jnp.log(10000.0) * jnp.arange(half, dtype=jnp.float32) / half)
    angle = timesteps.astype(jnp.float32)[:, None] * freq[None, :]
    return jnp.concatenate([jnp.sin(angle), jnp.cos(angle)], axis=1).astype(jnp.bfloat16)


def strip_codes(neighbours, tiles_y):
    rows_here = TILE * STRIP
    code = (neighbours // rows_here) % tiles_y * STRIP + neighbours % STRIP
    return jnp.where(neighbours < 0, -1, code).astype(jnp.float32)


def pack_kernel(feat_ref, cot_ref, near_ref, temb_ref, cond_ref, wt_ref, pack_ref, z_ref, code_ref):
    rows, width = feat_ref.shape
    shift = jnp.dot(temb_ref[...], wt_ref[...], preferred_element_type=jnp.float32)
    shift = shift + cond_ref[...].astype(jnp.float32)
    z_val = feat_ref[...].astype(jnp.float32) + shift
    z_ref[...] = z_val
    pack_ref[:rows, :width] = (z_val * jax.nn.sigmoid(z_val)).astype(jnp.bfloat16)
    pack_ref[:rows, width:] = cot_ref[...]
    code = strip_codes(near_ref[...], 2)
    code_ref[...] = code.T
    pack_ref[rows:, :] = code[:CODE_ROWS, :].astype(jnp.bfloat16)


def lay_strip(ground, to, tile_y, mine_ref, other_ref, u):
    span = 2 * STRIP
    for ref, place in ((mine_ref, tile_y), (other_ref, 1 - tile_y)):
        at = pl.multiple_of(to * span + place * STRIP, STRIP)
        ground[pl.ds(at, STRIP), :] = ref[u * STRIP:(u + 1) * STRIP, :]


def row_kernel(stage, final, *refs):
    refs = list(refs)
    where_ref = refs.pop(0)
    rows_refs = [refs.pop(0) for _ in range(2 + 2 * (stage > 0) + 2 * final)]
    before = [refs.pop(0) for _ in range(3 * (stage > 0))]
    outs = [refs.pop(0) for _ in range(2 if final else 3)]
    ground, turned, codes, near_act, near_cot = refs
    width = ground.shape[1] // 2
    rows = TILE * STRIP
    span = 2 * STRIP
    tile_y = where_ref[0] % 2
    strips = [(rows_refs[0], rows_refs[1], u) for u in range(TILE)]
    if stage > 0:
        strips.append((rows_refs[2], rows_refs[3], 0))
    for i, (mine, other, u) in enumerate(strips):
        lay_strip(ground, i, tile_y, mine, other, u)
        pair = [ref[rows:, u * STRIP:(u + 1) * STRIP].astype(jnp.float32) for ref in (mine, other)]
        first = jnp.where(tile_y == 0, pair[0], pair[1])
        second = jnp.where(tile_y == 0, pair[1], pair[0])
        codes[i] = jnp.concatenate([first, second], axis=1)
    sources = list(range(TILE))
    if final:
        lay_strip(ground, TILE + 1, tile_y, rows_refs[4], rows_refs[5], TILE - 1)
        sources.append(TILE + 1)
    for i in sources:
        turned[:, i * span:(i + 1) * span] = ground[i * span:(i + 1) * span, :].T
    place = lax.broadcasted_iota(jnp.int32, (span, span), 0).astype(jnp.float32)

    def gather(target, source, start, stop):
        picks = [(place == codes[target, k:k + 1, :]).astype(jnp.bfloat16) for k in range(start, stop)]
        near = jnp.dot(turned[:, source * span:(source + 1) * span], jnp.concatenate(picks, axis=1),
                       preferred_element_type=jnp.float32).astype(jnp.bfloat16)
        for k in range(start, stop):
            one = near[:, (k - start) * span:(k - start + 1) * span]
            near_act[k * width:(k + 1) * width, target * span:(target + 1) * span] = one[:width]
            near_cot[k * width:(k + 1) * width, target * span:(target + 1) * span] = one[width:]

    for u in range(TILE):
        gather(u, u, 9, HALF)
        if u > 0:
            gather(u, u - 1, 0, 9)
    if stage > 0:
        gather(TILE, TILE - 1, 0, 9)
    if final:
        gather(0, TILE + 1, 0, 9)
    low_from = 0 if final else span
    low_to = span * (TILE + (stage > 0))

    def product(near, start, stop, first, last, side):
        return jnp.dot(near[start * width:stop * width, first:last],
                       ground[first:last, side * width:(side + 1) * width], preferred_element_type=jnp.float32)

    pieces = []
    for near, side in ((near_act, 1), (near_cot, 0)):
        pieces.append(((0, 9), product(near, 0, 9, low_from, low_to, side)))
        pieces.append(((9, HALF), product(near, 9, HALF, 0, TILE * span, side)))
    centre = jnp.dot(turned[:width, :TILE * span], ground[:TILE * span, width:], preferred_element_type=jnp.float32)
    if stage > 0:
        centre = centre + before[2][...]
    for i, ((start, stop), value) in enumerate(pieces):
        turn = i // 2
        if stage > 0:
            value = value + before[turn][start * width:stop * width, :]
        if not final:
            outs[turn][start * width:stop * width, :] = value
            continue
        for k in range(start, stop):
            one = value[(k - start) * width:(k - start + 1) * width, :]
            one, to = (one.T, 2 * HALF - k) if turn else (one, k)
            outs[0][to] = one
            outs[1][to] = one.astype(jnp.bfloat16)
    if final:
        outs[0][HALF] = centre
        outs[1][HALF] = centre.astype(jnp.bfloat16)
    else:
        outs[2][...] = centre


def voxel_kernel(where_ref, mine_ref, other_ref, before_mine, before_other, after_mine, after_other,
                 code_ref, z_ref, w_ref, conv_ref, grad_ref, ground, near_act, near_cot, w_back):
    rows, width = z_ref.shape
    span = 2 * STRIP
    tile_y = where_ref[0] % 2
    lay_strip(ground, 0, tile_y, before_mine, before_other, TILE - 1)
    for u in range(TILE):
        lay_strip(ground, u + 1, tile_y, mine_ref, other_ref, u)
    lay_strip(ground, TILE + 1, tile_y, after_mine, after_other, 0)
    place = lax.broadcasted_iota(jnp.int32, (STRIP, span), 1).astype(jnp.float32)
    for u in range(TILE):
        here = u * STRIP
        code = code_ref[here:here + STRIP, :]
        for side in range(3):
            block = ground[(u + side) * span:(u + side + 1) * span, :]
            ks = range(9 * side, 9 * side + 9)
            picks = [(code[:, k:k + 1] == place).astype(jnp.bfloat16) for k in ks]
            near = jnp.dot(jnp.concatenate(picks, axis=0), block, preferred_element_type=jnp.float32)
            near = near.astype(jnp.bfloat16)
            for k in ks:
                rows_k = near[(k - 9 * side) * STRIP:(k - 9 * side + 1) * STRIP, :]
                near_act[here:here + STRIP, k * width:(k + 1) * width] = rows_k[:, :width]
                near_cot[here:here + STRIP, k * width:(k + 1) * width] = rows_k[:, width:]
    for k in range(27):
        w_back[:, k * width:(k + 1) * width] = w_ref[26 - k]
    conv = jnp.dot(near_act[...], w_ref[...].reshape(27 * width, width), preferred_element_type=jnp.float32)
    conv_ref[...] = conv.astype(jnp.bfloat16)
    back = lax.dot_general(near_cot[...], w_back[...], (((1,), (1,)), ((), ())), preferred_element_type=jnp.float32)
    z_val = z_ref[...]
    sig = jax.nn.sigmoid(z_val)
    grad_ref[...] = (back * sig * (1.0 + z_val * (1.0 - sig))).astype(jnp.bfloat16)


def whole_scene(features, cotangent, neighbours, timesteps, condition, w_time, w_conv, tiles_x, tiles_y):
    rows, width = features.shape[1:]
    peers = tiles_x * tiles_y
    span = 2 * STRIP
    vmem = pl.BlockSpec(memory_space=pltpu.VMEM)
    smem = pl.BlockSpec(memory_space=pltpu.SMEM)
    params = pltpu.CompilerParams(vmem_limit_bytes=KERNEL_VMEM)
    temb = time_embedding(timesteps, width)
    packed, z_val, code = pl.pallas_call(
        pack_kernel,
        out_shape=(
            jax.ShapeDtypeStruct((rows + CODE_ROWS, 2 * width), jnp.bfloat16),
            jax.ShapeDtypeStruct((rows, width), jnp.float32),
            jax.ShapeDtypeStruct((rows, 27), jnp.float32),
        ),
        out_specs=(vmem, vmem, vmem),
        name="pack_tile",
    )(features[0], cotangent[0], neighbours, temb, condition, w_time)
    here = lax.axis_index("brick").astype(jnp.int32).reshape(1)
    across = [(i, i ^ 1) for i in range(peers)]
    own_pair = (packed, lax.ppermute(packed, "brick", across))
    pairs = [own_pair]
    for turn in range(1, tiles_x):
        mine = lax.ppermute(packed, "brick", [(i, (i + turn * tiles_y) % peers) for i in range(peers)])
        pairs.append((mine, None))
    sums = ()
    for stage in range(tiles_x):
        final = stage == tiles_x - 1
        blocks = pairs[stage]
        if stage > 0:
            blocks = blocks + pairs[stage - 1]
        if final:
            blocks = blocks + own_pair
            out_shape = (
                jax.ShapeDtypeStruct((27, width, width), jnp.float32),
                jax.ShapeDtypeStruct((27, width, width), jnp.bfloat16),
            )
        else:
            out_shape = (
                jax.ShapeDtypeStruct((HALF * width, width), jnp.float32),
                jax.ShapeDtypeStruct((HALF * width, width), jnp.float32),
                jax.ShapeDtypeStruct((width, width), jnp.float32),
            )
        sums = pl.pallas_call(
            functools.partial(row_kernel, stage, final),
            out_shape=out_shape,
            in_specs=[smem] + [vmem] * (len(blocks) + len(sums)),
            out_specs=(vmem,) * len(out_shape),
            scratch_shapes=[
                pltpu.VMEM(((TILE + 2) * span, 2 * width), jnp.bfloat16),
                pltpu.VMEM((2 * width, (TILE + 2) * span), jnp.bfloat16),
                pltpu.VMEM((TILE + 1, CODE_ROWS, span), jnp.float32),
                pltpu.VMEM((HALF * width, (TILE + 1) * span), jnp.bfloat16),
                pltpu.VMEM((HALF * width, (TILE + 1) * span), jnp.bfloat16),
            ],
            compiler_params=params,
            cost_estimate=pl.CostEstimate(flops=2 * 10**9, bytes_accessed=4 * 10**6, transcendentals=0),
            name=f"weight_row_{stage}",
        )(here, *blocks, *sums)
        if stage == 0:
            for turn in range(1, tiles_x):
                mine, centre = lax.optimization_barrier((pairs[turn][0], sums[2]))
                sums = (sums[0], sums[1], centre)
                pairs[turn] = (mine, lax.ppermute(mine, "brick", across))
    own, sent = sums
    other = lax.ppermute(sent, "batch", [(0, 1), (1, 0)])
    conv_out, feature_grad = pl.pallas_call(
        voxel_kernel,
        out_shape=(
            jax.ShapeDtypeStruct((rows, width), jnp.bfloat16),
            jax.ShapeDtypeStruct((rows, width), jnp.bfloat16),
        ),
        in_specs=[smem] + [vmem] * 9,
        scratch_shapes=[
            pltpu.VMEM(((TILE + 2) * span, 2 * width), jnp.bfloat16),
            pltpu.VMEM((rows, 27 * width), jnp.bfloat16),
            pltpu.VMEM((rows, 27 * width), jnp.bfloat16),
            pltpu.VMEM((width, 27 * width), jnp.bfloat16),
        ],
        compiler_params=params,
        cost_estimate=pl.CostEstimate(flops=10**9, bytes_accessed=4 * 10**6, transcendentals=0),
        name="voxel_outputs",
    )(here, *own_pair, *pairs[1], *pairs[tiles_x - 1], code, z_val, w_conv)
    weight_grad = own + other.astype(jnp.float32)
    return (conv_out[None], feature_grad[None], weight_grad)


def passed_along(block, axis, distance):
    devices = range(lax.axis_size(axis))
    route = [(i - distance, i) for i in devices if i - distance in devices]
    return lax.ppermute(block, axis, route)


def slab_rows(block, side_recv, front_recv, width):
    widened = jnp.concatenate([side_recv[0], block, side_recv[1]], axis=1)
    slab = jnp.concatenate([front_recv[0][None], widened, front_recv[1][None]], axis=0)
    flat = slab.reshape(-1, width)
    return jnp.concatenate([flat, jnp.zeros((1, width), jnp.bfloat16)], axis=0)


def with_halo(block, tiles_y):
    width = block.shape[-1]
    side = TILE
    side_recv = tuple(passed_along(block[:, edge], "brick", by)[:, None] for by, edge in ((1, side - 1), (-1, 0)))
    wide = jnp.concatenate([side_recv[0], block, side_recv[1]], axis=1)
    front_recv = tuple(passed_along(wide[edge], "brick", by) for by, edge in ((tiles_y, side - 1), (-tiles_y, 0)))
    return slab_rows(block, side_recv, front_recv, width)


def halo_plan(features, cotangent, neighbours, timesteps, condition, w_time, w_conv, tiles_x, tiles_y):
    rows_here, width = features.shape[1:]
    here = lax.axis_index("brick")
    tile_x = here // tiles_y
    tile_y = here % tiles_y
    side = TILE
    layers = LAYERS
    wide = side + 2
    valid = neighbours >= 0
    safe = jnp.where(valid, neighbours, 0)
    owner = safe // rows_here
    inside = safe % rows_here
    column = inside // layers
    layer = inside % layers
    local_x = (owner // tiles_y - tile_x) * side + column // side + 1
    local_y = (owner % tiles_y - tile_y) * side + column % side + 1
    sentinel = wide * wide * layers
    ext_index = jnp.where(valid, (local_x * wide + local_y) * layers + layer, sentinel).T
    temb = time_embedding(timesteps, width)
    shift = jnp.dot(temb, w_time, preferred_element_type=jnp.float32) + condition.astype(jnp.float32)
    z_val = features[0].astype(jnp.float32) + shift[0][None, :]
    act = jax.nn.silu(z_val).astype(jnp.bfloat16)
    cot = cotangent[0]
    w_forward = w_conv.reshape(27 * width, width)
    w_backward = jnp.transpose(w_conv[::-1], (0, 2, 1)).reshape(27 * width, width)
    act_ext = with_halo(act.reshape(side, side, layers, width), tiles_y)
    gathered = act_ext[ext_index].reshape(rows_here, 27 * width)
    conv_out = jnp.dot(gathered, w_forward, preferred_element_type=jnp.float32).astype(jnp.bfloat16)
    partial_grad = lax.dot_general(
        gathered, cot, (((0,), (0,)), ((), ())), preferred_element_type=jnp.float32
    )
    both = ("brick", "batch")
    parts = tiles_x * tiles_y * lax.axis_size("batch")
    rows = 27 * width
    extra = -rows % (8 * parts)
    pieces = jnp.pad(partial_grad.astype(jnp.bfloat16), ((0, extra), (0, 0))).reshape(parts, -1, width)
    arrived = lax.all_to_all(pieces, both, 0, 0)
    summed = arrived.astype(jnp.float32).sum(0).astype(jnp.bfloat16)
    whole = lax.all_gather(summed, both, axis=0, tiled=True)
    weight_grad = whole[:rows].astype(jnp.float32).reshape(27, width, width)
    cot_ext = with_halo(cot.reshape(side, side, layers, width), tiles_y)
    cot_gathered = cot_ext[ext_index].reshape(rows_here, 27 * width)
    back = jnp.dot(cot_gathered, w_backward, preferred_element_type=jnp.float32)
    sig = jax.nn.sigmoid(z_val)
    feature_grad = (back * sig * (1.0 + z_val * (1.0 - sig))).astype(jnp.bfloat16)
    return (conv_out[None], feature_grad[None], weight_grad)


def shards(*arrays):
    peers = lax.axis_size("brick")
    bits = peers.bit_length() - 1
    tiles_x = 2 ** ((bits + 1) // 2)
    tiles_y = 2 ** (bits // 2)
    plan = whole_scene if tiles_y == 2 else halo_plan
    return plan(*arrays, tiles_x, tiles_y)


def solution(mesh):
    in_specs = (
        P(("groups", "batch"), "brick", None),
        P(("groups", "batch"), "brick", None),
        P(None, ("groups", "brick")),
        P(("groups", "batch")),
        P(("groups", "batch"), None),
        P(),
        P(),
    )
    out_specs = (
        P(("groups", "batch"), "brick", None),
        P(("groups", "batch"), "brick", None),
        P("groups", None, None),
    )
    return jax.shard_map(shards, mesh=mesh, in_specs=in_specs, out_specs=out_specs, check_vma=False)
```

```python
import functools

import jax
import jax.numpy as jnp
from jax import lax
from jax.experimental import pallas as pl
from jax.experimental.pallas import tpu as pltpu
from jax.sharding import PartitionSpec as P

LAYERS = 16
TILE = 4
STRIP = TILE * LAYERS
HALF = 13
CODE_ROWS = 16
ROW_STAGES = 4
KERNEL_VMEM = 24 * 1024 * 1024
PACK_VMEM = 4 * 1024 * 1024


def time_embedding(timesteps, width):
    half = width // 2
    freq = jnp.exp(-jnp.log(10000.0) * jnp.arange(half, dtype=jnp.float32) / half)
    angle = timesteps.astype(jnp.float32)[:, None] * freq[None, :]
    return jnp.concatenate([jnp.sin(angle), jnp.cos(angle)], axis=1).astype(jnp.bfloat16)


def strip_codes(neighbours, tiles_y):
    rows_here = TILE * STRIP
    code = (neighbours // rows_here) % tiles_y * STRIP + neighbours % STRIP
    return jnp.where(neighbours < 0, -1, code).astype(jnp.float32)


def pack_kernel(time_ref, feat_hbm, cot_hbm, near_hbm, cond_hbm, wt_hbm, pack_ref, z_ref, code_ref,
                feat_ref, near_ref, cond_ref, wt_ref, sems):
    rows, width = feat_ref.shape
    half = width // 2
    moves = (
        (wt_hbm, wt_ref),
        (cond_hbm, cond_ref),
        (feat_hbm.at[0], feat_ref),
        (near_hbm, near_ref),
        (cot_hbm.at[0], pack_ref.at[:rows, width:]),
    )
    copies = [pltpu.make_async_copy(source, to, sems.at[i]) for i, (source, to) in enumerate(moves)]
    for copy in copies:
        copy.start()
    lane = lax.broadcasted_iota(jnp.int32, (1, width), 1)
    freq = jnp.exp(-jnp.log(10000.0) * (lane % half).astype(jnp.float32) / half)
    angle = time_ref[0].astype(jnp.float32) * freq
    temb = jnp.where(lane < half, jnp.sin(angle), jnp.cos(angle)).astype(jnp.bfloat16)
    copies[0].wait()
    copies[1].wait()
    shift = jnp.dot(temb, wt_ref[...], preferred_element_type=jnp.float32)
    shift = shift + cond_ref[...].astype(jnp.float32)
    copies[2].wait()
    z_val = feat_ref[...].astype(jnp.float32) + shift
    z_ref[...] = z_val
    pack_ref[:rows, :width] = (z_val * jax.nn.sigmoid(z_val)).astype(jnp.bfloat16)
    copies[3].wait()
    code = strip_codes(near_ref[...], 2)
    code_ref[...] = code.T
    pack_ref[rows:, :] = code[:CODE_ROWS, :].astype(jnp.bfloat16)
    copies[4].wait()


def lay_strip(ground, to, tile_y, mine_ref, other_ref, u):
    span = 2 * STRIP
    for ref, place in ((mine_ref, tile_y), (other_ref, 1 - tile_y)):
        at = pl.multiple_of(to * span + place * STRIP, STRIP)
        ground[pl.ds(at, STRIP), :] = ref[u * STRIP:(u + 1) * STRIP, :]


def row_kernel(stage, strips, borders, *refs):
    refs = list(refs)
    first_stage, final = stage == 0, stage == ROW_STAGES - 1
    where_ref = refs.pop(0)
    pairs = [(refs.pop(0), refs.pop(0)) for _ in range(1 + max(pair for pair, _ in strips))]
    before = [refs.pop(0) for _ in range(0 if first_stage else 3)]
    outs = [refs.pop(0) for _ in range(2 if final else 3)]
    ground, turned, codes, near_act, near_cot = refs
    width = ground.shape[1] // 2
    rows = TILE * STRIP
    span = 2 * STRIP
    tile_y = where_ref[0] % 2
    borders = [(u, u - 1) for u in range(1, TILE)] + borders
    targets = sorted({target for target, _ in borders})
    for i, (pair, u) in enumerate(strips):
        lay_strip(ground, i, tile_y, *pairs[pair], u)
        if i < TILE or i in targets:
            both = [ref[rows:, u * STRIP:(u + 1) * STRIP].astype(jnp.float32) for ref in pairs[pair]]
            first = jnp.where(tile_y == 0, both[0], both[1])
            second = jnp.where(tile_y == 0, both[1], both[0])
            codes[i] = jnp.concatenate([first, second], axis=1)
        if i < TILE or i in [source for _, source in borders]:
            turned[:, i * span:(i + 1) * span] = ground[i * span:(i + 1) * span, :].T
    place = lax.broadcasted_iota(jnp.int32, (span, span), 0).astype(jnp.float32)

    def gather(target, source, start, stop):
        picks = [(place == codes[target, k:k + 1, :]).astype(jnp.bfloat16) for k in range(start, stop)]
        near = jnp.dot(turned[:, source * span:(source + 1) * span], jnp.concatenate(picks, axis=1),
                       preferred_element_type=jnp.float32).astype(jnp.bfloat16)
        for k in range(start, stop):
            one = near[:, (k - start) * span:(k - start + 1) * span]
            near_act[k * width:(k + 1) * width, target * span:(target + 1) * span] = one[:width]
            near_cot[k * width:(k + 1) * width, target * span:(target + 1) * span] = one[width:]

    for u in range(TILE):
        gather(u, u, 9, HALF)
    for target, source in borders:
        gather(target, source, 0, 9)
    low_from = span * targets[0]
    low_to = span * (targets[-1] + 1)

    def product(near, start, stop, first, last, side):
        return jnp.dot(near[start * width:stop * width, first:last],
                       ground[first:last, side * width:(side + 1) * width], preferred_element_type=jnp.float32)

    pieces = []
    for near, side in ((near_act, 1), (near_cot, 0)):
        pieces.append(((0, 9), product(near, 0, 9, low_from, low_to, side)))
        pieces.append(((9, HALF), product(near, 9, HALF, 0, TILE * span, side)))
    centre = jnp.dot(turned[:width, :TILE * span], ground[:TILE * span, width:], preferred_element_type=jnp.float32)
    if not first_stage:
        centre = centre + before[2][...]
    for i, ((start, stop), value) in enumerate(pieces):
        turn = i // 2
        if not first_stage:
            value = value + before[turn][start * width:stop * width, :]
        if not final:
            outs[turn][start * width:stop * width, :] = value
            continue
        for k in range(start, stop):
            one = value[(k - start) * width:(k - start + 1) * width, :]
            one, to = (one.T, 2 * HALF - k) if turn else (one, k)
            outs[0][to] = one
            outs[1][to] = one.astype(jnp.bfloat16)
    if final:
        outs[0][HALF] = centre
        outs[1][HALF] = centre.astype(jnp.bfloat16)
    else:
        outs[2][...] = centre


def voxel_kernel(where_ref, mine_ref, other_ref, before_mine, before_other, after_mine, after_other,
                 code_ref, z_ref, w_ref, conv_ref, grad_ref, ground, near_act, near_cot, w_back):
    rows, width = z_ref.shape
    span = 2 * STRIP
    tile_y = where_ref[0] % 2
    lay_strip(ground, 0, tile_y, before_mine, before_other, TILE - 1)
    for u in range(TILE):
        lay_strip(ground, u + 1, tile_y, mine_ref, other_ref, u)
    lay_strip(ground, TILE + 1, tile_y, after_mine, after_other, 0)
    place = lax.broadcasted_iota(jnp.int32, (STRIP, span), 1).astype(jnp.float32)
    for u in range(TILE):
        here = u * STRIP
        code = code_ref[here:here + STRIP, :]
        for side in range(3):
            block = ground[(u + side) * span:(u + side + 1) * span, :]
            ks = range(9 * side, 9 * side + 9)
            picks = [(code[:, k:k + 1] == place).astype(jnp.bfloat16) for k in ks]
            near = jnp.dot(jnp.concatenate(picks, axis=0), block, preferred_element_type=jnp.float32)
            near = near.astype(jnp.bfloat16)
            for k in ks:
                rows_k = near[(k - 9 * side) * STRIP:(k - 9 * side + 1) * STRIP, :]
                near_act[here:here + STRIP, k * width:(k + 1) * width] = rows_k[:, :width]
                near_cot[here:here + STRIP, k * width:(k + 1) * width] = rows_k[:, width:]
    for k in range(27):
        w_back[:, k * width:(k + 1) * width] = w_ref[26 - k]
    conv = jnp.dot(near_act[...], w_ref[...].reshape(27 * width, width), preferred_element_type=jnp.float32)
    conv_ref[...] = conv.astype(jnp.bfloat16)
    back = lax.dot_general(near_cot[...], w_back[...], (((1,), (1,)), ((), ())), preferred_element_type=jnp.float32)
    z_val = z_ref[...]
    sig = jax.nn.sigmoid(z_val)
    grad_ref[...] = (back * sig * (1.0 + z_val * (1.0 - sig))).astype(jnp.bfloat16)


def whole_scene(features, cotangent, neighbours, timesteps, condition, w_time, w_conv, tiles_x, tiles_y):
    rows, width = features.shape[1:]
    peers = tiles_x * tiles_y
    span = 2 * STRIP
    vmem = pl.BlockSpec(memory_space=pltpu.VMEM)
    smem = pl.BlockSpec(memory_space=pltpu.SMEM)
    params = pltpu.CompilerParams(vmem_limit_bytes=KERNEL_VMEM)
    packed, z_val, code = pl.pallas_call(
        pack_kernel,
        out_shape=(
            jax.ShapeDtypeStruct((rows + CODE_ROWS, 2 * width), jnp.bfloat16),
            jax.ShapeDtypeStruct((rows, width), jnp.float32),
            jax.ShapeDtypeStruct((rows, 27), jnp.float32),
        ),
        in_specs=[smem] + [pl.BlockSpec(memory_space=pltpu.HBM)] * 5,
        out_specs=(vmem, vmem, vmem),
        scratch_shapes=[
            pltpu.VMEM((rows, width), jnp.bfloat16),
            pltpu.VMEM(neighbours.shape, jnp.int32),
            pltpu.VMEM((1, width), jnp.bfloat16),
            pltpu.VMEM((width, width), jnp.bfloat16),
            pltpu.SemaphoreType.DMA((5,)),
        ],
        compiler_params=pltpu.CompilerParams(vmem_limit_bytes=PACK_VMEM),
        name="pack_tile",
    )(timesteps, features, cotangent, neighbours, condition, w_time)
    here = lax.axis_index("brick").astype(jnp.int32).reshape(1)

    def across(block):
        return lax.ppermute(block, "brick", [(i, i ^ 1) for i in range(peers)])

    def along(block, turn):
        return lax.ppermute(block, "brick", [(i, (i + turn * tiles_y) % peers) for i in range(peers)])

    before, after = along(packed, 1), along(packed, -1)
    far = along(before, 1)
    own_pair = (packed, across(packed))
    before_pair = (before, across(before))
    after_pair = (after, across(after))
    far_pair = (far, across(far))
    line = [(0, u) for u in range(TILE)]
    stages = (
        ((own_pair,), line, []),
        ((before_pair, own_pair), line + [(1, 0)], [(TILE, TILE - 1)]),
        ((after_pair, own_pair), line + [(1, TILE - 1)], [(0, TILE)]),
        ((far_pair, before_pair, after_pair), line + [(1, 0), (2, TILE - 1)], [(TILE, TILE - 1), (0, TILE + 1)]),
    )
    sums = ()
    for stage, (pairs, strips, borders) in enumerate(stages):
        blocks = [block for pair in pairs for block in pair]
        if stage == ROW_STAGES - 1:
            out_shape = (
                jax.ShapeDtypeStruct((27, width, width), jnp.float32),
                jax.ShapeDtypeStruct((27, width, width), jnp.bfloat16),
            )
        else:
            out_shape = (
                jax.ShapeDtypeStruct((HALF * width, width), jnp.float32),
                jax.ShapeDtypeStruct((HALF * width, width), jnp.float32),
                jax.ShapeDtypeStruct((width, width), jnp.float32),
            )
        sums = pl.pallas_call(
            functools.partial(row_kernel, stage, strips, borders),
            out_shape=out_shape,
            in_specs=[smem] + [vmem] * (len(blocks) + len(sums)),
            out_specs=(vmem,) * len(out_shape),
            scratch_shapes=[
                pltpu.VMEM(((TILE + 2) * span, 2 * width), jnp.bfloat16),
                pltpu.VMEM((2 * width, (TILE + 2) * span), jnp.bfloat16),
                pltpu.VMEM((TILE + 1, CODE_ROWS, span), jnp.float32),
                pltpu.VMEM((HALF * width, (TILE + 1) * span), jnp.bfloat16),
                pltpu.VMEM((HALF * width, (TILE + 1) * span), jnp.bfloat16),
            ],
            compiler_params=params,
            cost_estimate=pl.CostEstimate(flops=2 * 10**9, bytes_accessed=4 * 10**6, transcendentals=0),
            name=f"weight_row_{stage}",
        )(here, *blocks, *sums)
    own, sent = sums
    other = lax.ppermute(sent, "batch", [(0, 1), (1, 0)])
    conv_out, feature_grad = pl.pallas_call(
        voxel_kernel,
        out_shape=(
            jax.ShapeDtypeStruct((rows, width), jnp.bfloat16),
            jax.ShapeDtypeStruct((rows, width), jnp.bfloat16),
        ),
        in_specs=[smem] + [vmem] * 9,
        scratch_shapes=[
            pltpu.VMEM(((TILE + 2) * span, 2 * width), jnp.bfloat16),
            pltpu.VMEM((rows, 27 * width), jnp.bfloat16),
            pltpu.VMEM((rows, 27 * width), jnp.bfloat16),
            pltpu.VMEM((width, 27 * width), jnp.bfloat16),
        ],
        compiler_params=params,
        cost_estimate=pl.CostEstimate(flops=10**9, bytes_accessed=4 * 10**6, transcendentals=0),
        name="voxel_outputs",
    )(here, *own_pair, *before_pair, *after_pair, code, z_val, w_conv)
    weight_grad = own + other.astype(jnp.float32)
    return (conv_out[None], feature_grad[None], weight_grad)


def passed_along(block, axis, distance):
    devices = range(lax.axis_size(axis))
    route = [(i - distance, i) for i in devices if i - distance in devices]
    return lax.ppermute(block, axis, route)


def slab_rows(block, side_recv, front_recv, width):
    widened = jnp.concatenate([side_recv[0], block, side_recv[1]], axis=1)
    slab = jnp.concatenate([front_recv[0][None], widened, front_recv[1][None]], axis=0)
    flat = slab.reshape(-1, width)
    return jnp.concatenate([flat, jnp.zeros((1, width), jnp.bfloat16)], axis=0)


def with_halo(block, tiles_y):
    width = block.shape[-1]
    side = TILE
    side_recv = tuple(passed_along(block[:, edge], "brick", by)[:, None] for by, edge in ((1, side - 1), (-1, 0)))
    wide = jnp.concatenate([side_recv[0], block, side_recv[1]], axis=1)
    front_recv = tuple(passed_along(wide[edge], "brick", by) for by, edge in ((tiles_y, side - 1), (-tiles_y, 0)))
    return slab_rows(block, side_recv, front_recv, width)


def halo_plan(features, cotangent, neighbours, timesteps, condition, w_time, w_conv, tiles_x, tiles_y):
    rows_here, width = features.shape[1:]
    here = lax.axis_index("brick")
    tile_x = here // tiles_y
    tile_y = here % tiles_y
    side = TILE
    layers = LAYERS
    wide = side + 2
    valid = neighbours >= 0
    safe = jnp.where(valid, neighbours, 0)
    owner = safe // rows_here
    inside = safe % rows_here
    column = inside // layers
    layer = inside % layers
    local_x = (owner // tiles_y - tile_x) * side + column // side + 1
    local_y = (owner % tiles_y - tile_y) * side + column % side + 1
    sentinel = wide * wide * layers
    ext_index = jnp.where(valid, (local_x * wide + local_y) * layers + layer, sentinel).T
    temb = time_embedding(timesteps, width)
    shift = jnp.dot(temb, w_time, preferred_element_type=jnp.float32) + condition.astype(jnp.float32)
    z_val = features[0].astype(jnp.float32) + shift[0][None, :]
    act = jax.nn.silu(z_val).astype(jnp.bfloat16)
    cot = cotangent[0]
    w_forward = w_conv.reshape(27 * width, width)
    w_backward = jnp.transpose(w_conv[::-1], (0, 2, 1)).reshape(27 * width, width)
    act_ext = with_halo(act.reshape(side, side, layers, width), tiles_y)
    gathered = act_ext[ext_index].reshape(rows_here, 27 * width)
    conv_out = jnp.dot(gathered, w_forward, preferred_element_type=jnp.float32).astype(jnp.bfloat16)
    partial_grad = lax.dot_general(
        gathered, cot, (((0,), (0,)), ((), ())), preferred_element_type=jnp.float32
    )
    both = ("brick", "batch")
    parts = tiles_x * tiles_y * lax.axis_size("batch")
    rows = 27 * width
    extra = -rows % (8 * parts)
    pieces = jnp.pad(partial_grad.astype(jnp.bfloat16), ((0, extra), (0, 0))).reshape(parts, -1, width)
    arrived = lax.all_to_all(pieces, both, 0, 0)
    summed = arrived.astype(jnp.float32).sum(0).astype(jnp.bfloat16)
    whole = lax.all_gather(summed, both, axis=0, tiled=True)
    weight_grad = whole[:rows].astype(jnp.float32).reshape(27, width, width)
    cot_ext = with_halo(cot.reshape(side, side, layers, width), tiles_y)
    cot_gathered = cot_ext[ext_index].reshape(rows_here, 27 * width)
    back = jnp.dot(cot_gathered, w_backward, preferred_element_type=jnp.float32)
    sig = jax.nn.sigmoid(z_val)
    feature_grad = (back * sig * (1.0 + z_val * (1.0 - sig))).astype(jnp.bfloat16)
    return (conv_out[None], feature_grad[None], weight_grad)


def shards(*arrays):
    peers = lax.axis_size("brick")
    bits = peers.bit_length() - 1
    tiles_x = 2 ** ((bits + 1) // 2)
    tiles_y = 2 ** (bits // 2)
    plan = whole_scene if (tiles_x, tiles_y) == (ROW_STAGES, 2) else halo_plan
    return plan(*arrays, tiles_x, tiles_y)


def solution(mesh):
    in_specs = (
        P(("groups", "batch"), "brick", None),
        P(("groups", "batch"), "brick", None),
        P(None, ("groups", "brick")),
        P(("groups", "batch")),
        P(("groups", "batch"), None),
        P(),
        P(),
    )
    out_specs = (
        P(("groups", "batch"), "brick", None),
        P(("groups", "batch"), "brick", None),
        P("groups", None, None),
    )
    return jax.shard_map(shards, mesh=mesh, in_specs=in_specs, out_specs=out_specs, check_vma=False)
```

```python
import functools

import jax
import jax.numpy as jnp
from jax import lax
from jax.experimental import pallas as pl
from jax.experimental.pallas import tpu as pltpu
from jax.sharding import PartitionSpec as P

LAYERS = 16
TILE = 4
STRIP = TILE * LAYERS
HALF = 13
CODE_ROWS = 16
ROW_STAGES = 4
KERNEL_VMEM = 24 * 1024 * 1024


def time_embedding(timesteps, width):
    half = width // 2
    freq = jnp.exp(-jnp.log(10000.0) * jnp.arange(half, dtype=jnp.float32) / half)
    angle = timesteps.astype(jnp.float32)[:, None] * freq[None, :]
    return jnp.concatenate([jnp.sin(angle), jnp.cos(angle)], axis=1).astype(jnp.bfloat16)


def strip_codes(neighbours, tiles_y):
    rows_here = TILE * STRIP
    code = (neighbours // rows_here) % tiles_y * STRIP + neighbours % STRIP
    return jnp.where(neighbours < 0, -1, code).astype(jnp.float32)


def pack_kernel(time_ref, feat_hbm, cot_hbm, near_hbm, cond_hbm, wt_hbm, pack_ref, shift_ref,
                feat_ref, near_ref, cond_ref, wt_ref, sems):
    rows, width = feat_ref.shape
    half = width // 2
    moves = (
        (wt_hbm, wt_ref),
        (cond_hbm, cond_ref),
        (feat_hbm.at[0], feat_ref),
        (near_hbm, near_ref),
        (cot_hbm.at[0], pack_ref.at[:rows, width:]),
    )
    copies = [pltpu.make_async_copy(source, to, sems.at[i]) for i, (source, to) in enumerate(moves)]
    for copy in copies:
        copy.start()
    lane = lax.broadcasted_iota(jnp.int32, (1, width), 1)
    freq = jnp.exp(-jnp.log(10000.0) * (lane % half).astype(jnp.float32) / half)
    angle = time_ref[0].astype(jnp.float32) * freq
    temb = jnp.where(lane < half, jnp.sin(angle), jnp.cos(angle)).astype(jnp.bfloat16)
    copies[0].wait()
    copies[1].wait()
    shift = jnp.dot(temb, wt_ref[...], preferred_element_type=jnp.float32)
    shift = shift + cond_ref[...].astype(jnp.float32)
    copies[2].wait()
    z_val = feat_ref[...].astype(jnp.float32) + shift
    shift_ref[...] = shift
    pack_ref[:rows, :width] = (z_val * jax.nn.sigmoid(z_val)).astype(jnp.bfloat16)
    copies[3].wait()
    pack_ref[rows:, :] = strip_codes(near_ref[:CODE_ROWS, :], 2).astype(jnp.bfloat16)
    copies[4].wait()


def lay_strip(ground, to, tile_y, mine_ref, other_ref, u):
    span = 2 * STRIP
    for ref, place in ((mine_ref, tile_y), (other_ref, 1 - tile_y)):
        at = pl.multiple_of(to * span + place * STRIP, STRIP)
        ground[pl.ds(at, STRIP), :] = ref[u * STRIP:(u + 1) * STRIP, :]


def row_kernel(stage, strips, borders, *refs):
    refs = list(refs)
    first_stage, final = stage == 0, stage == ROW_STAGES - 1
    where_ref = refs.pop(0)
    pairs = [(refs.pop(0), refs.pop(0)) for _ in range(1 + max(pair for pair, _ in strips))]
    before = [refs.pop(0) for _ in range(0 if first_stage else 3)]
    outs = [refs.pop(0) for _ in range(2 if final else 3)]
    ground, turned, codes, near_act, near_cot = refs
    width = ground.shape[1] // 2
    rows = TILE * STRIP
    span = 2 * STRIP
    tile_y = where_ref[0] % 2
    borders = [(u, u - 1) for u in range(1, TILE)] + borders
    targets = sorted({target for target, _ in borders})
    for i, (pair, u) in enumerate(strips):
        lay_strip(ground, i, tile_y, *pairs[pair], u)
        if i < TILE or i in targets:
            both = [ref[rows:, u * STRIP:(u + 1) * STRIP].astype(jnp.float32) for ref in pairs[pair]]
            first = jnp.where(tile_y == 0, both[0], both[1])
            second = jnp.where(tile_y == 0, both[1], both[0])
            codes[i] = jnp.concatenate([first, second], axis=1)
        if i < TILE or i in [source for _, source in borders]:
            turned[:, i * span:(i + 1) * span] = ground[i * span:(i + 1) * span, :].T
    place = lax.broadcasted_iota(jnp.int32, (span, span), 0).astype(jnp.float32)

    def gather(target, source, start, stop):
        picks = [(place == codes[target, k:k + 1, :]).astype(jnp.bfloat16) for k in range(start, stop)]
        near = jnp.dot(turned[:, source * span:(source + 1) * span], jnp.concatenate(picks, axis=1),
                       preferred_element_type=jnp.float32).astype(jnp.bfloat16)
        for k in range(start, stop):
            one = near[:, (k - start) * span:(k - start + 1) * span]
            near_act[k * width:(k + 1) * width, target * span:(target + 1) * span] = one[:width]
            near_cot[k * width:(k + 1) * width, target * span:(target + 1) * span] = one[width:]

    for u in range(TILE):
        gather(u, u, 9, HALF)
    for target, source in borders:
        gather(target, source, 0, 9)
    low_from = span * targets[0]
    low_to = span * (targets[-1] + 1)

    def product(near, start, stop, first, last, side):
        return jnp.dot(near[start * width:stop * width, first:last],
                       ground[first:last, side * width:(side + 1) * width], preferred_element_type=jnp.float32)

    pieces = []
    for near, side in ((near_act, 1), (near_cot, 0)):
        pieces.append(((0, 9), product(near, 0, 9, low_from, low_to, side)))
        pieces.append(((9, HALF), product(near, 9, HALF, 0, TILE * span, side)))
    centre = jnp.dot(turned[:width, :TILE * span], ground[:TILE * span, width:], preferred_element_type=jnp.float32)
    if not first_stage:
        centre = centre + before[2][...]
    for i, ((start, stop), value) in enumerate(pieces):
        turn = i // 2
        if not first_stage:
            value = value + before[turn][start * width:stop * width, :]
        if not final:
            outs[turn][start * width:stop * width, :] = value
            continue
        for k in range(start, stop):
            one = value[(k - start) * width:(k - start + 1) * width, :]
            one, to = (one.T, 2 * HALF - k) if turn else (one, k)
            outs[0][to] = one
            outs[1][to] = one.astype(jnp.bfloat16)
    if final:
        outs[0][HALF] = centre
        outs[1][HALF] = centre.astype(jnp.bfloat16)
    else:
        outs[2][...] = centre


def turn_kernel(w_ref, forward_ref, back_ref):
    width = w_ref.shape[1]
    for k in range(27):
        forward_ref[:, k * width:(k + 1) * width] = w_ref[k].T
        back_ref[:, k * width:(k + 1) * width] = w_ref[26 - k]


def voxel_kernel(where_ref, mine_ref, other_ref, before_mine, before_other, after_mine, after_other,
                 near_ref, feat_ref, shift_ref, forward_ref, back_ref, conv_ref, grad_ref,
                 ground, turned, codes, near_act, near_cot):
    width = feat_ref.shape[1]
    span = 2 * STRIP
    tile_y = where_ref[0] % 2
    lay_strip(ground, 0, tile_y, before_mine, before_other, TILE - 1)
    for u in range(TILE):
        lay_strip(ground, u + 1, tile_y, mine_ref, other_ref, u)
    lay_strip(ground, TILE + 1, tile_y, after_mine, after_other, 0)
    for i in range(TILE + 2):
        turned[:, i * span:(i + 1) * span] = ground[i * span:(i + 1) * span, :].T
    code = strip_codes(near_ref[...], 2)
    lane = lax.broadcasted_iota(jnp.int32, code.shape, 1)
    codes[...] = jnp.where((code >= 0) & (lane // STRIP % 2 == 1), code + span, code)
    place = lax.broadcasted_iota(jnp.int32, (2 * span, span), 0).astype(jnp.float32)
    for half in range(TILE // 2):
        at = half * span
        for side in range(3):
            source = (2 * half + side) * span
            ks = range(9 * side, 9 * side + 9)
            picks = [(place == codes[k:k + 1, at:at + span]).astype(jnp.bfloat16) for k in ks]
            near = jnp.dot(turned[:, source:source + 2 * span], jnp.concatenate(picks, axis=1),
                           preferred_element_type=jnp.float32).astype(jnp.bfloat16)
            for k in ks:
                one = near[:, (k - 9 * side) * span:(k - 9 * side + 1) * span]
                near_act[k * width:(k + 1) * width, at:at + span] = one[:width]
                near_cot[k * width:(k + 1) * width, at:at + span] = one[width:]
    conv = jnp.dot(forward_ref[...], near_act[...], preferred_element_type=jnp.float32)
    conv_ref[...] = conv.T.astype(jnp.bfloat16)
    back = jnp.dot(back_ref[...], near_cot[...], preferred_element_type=jnp.float32).T
    z_val = feat_ref[...].astype(jnp.float32) + shift_ref[...]
    sig = jax.nn.sigmoid(z_val)
    grad_ref[...] = (back * sig * (1.0 + z_val * (1.0 - sig))).astype(jnp.bfloat16)


def whole_scene(features, cotangent, neighbours, timesteps, condition, w_time, w_conv, tiles_x, tiles_y):
    rows, width = features.shape[1:]
    peers = tiles_x * tiles_y
    span = 2 * STRIP
    vmem = pl.BlockSpec(memory_space=pltpu.VMEM)
    smem = pl.BlockSpec(memory_space=pltpu.SMEM)
    params = pltpu.CompilerParams(vmem_limit_bytes=KERNEL_VMEM)
    packed, shift = pl.pallas_call(
        pack_kernel,
        out_shape=(
            jax.ShapeDtypeStruct((rows + CODE_ROWS, 2 * width), jnp.bfloat16),
            jax.ShapeDtypeStruct((1, width), jnp.float32),
        ),
        in_specs=[smem] + [pl.BlockSpec(memory_space=pltpu.HBM)] * 5,
        out_specs=(vmem, vmem),
        scratch_shapes=[
            pltpu.VMEM((rows, width), jnp.bfloat16),
            pltpu.VMEM(neighbours.shape, jnp.int32),
            pltpu.VMEM((1, width), jnp.bfloat16),
            pltpu.VMEM((width, width), jnp.bfloat16),
            pltpu.SemaphoreType.DMA((5,)),
        ],
        name="pack_tile",
    )(timesteps, features, cotangent, neighbours, condition, w_time)
    here = lax.axis_index("brick").astype(jnp.int32).reshape(1)

    def across(block):
        return lax.ppermute(block, "brick", [(i, i ^ 1) for i in range(peers)])

    def along(block, turn):
        return lax.ppermute(block, "brick", [(i, (i + turn * tiles_y) % peers) for i in range(peers)])

    w_conv, packed = lax.optimization_barrier((w_conv, packed))
    w_forward, w_back = pl.pallas_call(
        turn_kernel,
        out_shape=(jax.ShapeDtypeStruct((width, 27 * width), jnp.bfloat16),) * 2,
        in_specs=[vmem],
        out_specs=(vmem, vmem),
        compiler_params=params,
        cost_estimate=pl.CostEstimate(flops=2 * 10**8, bytes_accessed=3 * 10**6, transcendentals=0),
        name="turn_weights",
    )(w_conv)
    before, after = along(packed, 1), along(packed, -1)
    before, w_forward = lax.optimization_barrier((before, w_forward))
    far = along(before, 1)
    own_pair = (packed, across(packed))
    before_pair = (before, across(before))
    after_pair = (after, across(after))
    far_pair = (far, across(far))
    line = [(0, u) for u in range(TILE)]
    stages = (
        ((own_pair,), line, []),
        ((before_pair, own_pair), line + [(1, 0)], [(TILE, TILE - 1)]),
        ((after_pair, own_pair), line + [(1, TILE - 1)], [(0, TILE)]),
        ((far_pair, before_pair, after_pair), line + [(1, 0), (2, TILE - 1)], [(TILE, TILE - 1), (0, TILE + 1)]),
    )
    sums = ()
    for stage, (pairs, strips, borders) in enumerate(stages):
        blocks = [block for pair in pairs for block in pair]
        if stage == ROW_STAGES - 1:
            out_shape = (
                jax.ShapeDtypeStruct((27, width, width), jnp.float32),
                jax.ShapeDtypeStruct((27, width, width), jnp.bfloat16),
            )
        else:
            out_shape = (
                jax.ShapeDtypeStruct((HALF * width, width), jnp.float32),
                jax.ShapeDtypeStruct((HALF * width, width), jnp.float32),
                jax.ShapeDtypeStruct((width, width), jnp.float32),
            )
        sums = pl.pallas_call(
            functools.partial(row_kernel, stage, strips, borders),
            out_shape=out_shape,
            in_specs=[smem] + [vmem] * (len(blocks) + len(sums)),
            out_specs=(vmem,) * len(out_shape),
            scratch_shapes=[
                pltpu.VMEM(((TILE + 2) * span, 2 * width), jnp.bfloat16),
                pltpu.VMEM((2 * width, (TILE + 2) * span), jnp.bfloat16),
                pltpu.VMEM((TILE + 1, CODE_ROWS, span), jnp.float32),
                pltpu.VMEM((HALF * width, (TILE + 1) * span), jnp.bfloat16),
                pltpu.VMEM((HALF * width, (TILE + 1) * span), jnp.bfloat16),
            ],
            compiler_params=params,
            cost_estimate=pl.CostEstimate(flops=2 * 10**9, bytes_accessed=4 * 10**6, transcendentals=0),
            name=f"weight_row_{stage}",
        )(here, *blocks, *sums)
    own, sent = sums
    other = lax.ppermute(sent, "batch", [(0, 1), (1, 0)])
    conv_out, feature_grad = pl.pallas_call(
        voxel_kernel,
        out_shape=(
            jax.ShapeDtypeStruct((rows, width), jnp.bfloat16),
            jax.ShapeDtypeStruct((rows, width), jnp.bfloat16),
        ),
        in_specs=[smem] + [vmem] * 11,
        scratch_shapes=[
            pltpu.VMEM(((TILE + 2) * span, 2 * width), jnp.bfloat16),
            pltpu.VMEM((2 * width, (TILE + 2) * span), jnp.bfloat16),
            pltpu.VMEM((27, rows), jnp.float32),
            pltpu.VMEM((27 * width, rows), jnp.bfloat16),
            pltpu.VMEM((27 * width, rows), jnp.bfloat16),
        ],
        compiler_params=params,
        cost_estimate=pl.CostEstimate(flops=10**9, bytes_accessed=4 * 10**6, transcendentals=0),
        name="voxel_outputs",
    )(here, *own_pair, *before_pair, *after_pair, neighbours, features[0], shift, w_forward, w_back)
    weight_grad = own + other.astype(jnp.float32)
    return (conv_out[None], feature_grad[None], weight_grad)


def passed_along(block, axis, distance):
    devices = range(lax.axis_size(axis))
    route = [(i - distance, i) for i in devices if i - distance in devices]
    return lax.ppermute(block, axis, route)


def slab_rows(block, side_recv, front_recv, width):
    widened = jnp.concatenate([side_recv[0], block, side_recv[1]], axis=1)
    slab = jnp.concatenate([front_recv[0][None], widened, front_recv[1][None]], axis=0)
    flat = slab.reshape(-1, width)
    return jnp.concatenate([flat, jnp.zeros((1, width), jnp.bfloat16)], axis=0)


def with_halo(block, tiles_y):
    width = block.shape[-1]
    side = TILE
    side_recv = tuple(passed_along(block[:, edge], "brick", by)[:, None] for by, edge in ((1, side - 1), (-1, 0)))
    wide = jnp.concatenate([side_recv[0], block, side_recv[1]], axis=1)
    front_recv = tuple(passed_along(wide[edge], "brick", by) for by, edge in ((tiles_y, side - 1), (-tiles_y, 0)))
    return slab_rows(block, side_recv, front_recv, width)


def halo_plan(features, cotangent, neighbours, timesteps, condition, w_time, w_conv, tiles_x, tiles_y):
    rows_here, width = features.shape[1:]
    here = lax.axis_index("brick")
    tile_x = here // tiles_y
    tile_y = here % tiles_y
    side = TILE
    layers = LAYERS
    wide = side + 2
    valid = neighbours >= 0
    safe = jnp.where(valid, neighbours, 0)
    owner = safe // rows_here
    inside = safe % rows_here
    column = inside // layers
    layer = inside % layers
    local_x = (owner // tiles_y - tile_x) * side + column // side + 1
    local_y = (owner % tiles_y - tile_y) * side + column % side + 1
    sentinel = wide * wide * layers
    ext_index = jnp.where(valid, (local_x * wide + local_y) * layers + layer, sentinel).T
    temb = time_embedding(timesteps, width)
    shift = jnp.dot(temb, w_time, preferred_element_type=jnp.float32) + condition.astype(jnp.float32)
    z_val = features[0].astype(jnp.float32) + shift[0][None, :]
    act = jax.nn.silu(z_val).astype(jnp.bfloat16)
    cot = cotangent[0]
    w_forward = w_conv.reshape(27 * width, width)
    w_backward = jnp.transpose(w_conv[::-1], (0, 2, 1)).reshape(27 * width, width)
    act_ext = with_halo(act.reshape(side, side, layers, width), tiles_y)
    gathered = act_ext[ext_index].reshape(rows_here, 27 * width)
    conv_out = jnp.dot(gathered, w_forward, preferred_element_type=jnp.float32).astype(jnp.bfloat16)
    partial_grad = lax.dot_general(
        gathered, cot, (((0,), (0,)), ((), ())), preferred_element_type=jnp.float32
    )
    both = ("brick", "batch")
    parts = tiles_x * tiles_y * lax.axis_size("batch")
    rows = 27 * width
    extra = -rows % (8 * parts)
    pieces = jnp.pad(partial_grad.astype(jnp.bfloat16), ((0, extra), (0, 0))).reshape(parts, -1, width)
    arrived = lax.all_to_all(pieces, both, 0, 0)
    summed = arrived.astype(jnp.float32).sum(0).astype(jnp.bfloat16)
    whole = lax.all_gather(summed, both, axis=0, tiled=True)
    weight_grad = whole[:rows].astype(jnp.float32).reshape(27, width, width)
    cot_ext = with_halo(cot.reshape(side, side, layers, width), tiles_y)
    cot_gathered = cot_ext[ext_index].reshape(rows_here, 27 * width)
    back = jnp.dot(cot_gathered, w_backward, preferred_element_type=jnp.float32)
    sig = jax.nn.sigmoid(z_val)
    feature_grad = (back * sig * (1.0 + z_val * (1.0 - sig))).astype(jnp.bfloat16)
    return (conv_out[None], feature_grad[None], weight_grad)


def shards(*arrays):
    peers = lax.axis_size("brick")
    bits = peers.bit_length() - 1
    tiles_x = 2 ** ((bits + 1) // 2)
    tiles_y = 2 ** (bits // 2)
    plan = whole_scene if (tiles_x, tiles_y) == (ROW_STAGES, 2) else halo_plan
    return plan(*arrays, tiles_x, tiles_y)


def solution(mesh):
    in_specs = (
        P(("groups", "batch"), "brick", None),
        P(("groups", "batch"), "brick", None),
        P(None, ("groups", "brick")),
        P(("groups", "batch")),
        P(("groups", "batch"), None),
        P(),
        P(),
    )
    out_specs = (
        P(("groups", "batch"), "brick", None),
        P(("groups", "batch"), "brick", None),
        P("groups", None, None),
    )
    return jax.shard_map(shards, mesh=mesh, in_specs=in_specs, out_specs=out_specs, check_vma=False)
```

```python
import functools

import jax
import jax.numpy as jnp
from jax import lax
from jax.experimental import pallas as pl
from jax.experimental.pallas import tpu as pltpu
from jax.sharding import PartitionSpec as P

LAYERS = 16
TILE = 4
STRIP = TILE * LAYERS
HALF = 13
CODE_ROWS = 16
ROW_STAGES = 4
KERNEL_VMEM = 24 * 1024 * 1024


def time_embedding(timesteps, width):
    half = width // 2
    freq = jnp.exp(-jnp.log(10000.0) * jnp.arange(half, dtype=jnp.float32) / half)
    angle = timesteps.astype(jnp.float32)[:, None] * freq[None, :]
    return jnp.concatenate([jnp.sin(angle), jnp.cos(angle)], axis=1).astype(jnp.bfloat16)


def strip_codes(neighbours, tiles_y):
    rows_here = TILE * STRIP
    code = (neighbours // rows_here) % tiles_y * STRIP + neighbours % STRIP
    return jnp.where(neighbours < 0, -1, code).astype(jnp.float32)


def pack_kernel(time_ref, feat_hbm, cot_hbm, near_hbm, cond_hbm, wt_hbm, pack_ref, shift_ref,
                feat_ref, near_ref, cond_ref, wt_ref, sems):
    rows, width = feat_ref.shape
    half = width // 2
    moves = (
        (wt_hbm, wt_ref),
        (cond_hbm, cond_ref),
        (feat_hbm.at[0], feat_ref),
        (near_hbm, near_ref),
        (cot_hbm.at[0], pack_ref.at[:rows, width:]),
    )
    copies = [pltpu.make_async_copy(source, to, sems.at[i]) for i, (source, to) in enumerate(moves)]
    for copy in copies:
        copy.start()
    lane = lax.broadcasted_iota(jnp.int32, (1, width), 1)
    freq = jnp.exp(-jnp.log(10000.0) * (lane % half).astype(jnp.float32) / half)
    angle = time_ref[0].astype(jnp.float32) * freq
    temb = jnp.where(lane < half, jnp.sin(angle), jnp.cos(angle)).astype(jnp.bfloat16)
    copies[0].wait()
    copies[1].wait()
    shift = jnp.dot(temb, wt_ref[...], preferred_element_type=jnp.float32)
    shift = shift + cond_ref[...].astype(jnp.float32)
    copies[2].wait()
    z_val = feat_ref[...].astype(jnp.float32) + shift
    shift_ref[...] = shift
    pack_ref[:rows, :width] = (z_val * jax.nn.sigmoid(z_val)).astype(jnp.bfloat16)
    copies[3].wait()
    pack_ref[rows:, :] = strip_codes(near_ref[:CODE_ROWS, :], 2).astype(jnp.bfloat16)
    copies[4].wait()


def lay_strip(ground, to, tile_y, mine_ref, other_ref, u):
    span = 2 * STRIP
    for ref, place in ((mine_ref, tile_y), (other_ref, 1 - tile_y)):
        at = pl.multiple_of(to * span + place * STRIP, STRIP)
        ground[pl.ds(at, STRIP), :] = ref[u * STRIP:(u + 1) * STRIP, :]


def row_kernel(stage, strips, borders, *refs):
    refs = list(refs)
    first_stage, final = stage == 0, stage == ROW_STAGES - 1
    where_ref = refs.pop(0)
    pairs = [(refs.pop(0), refs.pop(0)) for _ in range(1 + max(pair for pair, _ in strips))]
    before = [refs.pop(0) for _ in range(0 if first_stage else 3)]
    outs = [refs.pop(0) for _ in range(2 if final else 3)]
    ground, turned, codes, near_act, near_cot = refs
    width = ground.shape[1] // 2
    rows = TILE * STRIP
    span = 2 * STRIP
    tile_y = where_ref[0] % 2
    borders = [(u, u - 1) for u in range(1, TILE)] + borders
    targets = sorted({target for target, _ in borders})
    for i, (pair, u) in enumerate(strips):
        lay_strip(ground, i, tile_y, *pairs[pair], u)
        if i < TILE or i in targets:
            both = [ref[rows:, u * STRIP:(u + 1) * STRIP].astype(jnp.float32) for ref in pairs[pair]]
            first = jnp.where(tile_y == 0, both[0], both[1])
            second = jnp.where(tile_y == 0, both[1], both[0])
            codes[i] = jnp.concatenate([first, second], axis=1)
        if i < TILE or i in [source for _, source in borders]:
            turned[:, i * span:(i + 1) * span] = ground[i * span:(i + 1) * span, :].T
    place = lax.broadcasted_iota(jnp.int32, (span, span), 0).astype(jnp.float32)

    def gather(target, source, start, stop):
        picks = [(place == codes[target, k:k + 1, :]).astype(jnp.bfloat16) for k in range(start, stop)]
        near = jnp.dot(turned[:, source * span:(source + 1) * span], jnp.concatenate(picks, axis=1),
                       preferred_element_type=jnp.float32).astype(jnp.bfloat16)
        for k in range(start, stop):
            one = near[:, (k - start) * span:(k - start + 1) * span]
            near_act[k * width:(k + 1) * width, target * span:(target + 1) * span] = one[:width]
            near_cot[k * width:(k + 1) * width, target * span:(target + 1) * span] = one[width:]

    for u in range(TILE):
        gather(u, u, 9, HALF)
    for target, source in borders:
        gather(target, source, 0, 9)
    low_from = span * targets[0]
    low_to = span * (targets[-1] + 1)

    def product(near, start, stop, first, last, side):
        return jnp.dot(near[start * width:stop * width, first:last],
                       ground[first:last, side * width:(side + 1) * width], preferred_element_type=jnp.float32)

    pieces = []
    for near, side in ((near_act, 1), (near_cot, 0)):
        pieces.append(((0, 9), product(near, 0, 9, low_from, low_to, side)))
        pieces.append(((9, HALF), product(near, 9, HALF, 0, TILE * span, side)))
    centre = jnp.dot(turned[:width, :TILE * span], ground[:TILE * span, width:], preferred_element_type=jnp.float32)
    if not first_stage:
        centre = centre + before[2][...]
    for i, ((start, stop), value) in enumerate(pieces):
        turn = i // 2
        if not first_stage:
            value = value + before[turn][start * width:stop * width, :]
        if not final:
            outs[turn][start * width:stop * width, :] = value
            continue
        for k in range(start, stop):
            one = value[(k - start) * width:(k - start + 1) * width, :]
            one, to = (one.T, 2 * HALF - k) if turn else (one, k)
            outs[0][to] = one
            outs[1][to] = one.astype(jnp.bfloat16)
    if final:
        outs[0][HALF] = centre
        outs[1][HALF] = centre.astype(jnp.bfloat16)
    else:
        outs[2][...] = centre


def turn_kernel(w_ref, pack_ref, forward_ref, back_ref, own_ref):
    width = w_ref.shape[1]
    own_ref[...] = pack_ref[...]
    for k in range(27):
        forward_ref[:, k * width:(k + 1) * width] = w_ref[k].T
        back_ref[:, k * width:(k + 1) * width] = w_ref[26 - k]


def voxel_kernel(where_ref, mine_ref, other_ref, before_mine, before_other, after_mine, after_other,
                 near_ref, feat_ref, shift_ref, forward_ref, back_ref, conv_ref, grad_ref,
                 ground, turned, codes, near_act, near_cot):
    width = feat_ref.shape[1]
    span = 2 * STRIP
    tile_y = where_ref[0] % 2
    lay_strip(ground, 0, tile_y, before_mine, before_other, TILE - 1)
    for u in range(TILE):
        lay_strip(ground, u + 1, tile_y, mine_ref, other_ref, u)
    lay_strip(ground, TILE + 1, tile_y, after_mine, after_other, 0)
    for i in range(TILE + 2):
        turned[:, i * span:(i + 1) * span] = ground[i * span:(i + 1) * span, :].T
    code = strip_codes(near_ref[...], 2)
    lane = lax.broadcasted_iota(jnp.int32, code.shape, 1)
    codes[...] = jnp.where((code >= 0) & (lane // STRIP % 2 == 1), code + span, code)
    place = lax.broadcasted_iota(jnp.int32, (2 * span, span), 0).astype(jnp.float32)
    for half in range(TILE // 2):
        at = half * span
        for side in range(3):
            source = (2 * half + side) * span
            ks = range(9 * side, 9 * side + 9)
            picks = [(place == codes[k:k + 1, at:at + span]).astype(jnp.bfloat16) for k in ks]
            near = jnp.dot(turned[:, source:source + 2 * span], jnp.concatenate(picks, axis=1),
                           preferred_element_type=jnp.float32).astype(jnp.bfloat16)
            for k in ks:
                one = near[:, (k - 9 * side) * span:(k - 9 * side + 1) * span]
                near_act[k * width:(k + 1) * width, at:at + span] = one[:width]
                near_cot[k * width:(k + 1) * width, at:at + span] = one[width:]
    conv = jnp.dot(forward_ref[...], near_act[...], preferred_element_type=jnp.float32)
    conv_ref[...] = conv.T.astype(jnp.bfloat16)
    back = jnp.dot(back_ref[...], near_cot[...], preferred_element_type=jnp.float32).T
    z_val = feat_ref[...].astype(jnp.float32) + shift_ref[...]
    sig = jax.nn.sigmoid(z_val)
    grad_ref[...] = (back * sig * (1.0 + z_val * (1.0 - sig))).astype(jnp.bfloat16)


def whole_scene(features, cotangent, neighbours, timesteps, condition, w_time, w_conv, tiles_x, tiles_y):
    rows, width = features.shape[1:]
    peers = tiles_x * tiles_y
    span = 2 * STRIP
    vmem = pl.BlockSpec(memory_space=pltpu.VMEM)
    smem = pl.BlockSpec(memory_space=pltpu.SMEM)
    params = pltpu.CompilerParams(vmem_limit_bytes=KERNEL_VMEM)
    packed, shift = pl.pallas_call(
        pack_kernel,
        out_shape=(
            jax.ShapeDtypeStruct((rows + CODE_ROWS, 2 * width), jnp.bfloat16),
            jax.ShapeDtypeStruct((1, width), jnp.float32),
        ),
        in_specs=[smem] + [pl.BlockSpec(memory_space=pltpu.HBM)] * 5,
        out_specs=(vmem, vmem),
        scratch_shapes=[
            pltpu.VMEM((rows, width), jnp.bfloat16),
            pltpu.VMEM(neighbours.shape, jnp.int32),
            pltpu.VMEM((1, width), jnp.bfloat16),
            pltpu.VMEM((width, width), jnp.bfloat16),
            pltpu.SemaphoreType.DMA((5,)),
        ],
        name="pack_tile",
    )(timesteps, features, cotangent, neighbours, condition, w_time)
    here = lax.axis_index("brick").astype(jnp.int32).reshape(1)

    def across(block):
        return lax.ppermute(block, "brick", [(i, i ^ 1) for i in range(peers)])

    def along(block, turn):
        return lax.ppermute(block, "brick", [(i, (i + turn * tiles_y) % peers) for i in range(peers)])

    w_conv, packed = lax.optimization_barrier((w_conv, packed))
    w_forward, w_back, own = pl.pallas_call(
        turn_kernel,
        out_shape=(
            jax.ShapeDtypeStruct((width, 27 * width), jnp.bfloat16),
            jax.ShapeDtypeStruct((width, 27 * width), jnp.bfloat16),
            jax.ShapeDtypeStruct(packed.shape, jnp.bfloat16),
        ),
        in_specs=[vmem, vmem],
        out_specs=(vmem, vmem, vmem),
        compiler_params=params,
        cost_estimate=pl.CostEstimate(flops=2 * 10**8, bytes_accessed=3 * 10**6, transcendentals=0),
        name="turn_weights",
    )(w_conv, packed)
    after, before = along(packed, -1), along(packed, 1)
    own_pair = (own, across(packed))

    def row_sums(stage, pairs, strips, borders, sums):
        blocks = [block for pair in pairs for block in pair]
        if stage == ROW_STAGES - 1:
            out_shape = (
                jax.ShapeDtypeStruct((27, width, width), jnp.float32),
                jax.ShapeDtypeStruct((27, width, width), jnp.bfloat16),
            )
        else:
            out_shape = (
                jax.ShapeDtypeStruct((HALF * width, width), jnp.float32),
                jax.ShapeDtypeStruct((HALF * width, width), jnp.float32),
                jax.ShapeDtypeStruct((width, width), jnp.float32),
            )
        return pl.pallas_call(
            functools.partial(row_kernel, stage, strips, borders),
            out_shape=out_shape,
            in_specs=[smem] + [vmem] * (len(blocks) + len(sums)),
            out_specs=(vmem,) * len(out_shape),
            scratch_shapes=[
                pltpu.VMEM(((TILE + 2) * span, 2 * width), jnp.bfloat16),
                pltpu.VMEM((2 * width, (TILE + 2) * span), jnp.bfloat16),
                pltpu.VMEM((TILE + 1, CODE_ROWS, span), jnp.float32),
                pltpu.VMEM((HALF * width, (TILE + 1) * span), jnp.bfloat16),
                pltpu.VMEM((HALF * width, (TILE + 1) * span), jnp.bfloat16),
            ],
            compiler_params=params,
            cost_estimate=pl.CostEstimate(flops=2 * 10**9, bytes_accessed=4 * 10**6, transcendentals=0),
            name=f"weight_row_{stage}",
        )(here, *blocks, *sums)

    line = [(0, u) for u in range(TILE)]
    low, high, centre = row_sums(0, (own_pair,), line, [], ())
    before, w_forward, centre = lax.optimization_barrier((before, w_forward, centre))
    sums = (low, high, centre)
    far = along(before, 1)
    before_pair = (before, across(before))
    after_pair = (after, across(after))
    far_pair = (far, across(far))
    sums = row_sums(1, (before_pair, own_pair), line + [(1, 0)], [(TILE, TILE - 1)], sums)
    sums = row_sums(2, (after_pair, own_pair), line + [(1, TILE - 1)], [(0, TILE)], sums)
    sums = row_sums(3, (far_pair, before_pair, after_pair), line + [(1, 0), (2, TILE - 1)],
                    [(TILE, TILE - 1), (0, TILE + 1)], sums)
    kept, sent = sums
    other = lax.ppermute(sent, "batch", [(0, 1), (1, 0)])
    conv_out, feature_grad = pl.pallas_call(
        voxel_kernel,
        out_shape=(
            jax.ShapeDtypeStruct((rows, width), jnp.bfloat16),
            jax.ShapeDtypeStruct((rows, width), jnp.bfloat16),
        ),
        in_specs=[smem] + [vmem] * 11,
        scratch_shapes=[
            pltpu.VMEM(((TILE + 2) * span, 2 * width), jnp.bfloat16),
            pltpu.VMEM((2 * width, (TILE + 2) * span), jnp.bfloat16),
            pltpu.VMEM((27, rows), jnp.float32),
            pltpu.VMEM((27 * width, rows), jnp.bfloat16),
            pltpu.VMEM((27 * width, rows), jnp.bfloat16),
        ],
        compiler_params=params,
        cost_estimate=pl.CostEstimate(flops=10**9, bytes_accessed=4 * 10**6, transcendentals=0),
        name="voxel_outputs",
    )(here, *own_pair, *before_pair, *after_pair, neighbours, features[0], shift, w_forward, w_back)
    weight_grad = kept + other.astype(jnp.float32)
    return (conv_out[None], feature_grad[None], weight_grad)


def passed_along(block, axis, distance):
    devices = range(lax.axis_size(axis))
    route = [(i - distance, i) for i in devices if i - distance in devices]
    return lax.ppermute(block, axis, route)


def slab_rows(block, side_recv, front_recv, width):
    widened = jnp.concatenate([side_recv[0], block, side_recv[1]], axis=1)
    slab = jnp.concatenate([front_recv[0][None], widened, front_recv[1][None]], axis=0)
    flat = slab.reshape(-1, width)
    return jnp.concatenate([flat, jnp.zeros((1, width), jnp.bfloat16)], axis=0)


def with_halo(block, tiles_y):
    width = block.shape[-1]
    side = TILE
    side_recv = tuple(passed_along(block[:, edge], "brick", by)[:, None] for by, edge in ((1, side - 1), (-1, 0)))
    wide = jnp.concatenate([side_recv[0], block, side_recv[1]], axis=1)
    front_recv = tuple(passed_along(wide[edge], "brick", by) for by, edge in ((tiles_y, side - 1), (-tiles_y, 0)))
    return slab_rows(block, side_recv, front_recv, width)


def halo_plan(features, cotangent, neighbours, timesteps, condition, w_time, w_conv, tiles_x, tiles_y):
    rows_here, width = features.shape[1:]
    here = lax.axis_index("brick")
    tile_x = here // tiles_y
    tile_y = here % tiles_y
    side = TILE
    layers = LAYERS
    wide = side + 2
    valid = neighbours >= 0
    safe = jnp.where(valid, neighbours, 0)
    owner = safe // rows_here
    inside = safe % rows_here
    column = inside // layers
    layer = inside % layers
    local_x = (owner // tiles_y - tile_x) * side + column // side + 1
    local_y = (owner % tiles_y - tile_y) * side + column % side + 1
    sentinel = wide * wide * layers
    ext_index = jnp.where(valid, (local_x * wide + local_y) * layers + layer, sentinel).T
    temb = time_embedding(timesteps, width)
    shift = jnp.dot(temb, w_time, preferred_element_type=jnp.float32) + condition.astype(jnp.float32)
    z_val = features[0].astype(jnp.float32) + shift[0][None, :]
    act = jax.nn.silu(z_val).astype(jnp.bfloat16)
    cot = cotangent[0]
    w_forward = w_conv.reshape(27 * width, width)
    w_backward = jnp.transpose(w_conv[::-1], (0, 2, 1)).reshape(27 * width, width)
    act_ext = with_halo(act.reshape(side, side, layers, width), tiles_y)
    gathered = act_ext[ext_index].reshape(rows_here, 27 * width)
    conv_out = jnp.dot(gathered, w_forward, preferred_element_type=jnp.float32).astype(jnp.bfloat16)
    partial_grad = lax.dot_general(
        gathered, cot, (((0,), (0,)), ((), ())), preferred_element_type=jnp.float32
    )
    both = ("brick", "batch")
    parts = tiles_x * tiles_y * lax.axis_size("batch")
    rows = 27 * width
    extra = -rows % (8 * parts)
    pieces = jnp.pad(partial_grad.astype(jnp.bfloat16), ((0, extra), (0, 0))).reshape(parts, -1, width)
    arrived = lax.all_to_all(pieces, both, 0, 0)
    summed = arrived.astype(jnp.float32).sum(0).astype(jnp.bfloat16)
    whole = lax.all_gather(summed, both, axis=0, tiled=True)
    weight_grad = whole[:rows].astype(jnp.float32).reshape(27, width, width)
    cot_ext = with_halo(cot.reshape(side, side, layers, width), tiles_y)
    cot_gathered = cot_ext[ext_index].reshape(rows_here, 27 * width)
    back = jnp.dot(cot_gathered, w_backward, preferred_element_type=jnp.float32)
    sig = jax.nn.sigmoid(z_val)
    feature_grad = (back * sig * (1.0 + z_val * (1.0 - sig))).astype(jnp.bfloat16)
    return (conv_out[None], feature_grad[None], weight_grad)


def shards(*arrays):
    peers = lax.axis_size("brick")
    bits = peers.bit_length() - 1
    tiles_x = 2 ** ((bits + 1) // 2)
    tiles_y = 2 ** (bits // 2)
    plan = whole_scene if (tiles_x, tiles_y) == (ROW_STAGES, 2) else halo_plan
    return plan(*arrays, tiles_x, tiles_y)


def solution(mesh):
    in_specs = (
        P(("groups", "batch"), "brick", None),
        P(("groups", "batch"), "brick", None),
        P(None, ("groups", "brick")),
        P(("groups", "batch")),
        P(("groups", "batch"), None),
        P(),
        P(),
    )
    out_specs = (
        P(("groups", "batch"), "brick", None),
        P(("groups", "batch"), "brick", None),
        P("groups", None, None),
    )
    return jax.shard_map(shards, mesh=mesh, in_specs=in_specs, out_specs=out_specs, check_vma=False)
```

```python
import functools

import jax
import jax.numpy as jnp
from jax import lax
from jax.experimental import pallas as pl
from jax.experimental.pallas import tpu as pltpu
from jax.sharding import PartitionSpec as P

LAYERS = 16
TILE = 4
STRIP = TILE * LAYERS
HALF = 13
CODE_ROWS = 16
ROW_STAGES = 4
KERNEL_VMEM = 24 * 1024 * 1024


def time_embedding(timesteps, width):
    half = width // 2
    freq = jnp.exp(-jnp.log(10000.0) * jnp.arange(half, dtype=jnp.float32) / half)
    angle = timesteps.astype(jnp.float32)[:, None] * freq[None, :]
    return jnp.concatenate([jnp.sin(angle), jnp.cos(angle)], axis=1).astype(jnp.bfloat16)


def strip_codes(neighbours, tiles_y):
    rows_here = TILE * STRIP
    code = (neighbours // rows_here) % tiles_y * STRIP + neighbours % STRIP
    return jnp.where(neighbours < 0, -1, code).astype(jnp.float32)


def pack_kernel(time_ref, feat_hbm, cot_hbm, near_hbm, cond_hbm, wt_hbm, pack_ref, shift_ref,
                feat_ref, near_ref, cond_ref, wt_ref, sems):
    rows, width = feat_ref.shape
    half = width // 2
    moves = (
        (wt_hbm, wt_ref),
        (cond_hbm, cond_ref),
        (feat_hbm.at[0], feat_ref),
        (near_hbm, near_ref),
        (cot_hbm.at[0], pack_ref.at[:rows, width:]),
    )
    copies = [pltpu.make_async_copy(source, to, sems.at[i]) for i, (source, to) in enumerate(moves)]
    for copy in copies:
        copy.start()
    lane = lax.broadcasted_iota(jnp.int32, (1, width), 1)
    freq = jnp.exp(-jnp.log(10000.0) * (lane % half).astype(jnp.float32) / half)
    angle = time_ref[0].astype(jnp.float32) * freq
    temb = jnp.where(lane < half, jnp.sin(angle), jnp.cos(angle)).astype(jnp.bfloat16)
    copies[0].wait()
    copies[1].wait()
    shift = jnp.dot(temb, wt_ref[...], preferred_element_type=jnp.float32)
    shift = shift + cond_ref[...].astype(jnp.float32)
    copies[2].wait()
    z_val = feat_ref[...].astype(jnp.float32) + shift
    shift_ref[...] = shift
    pack_ref[:rows, :width] = (z_val * jax.nn.sigmoid(z_val)).astype(jnp.bfloat16)
    copies[3].wait()
    pack_ref[rows:, :] = strip_codes(near_ref[:CODE_ROWS, :], 2).astype(jnp.bfloat16)
    copies[4].wait()


def lay_strip(ground, to, tile_y, mine_ref, other_ref, u):
    span = 2 * STRIP
    for ref, place in ((mine_ref, tile_y), (other_ref, 1 - tile_y)):
        at = pl.multiple_of(to * span + place * STRIP, STRIP)
        ground[pl.ds(at, STRIP), :] = ref[u * STRIP:(u + 1) * STRIP, :]


def row_kernel(stage, strips, borders, *refs):
    refs = list(refs)
    first_stage, final = stage == 0, stage == ROW_STAGES - 1
    where_ref = refs.pop(0)
    pairs = [(refs.pop(0), refs.pop(0)) for _ in range(1 + max(pair for pair, _ in strips))]
    before = [refs.pop(0) for _ in range(0 if first_stage else 3)]
    outs = [refs.pop(0) for _ in range(2 if final else 3)]
    ground, turned, codes, near_act, near_cot = refs
    width = ground.shape[1] // 2
    rows = TILE * STRIP
    span = 2 * STRIP
    tile_y = where_ref[0] % 2
    borders = [(u, u - 1) for u in range(1, TILE)] + borders
    targets = sorted({target for target, _ in borders})
    for i, (pair, u) in enumerate(strips):
        lay_strip(ground, i, tile_y, *pairs[pair], u)
        if i < TILE or i in targets:
            both = [ref[rows:, u * STRIP:(u + 1) * STRIP].astype(jnp.float32) for ref in pairs[pair]]
            first = jnp.where(tile_y == 0, both[0], both[1])
            second = jnp.where(tile_y == 0, both[1], both[0])
            codes[i] = jnp.concatenate([first, second], axis=1)
        if i < TILE or i in [source for _, source in borders]:
            turned[:, i * span:(i + 1) * span] = ground[i * span:(i + 1) * span, :].T
    place = lax.broadcasted_iota(jnp.int32, (span, span), 0).astype(jnp.float32)

    def gather(target, source, start, stop):
        picks = [(place == codes[target, k:k + 1, :]).astype(jnp.bfloat16) for k in range(start, stop)]
        near = jnp.dot(turned[:, source * span:(source + 1) * span], jnp.concatenate(picks, axis=1),
                       preferred_element_type=jnp.float32).astype(jnp.bfloat16)
        for k in range(start, stop):
            one = near[:, (k - start) * span:(k - start + 1) * span]
            near_act[k * width:(k + 1) * width, target * span:(target + 1) * span] = one[:width]
            near_cot[k * width:(k + 1) * width, target * span:(target + 1) * span] = one[width:]

    for u in range(TILE):
        gather(u, u, 9, HALF)
    for target, source in borders:
        gather(target, source, 0, 9)
    low_from = span * targets[0]
    low_to = span * (targets[-1] + 1)

    def product(near, start, stop, first, last, side):
        return jnp.dot(near[start * width:stop * width, first:last],
                       ground[first:last, side * width:(side + 1) * width], preferred_element_type=jnp.float32)

    pieces = []
    for near, side in ((near_act, 1), (near_cot, 0)):
        pieces.append(((0, 9), product(near, 0, 9, low_from, low_to, side)))
        pieces.append(((9, HALF), product(near, 9, HALF, 0, TILE * span, side)))
    centre = jnp.dot(turned[:width, :TILE * span], ground[:TILE * span, width:], preferred_element_type=jnp.float32)
    if not first_stage:
        centre = centre + before[2][...]
    for i, ((start, stop), value) in enumerate(pieces):
        turn = i // 2
        if not first_stage:
            value = value + before[turn][start * width:stop * width, :]
        if not final:
            outs[turn][start * width:stop * width, :] = value
            continue
        for k in range(start, stop):
            one = value[(k - start) * width:(k - start + 1) * width, :]
            one, to = (one.T, 2 * HALF - k) if turn else (one, k)
            outs[0][to] = one
            outs[1][to] = one.astype(jnp.bfloat16)
    if final:
        outs[0][HALF] = centre
        outs[1][HALF] = centre.astype(jnp.bfloat16)
    else:
        outs[2][...] = centre


def turn_kernel(w_ref, pack_ref, forward_ref, back_ref, own_ref):
    width = w_ref.shape[1]
    own_ref[...] = pack_ref[...]
    for k in range(27):
        forward_ref[:, k * width:(k + 1) * width] = w_ref[k].T
        back_ref[:, k * width:(k + 1) * width] = w_ref[26 - k]


def voxel_kernel(where_ref, mine_ref, other_ref, before_mine, before_other, after_mine, after_other,
                 near_ref, feat_ref, shift_ref, forward_ref, back_ref, conv_ref, grad_ref,
                 ground, turned, codes, near_act, near_cot):
    width = feat_ref.shape[1]
    span = 2 * STRIP
    tile_y = where_ref[0] % 2
    lay_strip(ground, 0, tile_y, before_mine, before_other, TILE - 1)
    for u in range(TILE):
        lay_strip(ground, u + 1, tile_y, mine_ref, other_ref, u)
    lay_strip(ground, TILE + 1, tile_y, after_mine, after_other, 0)
    for i in range(TILE + 2):
        turned[:, i * span:(i + 1) * span] = ground[i * span:(i + 1) * span, :].T
    code = strip_codes(near_ref[...], 2)
    lane = lax.broadcasted_iota(jnp.int32, code.shape, 1)
    codes[...] = jnp.where((code >= 0) & (lane // STRIP % 2 == 1), code + span, code)
    place = lax.broadcasted_iota(jnp.int32, (2 * span, span), 0).astype(jnp.float32)
    for half in range(TILE // 2):
        at = half * span
        for side in range(3):
            source = (2 * half + side) * span
            ks = range(9 * side, 9 * side + 9)
            picks = [(place == codes[k:k + 1, at:at + span]).astype(jnp.bfloat16) for k in ks]
            near = jnp.dot(turned[:, source:source + 2 * span], jnp.concatenate(picks, axis=1),
                           preferred_element_type=jnp.float32).astype(jnp.bfloat16)
            for k in ks:
                one = near[:, (k - 9 * side) * span:(k - 9 * side + 1) * span]
                near_act[k * width:(k + 1) * width, at:at + span] = one[:width]
                near_cot[k * width:(k + 1) * width, at:at + span] = one[width:]
    conv = jnp.dot(forward_ref[...], near_act[...], preferred_element_type=jnp.float32)
    conv_ref[...] = conv.T.astype(jnp.bfloat16)
    back = jnp.dot(back_ref[...], near_cot[...], preferred_element_type=jnp.float32).T
    z_val = feat_ref[...].astype(jnp.float32) + shift_ref[...]
    sig = jax.nn.sigmoid(z_val)
    grad_ref[...] = (back * sig * (1.0 + z_val * (1.0 - sig))).astype(jnp.bfloat16)


def whole_scene(features, cotangent, neighbours, timesteps, condition, w_time, w_conv, tiles_x, tiles_y):
    rows, width = features.shape[1:]
    peers = tiles_x * tiles_y
    span = 2 * STRIP
    vmem = pl.BlockSpec(memory_space=pltpu.VMEM)
    smem = pl.BlockSpec(memory_space=pltpu.SMEM)
    params = pltpu.CompilerParams(vmem_limit_bytes=KERNEL_VMEM)
    packed, shift = pl.pallas_call(
        pack_kernel,
        out_shape=(
            jax.ShapeDtypeStruct((rows + CODE_ROWS, 2 * width), jnp.bfloat16),
            jax.ShapeDtypeStruct((1, width), jnp.float32),
        ),
        in_specs=[smem] + [pl.BlockSpec(memory_space=pltpu.HBM)] * 5,
        out_specs=(vmem, vmem),
        scratch_shapes=[
            pltpu.VMEM((rows, width), jnp.bfloat16),
            pltpu.VMEM(neighbours.shape, jnp.int32),
            pltpu.VMEM((1, width), jnp.bfloat16),
            pltpu.VMEM((width, width), jnp.bfloat16),
            pltpu.SemaphoreType.DMA((5,)),
        ],
        name="pack_tile",
    )(timesteps, features, cotangent, neighbours, condition, w_time)
    here = lax.axis_index("brick").astype(jnp.int32).reshape(1)

    def across(block):
        return lax.ppermute(block, "brick", [(i, i ^ 1) for i in range(peers)])

    def along(block, turn):
        return lax.ppermute(block, "brick", [(i, (i + turn * tiles_y) % peers) for i in range(peers)])

    w_conv, packed = lax.optimization_barrier((w_conv, packed))
    w_forward, w_back, own = pl.pallas_call(
        turn_kernel,
        out_shape=(
            jax.ShapeDtypeStruct((width, 27 * width), jnp.bfloat16),
            jax.ShapeDtypeStruct((width, 27 * width), jnp.bfloat16),
            jax.ShapeDtypeStruct(packed.shape, jnp.bfloat16),
        ),
        in_specs=[vmem, vmem],
        out_specs=(vmem, vmem, vmem),
        compiler_params=params,
        cost_estimate=pl.CostEstimate(flops=10**6, bytes_accessed=10**4, transcendentals=0),
        name="turn_weights",
    )(w_conv, packed)
    after, before = along(packed, -1), along(packed, 1)
    own_pair = (own, across(packed))

    def row_sums(stage, pairs, strips, borders, sums):
        blocks = [block for pair in pairs for block in pair]
        if stage == ROW_STAGES - 1:
            out_shape = (
                jax.ShapeDtypeStruct((27, width, width), jnp.float32),
                jax.ShapeDtypeStruct((27, width, width), jnp.bfloat16),
            )
        else:
            out_shape = (
                jax.ShapeDtypeStruct((HALF * width, width), jnp.float32),
                jax.ShapeDtypeStruct((HALF * width, width), jnp.float32),
                jax.ShapeDtypeStruct((width, width), jnp.float32),
            )
        return pl.pallas_call(
            functools.partial(row_kernel, stage, strips, borders),
            out_shape=out_shape,
            in_specs=[smem] + [vmem] * (len(blocks) + len(sums)),
            out_specs=(vmem,) * len(out_shape),
            scratch_shapes=[
                pltpu.VMEM(((TILE + 2) * span, 2 * width), jnp.bfloat16),
                pltpu.VMEM((2 * width, (TILE + 2) * span), jnp.bfloat16),
                pltpu.VMEM((TILE + 1, CODE_ROWS, span), jnp.float32),
                pltpu.VMEM((HALF * width, (TILE + 1) * span), jnp.bfloat16),
                pltpu.VMEM((HALF * width, (TILE + 1) * span), jnp.bfloat16),
            ],
            compiler_params=params,
            cost_estimate=pl.CostEstimate(flops=2 * 10**9 if stage else 10**8, bytes_accessed=10**4, transcendentals=0),
            name=f"weight_row_{stage}",
        )(here, *blocks, *sums)

    line = [(0, u) for u in range(TILE)]
    low, high, centre = row_sums(0, (own_pair,), line, [], ())
    before, w_forward, centre = lax.optimization_barrier((before, w_forward, centre))
    sums = (low, high, centre)
    far = along(before, 1)
    before_pair = (before, across(before))
    after_pair = (after, across(after))
    far_pair = (far, across(far))
    sums = row_sums(1, (before_pair, own_pair), line + [(1, 0)], [(TILE, TILE - 1)], sums)
    sums = row_sums(2, (after_pair, own_pair), line + [(1, TILE - 1)], [(0, TILE)], sums)
    sums = row_sums(3, (far_pair, before_pair, after_pair), line + [(1, 0), (2, TILE - 1)],
                    [(TILE, TILE - 1), (0, TILE + 1)], sums)
    kept, sent = sums
    other = lax.ppermute(sent, "batch", [(0, 1), (1, 0)])
    conv_out, feature_grad = pl.pallas_call(
        voxel_kernel,
        out_shape=(
            jax.ShapeDtypeStruct((rows, width), jnp.bfloat16),
            jax.ShapeDtypeStruct((rows, width), jnp.bfloat16),
        ),
        in_specs=[smem] + [vmem] * 11,
        scratch_shapes=[
            pltpu.VMEM(((TILE + 2) * span, 2 * width), jnp.bfloat16),
            pltpu.VMEM((2 * width, (TILE + 2) * span), jnp.bfloat16),
            pltpu.VMEM((27, rows), jnp.float32),
            pltpu.VMEM((27 * width, rows), jnp.bfloat16),
            pltpu.VMEM((27 * width, rows), jnp.bfloat16),
        ],
        compiler_params=params,
        cost_estimate=pl.CostEstimate(flops=10**9, bytes_accessed=4 * 10**6, transcendentals=0),
        name="voxel_outputs",
    )(here, *own_pair, *before_pair, *after_pair, neighbours, features[0], shift, w_forward, w_back)
    weight_grad = kept + other.astype(jnp.float32)
    return (conv_out[None], feature_grad[None], weight_grad)


def passed_along(block, axis, distance):
    devices = range(lax.axis_size(axis))
    route = [(i - distance, i) for i in devices if i - distance in devices]
    return lax.ppermute(block, axis, route)


def slab_rows(block, side_recv, front_recv, width):
    widened = jnp.concatenate([side_recv[0], block, side_recv[1]], axis=1)
    slab = jnp.concatenate([front_recv[0][None], widened, front_recv[1][None]], axis=0)
    flat = slab.reshape(-1, width)
    return jnp.concatenate([flat, jnp.zeros((1, width), jnp.bfloat16)], axis=0)


def with_halo(block, tiles_y):
    width = block.shape[-1]
    side = TILE
    side_recv = tuple(passed_along(block[:, edge], "brick", by)[:, None] for by, edge in ((1, side - 1), (-1, 0)))
    wide = jnp.concatenate([side_recv[0], block, side_recv[1]], axis=1)
    front_recv = tuple(passed_along(wide[edge], "brick", by) for by, edge in ((tiles_y, side - 1), (-tiles_y, 0)))
    return slab_rows(block, side_recv, front_recv, width)


def halo_plan(features, cotangent, neighbours, timesteps, condition, w_time, w_conv, tiles_x, tiles_y):
    rows_here, width = features.shape[1:]
    here = lax.axis_index("brick")
    tile_x = here // tiles_y
    tile_y = here % tiles_y
    side = TILE
    layers = LAYERS
    wide = side + 2
    valid = neighbours >= 0
    safe = jnp.where(valid, neighbours, 0)
    owner = safe // rows_here
    inside = safe % rows_here
    column = inside // layers
    layer = inside % layers
    local_x = (owner // tiles_y - tile_x) * side + column // side + 1
    local_y = (owner % tiles_y - tile_y) * side + column % side + 1
    sentinel = wide * wide * layers
    ext_index = jnp.where(valid, (local_x * wide + local_y) * layers + layer, sentinel).T
    temb = time_embedding(timesteps, width)
    shift = jnp.dot(temb, w_time, preferred_element_type=jnp.float32) + condition.astype(jnp.float32)
    z_val = features[0].astype(jnp.float32) + shift[0][None, :]
    act = jax.nn.silu(z_val).astype(jnp.bfloat16)
    cot = cotangent[0]
    w_forward = w_conv.reshape(27 * width, width)
    w_backward = jnp.transpose(w_conv[::-1], (0, 2, 1)).reshape(27 * width, width)
    act_ext = with_halo(act.reshape(side, side, layers, width), tiles_y)
    gathered = act_ext[ext_index].reshape(rows_here, 27 * width)
    conv_out = jnp.dot(gathered, w_forward, preferred_element_type=jnp.float32).astype(jnp.bfloat16)
    partial_grad = lax.dot_general(
        gathered, cot, (((0,), (0,)), ((), ())), preferred_element_type=jnp.float32
    )
    both = ("brick", "batch")
    parts = tiles_x * tiles_y * lax.axis_size("batch")
    rows = 27 * width
    extra = -rows % (8 * parts)
    pieces = jnp.pad(partial_grad.astype(jnp.bfloat16), ((0, extra), (0, 0))).reshape(parts, -1, width)
    arrived = lax.all_to_all(pieces, both, 0, 0)
    summed = arrived.astype(jnp.float32).sum(0).astype(jnp.bfloat16)
    whole = lax.all_gather(summed, both, axis=0, tiled=True)
    weight_grad = whole[:rows].astype(jnp.float32).reshape(27, width, width)
    cot_ext = with_halo(cot.reshape(side, side, layers, width), tiles_y)
    cot_gathered = cot_ext[ext_index].reshape(rows_here, 27 * width)
    back = jnp.dot(cot_gathered, w_backward, preferred_element_type=jnp.float32)
    sig = jax.nn.sigmoid(z_val)
    feature_grad = (back * sig * (1.0 + z_val * (1.0 - sig))).astype(jnp.bfloat16)
    return (conv_out[None], feature_grad[None], weight_grad)


def shards(*arrays):
    peers = lax.axis_size("brick")
    bits = peers.bit_length() - 1
    tiles_x = 2 ** ((bits + 1) // 2)
    tiles_y = 2 ** (bits // 2)
    plan = whole_scene if (tiles_x, tiles_y) == (ROW_STAGES, 2) else halo_plan
    return plan(*arrays, tiles_x, tiles_y)


def solution(mesh):
    in_specs = (
        P(("groups", "batch"), "brick", None),
        P(("groups", "batch"), "brick", None),
        P(None, ("groups", "brick")),
        P(("groups", "batch")),
        P(("groups", "batch"), None),
        P(),
        P(),
    )
    out_specs = (
        P(("groups", "batch"), "brick", None),
        P(("groups", "batch"), "brick", None),
        P("groups", None, None),
    )
    return jax.shard_map(shards, mesh=mesh, in_specs=in_specs, out_specs=out_specs, check_vma=False)
```

```python
import functools

import jax
import jax.numpy as jnp
from jax import lax
from jax.experimental import pallas as pl
from jax.experimental.pallas import tpu as pltpu
from jax.sharding import PartitionSpec as P

LAYERS = 16
TILE = 4
STRIP = TILE * LAYERS
HALF = 13
CODE_ROWS = 16
ROW_STAGES = 4
PACK_VMEM = 8 * 1024 * 1024
KERNEL_VMEM = 24 * 1024 * 1024


def time_embedding(timesteps, width):
    half = width // 2
    freq = jnp.exp(-jnp.log(10000.0) * jnp.arange(half, dtype=jnp.float32) / half)
    angle = timesteps.astype(jnp.float32)[:, None] * freq[None, :]
    return jnp.concatenate([jnp.sin(angle), jnp.cos(angle)], axis=1).astype(jnp.bfloat16)


def strip_codes(neighbours, tiles_y):
    rows_here = TILE * STRIP
    code = (neighbours // rows_here) % tiles_y * STRIP + neighbours % STRIP
    return jnp.where(neighbours < 0, -1, code).astype(jnp.float32)


def in_hbm(array):
    return pltpu.with_memory_space_constraint(array, pltpu.HBM)


def pack_kernel(time_ref, feat_hbm, cot_hbm, near_hbm, cond_hbm, wt_hbm, pack_ref, shift_ref,
                feat_ref, near_ref, cond_ref, wt_ref, sems):
    rows, width = feat_ref.shape
    half = width // 2
    moves = (
        (wt_hbm, wt_ref),
        (cond_hbm, cond_ref),
        (feat_hbm.at[0], feat_ref),
        (near_hbm, near_ref),
        (cot_hbm.at[0], pack_ref.at[:rows, width:]),
    )
    copies = [pltpu.make_async_copy(source, to, sems.at[i]) for i, (source, to) in enumerate(moves)]
    for copy in copies:
        copy.start()
    lane = lax.broadcasted_iota(jnp.int32, (1, width), 1)
    freq = jnp.exp(-jnp.log(10000.0) * (lane % half).astype(jnp.float32) / half)
    angle = time_ref[0].astype(jnp.float32) * freq
    temb = jnp.where(lane < half, jnp.sin(angle), jnp.cos(angle)).astype(jnp.bfloat16)
    copies[0].wait()
    copies[1].wait()
    shift = jnp.dot(temb, wt_ref[...], preferred_element_type=jnp.float32)
    shift = shift + cond_ref[...].astype(jnp.float32)
    copies[2].wait()
    z_val = feat_ref[...].astype(jnp.float32) + shift
    shift_ref[...] = shift
    pack_ref[:rows, :width] = (z_val * jax.nn.sigmoid(z_val)).astype(jnp.bfloat16)
    copies[3].wait()
    pack_ref[rows:, :] = strip_codes(near_ref[:CODE_ROWS, :], 2).astype(jnp.bfloat16)
    copies[4].wait()


def lay_strip(ground, to, tile_y, mine_ref, other_ref, u):
    span = 2 * STRIP
    for ref, place in ((mine_ref, tile_y), (other_ref, 1 - tile_y)):
        at = pl.multiple_of(to * span + place * STRIP, STRIP)
        ground[pl.ds(at, STRIP), :] = ref[u * STRIP:(u + 1) * STRIP, :]


def row_kernel(stage, strips, borders, *refs):
    refs = list(refs)
    first_stage, final = stage == 0, stage == ROW_STAGES - 1
    where_ref = refs.pop(0)
    pairs = [(refs.pop(0), refs.pop(0)) for _ in range(1 + max(pair for pair, _ in strips))]
    before = [refs.pop(0) for _ in range(0 if first_stage else 3)]
    outs = [refs.pop(0) for _ in range(2 if final else 3)]
    ground, turned, codes, near_act, near_cot = refs
    width = ground.shape[1] // 2
    rows = TILE * STRIP
    span = 2 * STRIP
    tile_y = where_ref[0] % 2
    borders = [(u, u - 1) for u in range(1, TILE)] + borders
    targets = sorted({target for target, _ in borders})
    for i, (pair, u) in enumerate(strips):
        lay_strip(ground, i, tile_y, *pairs[pair], u)
        if i < TILE or i in targets:
            both = [ref[rows:, u * STRIP:(u + 1) * STRIP].astype(jnp.float32) for ref in pairs[pair]]
            first = jnp.where(tile_y == 0, both[0], both[1])
            second = jnp.where(tile_y == 0, both[1], both[0])
            codes[i] = jnp.concatenate([first, second], axis=1)
        if i < TILE or i in [source for _, source in borders]:
            turned[:, i * span:(i + 1) * span] = ground[i * span:(i + 1) * span, :].T
    place = lax.broadcasted_iota(jnp.int32, (span, span), 0).astype(jnp.float32)

    def gather(target, source, start, stop):
        picks = [(place == codes[target, k:k + 1, :]).astype(jnp.bfloat16) for k in range(start, stop)]
        near = jnp.dot(turned[:, source * span:(source + 1) * span], jnp.concatenate(picks, axis=1),
                       preferred_element_type=jnp.float32).astype(jnp.bfloat16)
        for k in range(start, stop):
            one = near[:, (k - start) * span:(k - start + 1) * span]
            near_act[k * width:(k + 1) * width, target * span:(target + 1) * span] = one[:width]
            near_cot[k * width:(k + 1) * width, target * span:(target + 1) * span] = one[width:]

    for u in range(TILE):
        gather(u, u, 9, HALF)
    for target, source in borders:
        gather(target, source, 0, 9)
    low_from = span * targets[0]
    low_to = span * (targets[-1] + 1)

    def product(near, start, stop, first, last, side):
        return jnp.dot(near[start * width:stop * width, first:last],
                       ground[first:last, side * width:(side + 1) * width], preferred_element_type=jnp.float32)

    pieces = []
    for near, side in ((near_act, 1), (near_cot, 0)):
        pieces.append(((0, 9), product(near, 0, 9, low_from, low_to, side)))
        pieces.append(((9, HALF), product(near, 9, HALF, 0, TILE * span, side)))
    centre = jnp.dot(turned[:width, :TILE * span], ground[:TILE * span, width:], preferred_element_type=jnp.float32)
    if not first_stage:
        centre = centre + before[2][...]
    for i, ((start, stop), value) in enumerate(pieces):
        turn = i // 2
        if not first_stage:
            value = value + before[turn][start * width:stop * width, :]
        if not final:
            outs[turn][start * width:stop * width, :] = value
            continue
        for k in range(start, stop):
            one = value[(k - start) * width:(k - start + 1) * width, :]
            one, to = (one.T, 2 * HALF - k) if turn else (one, k)
            outs[0][to] = one
            outs[1][to] = one.astype(jnp.bfloat16)
    if final:
        outs[0][HALF] = centre
        outs[1][HALF] = centre.astype(jnp.bfloat16)
    else:
        outs[2][...] = centre


def turn_kernel(w_ref, forward_ref, back_ref):
    width = w_ref.shape[1]
    for k in range(27):
        forward_ref[:, k * width:(k + 1) * width] = w_ref[k].T
        back_ref[:, k * width:(k + 1) * width] = w_ref[26 - k]


def voxel_kernel(where_ref, mine_ref, other_ref, before_mine, before_other, after_mine, after_other,
                 near_ref, feat_ref, shift_ref, forward_ref, back_ref, conv_ref, grad_ref,
                 ground, turned, codes, near_act, near_cot):
    width = feat_ref.shape[1]
    span = 2 * STRIP
    tile_y = where_ref[0] % 2
    lay_strip(ground, 0, tile_y, before_mine, before_other, TILE - 1)
    for u in range(TILE):
        lay_strip(ground, u + 1, tile_y, mine_ref, other_ref, u)
    lay_strip(ground, TILE + 1, tile_y, after_mine, after_other, 0)
    for i in range(TILE + 2):
        turned[:, i * span:(i + 1) * span] = ground[i * span:(i + 1) * span, :].T
    code = strip_codes(near_ref[...], 2)
    lane = lax.broadcasted_iota(jnp.int32, code.shape, 1)
    codes[...] = jnp.where((code >= 0) & (lane // STRIP % 2 == 1), code + span, code)
    place = lax.broadcasted_iota(jnp.int32, (2 * span, span), 0).astype(jnp.float32)
    for half in range(TILE // 2):
        at = half * span
        for side in range(3):
            source = (2 * half + side) * span
            ks = range(9 * side, 9 * side + 9)
            picks = [(place == codes[k:k + 1, at:at + span]).astype(jnp.bfloat16) for k in ks]
            near = jnp.dot(turned[:, source:source + 2 * span], jnp.concatenate(picks, axis=1),
                           preferred_element_type=jnp.float32).astype(jnp.bfloat16)
            for k in ks:
                one = near[:, (k - 9 * side) * span:(k - 9 * side + 1) * span]
                near_act[k * width:(k + 1) * width, at:at + span] = one[:width]
                near_cot[k * width:(k + 1) * width, at:at + span] = one[width:]
    conv = jnp.dot(forward_ref[...], near_act[...], preferred_element_type=jnp.float32)
    conv_ref[...] = conv.T.astype(jnp.bfloat16)
    back = jnp.dot(back_ref[...], near_cot[...], preferred_element_type=jnp.float32).T
    z_val = feat_ref[...].astype(jnp.float32) + shift_ref[...]
    sig = jax.nn.sigmoid(z_val)
    grad_ref[...] = (back * sig * (1.0 + z_val * (1.0 - sig))).astype(jnp.bfloat16)


def whole_scene(features, cotangent, neighbours, timesteps, condition, w_time, w_conv, tiles_x, tiles_y):
    rows, width = features.shape[1:]
    peers = tiles_x * tiles_y
    span = 2 * STRIP
    vmem = pl.BlockSpec(memory_space=pltpu.VMEM)
    smem = pl.BlockSpec(memory_space=pltpu.SMEM)
    params = pltpu.CompilerParams(vmem_limit_bytes=KERNEL_VMEM)
    packed, shift = pl.pallas_call(
        pack_kernel,
        out_shape=(
            jax.ShapeDtypeStruct((rows + CODE_ROWS, 2 * width), jnp.bfloat16),
            jax.ShapeDtypeStruct((1, width), jnp.float32),
        ),
        in_specs=[smem] + [pl.BlockSpec(memory_space=pltpu.HBM)] * 5,
        out_specs=(vmem, vmem),
        scratch_shapes=[
            pltpu.VMEM((rows, width), jnp.bfloat16),
            pltpu.VMEM(neighbours.shape, jnp.int32),
            pltpu.VMEM((1, width), jnp.bfloat16),
            pltpu.VMEM((width, width), jnp.bfloat16),
            pltpu.SemaphoreType.DMA((5,)),
        ],
        compiler_params=pltpu.CompilerParams(vmem_limit_bytes=PACK_VMEM),
        name="pack_tile",
    )(timesteps, *[in_hbm(array) for array in (features, cotangent, neighbours, condition, w_time)])
    here = lax.axis_index("brick").astype(jnp.int32).reshape(1)

    def across(block):
        return lax.ppermute(block, "brick", [(i, i ^ 1) for i in range(peers)])

    def along(block, turn):
        return lax.ppermute(block, "brick", [(i, (i + turn * tiles_y) % peers) for i in range(peers)])

    w_conv, packed = lax.optimization_barrier((w_conv, packed))
    w_forward, w_back = pl.pallas_call(
        turn_kernel,
        out_shape=(jax.ShapeDtypeStruct((width, 27 * width), jnp.bfloat16),) * 2,
        in_specs=[vmem],
        out_specs=(vmem, vmem),
        compiler_params=params,
        cost_estimate=pl.CostEstimate(flops=2 * 10**8, bytes_accessed=3 * 10**6, transcendentals=0),
        name="turn_weights",
    )(w_conv)
    before, after = along(packed, 1), along(packed, -1)
    before, w_forward = lax.optimization_barrier((before, w_forward))
    far = along(before, 1)
    own_pair = (packed, across(packed))
    before_pair = (before, across(before))
    after_pair = (after, across(after))
    far_pair = (far, across(far))
    line = [(0, u) for u in range(TILE)]
    stages = (
        ((own_pair,), line, []),
        ((before_pair, own_pair), line + [(1, 0)], [(TILE, TILE - 1)]),
        ((after_pair, own_pair), line + [(1, TILE - 1)], [(0, TILE)]),
        ((far_pair, before_pair, after_pair), line + [(1, 0), (2, TILE - 1)], [(TILE, TILE - 1), (0, TILE + 1)]),
    )
    sums = ()
    for stage, (pairs, strips, borders) in enumerate(stages):
        blocks = [block for pair in pairs for block in pair]
        if stage == ROW_STAGES - 1:
            out_shape = (
                jax.ShapeDtypeStruct((27, width, width), jnp.float32),
                jax.ShapeDtypeStruct((27, width, width), jnp.bfloat16),
            )
        else:
            out_shape = (
                jax.ShapeDtypeStruct((HALF * width, width), jnp.float32),
                jax.ShapeDtypeStruct((HALF * width, width), jnp.float32),
                jax.ShapeDtypeStruct((width, width), jnp.float32),
            )
        sums = pl.pallas_call(
            functools.partial(row_kernel, stage, strips, borders),
            out_shape=out_shape,
            in_specs=[smem] + [vmem] * (len(blocks) + len(sums)),
            out_specs=(vmem,) * len(out_shape),
            scratch_shapes=[
                pltpu.VMEM(((TILE + 2) * span, 2 * width), jnp.bfloat16),
                pltpu.VMEM((2 * width, (TILE + 2) * span), jnp.bfloat16),
                pltpu.VMEM((TILE + 1, CODE_ROWS, span), jnp.float32),
                pltpu.VMEM((HALF * width, (TILE + 1) * span), jnp.bfloat16),
                pltpu.VMEM((HALF * width, (TILE + 1) * span), jnp.bfloat16),
            ],
            compiler_params=params,
            cost_estimate=pl.CostEstimate(flops=2 * 10**9, bytes_accessed=4 * 10**6, transcendentals=0),
            name=f"weight_row_{stage}",
        )(here, *blocks, *sums)
    own, sent = sums
    other = lax.ppermute(sent, "batch", [(0, 1), (1, 0)])
    conv_out, feature_grad = pl.pallas_call(
        voxel_kernel,
        out_shape=(
            jax.ShapeDtypeStruct((rows, width), jnp.bfloat16),
            jax.ShapeDtypeStruct((rows, width), jnp.bfloat16),
        ),
        in_specs=[smem] + [vmem] * 11,
        scratch_shapes=[
            pltpu.VMEM(((TILE + 2) * span, 2 * width), jnp.bfloat16),
            pltpu.VMEM((2 * width, (TILE + 2) * span), jnp.bfloat16),
            pltpu.VMEM((27, rows), jnp.float32),
            pltpu.VMEM((27 * width, rows), jnp.bfloat16),
            pltpu.VMEM((27 * width, rows), jnp.bfloat16),
        ],
        compiler_params=params,
        cost_estimate=pl.CostEstimate(flops=10**9, bytes_accessed=4 * 10**6, transcendentals=0),
        name="voxel_outputs",
    )(here, *own_pair, *before_pair, *after_pair, neighbours, features[0], shift, w_forward, w_back)
    weight_grad = own + other.astype(jnp.float32)
    return (conv_out[None], feature_grad[None], weight_grad)


def passed_along(block, axis, distance):
    devices = range(lax.axis_size(axis))
    route = [(i - distance, i) for i in devices if i - distance in devices]
    return lax.ppermute(block, axis, route)


def slab_rows(block, side_recv, front_recv, width):
    widened = jnp.concatenate([side_recv[0], block, side_recv[1]], axis=1)
    slab = jnp.concatenate([front_recv[0][None], widened, front_recv[1][None]], axis=0)
    flat = slab.reshape(-1, width)
    return jnp.concatenate([flat, jnp.zeros((1, width), jnp.bfloat16)], axis=0)


def with_halo(block, tiles_y):
    width = block.shape[-1]
    side = TILE
    side_recv = tuple(passed_along(block[:, edge], "brick", by)[:, None] for by, edge in ((1, side - 1), (-1, 0)))
    wide = jnp.concatenate([side_recv[0], block, side_recv[1]], axis=1)
    front_recv = tuple(passed_along(wide[edge], "brick", by) for by, edge in ((tiles_y, side - 1), (-tiles_y, 0)))
    return slab_rows(block, side_recv, front_recv, width)


def halo_plan(features, cotangent, neighbours, timesteps, condition, w_time, w_conv, tiles_x, tiles_y):
    rows_here, width = features.shape[1:]
    here = lax.axis_index("brick")
    tile_x = here // tiles_y
    tile_y = here % tiles_y
    side = TILE
    layers = LAYERS
    wide = side + 2
    valid = neighbours >= 0
    safe = jnp.where(valid, neighbours, 0)
    owner = safe // rows_here
    inside = safe % rows_here
    column = inside // layers
    layer = inside % layers
    local_x = (owner // tiles_y - tile_x) * side + column // side + 1
    local_y = (owner % tiles_y - tile_y) * side + column % side + 1
    sentinel = wide * wide * layers
    ext_index = jnp.where(valid, (local_x * wide + local_y) * layers + layer, sentinel).T
    temb = time_embedding(timesteps, width)
    shift = jnp.dot(temb, w_time, preferred_element_type=jnp.float32) + condition.astype(jnp.float32)
    z_val = features[0].astype(jnp.float32) + shift[0][None, :]
    act = jax.nn.silu(z_val).astype(jnp.bfloat16)
    cot = cotangent[0]
    w_forward = w_conv.reshape(27 * width, width)
    w_backward = jnp.transpose(w_conv[::-1], (0, 2, 1)).reshape(27 * width, width)
    act_ext = with_halo(act.reshape(side, side, layers, width), tiles_y)
    gathered = act_ext[ext_index].reshape(rows_here, 27 * width)
    conv_out = jnp.dot(gathered, w_forward, preferred_element_type=jnp.float32).astype(jnp.bfloat16)
    partial_grad = lax.dot_general(
        gathered, cot, (((0,), (0,)), ((), ())), preferred_element_type=jnp.float32
    )
    both = ("brick", "batch")
    parts = tiles_x * tiles_y * lax.axis_size("batch")
    rows = 27 * width
    extra = -rows % (8 * parts)
    pieces = jnp.pad(partial_grad.astype(jnp.bfloat16), ((0, extra), (0, 0))).reshape(parts, -1, width)
    arrived = lax.all_to_all(pieces, both, 0, 0)
    summed = arrived.astype(jnp.float32).sum(0).astype(jnp.bfloat16)
    whole = lax.all_gather(summed, both, axis=0, tiled=True)
    weight_grad = whole[:rows].astype(jnp.float32).reshape(27, width, width)
    cot_ext = with_halo(cot.reshape(side, side, layers, width), tiles_y)
    cot_gathered = cot_ext[ext_index].reshape(rows_here, 27 * width)
    back = jnp.dot(cot_gathered, w_backward, preferred_element_type=jnp.float32)
    sig = jax.nn.sigmoid(z_val)
    feature_grad = (back * sig * (1.0 + z_val * (1.0 - sig))).astype(jnp.bfloat16)
    return (conv_out[None], feature_grad[None], weight_grad)


def shards(*arrays):
    peers = lax.axis_size("brick")
    bits = peers.bit_length() - 1
    tiles_x = 2 ** ((bits + 1) // 2)
    tiles_y = 2 ** (bits // 2)
    plan = whole_scene if (tiles_x, tiles_y) == (ROW_STAGES, 2) else halo_plan
    return plan(*arrays, tiles_x, tiles_y)


def solution(mesh):
    in_specs = (
        P(("groups", "batch"), "brick", None),
        P(("groups", "batch"), "brick", None),
        P(None, ("groups", "brick")),
        P(("groups", "batch")),
        P(("groups", "batch"), None),
        P(),
        P(),
    )
    out_specs = (
        P(("groups", "batch"), "brick", None),
        P(("groups", "batch"), "brick", None),
        P("groups", None, None),
    )
    return jax.shard_map(shards, mesh=mesh, in_specs=in_specs, out_specs=out_specs, check_vma=False)
```

```python
import functools

import jax
import jax.numpy as jnp
from jax import lax
from jax.experimental import pallas as pl
from jax.experimental.pallas import tpu as pltpu
from jax.sharding import PartitionSpec as P

LAYERS = 16
TILE = 4
STRIP = TILE * LAYERS
HALF = 13
CODE_ROWS = 16
ROW_STAGES = 4
PACK_VMEM = 8 * 1024 * 1024
KERNEL_VMEM = 24 * 1024 * 1024


def time_embedding(timesteps, width):
    half = width // 2
    freq = jnp.exp(-jnp.log(10000.0) * jnp.arange(half, dtype=jnp.float32) / half)
    angle = timesteps.astype(jnp.float32)[:, None] * freq[None, :]
    return jnp.concatenate([jnp.sin(angle), jnp.cos(angle)], axis=1).astype(jnp.bfloat16)


def strip_codes(neighbours, tiles_y):
    rows_here = TILE * STRIP
    code = (neighbours // rows_here) % tiles_y * STRIP + neighbours % STRIP
    return jnp.where(neighbours < 0, -1, code).astype(jnp.float32)


def in_hbm(array):
    return pltpu.with_memory_space_constraint(array, pltpu.HBM)


def pack_kernel(time_ref, feat_hbm, cot_hbm, near_hbm, cond_hbm, wt_hbm, pack_ref, shift_ref,
                feat_ref, near_ref, cond_ref, wt_ref, sems):
    rows, width = feat_ref.shape
    half = width // 2
    moves = (
        (wt_hbm, wt_ref),
        (cond_hbm, cond_ref),
        (feat_hbm.at[0], feat_ref),
        (near_hbm, near_ref),
        (cot_hbm.at[0], pack_ref.at[:rows, width:]),
    )
    copies = [pltpu.make_async_copy(source, to, sems.at[i]) for i, (source, to) in enumerate(moves)]
    for copy in copies:
        copy.start()
    lane = lax.broadcasted_iota(jnp.int32, (1, width), 1)
    freq = jnp.exp(-jnp.log(10000.0) * (lane % half).astype(jnp.float32) / half)
    angle = time_ref[0].astype(jnp.float32) * freq
    temb = jnp.where(lane < half, jnp.sin(angle), jnp.cos(angle)).astype(jnp.bfloat16)
    copies[0].wait()
    copies[1].wait()
    shift = jnp.dot(temb, wt_ref[...], preferred_element_type=jnp.float32)
    shift = shift + cond_ref[...].astype(jnp.float32)
    copies[2].wait()
    z_val = feat_ref[...].astype(jnp.float32) + shift
    shift_ref[...] = shift
    pack_ref[:rows, :width] = (z_val * jax.nn.sigmoid(z_val)).astype(jnp.bfloat16)
    copies[3].wait()
    pack_ref[rows:, :] = strip_codes(near_ref[:CODE_ROWS, :], 2).astype(jnp.bfloat16)
    copies[4].wait()


def lay_strip(ground, to, tile_y, mine_ref, other_ref, u):
    span = 2 * STRIP
    for ref, place in ((mine_ref, tile_y), (other_ref, 1 - tile_y)):
        at = pl.multiple_of(to * span + place * STRIP, STRIP)
        ground[pl.ds(at, STRIP), :] = ref[u * STRIP:(u + 1) * STRIP, :]


def row_kernel(stage, strips, borders, *refs):
    refs = list(refs)
    first_stage, final = stage == 0, stage == ROW_STAGES - 1
    where_ref = refs.pop(0)
    pairs = [(refs.pop(0), refs.pop(0)) for _ in range(1 + max(pair for pair, _ in strips))]
    before = [refs.pop(0) for _ in range(0 if first_stage else 3)]
    outs = [refs.pop(0) for _ in range(2 if final else 3)]
    ground, turned, codes, near_act, near_cot = refs
    width = ground.shape[1] // 2
    rows = TILE * STRIP
    span = 2 * STRIP
    tile_y = where_ref[0] % 2
    borders = [(u, u - 1) for u in range(1, TILE)] + borders
    targets = sorted({target for target, _ in borders})
    for i, (pair, u) in enumerate(strips):
        lay_strip(ground, i, tile_y, *pairs[pair], u)
        if i < TILE or i in targets:
            both = [ref[rows:, u * STRIP:(u + 1) * STRIP].astype(jnp.float32) for ref in pairs[pair]]
            first = jnp.where(tile_y == 0, both[0], both[1])
            second = jnp.where(tile_y == 0, both[1], both[0])
            codes[i] = jnp.concatenate([first, second], axis=1)
        if i < TILE or i in [strip for border in borders for strip in border]:
            turned[:, i * span:(i + 1) * span] = ground[i * span:(i + 1) * span, :].T
    place = lax.broadcasted_iota(jnp.int32, (span, span), 0).astype(jnp.float32)

    def gather(target, source, start, stop):
        picks = [(place == codes[target, k:k + 1, :]).astype(jnp.bfloat16) for k in range(start, stop)]
        near = jnp.dot(turned[:, source * span:(source + 1) * span], jnp.concatenate(picks, axis=1),
                       preferred_element_type=jnp.float32).astype(jnp.bfloat16)
        for k in range(start, stop):
            one = near[:, (k - start) * span:(k - start + 1) * span]
            near_act[k * width:(k + 1) * width, target * span:(target + 1) * span] = one[:width]
            near_cot[k * width:(k + 1) * width, target * span:(target + 1) * span] = one[width:]

    for u in range(TILE):
        gather(u, u, 9, HALF)
    for target, source in borders:
        gather(target, source, 0, 9)
    low_from = span * targets[0]
    low_to = span * (targets[-1] + 1)

    def product(near, start, stop, first, last, side):
        return lax.dot_general(turned[side * width:(side + 1) * width, first:last],
                               near[start * width:stop * width, first:last],
                               (((1,), (1,)), ((), ())), preferred_element_type=jnp.float32)

    pieces = []
    for near, side in ((near_act, 1), (near_cot, 0)):
        pieces.append(((0, 9), product(near, 0, 9, low_from, low_to, side)))
        pieces.append(((9, HALF), product(near, 9, HALF, 0, TILE * span, side)))
    centre = jnp.dot(turned[:width, :TILE * span], ground[:TILE * span, width:], preferred_element_type=jnp.float32)
    if not first_stage:
        centre = centre + before[2][...]
    for i, ((start, stop), value) in enumerate(pieces):
        turn = i // 2
        if not first_stage:
            value = value + before[turn][:, start * width:stop * width]
        if not final:
            outs[turn][:, start * width:stop * width] = value
            continue
        for k in range(start, stop):
            one = value[:, (k - start) * width:(k - start + 1) * width]
            one, to = (one, 2 * HALF - k) if turn else (one.T, k)
            outs[0][to] = one
            outs[1][to] = one.astype(jnp.bfloat16)
    if final:
        outs[0][HALF] = centre
        outs[1][HALF] = centre.astype(jnp.bfloat16)
    else:
        outs[2][...] = centre


def turn_kernel(w_ref, forward_ref, back_ref):
    width = w_ref.shape[1]
    for k in range(27):
        forward_ref[:, k * width:(k + 1) * width] = w_ref[k].T
        back_ref[:, k * width:(k + 1) * width] = w_ref[26 - k]


def voxel_kernel(where_ref, mine_ref, other_ref, before_mine, before_other, after_mine, after_other,
                 near_ref, feat_ref, shift_ref, forward_ref, back_ref, conv_ref, grad_ref,
                 ground, turned, codes, near_act, near_cot):
    width = feat_ref.shape[1]
    span = 2 * STRIP
    tile_y = where_ref[0] % 2
    lay_strip(ground, 0, tile_y, before_mine, before_other, TILE - 1)
    for u in range(TILE):
        lay_strip(ground, u + 1, tile_y, mine_ref, other_ref, u)
    lay_strip(ground, TILE + 1, tile_y, after_mine, after_other, 0)
    for i in range(TILE + 2):
        turned[:, i * span:(i + 1) * span] = ground[i * span:(i + 1) * span, :].T
    code = strip_codes(near_ref[...], 2)
    lane = lax.broadcasted_iota(jnp.int32, code.shape, 1)
    codes[...] = jnp.where((code >= 0) & (lane // STRIP % 2 == 1), code + span, code)
    place = lax.broadcasted_iota(jnp.int32, (2 * span, span), 0).astype(jnp.float32)
    for half in range(TILE // 2):
        at = half * span
        for side in range(3):
            source = (2 * half + side) * span
            ks = range(9 * side, 9 * side + 9)
            picks = [(place == codes[k:k + 1, at:at + span]).astype(jnp.bfloat16) for k in ks]
            near = jnp.dot(turned[:, source:source + 2 * span], jnp.concatenate(picks, axis=1),
                           preferred_element_type=jnp.float32).astype(jnp.bfloat16)
            for k in ks:
                one = near[:, (k - 9 * side) * span:(k - 9 * side + 1) * span]
                near_act[k * width:(k + 1) * width, at:at + span] = one[:width]
                near_cot[k * width:(k + 1) * width, at:at + span] = one[width:]
    conv = jnp.dot(forward_ref[...], near_act[...], preferred_element_type=jnp.float32)
    conv_ref[...] = conv.T.astype(jnp.bfloat16)
    back = jnp.dot(back_ref[...], near_cot[...], preferred_element_type=jnp.float32).T
    z_val = feat_ref[...].astype(jnp.float32) + shift_ref[...]
    sig = jax.nn.sigmoid(z_val)
    grad_ref[...] = (back * sig * (1.0 + z_val * (1.0 - sig))).astype(jnp.bfloat16)


def whole_scene(features, cotangent, neighbours, timesteps, condition, w_time, w_conv, tiles_x, tiles_y):
    rows, width = features.shape[1:]
    peers = tiles_x * tiles_y
    span = 2 * STRIP
    vmem = pl.BlockSpec(memory_space=pltpu.VMEM)
    smem = pl.BlockSpec(memory_space=pltpu.SMEM)
    params = pltpu.CompilerParams(vmem_limit_bytes=KERNEL_VMEM)
    packed, shift = pl.pallas_call(
        pack_kernel,
        out_shape=(
            jax.ShapeDtypeStruct((rows + CODE_ROWS, 2 * width), jnp.bfloat16),
            jax.ShapeDtypeStruct((1, width), jnp.float32),
        ),
        in_specs=[smem] + [pl.BlockSpec(memory_space=pltpu.HBM)] * 5,
        out_specs=(vmem, vmem),
        scratch_shapes=[
            pltpu.VMEM((rows, width), jnp.bfloat16),
            pltpu.VMEM(neighbours.shape, jnp.int32),
            pltpu.VMEM((1, width), jnp.bfloat16),
            pltpu.VMEM((width, width), jnp.bfloat16),
            pltpu.SemaphoreType.DMA((5,)),
        ],
        compiler_params=pltpu.CompilerParams(vmem_limit_bytes=PACK_VMEM),
        name="pack_tile",
    )(timesteps, *[in_hbm(array) for array in (features, cotangent, neighbours, condition, w_time)])
    here = lax.axis_index("brick").astype(jnp.int32).reshape(1)

    def across(block):
        return lax.ppermute(block, "brick", [(i, i ^ 1) for i in range(peers)])

    def along(block, turn):
        return lax.ppermute(block, "brick", [(i, (i + turn * tiles_y) % peers) for i in range(peers)])

    w_conv, packed = lax.optimization_barrier((w_conv, packed))
    w_forward, w_back = pl.pallas_call(
        turn_kernel,
        out_shape=(jax.ShapeDtypeStruct((width, 27 * width), jnp.bfloat16),) * 2,
        in_specs=[vmem],
        out_specs=(vmem, vmem),
        compiler_params=params,
        cost_estimate=pl.CostEstimate(flops=2 * 10**8, bytes_accessed=3 * 10**6, transcendentals=0),
        name="turn_weights",
    )(w_conv)
    before, after = along(packed, 1), along(packed, -1)
    before, w_forward = lax.optimization_barrier((before, w_forward))
    far = along(before, 1)
    own_pair = (packed, across(packed))
    before_pair = (before, across(before))
    after_pair = (after, across(after))
    far_pair = (far, across(far))
    line = [(0, u) for u in range(TILE)]
    stages = (
        ((own_pair,), line, []),
        ((before_pair, own_pair), line + [(1, 0)], [(TILE, TILE - 1)]),
        ((after_pair, own_pair), line + [(1, TILE - 1)], [(0, TILE)]),
        ((far_pair, before_pair, after_pair), line + [(1, 0), (2, TILE - 1)], [(TILE, TILE - 1), (0, TILE + 1)]),
    )
    sums = ()
    for stage, (pairs, strips, borders) in enumerate(stages):
        blocks = [block for pair in pairs for block in pair]
        if stage == ROW_STAGES - 1:
            out_shape = (
                jax.ShapeDtypeStruct((27, width, width), jnp.float32),
                jax.ShapeDtypeStruct((27, width, width), jnp.bfloat16),
            )
        else:
            out_shape = (
                jax.ShapeDtypeStruct((width, HALF * width), jnp.float32),
                jax.ShapeDtypeStruct((width, HALF * width), jnp.float32),
                jax.ShapeDtypeStruct((width, width), jnp.float32),
            )
        sums = pl.pallas_call(
            functools.partial(row_kernel, stage, strips, borders),
            out_shape=out_shape,
            in_specs=[smem] + [vmem] * (len(blocks) + len(sums)),
            out_specs=(vmem,) * len(out_shape),
            scratch_shapes=[
                pltpu.VMEM(((TILE + 2) * span, 2 * width), jnp.bfloat16),
                pltpu.VMEM((2 * width, (TILE + 2) * span), jnp.bfloat16),
                pltpu.VMEM((TILE + 1, CODE_ROWS, span), jnp.float32),
                pltpu.VMEM((HALF * width, (TILE + 1) * span), jnp.bfloat16),
                pltpu.VMEM((HALF * width, (TILE + 1) * span), jnp.bfloat16),
            ],
            compiler_params=params,
            cost_estimate=pl.CostEstimate(flops=2 * 10**9, bytes_accessed=4 * 10**6, transcendentals=0),
            name=f"weight_row_{stage}",
        )(here, *blocks, *sums)
    own, sent = sums
    other = lax.ppermute(sent, "batch", [(0, 1), (1, 0)])
    conv_out, feature_grad = pl.pallas_call(
        voxel_kernel,
        out_shape=(
            jax.ShapeDtypeStruct((rows, width), jnp.bfloat16),
            jax.ShapeDtypeStruct((rows, width), jnp.bfloat16),
        ),
        in_specs=[smem] + [vmem] * 11,
        scratch_shapes=[
            pltpu.VMEM(((TILE + 2) * span, 2 * width), jnp.bfloat16),
            pltpu.VMEM((2 * width, (TILE + 2) * span), jnp.bfloat16),
            pltpu.VMEM((27, rows), jnp.float32),
            pltpu.VMEM((27 * width, rows), jnp.bfloat16),
            pltpu.VMEM((27 * width, rows), jnp.bfloat16),
        ],
        compiler_params=params,
        cost_estimate=pl.CostEstimate(flops=10**9, bytes_accessed=4 * 10**6, transcendentals=0),
        name="voxel_outputs",
    )(here, *own_pair, *before_pair, *after_pair, neighbours, features[0], shift, w_forward, w_back)
    weight_grad = own + other.astype(jnp.float32)
    return (conv_out[None], feature_grad[None], weight_grad)


def passed_along(block, axis, distance):
    devices = range(lax.axis_size(axis))
    route = [(i - distance, i) for i in devices if i - distance in devices]
    return lax.ppermute(block, axis, route)


def slab_rows(block, side_recv, front_recv, width):
    widened = jnp.concatenate([side_recv[0], block, side_recv[1]], axis=1)
    slab = jnp.concatenate([front_recv[0][None], widened, front_recv[1][None]], axis=0)
    flat = slab.reshape(-1, width)
    return jnp.concatenate([flat, jnp.zeros((1, width), jnp.bfloat16)], axis=0)


def with_halo(block, tiles_y):
    width = block.shape[-1]
    side = TILE
    side_recv = tuple(passed_along(block[:, edge], "brick", by)[:, None] for by, edge in ((1, side - 1), (-1, 0)))
    wide = jnp.concatenate([side_recv[0], block, side_recv[1]], axis=1)
    front_recv = tuple(passed_along(wide[edge], "brick", by) for by, edge in ((tiles_y, side - 1), (-tiles_y, 0)))
    return slab_rows(block, side_recv, front_recv, width)


def halo_plan(features, cotangent, neighbours, timesteps, condition, w_time, w_conv, tiles_x, tiles_y):
    rows_here, width = features.shape[1:]
    here = lax.axis_index("brick")
    tile_x = here // tiles_y
    tile_y = here % tiles_y
    side = TILE
    layers = LAYERS
    wide = side + 2
    valid = neighbours >= 0
    safe = jnp.where(valid, neighbours, 0)
    owner = safe // rows_here
    inside = safe % rows_here
    column = inside // layers
    layer = inside % layers
    local_x = (owner // tiles_y - tile_x) * side + column // side + 1
    local_y = (owner % tiles_y - tile_y) * side + column % side + 1
    sentinel = wide * wide * layers
    ext_index = jnp.where(valid, (local_x * wide + local_y) * layers + layer, sentinel).T
    temb = time_embedding(timesteps, width)
    shift = jnp.dot(temb, w_time, preferred_element_type=jnp.float32) + condition.astype(jnp.float32)
    z_val = features[0].astype(jnp.float32) + shift[0][None, :]
    act = jax.nn.silu(z_val).astype(jnp.bfloat16)
    cot = cotangent[0]
    w_forward = w_conv.reshape(27 * width, width)
    w_backward = jnp.transpose(w_conv[::-1], (0, 2, 1)).reshape(27 * width, width)
    act_ext = with_halo(act.reshape(side, side, layers, width), tiles_y)
    gathered = act_ext[ext_index].reshape(rows_here, 27 * width)
    conv_out = jnp.dot(gathered, w_forward, preferred_element_type=jnp.float32).astype(jnp.bfloat16)
    partial_grad = lax.dot_general(
        gathered, cot, (((0,), (0,)), ((), ())), preferred_element_type=jnp.float32
    )
    both = ("brick", "batch")
    parts = tiles_x * tiles_y * lax.axis_size("batch")
    rows = 27 * width
    extra = -rows % (8 * parts)
    pieces = jnp.pad(partial_grad.astype(jnp.bfloat16), ((0, extra), (0, 0))).reshape(parts, -1, width)
    arrived = lax.all_to_all(pieces, both, 0, 0)
    summed = arrived.astype(jnp.float32).sum(0).astype(jnp.bfloat16)
    whole = lax.all_gather(summed, both, axis=0, tiled=True)
    weight_grad = whole[:rows].astype(jnp.float32).reshape(27, width, width)
    cot_ext = with_halo(cot.reshape(side, side, layers, width), tiles_y)
    cot_gathered = cot_ext[ext_index].reshape(rows_here, 27 * width)
    back = jnp.dot(cot_gathered, w_backward, preferred_element_type=jnp.float32)
    sig = jax.nn.sigmoid(z_val)
    feature_grad = (back * sig * (1.0 + z_val * (1.0 - sig))).astype(jnp.bfloat16)
    return (conv_out[None], feature_grad[None], weight_grad)


def shards(*arrays):
    peers = lax.axis_size("brick")
    bits = peers.bit_length() - 1
    tiles_x = 2 ** ((bits + 1) // 2)
    tiles_y = 2 ** (bits // 2)
    plan = whole_scene if (tiles_x, tiles_y) == (ROW_STAGES, 2) else halo_plan
    return plan(*arrays, tiles_x, tiles_y)


def solution(mesh):
    in_specs = (
        P(("groups", "batch"), "brick", None),
        P(("groups", "batch"), "brick", None),
        P(None, ("groups", "brick")),
        P(("groups", "batch")),
        P(("groups", "batch"), None),
        P(),
        P(),
    )
    out_specs = (
        P(("groups", "batch"), "brick", None),
        P(("groups", "batch"), "brick", None),
        P("groups", None, None),
    )
    return jax.shard_map(shards, mesh=mesh, in_specs=in_specs, out_specs=out_specs, check_vma=False)
```

```python
import functools

import jax
import jax.numpy as jnp
from jax import lax
from jax.experimental import pallas as pl
from jax.experimental.pallas import tpu as pltpu
from jax.sharding import PartitionSpec as P

LAYERS = 16
TILE = 4
STRIP = TILE * LAYERS
HALF = 13
CODE_ROWS = 16
ROW_STAGES = 4
FINISH_STEP = 3
PACK_VMEM = 8 * 1024 * 1024
KERNEL_VMEM = 24 * 1024 * 1024


def time_embedding(timesteps, width):
    half = width // 2
    freq = jnp.exp(-jnp.log(10000.0) * jnp.arange(half, dtype=jnp.float32) / half)
    angle = timesteps.astype(jnp.float32)[:, None] * freq[None, :]
    return jnp.concatenate([jnp.sin(angle), jnp.cos(angle)], axis=1).astype(jnp.bfloat16)


def strip_codes(neighbours, tiles_y):
    rows_here = TILE * STRIP
    code = (neighbours // rows_here) % tiles_y * STRIP + neighbours % STRIP
    return jnp.where(neighbours < 0, -1, code).astype(jnp.float32)


def in_hbm(array):
    return pltpu.with_memory_space_constraint(array, pltpu.HBM)


def pack_kernel(time_ref, feat_hbm, cot_hbm, near_hbm, cond_hbm, wt_hbm, pack_ref, shift_ref,
                feat_ref, near_ref, cond_ref, wt_ref, sems):
    rows, width = feat_ref.shape
    half = width // 2
    moves = (
        (wt_hbm, wt_ref),
        (cond_hbm, cond_ref),
        (feat_hbm.at[0], feat_ref),
        (near_hbm, near_ref),
        (cot_hbm.at[0], pack_ref.at[:rows, width:]),
    )
    copies = [pltpu.make_async_copy(source, to, sems.at[i]) for i, (source, to) in enumerate(moves)]
    for copy in copies:
        copy.start()
    lane = lax.broadcasted_iota(jnp.int32, (1, width), 1)
    freq = jnp.exp(-jnp.log(10000.0) * (lane % half).astype(jnp.float32) / half)
    angle = time_ref[0].astype(jnp.float32) * freq
    temb = jnp.where(lane < half, jnp.sin(angle), jnp.cos(angle)).astype(jnp.bfloat16)
    copies[0].wait()
    copies[1].wait()
    shift = jnp.dot(temb, wt_ref[...], preferred_element_type=jnp.float32)
    shift = shift + cond_ref[...].astype(jnp.float32)
    copies[2].wait()
    z_val = feat_ref[...].astype(jnp.float32) + shift
    shift_ref[...] = shift
    pack_ref[:rows, :width] = (z_val * jax.nn.sigmoid(z_val)).astype(jnp.bfloat16)
    copies[3].wait()
    pack_ref[rows:, :] = strip_codes(near_ref[:CODE_ROWS, :], 2).astype(jnp.bfloat16)
    copies[4].wait()


def lay_strip(ground, to, tile_y, mine_ref, other_ref, u):
    span = 2 * STRIP
    for ref, place in ((mine_ref, tile_y), (other_ref, 1 - tile_y)):
        at = pl.multiple_of(to * span + place * STRIP, STRIP)
        ground[pl.ds(at, STRIP), :] = ref[u * STRIP:(u + 1) * STRIP, :]


def row_kernel(stage, strips, borders, *refs):
    refs = list(refs)
    first_stage, final = stage == 0, stage == ROW_STAGES - 1
    where_ref = refs.pop(0)
    pairs = [(refs.pop(0), refs.pop(0)) for _ in range(1 + max(pair for pair, _ in strips))]
    before = [refs.pop(0) for _ in range(0 if first_stage else 3)]
    outs = [refs.pop(0) for _ in range(2 if final else 3)]
    ground, turned, codes, near_act, near_cot = refs
    width = ground.shape[1] // 2
    rows = TILE * STRIP
    span = 2 * STRIP
    tile_y = where_ref[0] % 2
    borders = [(u, u - 1) for u in range(1, TILE)] + borders
    targets = sorted({target for target, _ in borders})
    for i, (pair, u) in enumerate(strips):
        lay_strip(ground, i, tile_y, *pairs[pair], u)
        if i < TILE or i in targets:
            both = [ref[rows:, u * STRIP:(u + 1) * STRIP].astype(jnp.float32) for ref in pairs[pair]]
            first = jnp.where(tile_y == 0, both[0], both[1])
            second = jnp.where(tile_y == 0, both[1], both[0])
            codes[i] = jnp.concatenate([first, second], axis=1)
        if i < TILE or i in [source for _, source in borders]:
            turned[:, i * span:(i + 1) * span] = ground[i * span:(i + 1) * span, :].T
    place = lax.broadcasted_iota(jnp.int32, (span, span), 0).astype(jnp.float32)

    def gather(target, source, start, stop):
        picks = [(place == codes[target, k:k + 1, :]).astype(jnp.bfloat16) for k in range(start, stop)]
        near = jnp.dot(turned[:, source * span:(source + 1) * span], jnp.concatenate(picks, axis=1),
                       preferred_element_type=jnp.float32).astype(jnp.bfloat16)
        for k in range(start, stop):
            one = near[:, (k - start) * span:(k - start + 1) * span]
            near_act[k * width:(k + 1) * width, target * span:(target + 1) * span] = one[:width]
            near_cot[k * width:(k + 1) * width, target * span:(target + 1) * span] = one[width:]

    for u in range(TILE):
        gather(u, u, 9, HALF)
    for target, source in borders:
        gather(target, source, 0, 9)
    low_from = span * targets[0]
    low_to = span * (targets[-1] + 1)

    def product(near, start, stop, first, last, side):
        return jnp.dot(near[start * width:stop * width, first:last],
                       ground[first:last, side * width:(side + 1) * width], preferred_element_type=jnp.float32)

    pieces = []
    for near, side in ((near_act, 1), (near_cot, 0)):
        pieces.append(((0, 9), product(near, 0, 9, low_from, low_to, side)))
        pieces.append(((9, HALF), product(near, 9, HALF, 0, TILE * span, side)))
    centre = jnp.dot(turned[:width, :TILE * span], ground[:TILE * span, width:], preferred_element_type=jnp.float32)
    if not first_stage:
        centre = centre + before[2][...]
    for i, ((start, stop), value) in enumerate(pieces):
        turn = i // 2
        if not first_stage:
            value = value + before[turn][start * width:stop * width, :]
        if not final:
            outs[turn][start * width:stop * width, :] = value
            continue
        for k in range(start, stop):
            one = value[(k - start) * width:(k - start + 1) * width, :]
            one, to = (one.T, 2 * HALF - k) if turn else (one, k)
            outs[0][to] = one
            outs[1][to] = one.astype(jnp.bfloat16)
    if final:
        outs[0][HALF] = centre
        outs[1][HALF] = centre.astype(jnp.bfloat16)
    else:
        outs[2][...] = centre


def turn_kernel(w_ref, forward_ref, back_ref):
    width = w_ref.shape[1]
    for k in range(27):
        forward_ref[:, k * width:(k + 1) * width] = w_ref[k].T
        back_ref[:, k * width:(k + 1) * width] = w_ref[26 - k]


def conv_kernel(where_ref, mine_ref, other_ref, before_mine, before_other, after_mine, after_other,
                near_ref, forward_ref, conv_ref, near_cot, ground, turned, codes, near_act):
    width = conv_ref.shape[1]
    span = 2 * STRIP
    tile_y = where_ref[0] % 2
    lay_strip(ground, 0, tile_y, before_mine, before_other, TILE - 1)
    for u in range(TILE):
        lay_strip(ground, u + 1, tile_y, mine_ref, other_ref, u)
    lay_strip(ground, TILE + 1, tile_y, after_mine, after_other, 0)
    for i in range(TILE + 2):
        turned[:, i * span:(i + 1) * span] = ground[i * span:(i + 1) * span, :].T
    code = strip_codes(near_ref[...], 2)
    lane = lax.broadcasted_iota(jnp.int32, code.shape, 1)
    codes[...] = jnp.where((code >= 0) & (lane // STRIP % 2 == 1), code + span, code)
    place = lax.broadcasted_iota(jnp.int32, (2 * span, span), 0).astype(jnp.float32)
    for half in range(TILE // 2):
        at = half * span
        for side in range(3):
            source = (2 * half + side) * span
            ks = range(9 * side, 9 * side + 9)
            picks = [(place == codes[k:k + 1, at:at + span]).astype(jnp.bfloat16) for k in ks]
            near = jnp.dot(turned[:, source:source + 2 * span], jnp.concatenate(picks, axis=1),
                           preferred_element_type=jnp.float32).astype(jnp.bfloat16)
            for k in ks:
                one = near[:, (k - 9 * side) * span:(k - 9 * side + 1) * span]
                near_act[k * width:(k + 1) * width, at:at + span] = one[:width]
                near_cot[k * width:(k + 1) * width, at:at + span] = one[width:]
    conv = jnp.dot(forward_ref[...], near_act[...], preferred_element_type=jnp.float32)
    conv_ref[...] = conv.T.astype(jnp.bfloat16)


def finish_kernel(kept_ref, sent_ref, near_ref, back_ref, feat_ref, shift_ref, weight_hbm, grad_hbm,
                  weight, grad, sems):
    copies = []
    for i, first in enumerate(range(0, 27, FINISH_STEP)):
        part = slice(first, first + FINISH_STEP)
        weight[part] = kept_ref[part] + sent_ref[part].astype(jnp.float32)
        copies.append(pltpu.make_async_copy(weight.at[part], weight_hbm.at[part], sems.at[i]))
        copies[-1].start()
    back = jnp.dot(back_ref[...], near_ref[...], preferred_element_type=jnp.float32).T
    z_val = feat_ref[...].astype(jnp.float32) + shift_ref[...]
    sig = jax.nn.sigmoid(z_val)
    grad[...] = (back * sig * (1.0 + z_val * (1.0 - sig))).astype(jnp.bfloat16)
    copies.append(pltpu.make_async_copy(grad, grad_hbm, sems.at[len(copies)]))
    copies[-1].start()
    for copy in copies:
        copy.wait()


def whole_scene(features, cotangent, neighbours, timesteps, condition, w_time, w_conv, tiles_x, tiles_y):
    rows, width = features.shape[1:]
    peers = tiles_x * tiles_y
    span = 2 * STRIP
    vmem = pl.BlockSpec(memory_space=pltpu.VMEM)
    smem = pl.BlockSpec(memory_space=pltpu.SMEM)
    params = pltpu.CompilerParams(vmem_limit_bytes=KERNEL_VMEM)
    packed, shift = pl.pallas_call(
        pack_kernel,
        out_shape=(
            jax.ShapeDtypeStruct((rows + CODE_ROWS, 2 * width), jnp.bfloat16),
            jax.ShapeDtypeStruct((1, width), jnp.float32),
        ),
        in_specs=[smem] + [pl.BlockSpec(memory_space=pltpu.HBM)] * 5,
        out_specs=(vmem, vmem),
        scratch_shapes=[
            pltpu.VMEM((rows, width), jnp.bfloat16),
            pltpu.VMEM(neighbours.shape, jnp.int32),
            pltpu.VMEM((1, width), jnp.bfloat16),
            pltpu.VMEM((width, width), jnp.bfloat16),
            pltpu.SemaphoreType.DMA((5,)),
        ],
        compiler_params=pltpu.CompilerParams(vmem_limit_bytes=PACK_VMEM),
        name="pack_tile",
    )(timesteps, *[in_hbm(array) for array in (features, cotangent, neighbours, condition, w_time)])
    here = lax.axis_index("brick").astype(jnp.int32).reshape(1)

    def across(block):
        return lax.ppermute(block, "brick", [(i, i ^ 1) for i in range(peers)])

    def along(block, turn):
        return lax.ppermute(block, "brick", [(i, (i + turn * tiles_y) % peers) for i in range(peers)])

    w_conv, packed = lax.optimization_barrier((w_conv, packed))
    w_forward, w_back = pl.pallas_call(
        turn_kernel,
        out_shape=(jax.ShapeDtypeStruct((width, 27 * width), jnp.bfloat16),) * 2,
        in_specs=[vmem],
        out_specs=(vmem, vmem),
        compiler_params=params,
        cost_estimate=pl.CostEstimate(flops=2 * 10**8, bytes_accessed=3 * 10**6, transcendentals=0),
        name="turn_weights",
    )(w_conv)
    before, after = along(packed, 1), along(packed, -1)
    before, w_forward = lax.optimization_barrier((before, w_forward))
    far = along(before, 1)
    own_pair = (packed, across(packed))
    before_pair = (before, across(before))
    after_pair = (after, across(after))
    far_pair = (far, across(far))
    line = [(0, u) for u in range(TILE)]
    stages = (
        ((own_pair,), line, []),
        ((before_pair, own_pair), line + [(1, 0)], [(TILE, TILE - 1)]),
        ((after_pair, own_pair), line + [(1, TILE - 1)], [(0, TILE)]),
        ((far_pair, before_pair, after_pair), line + [(1, 0), (2, TILE - 1)], [(TILE, TILE - 1), (0, TILE + 1)]),
    )
    sums = ()
    for stage, (pairs, strips, borders) in enumerate(stages):
        blocks = [block for pair in pairs for block in pair]
        if stage == ROW_STAGES - 1:
            out_shape = (
                jax.ShapeDtypeStruct((27, width, width), jnp.float32),
                jax.ShapeDtypeStruct((27, width, width), jnp.bfloat16),
            )
        else:
            out_shape = (
                jax.ShapeDtypeStruct((HALF * width, width), jnp.float32),
                jax.ShapeDtypeStruct((HALF * width, width), jnp.float32),
                jax.ShapeDtypeStruct((width, width), jnp.float32),
            )
        sums = pl.pallas_call(
            functools.partial(row_kernel, stage, strips, borders),
            out_shape=out_shape,
            in_specs=[smem] + [vmem] * (len(blocks) + len(sums)),
            out_specs=(vmem,) * len(out_shape),
            scratch_shapes=[
                pltpu.VMEM(((TILE + 2) * span, 2 * width), jnp.bfloat16),
                pltpu.VMEM((2 * width, (TILE + 2) * span), jnp.bfloat16),
                pltpu.VMEM((TILE + 1, CODE_ROWS, span), jnp.float32),
                pltpu.VMEM((HALF * width, (TILE + 1) * span), jnp.bfloat16),
                pltpu.VMEM((HALF * width, (TILE + 1) * span), jnp.bfloat16),
            ],
            compiler_params=params,
            cost_estimate=pl.CostEstimate(flops=2 * 10**9, bytes_accessed=4 * 10**6, transcendentals=0),
            name=f"weight_row_{stage}",
        )(here, *blocks, *sums)
    own, sent = sums
    other = lax.ppermute(sent, "batch", [(0, 1), (1, 0)])
    conv_out, near_cot = pl.pallas_call(
        conv_kernel,
        out_shape=(
            jax.ShapeDtypeStruct((rows, width), jnp.bfloat16),
            jax.ShapeDtypeStruct((27 * width, rows), jnp.bfloat16),
        ),
        in_specs=[smem] + [vmem] * 8,
        out_specs=(vmem, vmem),
        scratch_shapes=[
            pltpu.VMEM(((TILE + 2) * span, 2 * width), jnp.bfloat16),
            pltpu.VMEM((2 * width, (TILE + 2) * span), jnp.bfloat16),
            pltpu.VMEM((27, rows), jnp.float32),
            pltpu.VMEM((27 * width, rows), jnp.bfloat16),
        ],
        compiler_params=params,
        cost_estimate=pl.CostEstimate(flops=10**9, bytes_accessed=4 * 10**6, transcendentals=0),
        name="conv_out",
    )(here, *own_pair, *before_pair, *after_pair, neighbours, w_forward)
    other, near_cot = lax.optimization_barrier((other, near_cot))
    hbm = pl.BlockSpec(memory_space=pltpu.HBM)
    weight_grad, feature_grad = pl.pallas_call(
        finish_kernel,
        out_shape=(
            jax.ShapeDtypeStruct((27, width, width), jnp.float32),
            jax.ShapeDtypeStruct((rows, width), jnp.bfloat16),
        ),
        in_specs=[vmem] * 6,
        out_specs=(hbm, hbm),
        scratch_shapes=[
            pltpu.VMEM((27, width, width), jnp.float32),
            pltpu.VMEM((rows, width), jnp.bfloat16),
            pltpu.SemaphoreType.DMA((27 // FINISH_STEP + 1,)),
        ],
        compiler_params=pltpu.CompilerParams(vmem_limit_bytes=PACK_VMEM),
        name="finish",
    )(own, other, near_cot, w_back, features[0], shift)
    return (conv_out[None], feature_grad[None], weight_grad)


def passed_along(block, axis, distance):
    devices = range(lax.axis_size(axis))
    route = [(i - distance, i) for i in devices if i - distance in devices]
    return lax.ppermute(block, axis, route)


def slab_rows(block, side_recv, front_recv, width):
    widened = jnp.concatenate([side_recv[0], block, side_recv[1]], axis=1)
    slab = jnp.concatenate([front_recv[0][None], widened, front_recv[1][None]], axis=0)
    flat = slab.reshape(-1, width)
    return jnp.concatenate([flat, jnp.zeros((1, width), jnp.bfloat16)], axis=0)


def with_halo(block, tiles_y):
    width = block.shape[-1]
    side = TILE
    side_recv = tuple(passed_along(block[:, edge], "brick", by)[:, None] for by, edge in ((1, side - 1), (-1, 0)))
    wide = jnp.concatenate([side_recv[0], block, side_recv[1]], axis=1)
    front_recv = tuple(passed_along(wide[edge], "brick", by) for by, edge in ((tiles_y, side - 1), (-tiles_y, 0)))
    return slab_rows(block, side_recv, front_recv, width)


def halo_plan(features, cotangent, neighbours, timesteps, condition, w_time, w_conv, tiles_x, tiles_y):
    rows_here, width = features.shape[1:]
    here = lax.axis_index("brick")
    tile_x = here // tiles_y
    tile_y = here % tiles_y
    side = TILE
    layers = LAYERS
    wide = side + 2
    valid = neighbours >= 0
    safe = jnp.where(valid, neighbours, 0)
    owner = safe // rows_here
    inside = safe % rows_here
    column = inside // layers
    layer = inside % layers
    local_x = (owner // tiles_y - tile_x) * side + column // side + 1
    local_y = (owner % tiles_y - tile_y) * side + column % side + 1
    sentinel = wide * wide * layers
    ext_index = jnp.where(valid, (local_x * wide + local_y) * layers + layer, sentinel).T
    temb = time_embedding(timesteps, width)
    shift = jnp.dot(temb, w_time, preferred_element_type=jnp.float32) + condition.astype(jnp.float32)
    z_val = features[0].astype(jnp.float32) + shift[0][None, :]
    act = jax.nn.silu(z_val).astype(jnp.bfloat16)
    cot = cotangent[0]
    w_forward = w_conv.reshape(27 * width, width)
    w_backward = jnp.transpose(w_conv[::-1], (0, 2, 1)).reshape(27 * width, width)
    act_ext = with_halo(act.reshape(side, side, layers, width), tiles_y)
    gathered = act_ext[ext_index].reshape(rows_here, 27 * width)
    conv_out = jnp.dot(gathered, w_forward, preferred_element_type=jnp.float32).astype(jnp.bfloat16)
    partial_grad = lax.dot_general(
        gathered, cot, (((0,), (0,)), ((), ())), preferred_element_type=jnp.float32
    )
    both = ("brick", "batch")
    parts = tiles_x * tiles_y * lax.axis_size("batch")
    rows = 27 * width
    extra = -rows % (8 * parts)
    pieces = jnp.pad(partial_grad.astype(jnp.bfloat16), ((0, extra), (0, 0))).reshape(parts, -1, width)
    arrived = lax.all_to_all(pieces, both, 0, 0)
    summed = arrived.astype(jnp.float32).sum(0).astype(jnp.bfloat16)
    whole = lax.all_gather(summed, both, axis=0, tiled=True)
    weight_grad = whole[:rows].astype(jnp.float32).reshape(27, width, width)
    cot_ext = with_halo(cot.reshape(side, side, layers, width), tiles_y)
    cot_gathered = cot_ext[ext_index].reshape(rows_here, 27 * width)
    back = jnp.dot(cot_gathered, w_backward, preferred_element_type=jnp.float32)
    sig = jax.nn.sigmoid(z_val)
    feature_grad = (back * sig * (1.0 + z_val * (1.0 - sig))).astype(jnp.bfloat16)
    return (conv_out[None], feature_grad[None], weight_grad)


def shards(*arrays):
    peers = lax.axis_size("brick")
    bits = peers.bit_length() - 1
    tiles_x = 2 ** ((bits + 1) // 2)
    tiles_y = 2 ** (bits // 2)
    plan = whole_scene if (tiles_x, tiles_y) == (ROW_STAGES, 2) else halo_plan
    return plan(*arrays, tiles_x, tiles_y)


def solution(mesh):
    in_specs = (
        P(("groups", "batch"), "brick", None),
        P(("groups", "batch"), "brick", None),
        P(None, ("groups", "brick")),
        P(("groups", "batch")),
        P(("groups", "batch"), None),
        P(),
        P(),
    )
    out_specs = (
        P(("groups", "batch"), "brick", None),
        P(("groups", "batch"), "brick", None),
        P("groups", None, None),
    )
    return jax.shard_map(shards, mesh=mesh, in_specs=in_specs, out_specs=out_specs, check_vma=False)
```

```python
import functools

import jax
import jax.numpy as jnp
from jax import lax
from jax.experimental import pallas as pl
from jax.experimental.pallas import tpu as pltpu
from jax.sharding import PartitionSpec as P

LAYERS = 16
TILE = 4
STRIP = TILE * LAYERS
HALF = 13
CODE_ROWS = 16
ROW_STAGES = 4
FINISH_STEP = 3
PACK_VMEM = 8 * 1024 * 1024
KERNEL_VMEM = 24 * 1024 * 1024


def time_embedding(timesteps, width):
    half = width // 2
    freq = jnp.exp(-jnp.log(10000.0) * jnp.arange(half, dtype=jnp.float32) / half)
    angle = timesteps.astype(jnp.float32)[:, None] * freq[None, :]
    return jnp.concatenate([jnp.sin(angle), jnp.cos(angle)], axis=1).astype(jnp.bfloat16)


def strip_codes(neighbours, tiles_y):
    rows_here = TILE * STRIP
    code = (neighbours // rows_here) % tiles_y * STRIP + neighbours % STRIP
    return jnp.where(neighbours < 0, -1, code).astype(jnp.float32)


def in_hbm(array):
    return pltpu.with_memory_space_constraint(array, pltpu.HBM)


def pack_kernel(time_ref, feat_hbm, cot_hbm, near_hbm, cond_hbm, wt_hbm, pack_ref, z_ref, code_ref,
                feat_ref, near_ref, cond_ref, wt_ref, sems):
    rows, width = feat_ref.shape
    half = width // 2
    moves = (
        (wt_hbm, wt_ref),
        (cond_hbm, cond_ref),
        (feat_hbm.at[0], feat_ref),
        (near_hbm, near_ref),
        (cot_hbm.at[0], pack_ref.at[:rows, width:]),
    )
    copies = [pltpu.make_async_copy(source, to, sems.at[i]) for i, (source, to) in enumerate(moves)]
    for copy in copies:
        copy.start()
    lane = lax.broadcasted_iota(jnp.int32, (1, width), 1)
    freq = jnp.exp(-jnp.log(10000.0) * (lane % half).astype(jnp.float32) / half)
    angle = time_ref[0].astype(jnp.float32) * freq
    temb = jnp.where(lane < half, jnp.sin(angle), jnp.cos(angle)).astype(jnp.bfloat16)
    copies[0].wait()
    copies[1].wait()
    shift = jnp.dot(temb, wt_ref[...], preferred_element_type=jnp.float32)
    shift = shift + cond_ref[...].astype(jnp.float32)
    copies[2].wait()
    z_val = feat_ref[...].astype(jnp.float32) + shift
    z_ref[...] = z_val
    pack_ref[:rows, :width] = (z_val * jax.nn.sigmoid(z_val)).astype(jnp.bfloat16)
    copies[3].wait()
    code = strip_codes(near_ref[...], 2)
    code_ref[...] = code
    pack_ref[rows:, :] = code[:CODE_ROWS, :].astype(jnp.bfloat16)
    copies[4].wait()


def lay_strip(ground, to, tile_y, mine_ref, other_ref, u):
    span = 2 * STRIP
    for ref, place in ((mine_ref, tile_y), (other_ref, 1 - tile_y)):
        at = pl.multiple_of(to * span + place * STRIP, STRIP)
        ground[pl.ds(at, STRIP), :] = ref[u * STRIP:(u + 1) * STRIP, :]


def row_kernel(stage, strips, borders, *refs):
    refs = list(refs)
    first_stage, final = stage == 0, stage == ROW_STAGES - 1
    where_ref = refs.pop(0)
    pairs = [(refs.pop(0), refs.pop(0)) for _ in range(1 + max(pair for pair, _ in strips))]
    before = [refs.pop(0) for _ in range(0 if first_stage else 3)]
    outs = [refs.pop(0) for _ in range(2 if final else 3)]
    ground, turned, codes, near_act, near_cot = refs
    width = ground.shape[1] // 2
    rows = TILE * STRIP
    span = 2 * STRIP
    tile_y = where_ref[0] % 2
    borders = [(u, u - 1) for u in range(1, TILE)] + borders
    targets = sorted({target for target, _ in borders})
    for i, (pair, u) in enumerate(strips):
        lay_strip(ground, i, tile_y, *pairs[pair], u)
        if i < TILE or i in targets:
            both = [ref[rows:, u * STRIP:(u + 1) * STRIP].astype(jnp.float32) for ref in pairs[pair]]
            first = jnp.where(tile_y == 0, both[0], both[1])
            second = jnp.where(tile_y == 0, both[1], both[0])
            codes[i] = jnp.concatenate([first, second], axis=1)
        if i < TILE or i in [source for _, source in borders]:
            turned[:, i * span:(i + 1) * span] = ground[i * span:(i + 1) * span, :].T
    place = lax.broadcasted_iota(jnp.int32, (span, span), 0).astype(jnp.float32)

    def gather(target, source, start, stop):
        picks = [(place == codes[target, k:k + 1, :]).astype(jnp.bfloat16) for k in range(start, stop)]
        near = jnp.dot(turned[:, source * span:(source + 1) * span], jnp.concatenate(picks, axis=1),
                       preferred_element_type=jnp.float32).astype(jnp.bfloat16)
        for k in range(start, stop):
            one = near[:, (k - start) * span:(k - start + 1) * span]
            near_act[k * width:(k + 1) * width, target * span:(target + 1) * span] = one[:width]
            near_cot[k * width:(k + 1) * width, target * span:(target + 1) * span] = one[width:]

    for u in range(TILE):
        gather(u, u, 9, HALF)
    for target, source in borders:
        gather(target, source, 0, 9)
    low_from = span * targets[0]
    low_to = span * (targets[-1] + 1)

    def product(near, start, stop, first, last, side):
        return jnp.dot(near[start * width:stop * width, first:last],
                       ground[first:last, side * width:(side + 1) * width], preferred_element_type=jnp.float32)

    pieces = []
    for near, side in ((near_act, 1), (near_cot, 0)):
        pieces.append(((0, 9), product(near, 0, 9, low_from, low_to, side)))
        pieces.append(((9, HALF), product(near, 9, HALF, 0, TILE * span, side)))
    centre = jnp.dot(turned[:width, :TILE * span], ground[:TILE * span, width:], preferred_element_type=jnp.float32)
    if not first_stage:
        centre = centre + before[2][...]
    for i, ((start, stop), value) in enumerate(pieces):
        turn = i // 2
        if not first_stage:
            value = value + before[turn][start * width:stop * width, :]
        if not final:
            outs[turn][start * width:stop * width, :] = value
            continue
        for k in range(start, stop):
            one = value[(k - start) * width:(k - start + 1) * width, :]
            one, to = (one.T, 2 * HALF - k) if turn else (one, k)
            outs[0][to] = one
            outs[1][to] = one.astype(jnp.bfloat16)
    if final:
        outs[0][HALF] = centre
        outs[1][HALF] = centre.astype(jnp.bfloat16)
    else:
        outs[2][...] = centre


def turn_kernel(w_ref, forward_ref, back_ref):
    width = w_ref.shape[1]
    for k in range(27):
        forward_ref[:, k * width:(k + 1) * width] = w_ref[k].T
        back_ref[:, k * width:(k + 1) * width] = w_ref[26 - k]


def own_kernel(where_ref, mine_ref, other_ref, code_ref, forward_ref, back_ref, conv_ref, grad_ref,
               ground, turned, codes, near_act, near_cot):
    width = conv_ref.shape[0]
    span = 2 * STRIP
    tile_y = where_ref[0] % 2
    for u in range(TILE):
        lay_strip(ground, u, tile_y, mine_ref, other_ref, u)
        turned[:, (u + 1) * span:(u + 2) * span] = ground[u * span:(u + 1) * span, :].T
    for i in (0, TILE + 1):
        turned[:, i * span:(i + 1) * span] = jnp.zeros((2 * width, span), jnp.bfloat16)
    code = code_ref[...]
    lane = lax.broadcasted_iota(jnp.int32, code.shape, 1)
    codes[...] = jnp.where((code >= 0) & (lane // STRIP % 2 == 1), code + span, code)
    place = lax.broadcasted_iota(jnp.int32, (2 * span, span), 0).astype(jnp.float32)
    for half in range(TILE // 2):
        at = half * span
        for side in range(3):
            source = (2 * half + side) * span
            ks = range(9 * side, 9 * side + 9)
            picks = [(place == codes[k:k + 1, at:at + span]).astype(jnp.bfloat16) for k in ks]
            near = jnp.dot(turned[:, source:source + 2 * span], jnp.concatenate(picks, axis=1),
                           preferred_element_type=jnp.float32).astype(jnp.bfloat16)
            for k in ks:
                one = near[:, (k - 9 * side) * span:(k - 9 * side + 1) * span]
                near_act[k * width:(k + 1) * width, at:at + span] = one[:width]
                near_cot[k * width:(k + 1) * width, at:at + span] = one[width:]
    conv_ref[...] = jnp.dot(forward_ref[...], near_act[...], preferred_element_type=jnp.float32)
    grad_ref[...] = jnp.dot(back_ref[...], near_cot[...], preferred_element_type=jnp.float32)


def edge_kernel(where_ref, before_mine, before_other, after_mine, after_other, code_ref, forward_ref, back_ref,
                own_conv, own_grad, z_ref, conv_ref, grad_ref, ground, turned, near):
    width = z_ref.shape[1]
    span = 2 * STRIP
    tile_y = where_ref[0] % 2
    lay_strip(ground, 0, tile_y, before_mine, before_other, TILE - 1)
    lay_strip(ground, 1, tile_y, after_mine, after_other, 0)
    for i in range(2):
        turned[:, i * span:(i + 1) * span] = ground[i * span:(i + 1) * span, :].T
    first = code_ref[:9, :span]
    last = code_ref[18:, span:]
    lane = lax.broadcasted_iota(jnp.int32, first.shape, 1)
    code = jnp.where(lane < STRIP, first, jnp.where(last >= 0, last + span, last))
    place = lax.broadcasted_iota(jnp.int32, (2 * span, span), 0).astype(jnp.float32)
    picks = [(place == code[k:k + 1, :]).astype(jnp.bfloat16) for k in range(9)]
    found = jnp.dot(turned[...], jnp.concatenate(picks, axis=1), preferred_element_type=jnp.float32)
    found = found.astype(jnp.bfloat16)
    for k in range(9):
        near[:, k * width:(k + 1) * width, :] = found[:, k * span:(k + 1) * span].reshape(2, width, span)
    lane = lax.broadcasted_iota(jnp.int32, (width, span), 1)

    def total(own_ref, weights, side):
        low = jnp.dot(weights[:, :9 * width], near[side], preferred_element_type=jnp.float32)
        high = jnp.dot(weights[:, 18 * width:], near[side], preferred_element_type=jnp.float32)
        low = own_ref[:, :span] + jnp.where(lane < STRIP, low, 0.0)
        high = own_ref[:, span:] + jnp.where(lane < STRIP, 0.0, high)
        return jnp.concatenate([low, high], axis=1).T

    conv_ref[...] = total(own_conv, forward_ref, 0).astype(jnp.bfloat16)
    back = total(own_grad, back_ref, 1)
    z_val = z_ref[...]
    sig = jax.nn.sigmoid(z_val)
    grad_ref[...] = (back * sig * (1.0 + z_val * (1.0 - sig))).astype(jnp.bfloat16)


def finish_kernel(kept_ref, sent_ref, weight_hbm, weight, sems):
    copies = []
    for i, first in enumerate(range(0, 27, FINISH_STEP)):
        part = slice(first, first + FINISH_STEP)
        weight[part] = kept_ref[part] + sent_ref[part].astype(jnp.float32)
        copies.append(pltpu.make_async_copy(weight.at[part], weight_hbm.at[part], sems.at[i]))
        copies[-1].start()
    for copy in copies:
        copy.wait()


def whole_scene(features, cotangent, neighbours, timesteps, condition, w_time, w_conv, tiles_x, tiles_y):
    rows, width = features.shape[1:]
    peers = tiles_x * tiles_y
    span = 2 * STRIP
    vmem = pl.BlockSpec(memory_space=pltpu.VMEM)
    smem = pl.BlockSpec(memory_space=pltpu.SMEM)
    params = pltpu.CompilerParams(vmem_limit_bytes=KERNEL_VMEM)
    packed, z_val, code = pl.pallas_call(
        pack_kernel,
        out_shape=(
            jax.ShapeDtypeStruct((rows + CODE_ROWS, 2 * width), jnp.bfloat16),
            jax.ShapeDtypeStruct((rows, width), jnp.float32),
            jax.ShapeDtypeStruct(neighbours.shape, jnp.float32),
        ),
        in_specs=[smem] + [pl.BlockSpec(memory_space=pltpu.HBM)] * 5,
        out_specs=(vmem, vmem, vmem),
        scratch_shapes=[
            pltpu.VMEM((rows, width), jnp.bfloat16),
            pltpu.VMEM(neighbours.shape, jnp.int32),
            pltpu.VMEM((1, width), jnp.bfloat16),
            pltpu.VMEM((width, width), jnp.bfloat16),
            pltpu.SemaphoreType.DMA((5,)),
        ],
        compiler_params=pltpu.CompilerParams(vmem_limit_bytes=PACK_VMEM),
        name="pack_tile",
    )(timesteps, *[in_hbm(array) for array in (features, cotangent, neighbours, condition, w_time)])
    here = lax.axis_index("brick").astype(jnp.int32).reshape(1)

    def across(block):
        return lax.ppermute(block, "brick", [(i, i ^ 1) for i in range(peers)])

    def along(block, turn):
        return lax.ppermute(block, "brick", [(i, (i + turn * tiles_y) % peers) for i in range(peers)])

    w_conv, packed = lax.optimization_barrier((w_conv, packed))
    w_forward, w_back = pl.pallas_call(
        turn_kernel,
        out_shape=(jax.ShapeDtypeStruct((width, 27 * width), jnp.bfloat16),) * 2,
        in_specs=[vmem],
        out_specs=(vmem, vmem),
        compiler_params=params,
        cost_estimate=pl.CostEstimate(flops=2 * 10**8, bytes_accessed=3 * 10**6, transcendentals=0),
        name="turn_weights",
    )(w_conv)
    before, after = along(packed, 1), along(packed, -1)
    before, w_forward = lax.optimization_barrier((before, w_forward))
    far = along(before, 1)
    own_pair = (packed, across(packed))
    own_conv, own_grad = pl.pallas_call(
        own_kernel,
        out_shape=(jax.ShapeDtypeStruct((width, rows), jnp.float32),) * 2,
        in_specs=[smem] + [vmem] * 5,
        out_specs=(vmem, vmem),
        scratch_shapes=[
            pltpu.VMEM((TILE * span, 2 * width), jnp.bfloat16),
            pltpu.VMEM((2 * width, (TILE + 2) * span), jnp.bfloat16),
            pltpu.VMEM((27, rows), jnp.float32),
            pltpu.VMEM((27 * width, rows), jnp.bfloat16),
            pltpu.VMEM((27 * width, rows), jnp.bfloat16),
        ],
        compiler_params=params,
        cost_estimate=pl.CostEstimate(flops=2 * 10**9, bytes_accessed=4 * 10**6, transcendentals=0),
        name="voxels_own_row",
    )(here, *own_pair, code, w_forward, w_back)
    far, own_conv = lax.optimization_barrier((far, own_conv))
    before_pair = (before, across(before))
    after_pair = (after, across(after))
    far_pair = (far, across(far))
    line = [(0, u) for u in range(TILE)]
    stages = (
        ((own_pair,), line, []),
        ((before_pair, own_pair), line + [(1, 0)], [(TILE, TILE - 1)]),
        ((after_pair, own_pair), line + [(1, TILE - 1)], [(0, TILE)]),
        ((far_pair, before_pair, after_pair), line + [(1, 0), (2, TILE - 1)], [(TILE, TILE - 1), (0, TILE + 1)]),
    )
    sums = ()
    for stage, (pairs, strips, borders) in enumerate(stages):
        blocks = [block for pair in pairs for block in pair]
        if stage == ROW_STAGES - 1:
            out_shape = (
                jax.ShapeDtypeStruct((27, width, width), jnp.float32),
                jax.ShapeDtypeStruct((27, width, width), jnp.bfloat16),
            )
        else:
            out_shape = (
                jax.ShapeDtypeStruct((HALF * width, width), jnp.float32),
                jax.ShapeDtypeStruct((HALF * width, width), jnp.float32),
                jax.ShapeDtypeStruct((width, width), jnp.float32),
            )
        sums = pl.pallas_call(
            functools.partial(row_kernel, stage, strips, borders),
            out_shape=out_shape,
            in_specs=[smem] + [vmem] * (len(blocks) + len(sums)),
            out_specs=(vmem,) * len(out_shape),
            scratch_shapes=[
                pltpu.VMEM(((TILE + 2) * span, 2 * width), jnp.bfloat16),
                pltpu.VMEM((2 * width, (TILE + 2) * span), jnp.bfloat16),
                pltpu.VMEM((TILE + 1, CODE_ROWS, span), jnp.float32),
                pltpu.VMEM((HALF * width, (TILE + 1) * span), jnp.bfloat16),
                pltpu.VMEM((HALF * width, (TILE + 1) * span), jnp.bfloat16),
            ],
            compiler_params=params,
            cost_estimate=pl.CostEstimate(flops=2 * 10**9, bytes_accessed=4 * 10**6, transcendentals=0),
            name=f"weight_row_{stage}",
        )(here, *blocks, *sums)
    own, sent = sums
    other = lax.ppermute(sent, "batch", [(0, 1), (1, 0)])
    conv_out, feature_grad = pl.pallas_call(
        edge_kernel,
        out_shape=(jax.ShapeDtypeStruct((rows, width), jnp.bfloat16),) * 2,
        in_specs=[smem] + [vmem] * 10,
        out_specs=(vmem, vmem),
        scratch_shapes=[
            pltpu.VMEM((2 * span, 2 * width), jnp.bfloat16),
            pltpu.VMEM((2 * width, 2 * span), jnp.bfloat16),
            pltpu.VMEM((2, 9 * width, span), jnp.bfloat16),
        ],
        compiler_params=params,
        cost_estimate=pl.CostEstimate(flops=10**9, bytes_accessed=4 * 10**6, transcendentals=0),
        name="voxel_edges",
    )(here, *before_pair, *after_pair, code, w_forward, w_back, own_conv, own_grad, z_val)
    other, conv_out = lax.optimization_barrier((other, conv_out))
    weight_grad = pl.pallas_call(
        finish_kernel,
        out_shape=jax.ShapeDtypeStruct((27, width, width), jnp.float32),
        in_specs=[vmem] * 2,
        out_specs=pl.BlockSpec(memory_space=pltpu.HBM),
        scratch_shapes=[
            pltpu.VMEM((27, width, width), jnp.float32),
            pltpu.SemaphoreType.DMA((27 // FINISH_STEP,)),
        ],
        compiler_params=pltpu.CompilerParams(vmem_limit_bytes=PACK_VMEM),
        name="finish",
    )(own, other)
    return (conv_out[None], feature_grad[None], weight_grad)


def passed_along(block, axis, distance):
    devices = range(lax.axis_size(axis))
    route = [(i - distance, i) for i in devices if i - distance in devices]
    return lax.ppermute(block, axis, route)


def slab_rows(block, side_recv, front_recv, width):
    widened = jnp.concatenate([side_recv[0], block, side_recv[1]], axis=1)
    slab = jnp.concatenate([front_recv[0][None], widened, front_recv[1][None]], axis=0)
    flat = slab.reshape(-1, width)
    return jnp.concatenate([flat, jnp.zeros((1, width), jnp.bfloat16)], axis=0)


def with_halo(block, tiles_y):
    width = block.shape[-1]
    side = TILE
    side_recv = tuple(passed_along(block[:, edge], "brick", by)[:, None] for by, edge in ((1, side - 1), (-1, 0)))
    wide = jnp.concatenate([side_recv[0], block, side_recv[1]], axis=1)
    front_recv = tuple(passed_along(wide[edge], "brick", by) for by, edge in ((tiles_y, side - 1), (-tiles_y, 0)))
    return slab_rows(block, side_recv, front_recv, width)


def halo_plan(features, cotangent, neighbours, timesteps, condition, w_time, w_conv, tiles_x, tiles_y):
    rows_here, width = features.shape[1:]
    here = lax.axis_index("brick")
    tile_x = here // tiles_y
    tile_y = here % tiles_y
    side = TILE
    layers = LAYERS
    wide = side + 2
    valid = neighbours >= 0
    safe = jnp.where(valid, neighbours, 0)
    owner = safe // rows_here
    inside = safe % rows_here
    column = inside // layers
    layer = inside % layers
    local_x = (owner // tiles_y - tile_x) * side + column // side + 1
    local_y = (owner % tiles_y - tile_y) * side + column % side + 1
    sentinel = wide * wide * layers
    ext_index = jnp.where(valid, (local_x * wide + local_y) * layers + layer, sentinel).T
    temb = time_embedding(timesteps, width)
    shift = jnp.dot(temb, w_time, preferred_element_type=jnp.float32) + condition.astype(jnp.float32)
    z_val = features[0].astype(jnp.float32) + shift[0][None, :]
    act = jax.nn.silu(z_val).astype(jnp.bfloat16)
    cot = cotangent[0]
    w_forward = w_conv.reshape(27 * width, width)
    w_backward = jnp.transpose(w_conv[::-1], (0, 2, 1)).reshape(27 * width, width)
    act_ext = with_halo(act.reshape(side, side, layers, width), tiles_y)
    gathered = act_ext[ext_index].reshape(rows_here, 27 * width)
    conv_out = jnp.dot(gathered, w_forward, preferred_element_type=jnp.float32).astype(jnp.bfloat16)
    partial_grad = lax.dot_general(
        gathered, cot, (((0,), (0,)), ((), ())), preferred_element_type=jnp.float32
    )
    both = ("brick", "batch")
    parts = tiles_x * tiles_y * lax.axis_size("batch")
    rows = 27 * width
    extra = -rows % (8 * parts)
    pieces = jnp.pad(partial_grad.astype(jnp.bfloat16), ((0, extra), (0, 0))).reshape(parts, -1, width)
    arrived = lax.all_to_all(pieces, both, 0, 0)
    summed = arrived.astype(jnp.float32).sum(0).astype(jnp.bfloat16)
    whole = lax.all_gather(summed, both, axis=0, tiled=True)
    weight_grad = whole[:rows].astype(jnp.float32).reshape(27, width, width)
    cot_ext = with_halo(cot.reshape(side, side, layers, width), tiles_y)
    cot_gathered = cot_ext[ext_index].reshape(rows_here, 27 * width)
    back = jnp.dot(cot_gathered, w_backward, preferred_element_type=jnp.float32)
    sig = jax.nn.sigmoid(z_val)
    feature_grad = (back * sig * (1.0 + z_val * (1.0 - sig))).astype(jnp.bfloat16)
    return (conv_out[None], feature_grad[None], weight_grad)


def shards(*arrays):
    peers = lax.axis_size("brick")
    bits = peers.bit_length() - 1
    tiles_x = 2 ** ((bits + 1) // 2)
    tiles_y = 2 ** (bits // 2)
    plan = whole_scene if (tiles_x, tiles_y) == (ROW_STAGES, 2) else halo_plan
    return plan(*arrays, tiles_x, tiles_y)


def solution(mesh):
    in_specs = (
        P(("groups", "batch"), "brick", None),
        P(("groups", "batch"), "brick", None),
        P(None, ("groups", "brick")),
        P(("groups", "batch")),
        P(("groups", "batch"), None),
        P(),
        P(),
    )
    out_specs = (
        P(("groups", "batch"), "brick", None),
        P(("groups", "batch"), "brick", None),
        P("groups", None, None),
    )
    return jax.shard_map(shards, mesh=mesh, in_specs=in_specs, out_specs=out_specs, check_vma=False)
```

```python
import functools

import jax
import jax.numpy as jnp
from jax import lax
from jax.experimental import pallas as pl
from jax.experimental.pallas import tpu as pltpu
from jax.sharding import PartitionSpec as P

LAYERS = 16
TILE = 4
STRIP = TILE * LAYERS
HALF = 13
CODE_ROWS = 16
ROW_STAGES = 4
FINISH_STEP = 3
PACK_VMEM = 8 * 1024 * 1024
KERNEL_VMEM = 24 * 1024 * 1024


def time_embedding(timesteps, width):
    half = width // 2
    freq = jnp.exp(-jnp.log(10000.0) * jnp.arange(half, dtype=jnp.float32) / half)
    angle = timesteps.astype(jnp.float32)[:, None] * freq[None, :]
    return jnp.concatenate([jnp.sin(angle), jnp.cos(angle)], axis=1).astype(jnp.bfloat16)


def strip_codes(neighbours, tiles_y):
    rows_here = TILE * STRIP
    code = (neighbours // rows_here) % tiles_y * STRIP + neighbours % STRIP
    return jnp.where(neighbours < 0, -1, code).astype(jnp.float32)


def in_hbm(array):
    return pltpu.with_memory_space_constraint(array, pltpu.HBM)


def pack_kernel(time_ref, feat_hbm, cot_hbm, near_hbm, cond_hbm, wt_hbm, pack_ref, z_ref, code_ref,
                feat_ref, near_ref, cond_ref, wt_ref, sems):
    rows, width = feat_ref.shape
    half = width // 2
    moves = (
        (wt_hbm, wt_ref),
        (cond_hbm, cond_ref),
        (feat_hbm.at[0], feat_ref),
        (near_hbm, near_ref),
        (cot_hbm.at[0], pack_ref.at[:rows, width:]),
    )
    copies = [pltpu.make_async_copy(source, to, sems.at[i]) for i, (source, to) in enumerate(moves)]
    for copy in copies:
        copy.start()
    lane = lax.broadcasted_iota(jnp.int32, (1, width), 1)
    freq = jnp.exp(-jnp.log(10000.0) * (lane % half).astype(jnp.float32) / half)
    angle = time_ref[0].astype(jnp.float32) * freq
    temb = jnp.where(lane < half, jnp.sin(angle), jnp.cos(angle)).astype(jnp.bfloat16)
    copies[0].wait()
    copies[1].wait()
    shift = jnp.dot(temb, wt_ref[...], preferred_element_type=jnp.float32)
    shift = shift + cond_ref[...].astype(jnp.float32)
    copies[2].wait()
    z_val = feat_ref[...].astype(jnp.float32) + shift
    z_ref[...] = z_val
    pack_ref[:rows, :width] = (z_val * jax.nn.sigmoid(z_val)).astype(jnp.bfloat16)
    copies[3].wait()
    code = strip_codes(near_ref[...], 2)
    code_ref[...] = code
    pack_ref[rows:, :] = code[:CODE_ROWS, :].astype(jnp.bfloat16)
    copies[4].wait()


def lay_strip(ground, to, tile_y, mine_ref, other_ref, u):
    span = 2 * STRIP
    for ref, place in ((mine_ref, tile_y), (other_ref, 1 - tile_y)):
        at = pl.multiple_of(to * span + place * STRIP, STRIP)
        ground[pl.ds(at, STRIP), :] = ref[u * STRIP:(u + 1) * STRIP, :]


def row_kernel(stage, strips, borders, *refs):
    refs = list(refs)
    first_stage, final = stage == 0, stage == ROW_STAGES - 1
    where_ref = refs.pop(0)
    pairs = [(refs.pop(0), refs.pop(0)) for _ in range(1 + max(pair for pair, _ in strips))]
    before = [refs.pop(0) for _ in range(0 if first_stage else 3)]
    outs = [refs.pop(0) for _ in range(2 if final else 3)]
    ground, turned, codes, near_act, near_cot = refs
    width = ground.shape[1] // 2
    rows = TILE * STRIP
    span = 2 * STRIP
    tile_y = where_ref[0] % 2
    borders = [(u, u - 1) for u in range(1, TILE)] + borders
    targets = sorted({target for target, _ in borders})
    for i, (pair, u) in enumerate(strips):
        lay_strip(ground, i, tile_y, *pairs[pair], u)
        if i < TILE or i in targets:
            both = [ref[rows:, u * STRIP:(u + 1) * STRIP].astype(jnp.float32) for ref in pairs[pair]]
            first = jnp.where(tile_y == 0, both[0], both[1])
            second = jnp.where(tile_y == 0, both[1], both[0])
            codes[i] = jnp.concatenate([first, second], axis=1)
        if i < TILE or i in [source for _, source in borders]:
            turned[:, i * span:(i + 1) * span] = ground[i * span:(i + 1) * span, :].T
    place = lax.broadcasted_iota(jnp.int32, (span, span), 0).astype(jnp.float32)

    def gather(target, source, start, stop):
        picks = [(place == codes[target, k:k + 1, :]).astype(jnp.bfloat16) for k in range(start, stop)]
        near = jnp.dot(turned[:, source * span:(source + 1) * span], jnp.concatenate(picks, axis=1),
                       preferred_element_type=jnp.float32).astype(jnp.bfloat16)
        for k in range(start, stop):
            one = near[:, (k - start) * span:(k - start + 1) * span]
            near_act[k * width:(k + 1) * width, target * span:(target + 1) * span] = one[:width]
            near_cot[k * width:(k + 1) * width, target * span:(target + 1) * span] = one[width:]

    for u in range(TILE):
        gather(u, u, 9, HALF)
    for target, source in borders:
        gather(target, source, 0, 9)
    low_from = span * targets[0]
    low_to = span * (targets[-1] + 1)

    def product(near, start, stop, first, last, side):
        return jnp.dot(near[start * width:stop * width, first:last],
                       ground[first:last, side * width:(side + 1) * width], preferred_element_type=jnp.float32)

    pieces = []
    for near, side in ((near_act, 1), (near_cot, 0)):
        pieces.append(((0, 9), product(near, 0, 9, low_from, low_to, side)))
        pieces.append(((9, HALF), product(near, 9, HALF, 0, TILE * span, side)))
    centre = jnp.dot(turned[:width, :TILE * span], ground[:TILE * span, width:], preferred_element_type=jnp.float32)
    if not first_stage:
        centre = centre + before[2][...]
    for i, ((start, stop), value) in enumerate(pieces):
        turn = i // 2
        if not first_stage:
            value = value + before[turn][start * width:stop * width, :]
        if not final:
            outs[turn][start * width:stop * width, :] = value
            continue
        for k in range(start, stop):
            one = value[(k - start) * width:(k - start + 1) * width, :]
            one, to = (one.T, 2 * HALF - k) if turn else (one, k)
            outs[0][to] = one
            outs[1][to] = one.astype(jnp.bfloat16)
    if final:
        outs[0][HALF] = centre
        outs[1][HALF] = centre.astype(jnp.bfloat16)
    else:
        outs[2][...] = centre


def turn_kernel(w_ref, forward_ref, back_ref):
    width = w_ref.shape[1]
    for k in range(27):
        forward_ref[:, k * width:(k + 1) * width] = w_ref[k].T
        back_ref[:, k * width:(k + 1) * width] = w_ref[26 - k]


def paired_codes(code_ref):
    code = code_ref[...]
    lane = lax.broadcasted_iota(jnp.int32, code.shape, 1)
    return jnp.where((code >= 0) & (lane // STRIP % 2 == 1), code + 2 * STRIP, code)


def look_up(window, codes, to_act, to_cot, columns):
    width = window.shape[0] // 2
    span = codes.shape[1]
    place = lax.broadcasted_iota(jnp.int32, (window.shape[1], span), 0).astype(jnp.float32)
    picks = [(place == codes[k:k + 1, :]).astype(jnp.bfloat16) for k in range(codes.shape[0])]
    near = jnp.dot(window, jnp.concatenate(picks, axis=1), preferred_element_type=jnp.float32).astype(jnp.bfloat16)
    for k in range(codes.shape[0]):
        one = near[:, k * span:(k + 1) * span]
        to_act[k * width:(k + 1) * width, columns:columns + span] = one[:width]
        to_cot[k * width:(k + 1) * width, columns:columns + span] = one[width:]


def own_kernel(where_ref, mine_ref, other_ref, code_ref, forward_ref, back_ref, conv_ref, grad_ref,
               ground, turned, codes, near_act, near_cot):
    width = conv_ref.shape[0]
    span = 2 * STRIP
    tile_y = where_ref[0] % 2
    for u in range(TILE):
        lay_strip(ground, u, tile_y, mine_ref, other_ref, u)
        turned[:, (u + 1) * span:(u + 2) * span] = ground[u * span:(u + 1) * span, :].T
    turned[:, :span] = jnp.zeros((2 * width, span), jnp.bfloat16)
    codes[...] = paired_codes(code_ref)
    for half in range(TILE // 2):
        for side in range(2):
            source = (2 * half + side) * span
            rows = slice(9 * side * width, 9 * (side + 1) * width)
            look_up(turned[:, source:source + 2 * span], codes[9 * side:9 * side + 9, half * span:(half + 1) * span],
                    near_act.at[rows], near_cot.at[rows], half * span)
    conv_ref[...] = jnp.dot(forward_ref[:, :18 * width], near_act[...], preferred_element_type=jnp.float32)
    grad_ref[...] = jnp.dot(back_ref[:, :18 * width], near_cot[...], preferred_element_type=jnp.float32)


def edge_kernel(where_ref, mine_ref, other_ref, before_mine, before_other, after_mine, after_other,
                code_ref, forward_ref, back_ref, own_conv, own_grad, z_ref, conv_ref, grad_ref,
                ground, turned, codes, near_act, near_cot, edge_act, edge_cot):
    width = z_ref.shape[1]
    span = 2 * STRIP
    tile_y = where_ref[0] % 2
    strips = [(mine_ref, other_ref, u) for u in range(1, TILE)]
    strips += [(after_mine, after_other, 0), (before_mine, before_other, TILE - 1)]
    for i, strip in enumerate(strips):
        lay_strip(ground, i, tile_y, *strip)
        turned[:, i * span:(i + 1) * span] = ground[i * span:(i + 1) * span, :].T
    codes[...] = paired_codes(code_ref)
    for half in range(TILE // 2):
        columns = slice(half * span, (half + 1) * span)
        look_up(turned[:, 2 * half * span:2 * (half + 1) * span], codes[18:, columns], near_act, near_cot, half * span)
    code = codes[:9, :span]
    lane = lax.broadcasted_iota(jnp.int32, code.shape, 1)
    look_up(turned[:, TILE * span:], jnp.where(lane < STRIP, code, -1.0), edge_act, edge_cot, 0)

    def total(own_ref, weights, near, edge):
        value = own_ref[...] + jnp.dot(weights[:, 18 * width:], near[...], preferred_element_type=jnp.float32)
        first = value[:, :span] + jnp.dot(weights[:, :9 * width], edge[...], preferred_element_type=jnp.float32)
        return jnp.concatenate([first, value[:, span:]], axis=1).T

    conv_ref[...] = total(own_conv, forward_ref, near_act, edge_act).astype(jnp.bfloat16)
    back = total(own_grad, back_ref, near_cot, edge_cot)
    z_val = z_ref[...]
    sig = jax.nn.sigmoid(z_val)
    grad_ref[...] = (back * sig * (1.0 + z_val * (1.0 - sig))).astype(jnp.bfloat16)


def finish_kernel(kept_ref, sent_ref, weight_hbm, weight, sems):
    copies = []
    for i, first in enumerate(range(0, 27, FINISH_STEP)):
        part = slice(first, first + FINISH_STEP)
        weight[part] = kept_ref[part] + sent_ref[part].astype(jnp.float32)
        copies.append(pltpu.make_async_copy(weight.at[part], weight_hbm.at[part], sems.at[i]))
        copies[-1].start()
    for copy in copies:
        copy.wait()


def whole_scene(features, cotangent, neighbours, timesteps, condition, w_time, w_conv, tiles_x, tiles_y):
    rows, width = features.shape[1:]
    peers = tiles_x * tiles_y
    span = 2 * STRIP
    vmem = pl.BlockSpec(memory_space=pltpu.VMEM)
    smem = pl.BlockSpec(memory_space=pltpu.SMEM)
    params = pltpu.CompilerParams(vmem_limit_bytes=KERNEL_VMEM)
    packed, z_val, code = pl.pallas_call(
        pack_kernel,
        out_shape=(
            jax.ShapeDtypeStruct((rows + CODE_ROWS, 2 * width), jnp.bfloat16),
            jax.ShapeDtypeStruct((rows, width), jnp.float32),
            jax.ShapeDtypeStruct(neighbours.shape, jnp.float32),
        ),
        in_specs=[smem] + [pl.BlockSpec(memory_space=pltpu.HBM)] * 5,
        out_specs=(vmem, vmem, vmem),
        scratch_shapes=[
            pltpu.VMEM((rows, width), jnp.bfloat16),
            pltpu.VMEM(neighbours.shape, jnp.int32),
            pltpu.VMEM((1, width), jnp.bfloat16),
            pltpu.VMEM((width, width), jnp.bfloat16),
            pltpu.SemaphoreType.DMA((5,)),
        ],
        compiler_params=pltpu.CompilerParams(vmem_limit_bytes=PACK_VMEM),
        name="pack_tile",
    )(timesteps, *[in_hbm(array) for array in (features, cotangent, neighbours, condition, w_time)])
    here = lax.axis_index("brick").astype(jnp.int32).reshape(1)

    def across(block):
        return lax.ppermute(block, "brick", [(i, i ^ 1) for i in range(peers)])

    def along(block, turn):
        return lax.ppermute(block, "brick", [(i, (i + turn * tiles_y) % peers) for i in range(peers)])

    w_conv, packed = lax.optimization_barrier((w_conv, packed))
    w_forward, w_back = pl.pallas_call(
        turn_kernel,
        out_shape=(jax.ShapeDtypeStruct((width, 27 * width), jnp.bfloat16),) * 2,
        in_specs=[vmem],
        out_specs=(vmem, vmem),
        compiler_params=params,
        cost_estimate=pl.CostEstimate(flops=2 * 10**8, bytes_accessed=3 * 10**6, transcendentals=0),
        name="turn_weights",
    )(w_conv)
    before, after = along(packed, 1), along(packed, -1)
    before, w_forward = lax.optimization_barrier((before, w_forward))
    far = along(before, 1)
    own_pair = (packed, across(packed))
    own_conv, own_grad = pl.pallas_call(
        own_kernel,
        out_shape=(jax.ShapeDtypeStruct((width, rows), jnp.float32),) * 2,
        in_specs=[smem] + [vmem] * 5,
        out_specs=(vmem, vmem),
        scratch_shapes=[
            pltpu.VMEM((TILE * span, 2 * width), jnp.bfloat16),
            pltpu.VMEM((2 * width, (TILE + 1) * span), jnp.bfloat16),
            pltpu.VMEM((27, rows), jnp.float32),
            pltpu.VMEM((18 * width, rows), jnp.bfloat16),
            pltpu.VMEM((18 * width, rows), jnp.bfloat16),
        ],
        compiler_params=params,
        cost_estimate=pl.CostEstimate(flops=2 * 10**9, bytes_accessed=4 * 10**6, transcendentals=0),
        name="voxels_own_row",
    )(here, *own_pair, code, w_forward, w_back)
    far, own_conv = lax.optimization_barrier((far, own_conv))
    before_pair = (before, across(before))
    after_pair = (after, across(after))
    far_pair = (far, across(far))
    line = [(0, u) for u in range(TILE)]
    stages = (
        ((own_pair,), line, []),
        ((before_pair, own_pair), line + [(1, 0)], [(TILE, TILE - 1)]),
        ((after_pair, own_pair), line + [(1, TILE - 1)], [(0, TILE)]),
        ((far_pair, before_pair, after_pair), line + [(1, 0), (2, TILE - 1)], [(TILE, TILE - 1), (0, TILE + 1)]),
    )
    sums = ()
    for stage, (pairs, strips, borders) in enumerate(stages):
        blocks = [block for pair in pairs for block in pair]
        if stage == ROW_STAGES - 1:
            out_shape = (
                jax.ShapeDtypeStruct((27, width, width), jnp.float32),
                jax.ShapeDtypeStruct((27, width, width), jnp.bfloat16),
            )
        else:
            out_shape = (
                jax.ShapeDtypeStruct((HALF * width, width), jnp.float32),
                jax.ShapeDtypeStruct((HALF * width, width), jnp.float32),
                jax.ShapeDtypeStruct((width, width), jnp.float32),
            )
        sums = pl.pallas_call(
            functools.partial(row_kernel, stage, strips, borders),
            out_shape=out_shape,
            in_specs=[smem] + [vmem] * (len(blocks) + len(sums)),
            out_specs=(vmem,) * len(out_shape),
            scratch_shapes=[
                pltpu.VMEM(((TILE + 2) * span, 2 * width), jnp.bfloat16),
                pltpu.VMEM((2 * width, (TILE + 2) * span), jnp.bfloat16),
                pltpu.VMEM((TILE + 1, CODE_ROWS, span), jnp.float32),
                pltpu.VMEM((HALF * width, (TILE + 1) * span), jnp.bfloat16),
                pltpu.VMEM((HALF * width, (TILE + 1) * span), jnp.bfloat16),
            ],
            compiler_params=params,
            cost_estimate=pl.CostEstimate(flops=2 * 10**9, bytes_accessed=4 * 10**6, transcendentals=0),
            name=f"weight_row_{stage}",
        )(here, *blocks, *sums)
    own, sent = sums
    other = lax.ppermute(sent, "batch", [(0, 1), (1, 0)])
    conv_out, feature_grad = pl.pallas_call(
        edge_kernel,
        out_shape=(jax.ShapeDtypeStruct((rows, width), jnp.bfloat16),) * 2,
        in_specs=[smem] + [vmem] * 12,
        out_specs=(vmem, vmem),
        scratch_shapes=[
            pltpu.VMEM(((TILE + 1) * span, 2 * width), jnp.bfloat16),
            pltpu.VMEM((2 * width, (TILE + 1) * span), jnp.bfloat16),
            pltpu.VMEM((27, rows), jnp.float32),
            pltpu.VMEM((9 * width, rows), jnp.bfloat16),
            pltpu.VMEM((9 * width, rows), jnp.bfloat16),
            pltpu.VMEM((9 * width, span), jnp.bfloat16),
            pltpu.VMEM((9 * width, span), jnp.bfloat16),
        ],
        compiler_params=params,
        cost_estimate=pl.CostEstimate(flops=10**9, bytes_accessed=4 * 10**6, transcendentals=0),
        name="voxel_edges",
    )(here, *own_pair, *before_pair, *after_pair, code, w_forward, w_back, own_conv, own_grad, z_val)
    other, conv_out = lax.optimization_barrier((other, conv_out))
    weight_grad = pl.pallas_call(
        finish_kernel,
        out_shape=jax.ShapeDtypeStruct((27, width, width), jnp.float32),
        in_specs=[vmem] * 2,
        out_specs=pl.BlockSpec(memory_space=pltpu.HBM),
        scratch_shapes=[
            pltpu.VMEM((27, width, width), jnp.float32),
            pltpu.SemaphoreType.DMA((27 // FINISH_STEP,)),
        ],
        compiler_params=pltpu.CompilerParams(vmem_limit_bytes=PACK_VMEM),
        name="finish",
    )(own, other)
    return (conv_out[None], feature_grad[None], weight_grad)


def passed_along(block, axis, distance):
    devices = range(lax.axis_size(axis))
    route = [(i - distance, i) for i in devices if i - distance in devices]
    return lax.ppermute(block, axis, route)


def slab_rows(block, side_recv, front_recv, width):
    widened = jnp.concatenate([side_recv[0], block, side_recv[1]], axis=1)
    slab = jnp.concatenate([front_recv[0][None], widened, front_recv[1][None]], axis=0)
    flat = slab.reshape(-1, width)
    return jnp.concatenate([flat, jnp.zeros((1, width), jnp.bfloat16)], axis=0)


def with_halo(block, tiles_y):
    width = block.shape[-1]
    side = TILE
    side_recv = tuple(passed_along(block[:, edge], "brick", by)[:, None] for by, edge in ((1, side - 1), (-1, 0)))
    wide = jnp.concatenate([side_recv[0], block, side_recv[1]], axis=1)
    front_recv = tuple(passed_along(wide[edge], "brick", by) for by, edge in ((tiles_y, side - 1), (-tiles_y, 0)))
    return slab_rows(block, side_recv, front_recv, width)


def halo_plan(features, cotangent, neighbours, timesteps, condition, w_time, w_conv, tiles_x, tiles_y):
    rows_here, width = features.shape[1:]
    here = lax.axis_index("brick")
    tile_x = here // tiles_y
    tile_y = here % tiles_y
    side = TILE
    layers = LAYERS
    wide = side + 2
    valid = neighbours >= 0
    safe = jnp.where(valid, neighbours, 0)
    owner = safe // rows_here
    inside = safe % rows_here
    column = inside // layers
    layer = inside % layers
    local_x = (owner // tiles_y - tile_x) * side + column // side + 1
    local_y = (owner % tiles_y - tile_y) * side + column % side + 1
    sentinel = wide * wide * layers
    ext_index = jnp.where(valid, (local_x * wide + local_y) * layers + layer, sentinel).T
    temb = time_embedding(timesteps, width)
    shift = jnp.dot(temb, w_time, preferred_element_type=jnp.float32) + condition.astype(jnp.float32)
    z_val = features[0].astype(jnp.float32) + shift[0][None, :]
    act = jax.nn.silu(z_val).astype(jnp.bfloat16)
    cot = cotangent[0]
    w_forward = w_conv.reshape(27 * width, width)
    w_backward = jnp.transpose(w_conv[::-1], (0, 2, 1)).reshape(27 * width, width)
    act_ext = with_halo(act.reshape(side, side, layers, width), tiles_y)
    gathered = act_ext[ext_index].reshape(rows_here, 27 * width)
    conv_out = jnp.dot(gathered, w_forward, preferred_element_type=jnp.float32).astype(jnp.bfloat16)
    partial_grad = lax.dot_general(
        gathered, cot, (((0,), (0,)), ((), ())), preferred_element_type=jnp.float32
    )
    both = ("brick", "batch")
    parts = tiles_x * tiles_y * lax.axis_size("batch")
    rows = 27 * width
    extra = -rows % (8 * parts)
    pieces = jnp.pad(partial_grad.astype(jnp.bfloat16), ((0, extra), (0, 0))).reshape(parts, -1, width)
    arrived = lax.all_to_all(pieces, both, 0, 0)
    summed = arrived.astype(jnp.float32).sum(0).astype(jnp.bfloat16)
    whole = lax.all_gather(summed, both, axis=0, tiled=True)
    weight_grad = whole[:rows].astype(jnp.float32).reshape(27, width, width)
    cot_ext = with_halo(cot.reshape(side, side, layers, width), tiles_y)
    cot_gathered = cot_ext[ext_index].reshape(rows_here, 27 * width)
    back = jnp.dot(cot_gathered, w_backward, preferred_element_type=jnp.float32)
    sig = jax.nn.sigmoid(z_val)
    feature_grad = (back * sig * (1.0 + z_val * (1.0 - sig))).astype(jnp.bfloat16)
    return (conv_out[None], feature_grad[None], weight_grad)


def shards(*arrays):
    peers = lax.axis_size("brick")
    bits = peers.bit_length() - 1
    tiles_x = 2 ** ((bits + 1) // 2)
    tiles_y = 2 ** (bits // 2)
    plan = whole_scene if (tiles_x, tiles_y) == (ROW_STAGES, 2) else halo_plan
    return plan(*arrays, tiles_x, tiles_y)


def solution(mesh):
    in_specs = (
        P(("groups", "batch"), "brick", None),
        P(("groups", "batch"), "brick", None),
        P(None, ("groups", "brick")),
        P(("groups", "batch")),
        P(("groups", "batch"), None),
        P(),
        P(),
    )
    out_specs = (
        P(("groups", "batch"), "brick", None),
        P(("groups", "batch"), "brick", None),
        P("groups", None, None),
    )
    return jax.shard_map(shards, mesh=mesh, in_specs=in_specs, out_specs=out_specs, check_vma=False)
```

```python
import functools

import jax
import jax.numpy as jnp
from jax import lax
from jax.experimental import pallas as pl
from jax.experimental.pallas import tpu as pltpu
from jax.sharding import PartitionSpec as P

LAYERS = 16
TILE = 4
STRIP = TILE * LAYERS
HALF = 13
CODE_ROWS = 16
ROW_STAGES = 4
FINISH_STEP = 3
PACK_VMEM = 8 * 1024 * 1024
KERNEL_VMEM = 24 * 1024 * 1024


def time_embedding(timesteps, width):
    half = width // 2
    freq = jnp.exp(-jnp.log(10000.0) * jnp.arange(half, dtype=jnp.float32) / half)
    angle = timesteps.astype(jnp.float32)[:, None] * freq[None, :]
    return jnp.concatenate([jnp.sin(angle), jnp.cos(angle)], axis=1).astype(jnp.bfloat16)


def strip_codes(neighbours, tiles_y):
    rows_here = TILE * STRIP
    code = (neighbours // rows_here) % tiles_y * STRIP + neighbours % STRIP
    return jnp.where(neighbours < 0, -1, code).astype(jnp.float32)


def in_hbm(array):
    return pltpu.with_memory_space_constraint(array, pltpu.HBM)


def pack_kernel(time_ref, feat_hbm, cot_hbm, near_hbm, cond_hbm, wt_hbm, pack_ref, z_ref, code_ref,
                feat_ref, near_ref, cond_ref, wt_ref, sems):
    rows, width = feat_ref.shape
    half = width // 2
    moves = (
        (wt_hbm, wt_ref),
        (cond_hbm, cond_ref),
        (feat_hbm.at[0], feat_ref),
        (near_hbm, near_ref),
        (cot_hbm.at[0], pack_ref.at[:rows, width:]),
    )
    copies = [pltpu.make_async_copy(source, to, sems.at[i]) for i, (source, to) in enumerate(moves)]
    for copy in copies:
        copy.start()
    lane = lax.broadcasted_iota(jnp.int32, (1, width), 1)
    freq = jnp.exp(-jnp.log(10000.0) * (lane % half).astype(jnp.float32) / half)
    angle = time_ref[0].astype(jnp.float32) * freq
    temb = jnp.where(lane < half, jnp.sin(angle), jnp.cos(angle)).astype(jnp.bfloat16)
    copies[0].wait()
    copies[1].wait()
    shift = jnp.dot(temb, wt_ref[...], preferred_element_type=jnp.float32)
    shift = shift + cond_ref[...].astype(jnp.float32)
    copies[2].wait()
    z_val = feat_ref[...].astype(jnp.float32) + shift
    z_ref[...] = z_val
    pack_ref[:rows, :width] = (z_val * jax.nn.sigmoid(z_val)).astype(jnp.bfloat16)
    copies[3].wait()
    code = strip_codes(near_ref[...], 2)
    code_ref[...] = code
    pack_ref[rows:, :] = code[:CODE_ROWS, :].astype(jnp.bfloat16)
    copies[4].wait()


def lay_strip(ground, to, tile_y, mine_ref, other_ref, u):
    span = 2 * STRIP
    for ref, place in ((mine_ref, tile_y), (other_ref, 1 - tile_y)):
        at = pl.multiple_of(to * span + place * STRIP, STRIP)
        ground[pl.ds(at, STRIP), :] = ref[u * STRIP:(u + 1) * STRIP, :]


def row_kernel(stage, strips, borders, *refs):
    refs = list(refs)
    first_stage, final = stage == 0, stage == ROW_STAGES - 1
    where_ref = refs.pop(0)
    pairs = [(refs.pop(0), refs.pop(0)) for _ in range(1 + max(pair for pair, _ in strips))]
    before = [refs.pop(0) for _ in range(0 if first_stage else 3)]
    outs = [refs.pop(0) for _ in range(2 if final else 3)]
    ground, turned, codes, near_act, near_cot = refs
    width = ground.shape[1] // 2
    rows = TILE * STRIP
    span = 2 * STRIP
    tile_y = where_ref[0] % 2
    borders = [(u, u - 1) for u in range(1, TILE)] + borders
    targets = sorted({target for target, _ in borders})
    for i, (pair, u) in enumerate(strips):
        lay_strip(ground, i, tile_y, *pairs[pair], u)
        if i < TILE or i in targets:
            both = [ref[rows:, u * STRIP:(u + 1) * STRIP].astype(jnp.float32) for ref in pairs[pair]]
            first = jnp.where(tile_y == 0, both[0], both[1])
            second = jnp.where(tile_y == 0, both[1], both[0])
            codes[i] = jnp.concatenate([first, second], axis=1)
        if i < TILE or i in [source for _, source in borders]:
            turned[:, i * span:(i + 1) * span] = ground[i * span:(i + 1) * span, :].T
    place = lax.broadcasted_iota(jnp.int32, (span, span), 0).astype(jnp.float32)

    def gather(target, source, start, stop):
        picks = [(place == codes[target, k:k + 1, :]).astype(jnp.bfloat16) for k in range(start, stop)]
        near = jnp.dot(turned[:, source * span:(source + 1) * span], jnp.concatenate(picks, axis=1),
                       preferred_element_type=jnp.float32).astype(jnp.bfloat16)
        for k in range(start, stop):
            one = near[:, (k - start) * span:(k - start + 1) * span]
            near_act[k * width:(k + 1) * width, target * span:(target + 1) * span] = one[:width]
            near_cot[k * width:(k + 1) * width, target * span:(target + 1) * span] = one[width:]

    for u in range(TILE):
        gather(u, u, 9, HALF)
    for target, source in borders:
        gather(target, source, 0, 9)
    low_from = span * targets[0]
    low_to = span * (targets[-1] + 1)

    def product(near, start, stop, first, last, side):
        return jnp.dot(near[start * width:stop * width, first:last],
                       ground[first:last, side * width:(side + 1) * width], preferred_element_type=jnp.float32)

    pieces = []
    for near, side in ((near_act, 1), (near_cot, 0)):
        pieces.append(((0, 9), product(near, 0, 9, low_from, low_to, side)))
        pieces.append(((9, HALF), product(near, 9, HALF, 0, TILE * span, side)))
    centre = jnp.dot(turned[:width, :TILE * span], ground[:TILE * span, width:], preferred_element_type=jnp.float32)
    if not first_stage:
        centre = centre + before[2][...]
    for i, ((start, stop), value) in enumerate(pieces):
        turn = i // 2
        if not first_stage:
            value = value + before[turn][start * width:stop * width, :]
        if not final:
            outs[turn][start * width:stop * width, :] = value
            continue
        for k in range(start, stop):
            one = value[(k - start) * width:(k - start + 1) * width, :]
            one, to = (one.T, 2 * HALF - k) if turn else (one, k)
            outs[0][to] = one
            outs[1][to] = one.astype(jnp.bfloat16)
    if final:
        outs[0][HALF] = centre
        outs[1][HALF] = centre.astype(jnp.bfloat16)
    else:
        outs[2][...] = centre


def turn_kernel(w_ref, forward_ref, back_ref):
    width = w_ref.shape[1]
    for k in range(27):
        forward_ref[:, k * width:(k + 1) * width] = w_ref[k].T
        back_ref[:, k * width:(k + 1) * width] = w_ref[26 - k]


def paired_codes(code_ref):
    code = code_ref[...]
    lane = lax.broadcasted_iota(jnp.int32, code.shape, 1)
    return jnp.where((code >= 0) & (lane // STRIP % 2 == 1), code + 2 * STRIP, code)


def look_up(window, codes, to_act, to_cot, columns):
    width = window.shape[0] // 2
    span = codes.shape[1]
    place = lax.broadcasted_iota(jnp.int32, (window.shape[1], span), 0).astype(jnp.float32)
    picks = [(place == codes[k:k + 1, :]).astype(jnp.bfloat16) for k in range(codes.shape[0])]
    near = jnp.dot(window, jnp.concatenate(picks, axis=1), preferred_element_type=jnp.float32).astype(jnp.bfloat16)
    for k in range(codes.shape[0]):
        one = near[:, k * span:(k + 1) * span]
        to_act[k * width:(k + 1) * width, columns:columns + span] = one[:width]
        to_cot[k * width:(k + 1) * width, columns:columns + span] = one[width:]


def own_kernel(where_ref, mine_ref, other_ref, code_ref, forward_ref, back_ref, conv_ref, grad_ref,
               ground, turned, codes, near_act, near_cot):
    width = conv_ref.shape[0]
    span = 2 * STRIP
    tile_y = where_ref[0] % 2
    for u in range(TILE):
        lay_strip(ground, u, tile_y, mine_ref, other_ref, u)
        turned[:, (u + 1) * span:(u + 2) * span] = ground[u * span:(u + 1) * span, :].T
    turned[:, :span] = jnp.zeros((2 * width, span), jnp.bfloat16)
    codes[...] = paired_codes(code_ref)
    for half in range(TILE // 2):
        for side in range(2):
            source = (2 * half + side) * span
            rows = slice(9 * side * width, 9 * (side + 1) * width)
            look_up(turned[:, source:source + 2 * span], codes[9 * side:9 * side + 9, half * span:(half + 1) * span],
                    near_act.at[rows], near_cot.at[rows], half * span)
    conv_ref[...] = jnp.dot(forward_ref[:, :18 * width], near_act[...], preferred_element_type=jnp.float32)
    grad_ref[...] = jnp.dot(back_ref[:, :18 * width], near_cot[...], preferred_element_type=jnp.float32)


def edge_kernel(where_ref, mine_ref, other_ref, before_mine, before_other, after_mine, after_other,
                code_ref, forward_ref, back_ref, own_conv, own_grad, z_ref, conv_ref, grad_ref,
                ground, turned, codes, near_act, near_cot, edge_act, edge_cot):
    width = z_ref.shape[1]
    span = 2 * STRIP
    tile_y = where_ref[0] % 2
    strips = [(mine_ref, other_ref, u) for u in range(1, TILE)]
    strips += [(after_mine, after_other, 0), (before_mine, before_other, TILE - 1)]
    for i, strip in enumerate(strips):
        lay_strip(ground, i, tile_y, *strip)
        turned[:, i * span:(i + 1) * span] = ground[i * span:(i + 1) * span, :].T
    codes[...] = paired_codes(code_ref)
    for half in range(TILE // 2):
        columns = slice(half * span, (half + 1) * span)
        look_up(turned[:, 2 * half * span:2 * (half + 1) * span], codes[18:, columns], near_act, near_cot, half * span)
    code = codes[:9, :span]
    lane = lax.broadcasted_iota(jnp.int32, code.shape, 1)
    look_up(turned[:, TILE * span:], jnp.where(lane < STRIP, code, -1.0), edge_act, edge_cot, 0)

    def total(own_ref, weights, near, edge):
        value = own_ref[...] + jnp.dot(weights[:, 18 * width:], near[...], preferred_element_type=jnp.float32)
        first = value[:, :span] + jnp.dot(weights[:, :9 * width], edge[...], preferred_element_type=jnp.float32)
        return jnp.concatenate([first, value[:, span:]], axis=1).T

    conv_ref[...] = total(own_conv, forward_ref, near_act, edge_act).astype(jnp.bfloat16)
    back = total(own_grad, back_ref, near_cot, edge_cot)
    z_val = z_ref[...]
    sig = jax.nn.sigmoid(z_val)
    grad_ref[...] = (back * sig * (1.0 + z_val * (1.0 - sig))).astype(jnp.bfloat16)


def finish_kernel(kept_ref, sent_ref, weight_hbm, weight, sems):
    copies = []
    for i, first in enumerate(range(0, 27, FINISH_STEP)):
        part = slice(first, first + FINISH_STEP)
        weight[part] = kept_ref[part] + sent_ref[part].astype(jnp.float32)
        copies.append(pltpu.make_async_copy(weight.at[part], weight_hbm.at[part], sems.at[i]))
        copies[-1].start()
    for copy in copies:
        copy.wait()


def whole_scene(features, cotangent, neighbours, timesteps, condition, w_time, w_conv, tiles_x, tiles_y):
    rows, width = features.shape[1:]
    peers = tiles_x * tiles_y
    span = 2 * STRIP
    vmem = pl.BlockSpec(memory_space=pltpu.VMEM)
    smem = pl.BlockSpec(memory_space=pltpu.SMEM)
    params = pltpu.CompilerParams(vmem_limit_bytes=KERNEL_VMEM)
    packed, z_val, code = pl.pallas_call(
        pack_kernel,
        out_shape=(
            jax.ShapeDtypeStruct((rows + CODE_ROWS, 2 * width), jnp.bfloat16),
            jax.ShapeDtypeStruct((rows, width), jnp.float32),
            jax.ShapeDtypeStruct(neighbours.shape, jnp.float32),
        ),
        in_specs=[smem] + [pl.BlockSpec(memory_space=pltpu.HBM)] * 5,
        out_specs=(vmem, vmem, vmem),
        scratch_shapes=[
            pltpu.VMEM((rows, width), jnp.bfloat16),
            pltpu.VMEM(neighbours.shape, jnp.int32),
            pltpu.VMEM((1, width), jnp.bfloat16),
            pltpu.VMEM((width, width), jnp.bfloat16),
            pltpu.SemaphoreType.DMA((5,)),
        ],
        compiler_params=pltpu.CompilerParams(vmem_limit_bytes=PACK_VMEM),
        name="pack_tile",
    )(timesteps, *[in_hbm(array) for array in (features, cotangent, neighbours, condition, w_time)])
    here = lax.axis_index("brick").astype(jnp.int32).reshape(1)

    def across(block):
        return lax.ppermute(block, "brick", [(i, i ^ 1) for i in range(peers)])

    def along(block, turn):
        return lax.ppermute(block, "brick", [(i, (i + turn * tiles_y) % peers) for i in range(peers)])

    w_conv, packed = lax.optimization_barrier((w_conv, packed))
    w_forward, w_back = pl.pallas_call(
        turn_kernel,
        out_shape=(jax.ShapeDtypeStruct((width, 27 * width), jnp.bfloat16),) * 2,
        in_specs=[vmem],
        out_specs=(vmem, vmem),
        compiler_params=params,
        cost_estimate=pl.CostEstimate(flops=2 * 10**8, bytes_accessed=3 * 10**6, transcendentals=0),
        name="turn_weights",
    )(w_conv)
    after, before = along(packed, -1), along(packed, 1)
    after, w_forward = lax.optimization_barrier((after, w_forward))
    far = along(after, -1)
    own_pair = (packed, across(packed))
    own_conv, own_grad = pl.pallas_call(
        own_kernel,
        out_shape=(jax.ShapeDtypeStruct((width, rows), jnp.float32),) * 2,
        in_specs=[smem] + [vmem] * 5,
        out_specs=(vmem, vmem),
        scratch_shapes=[
            pltpu.VMEM((TILE * span, 2 * width), jnp.bfloat16),
            pltpu.VMEM((2 * width, (TILE + 1) * span), jnp.bfloat16),
            pltpu.VMEM((27, rows), jnp.float32),
            pltpu.VMEM((18 * width, rows), jnp.bfloat16),
            pltpu.VMEM((18 * width, rows), jnp.bfloat16),
        ],
        compiler_params=params,
        cost_estimate=pl.CostEstimate(flops=2 * 10**9, bytes_accessed=4 * 10**6, transcendentals=0),
        name="voxels_own_row",
    )(here, *own_pair, code, w_forward, w_back)
    far, own_conv = lax.optimization_barrier((far, own_conv))
    after_pair = (after, across(after))
    before_pair = (before, across(before))
    far_pair = (far, across(far))
    line = [(0, u) for u in range(TILE)]
    stages = (
        ((own_pair,), line, []),
        ((after_pair, own_pair), line + [(1, TILE - 1)], [(0, TILE)]),
        ((before_pair, own_pair), line + [(1, 0)], [(TILE, TILE - 1)]),
        ((far_pair, before_pair, after_pair), line + [(1, 0), (2, TILE - 1)], [(TILE, TILE - 1), (0, TILE + 1)]),
    )
    sums = ()
    for stage, (pairs, strips, borders) in enumerate(stages):
        blocks = [block for pair in pairs for block in pair]
        if stage == ROW_STAGES - 1:
            out_shape = (
                jax.ShapeDtypeStruct((27, width, width), jnp.float32),
                jax.ShapeDtypeStruct((27, width, width), jnp.bfloat16),
            )
        else:
            out_shape = (
                jax.ShapeDtypeStruct((HALF * width, width), jnp.float32),
                jax.ShapeDtypeStruct((HALF * width, width), jnp.float32),
                jax.ShapeDtypeStruct((width, width), jnp.float32),
            )
        sums = pl.pallas_call(
            functools.partial(row_kernel, stage, strips, borders),
            out_shape=out_shape,
            in_specs=[smem] + [vmem] * (len(blocks) + len(sums)),
            out_specs=(vmem,) * len(out_shape),
            scratch_shapes=[
                pltpu.VMEM(((TILE + 2) * span, 2 * width), jnp.bfloat16),
                pltpu.VMEM((2 * width, (TILE + 2) * span), jnp.bfloat16),
                pltpu.VMEM((TILE + 1, CODE_ROWS, span), jnp.float32),
                pltpu.VMEM((HALF * width, (TILE + 1) * span), jnp.bfloat16),
                pltpu.VMEM((HALF * width, (TILE + 1) * span), jnp.bfloat16),
            ],
            compiler_params=params,
            cost_estimate=pl.CostEstimate(flops=2 * 10**9, bytes_accessed=4 * 10**6, transcendentals=0),
            name=f"weight_row_{stage}",
        )(here, *blocks, *sums)
    own, sent = sums
    other = lax.ppermute(sent, "batch", [(0, 1), (1, 0)])
    conv_out, feature_grad = pl.pallas_call(
        edge_kernel,
        out_shape=(jax.ShapeDtypeStruct((rows, width), jnp.bfloat16),) * 2,
        in_specs=[smem] + [vmem] * 12,
        out_specs=(vmem, vmem),
        scratch_shapes=[
            pltpu.VMEM(((TILE + 1) * span, 2 * width), jnp.bfloat16),
            pltpu.VMEM((2 * width, (TILE + 1) * span), jnp.bfloat16),
            pltpu.VMEM((27, rows), jnp.float32),
            pltpu.VMEM((9 * width, rows), jnp.bfloat16),
            pltpu.VMEM((9 * width, rows), jnp.bfloat16),
            pltpu.VMEM((9 * width, span), jnp.bfloat16),
            pltpu.VMEM((9 * width, span), jnp.bfloat16),
        ],
        compiler_params=params,
        cost_estimate=pl.CostEstimate(flops=10**9, bytes_accessed=4 * 10**6, transcendentals=0),
        name="voxel_edges",
    )(here, *own_pair, *before_pair, *after_pair, code, w_forward, w_back, own_conv, own_grad, z_val)
    other, conv_out = lax.optimization_barrier((other, conv_out))
    weight_grad = pl.pallas_call(
        finish_kernel,
        out_shape=jax.ShapeDtypeStruct((27, width, width), jnp.float32),
        in_specs=[vmem] * 2,
        out_specs=pl.BlockSpec(memory_space=pltpu.HBM),
        scratch_shapes=[
            pltpu.VMEM((27, width, width), jnp.float32),
            pltpu.SemaphoreType.DMA((27 // FINISH_STEP,)),
        ],
        compiler_params=pltpu.CompilerParams(vmem_limit_bytes=PACK_VMEM),
        name="finish",
    )(own, other)
    return (conv_out[None], feature_grad[None], weight_grad)


def passed_along(block, axis, distance):
    devices = range(lax.axis_size(axis))
    route = [(i - distance, i) for i in devices if i - distance in devices]
    return lax.ppermute(block, axis, route)


def slab_rows(block, side_recv, front_recv, width):
    widened = jnp.concatenate([side_recv[0], block, side_recv[1]], axis=1)
    slab = jnp.concatenate([front_recv[0][None], widened, front_recv[1][None]], axis=0)
    flat = slab.reshape(-1, width)
    return jnp.concatenate([flat, jnp.zeros((1, width), jnp.bfloat16)], axis=0)


def with_halo(block, tiles_y):
    width = block.shape[-1]
    side = TILE
    side_recv = tuple(passed_along(block[:, edge], "brick", by)[:, None] for by, edge in ((1, side - 1), (-1, 0)))
    wide = jnp.concatenate([side_recv[0], block, side_recv[1]], axis=1)
    front_recv = tuple(passed_along(wide[edge], "brick", by) for by, edge in ((tiles_y, side - 1), (-tiles_y, 0)))
    return slab_rows(block, side_recv, front_recv, width)


def halo_plan(features, cotangent, neighbours, timesteps, condition, w_time, w_conv, tiles_x, tiles_y):
    rows_here, width = features.shape[1:]
    here = lax.axis_index("brick")
    tile_x = here // tiles_y
    tile_y = here % tiles_y
    side = TILE
    layers = LAYERS
    wide = side + 2
    valid = neighbours >= 0
    safe = jnp.where(valid, neighbours, 0)
    owner = safe // rows_here
    inside = safe % rows_here
    column = inside // layers
    layer = inside % layers
    local_x = (owner // tiles_y - tile_x) * side + column // side + 1
    local_y = (owner % tiles_y - tile_y) * side + column % side + 1
    sentinel = wide * wide * layers
    ext_index = jnp.where(valid, (local_x * wide + local_y) * layers + layer, sentinel).T
    temb = time_embedding(timesteps, width)
    shift = jnp.dot(temb, w_time, preferred_element_type=jnp.float32) + condition.astype(jnp.float32)
    z_val = features[0].astype(jnp.float32) + shift[0][None, :]
    act = jax.nn.silu(z_val).astype(jnp.bfloat16)
    cot = cotangent[0]
    w_forward = w_conv.reshape(27 * width, width)
    w_backward = jnp.transpose(w_conv[::-1], (0, 2, 1)).reshape(27 * width, width)
    act_ext = with_halo(act.reshape(side, side, layers, width), tiles_y)
    gathered = act_ext[ext_index].reshape(rows_here, 27 * width)
    conv_out = jnp.dot(gathered, w_forward, preferred_element_type=jnp.float32).astype(jnp.bfloat16)
    partial_grad = lax.dot_general(
        gathered, cot, (((0,), (0,)), ((), ())), preferred_element_type=jnp.float32
    )
    both = ("brick", "batch")
    parts = tiles_x * tiles_y * lax.axis_size("batch")
    rows = 27 * width
    extra = -rows % (8 * parts)
    pieces = jnp.pad(partial_grad.astype(jnp.bfloat16), ((0, extra), (0, 0))).reshape(parts, -1, width)
    arrived = lax.all_to_all(pieces, both, 0, 0)
    summed = arrived.astype(jnp.float32).sum(0).astype(jnp.bfloat16)
    whole = lax.all_gather(summed, both, axis=0, tiled=True)
    weight_grad = whole[:rows].astype(jnp.float32).reshape(27, width, width)
    cot_ext = with_halo(cot.reshape(side, side, layers, width), tiles_y)
    cot_gathered = cot_ext[ext_index].reshape(rows_here, 27 * width)
    back = jnp.dot(cot_gathered, w_backward, preferred_element_type=jnp.float32)
    sig = jax.nn.sigmoid(z_val)
    feature_grad = (back * sig * (1.0 + z_val * (1.0 - sig))).astype(jnp.bfloat16)
    return (conv_out[None], feature_grad[None], weight_grad)


def shards(*arrays):
    peers = lax.axis_size("brick")
    bits = peers.bit_length() - 1
    tiles_x = 2 ** ((bits + 1) // 2)
    tiles_y = 2 ** (bits // 2)
    plan = whole_scene if (tiles_x, tiles_y) == (ROW_STAGES, 2) else halo_plan
    return plan(*arrays, tiles_x, tiles_y)


def solution(mesh):
    in_specs = (
        P(("groups", "batch"), "brick", None),
        P(("groups", "batch"), "brick", None),
        P(None, ("groups", "brick")),
        P(("groups", "batch")),
        P(("groups", "batch"), None),
        P(),
        P(),
    )
    out_specs = (
        P(("groups", "batch"), "brick", None),
        P(("groups", "batch"), "brick", None),
        P("groups", None, None),
    )
    return jax.shard_map(shards, mesh=mesh, in_specs=in_specs, out_specs=out_specs, check_vma=False)
```

```python
import functools

import jax
import jax.numpy as jnp
from jax import lax
from jax.experimental import pallas as pl
from jax.experimental.pallas import tpu as pltpu
from jax.sharding import PartitionSpec as P

LAYERS = 16
TILE = 4
STRIP = TILE * LAYERS
HALF = 13
CODE_ROWS = 16
ROW_STAGES = 4
FINISH_STEP = 3
PACK_VMEM = 8 * 1024 * 1024
KERNEL_VMEM = 24 * 1024 * 1024


def time_embedding(timesteps, width):
    half = width // 2
    freq = jnp.exp(-jnp.log(10000.0) * jnp.arange(half, dtype=jnp.float32) / half)
    angle = timesteps.astype(jnp.float32)[:, None] * freq[None, :]
    return jnp.concatenate([jnp.sin(angle), jnp.cos(angle)], axis=1).astype(jnp.bfloat16)


def strip_codes(neighbours, tiles_y):
    rows_here = TILE * STRIP
    code = (neighbours // rows_here) % tiles_y * STRIP + neighbours % STRIP
    return jnp.where(neighbours < 0, -1, code).astype(jnp.float32)


def in_hbm(array):
    return pltpu.with_memory_space_constraint(array, pltpu.HBM)


def pack_kernel(time_ref, feat_hbm, cot_hbm, near_hbm, cond_hbm, wt_hbm, pack_ref, z_ref, code_ref,
                feat_ref, near_ref, cond_ref, wt_ref, sems):
    rows, width = feat_ref.shape
    half = width // 2
    moves = (
        (wt_hbm, wt_ref),
        (cond_hbm, cond_ref),
        (feat_hbm.at[0], feat_ref),
        (near_hbm, near_ref),
        (cot_hbm.at[0], pack_ref.at[:rows, width:]),
    )
    copies = [pltpu.make_async_copy(source, to, sems.at[i]) for i, (source, to) in enumerate(moves)]
    for copy in copies:
        copy.start()
    lane = lax.broadcasted_iota(jnp.int32, (1, width), 1)
    freq = jnp.exp(-jnp.log(10000.0) * (lane % half).astype(jnp.float32) / half)
    angle = time_ref[0].astype(jnp.float32) * freq
    temb = jnp.where(lane < half, jnp.sin(angle), jnp.cos(angle)).astype(jnp.bfloat16)
    copies[0].wait()
    copies[1].wait()
    shift = jnp.dot(temb, wt_ref[...], preferred_element_type=jnp.float32)
    shift = shift + cond_ref[...].astype(jnp.float32)
    copies[2].wait()
    z_val = feat_ref[...].astype(jnp.float32) + shift
    z_ref[...] = z_val
    pack_ref[:rows, :width] = (z_val * jax.nn.sigmoid(z_val)).astype(jnp.bfloat16)
    copies[3].wait()
    code = strip_codes(near_ref[...], 2)
    code_ref[...] = code
    pack_ref[rows:, :] = code[:CODE_ROWS, :].astype(jnp.bfloat16)
    copies[4].wait()


def lay_strip(ground, to, tile_y, mine_ref, other_ref, u):
    span = 2 * STRIP
    for ref, place in ((mine_ref, tile_y), (other_ref, 1 - tile_y)):
        at = pl.multiple_of(to * span + place * STRIP, STRIP)
        ground[pl.ds(at, STRIP), :] = ref[u * STRIP:(u + 1) * STRIP, :]


def row_kernel(first_stage, final, groups, strips, borders, *refs):
    refs = list(refs)
    where_ref = refs.pop(0)
    pairs = [(refs.pop(0), refs.pop(0)) for _ in range(1 + max(pair for pair, _ in strips))]
    before = [refs.pop(0) for _ in range(0 if first_stage else 3)]
    outs = [refs.pop(0) for _ in range(2 if final else 3)]
    ground, turned, codes, near_act, near_cot = refs
    width = ground.shape[1] // 2
    rows = TILE * STRIP
    span = 2 * STRIP
    tile_y = where_ref[0] % 2
    borders = [(u, u - 1) for u in range(1, TILE)] + borders
    targets = sorted({target for target, _ in borders})
    for i, (pair, u) in enumerate(strips):
        lay_strip(ground, i, tile_y, *pairs[pair], u)
        if i < TILE or i in targets:
            both = [ref[rows:, u * STRIP:(u + 1) * STRIP].astype(jnp.float32) for ref in pairs[pair]]
            first = jnp.where(tile_y == 0, both[0], both[1])
            second = jnp.where(tile_y == 0, both[1], both[0])
            codes[i] = jnp.concatenate([first, second], axis=1)
        if i < TILE or i in [source for _, source in borders]:
            turned[:, i * span:(i + 1) * span] = ground[i * span:(i + 1) * span, :].T
    place = lax.broadcasted_iota(jnp.int32, (span, span), 0).astype(jnp.float32)

    def gather(target, source, start, stop):
        picks = [(place == codes[target, k:k + 1, :]).astype(jnp.bfloat16) for k in range(start, stop)]
        near = jnp.dot(turned[:, source * span:(source + 1) * span], jnp.concatenate(picks, axis=1),
                       preferred_element_type=jnp.float32).astype(jnp.bfloat16)
        for k in range(start, stop):
            one = near[:, (k - start) * span:(k - start + 1) * span]
            near_act[k * width:(k + 1) * width, target * span:(target + 1) * span] = one[:width]
            near_cot[k * width:(k + 1) * width, target * span:(target + 1) * span] = one[width:]

    if 1 in groups:
        for u in range(TILE):
            gather(u, u, 9, HALF)
    if 0 in groups:
        for target, source in borders:
            gather(target, source, 0, 9)
    extents = ((0, 9, span * targets[0], span * (targets[-1] + 1)), (9, HALF, 0, TILE * span))
    for turn, near in ((0, near_act), (1, near_cot)):
        for group in groups:
            start, stop, first, last = extents[group]
            other = ground[first:last, (1 - turn) * width:(2 - turn) * width]
            value = jnp.dot(near[start * width:stop * width, first:last], other, preferred_element_type=jnp.float32)
            if not first_stage:
                value = value + before[turn][start * width:stop * width, :]
            if not final:
                outs[turn][start * width:stop * width, :] = value
                continue
            for k in range(start, stop):
                one = value[(k - start) * width:(k - start + 1) * width, :]
                to = 2 * HALF - k if turn else k
                if turn:
                    one = one.T
                to = to - 9 if group == 1 else to - 9 * turn
                outs[0][to] = one
                outs[1][to] = one.astype(jnp.bfloat16)
    if 1 in groups:
        centre = jnp.dot(turned[:width, :TILE * span], ground[:TILE * span, width:], preferred_element_type=jnp.float32)
        if not first_stage:
            centre = centre + before[2][...]
        if final:
            outs[0][HALF - 9] = centre
            outs[1][HALF - 9] = centre.astype(jnp.bfloat16)
        else:
            outs[2][...] = centre


def turn_kernel(w_ref, forward_ref, back_ref):
    width = w_ref.shape[1]
    for k in range(27):
        forward_ref[:, k * width:(k + 1) * width] = w_ref[k].T
        back_ref[:, k * width:(k + 1) * width] = w_ref[26 - k]


def own_kernel(where_ref, mine_ref, other_ref, code_ref, forward_ref, back_ref, conv_ref, grad_ref,
               ground, turned, codes, near_act, near_cot):
    width = conv_ref.shape[0]
    span = 2 * STRIP
    tile_y = where_ref[0] % 2
    for u in range(TILE):
        lay_strip(ground, u, tile_y, mine_ref, other_ref, u)
        turned[:, (u + 1) * span:(u + 2) * span] = ground[u * span:(u + 1) * span, :].T
    for i in (0, TILE + 1):
        turned[:, i * span:(i + 1) * span] = jnp.zeros((2 * width, span), jnp.bfloat16)
    code = code_ref[...]
    lane = lax.broadcasted_iota(jnp.int32, code.shape, 1)
    codes[...] = jnp.where((code >= 0) & (lane // STRIP % 2 == 1), code + span, code)
    place = lax.broadcasted_iota(jnp.int32, (2 * span, span), 0).astype(jnp.float32)
    for half in range(TILE // 2):
        at = half * span
        for side in range(3):
            source = (2 * half + side) * span
            ks = range(9 * side, 9 * side + 9)
            picks = [(place == codes[k:k + 1, at:at + span]).astype(jnp.bfloat16) for k in ks]
            near = jnp.dot(turned[:, source:source + 2 * span], jnp.concatenate(picks, axis=1),
                           preferred_element_type=jnp.float32).astype(jnp.bfloat16)
            for k in ks:
                one = near[:, (k - 9 * side) * span:(k - 9 * side + 1) * span]
                near_act[k * width:(k + 1) * width, at:at + span] = one[:width]
                near_cot[k * width:(k + 1) * width, at:at + span] = one[width:]
    conv_ref[...] = jnp.dot(forward_ref[...], near_act[...], preferred_element_type=jnp.float32)
    grad_ref[...] = jnp.dot(back_ref[...], near_cot[...], preferred_element_type=jnp.float32)


def edge_kernel(where_ref, before_mine, before_other, after_mine, after_other, code_ref, forward_ref, back_ref,
                own_conv, own_grad, z_ref, conv_ref, grad_ref, ground, turned, near):
    width = z_ref.shape[1]
    span = 2 * STRIP
    tile_y = where_ref[0] % 2
    lay_strip(ground, 0, tile_y, before_mine, before_other, TILE - 1)
    lay_strip(ground, 1, tile_y, after_mine, after_other, 0)
    for i in range(2):
        turned[:, i * span:(i + 1) * span] = ground[i * span:(i + 1) * span, :].T
    first = code_ref[:9, :span]
    last = code_ref[18:, span:]
    lane = lax.broadcasted_iota(jnp.int32, first.shape, 1)
    code = jnp.where(lane < STRIP, first, jnp.where(last >= 0, last + span, last))
    place = lax.broadcasted_iota(jnp.int32, (2 * span, span), 0).astype(jnp.float32)
    picks = [(place == code[k:k + 1, :]).astype(jnp.bfloat16) for k in range(9)]
    found = jnp.dot(turned[...], jnp.concatenate(picks, axis=1), preferred_element_type=jnp.float32)
    found = found.astype(jnp.bfloat16)
    for k in range(9):
        near[:, k * width:(k + 1) * width, :] = found[:, k * span:(k + 1) * span].reshape(2, width, span)
    lane = lax.broadcasted_iota(jnp.int32, (width, span), 1)

    def total(own_ref, weights, side):
        low = jnp.dot(weights[:, :9 * width], near[side], preferred_element_type=jnp.float32)
        high = jnp.dot(weights[:, 18 * width:], near[side], preferred_element_type=jnp.float32)
        low = own_ref[:, :span] + jnp.where(lane < STRIP, low, 0.0)
        high = own_ref[:, span:] + jnp.where(lane < STRIP, 0.0, high)
        return jnp.concatenate([low, high], axis=1).T

    conv_ref[...] = total(own_conv, forward_ref, 0).astype(jnp.bfloat16)
    back = total(own_grad, back_ref, 1)
    z_val = z_ref[...]
    sig = jax.nn.sigmoid(z_val)
    grad_ref[...] = (back * sig * (1.0 + z_val * (1.0 - sig))).astype(jnp.bfloat16)


def finish_kernel(sides_ref, sides_sent, middle_ref, middle_sent, weight_hbm, weight, sems):
    copies = []
    for i, first in enumerate(range(0, 27, FINISH_STEP)):
        kept, sent, at = (middle_ref, middle_sent, first - 9) if first // 9 == 1 else (
            sides_ref, sides_sent, first if first < 9 else first - 9)
        part, taken = pl.ds(first, FINISH_STEP), pl.ds(at, FINISH_STEP)
        weight[part] = kept[taken] + sent[taken].astype(jnp.float32)
        copies.append(pltpu.make_async_copy(weight.at[part], weight_hbm.at[part], sems.at[i]))
        copies[-1].start()
    for copy in copies:
        copy.wait()


def whole_scene(features, cotangent, neighbours, timesteps, condition, w_time, w_conv, tiles_x, tiles_y):
    rows, width = features.shape[1:]
    peers = tiles_x * tiles_y
    span = 2 * STRIP
    vmem = pl.BlockSpec(memory_space=pltpu.VMEM)
    smem = pl.BlockSpec(memory_space=pltpu.SMEM)
    params = pltpu.CompilerParams(vmem_limit_bytes=KERNEL_VMEM)
    packed, z_val, code = pl.pallas_call(
        pack_kernel,
        out_shape=(
            jax.ShapeDtypeStruct((rows + CODE_ROWS, 2 * width), jnp.bfloat16),
            jax.ShapeDtypeStruct((rows, width), jnp.float32),
            jax.ShapeDtypeStruct(neighbours.shape, jnp.float32),
        ),
        in_specs=[smem] + [pl.BlockSpec(memory_space=pltpu.HBM)] * 5,
        out_specs=(vmem, vmem, vmem),
        scratch_shapes=[
            pltpu.VMEM((rows, width), jnp.bfloat16),
            pltpu.VMEM(neighbours.shape, jnp.int32),
            pltpu.VMEM((1, width), jnp.bfloat16),
            pltpu.VMEM((width, width), jnp.bfloat16),
            pltpu.SemaphoreType.DMA((5,)),
        ],
        compiler_params=pltpu.CompilerParams(vmem_limit_bytes=PACK_VMEM),
        name="pack_tile",
    )(timesteps, *[in_hbm(array) for array in (features, cotangent, neighbours, condition, w_time)])
    here = lax.axis_index("brick").astype(jnp.int32).reshape(1)

    def across(block):
        return lax.ppermute(block, "brick", [(i, i ^ 1) for i in range(peers)])

    def along(block, turn):
        return lax.ppermute(block, "brick", [(i, (i + turn * tiles_y) % peers) for i in range(peers)])

    w_conv, packed = lax.optimization_barrier((w_conv, packed))
    w_forward, w_back = pl.pallas_call(
        turn_kernel,
        out_shape=(jax.ShapeDtypeStruct((width, 27 * width), jnp.bfloat16),) * 2,
        in_specs=[vmem],
        out_specs=(vmem, vmem),
        compiler_params=params,
        cost_estimate=pl.CostEstimate(flops=2 * 10**8, bytes_accessed=3 * 10**6, transcendentals=0),
        name="turn_weights",
    )(w_conv)
    before, after = along(packed, 1), along(packed, -1)
    before, w_forward = lax.optimization_barrier((before, w_forward))
    far = along(before, 1)
    own_pair = (packed, across(packed))
    own_conv, own_grad = pl.pallas_call(
        own_kernel,
        out_shape=(jax.ShapeDtypeStruct((width, rows), jnp.float32),) * 2,
        in_specs=[smem] + [vmem] * 5,
        out_specs=(vmem, vmem),
        scratch_shapes=[
            pltpu.VMEM((TILE * span, 2 * width), jnp.bfloat16),
            pltpu.VMEM((2 * width, (TILE + 2) * span), jnp.bfloat16),
            pltpu.VMEM((27, rows), jnp.float32),
            pltpu.VMEM((27 * width, rows), jnp.bfloat16),
            pltpu.VMEM((27 * width, rows), jnp.bfloat16),
        ],
        compiler_params=params,
        cost_estimate=pl.CostEstimate(flops=2 * 10**9, bytes_accessed=4 * 10**6, transcendentals=0),
        name="voxels_own_row",
    )(here, *own_pair, code, w_forward, w_back)
    far, own_conv = lax.optimization_barrier((far, own_conv))
    before_pair = (before, across(before))
    after_pair = (after, across(after))
    far_pair = (far, across(far))
    def row_sums(name, pairs, strips, borders, sums, groups=(0, 1), final=0):
        blocks = [block for pair in pairs for block in pair]
        if final:
            out_shape = (
                jax.ShapeDtypeStruct((final, width, width), jnp.float32),
                jax.ShapeDtypeStruct((final, width, width), jnp.bfloat16),
            )
        else:
            out_shape = (
                jax.ShapeDtypeStruct((HALF * width, width), jnp.float32),
                jax.ShapeDtypeStruct((HALF * width, width), jnp.float32),
                jax.ShapeDtypeStruct((width, width), jnp.float32),
            )
        return pl.pallas_call(
            functools.partial(row_kernel, not sums, bool(final), groups, strips, borders),
            out_shape=out_shape,
            in_specs=[smem] + [vmem] * (len(blocks) + len(sums)),
            out_specs=(vmem,) * len(out_shape),
            scratch_shapes=[
                pltpu.VMEM(((TILE + 2) * span, 2 * width), jnp.bfloat16),
                pltpu.VMEM((2 * width, (TILE + 2) * span), jnp.bfloat16),
                pltpu.VMEM((TILE + 1, CODE_ROWS, span), jnp.float32),
                pltpu.VMEM((HALF * width, (TILE + 1) * span), jnp.bfloat16),
                pltpu.VMEM((HALF * width, (TILE + 1) * span), jnp.bfloat16),
            ],
            compiler_params=params,
            cost_estimate=pl.CostEstimate(flops=2 * 10**9, bytes_accessed=4 * 10**6, transcendentals=0),
            name=name,
        )(here, *blocks, *sums)

    def swapped(block):
        return lax.ppermute(block, "batch", [(0, 1), (1, 0)])

    line = [(0, u) for u in range(TILE)]
    sums = row_sums("weight_row_0", (own_pair,), line, [], ())
    sums = row_sums("weight_row_1", (before_pair, own_pair), line + [(1, 0)], [(TILE, TILE - 1)], sums)
    sums = row_sums("weight_row_2", (after_pair, own_pair), line + [(1, TILE - 1)], [(0, TILE)], sums)
    sides, sides_sent = row_sums("weight_row_3", (far_pair, before_pair, after_pair),
                                 line + [(1, 0), (2, TILE - 1)], [(TILE, TILE - 1), (0, TILE + 1)],
                                 sums, groups=(0,), final=18)
    sides_other = swapped(sides_sent)
    centre, sides = lax.optimization_barrier((sums[2], sides))
    middle, middle_sent = row_sums("weight_row_3_middle", (far_pair,), line, [], (sums[0], sums[1], centre),
                                   groups=(1,), final=9)
    middle_other = swapped(middle_sent)
    conv_out, feature_grad = pl.pallas_call(
        edge_kernel,
        out_shape=(jax.ShapeDtypeStruct((rows, width), jnp.bfloat16),) * 2,
        in_specs=[smem] + [vmem] * 10,
        out_specs=(vmem, vmem),
        scratch_shapes=[
            pltpu.VMEM((2 * span, 2 * width), jnp.bfloat16),
            pltpu.VMEM((2 * width, 2 * span), jnp.bfloat16),
            pltpu.VMEM((2, 9 * width, span), jnp.bfloat16),
        ],
        compiler_params=params,
        cost_estimate=pl.CostEstimate(flops=10**9, bytes_accessed=4 * 10**6, transcendentals=0),
        name="voxel_edges",
    )(here, *before_pair, *after_pair, code, w_forward, w_back, own_conv, own_grad, z_val)
    middle_other, conv_out = lax.optimization_barrier((middle_other, conv_out))
    weight_grad = pl.pallas_call(
        finish_kernel,
        out_shape=jax.ShapeDtypeStruct((27, width, width), jnp.float32),
        in_specs=[vmem] * 4,
        out_specs=pl.BlockSpec(memory_space=pltpu.HBM),
        scratch_shapes=[
            pltpu.VMEM((27, width, width), jnp.float32),
            pltpu.SemaphoreType.DMA((27 // FINISH_STEP,)),
        ],
        compiler_params=pltpu.CompilerParams(vmem_limit_bytes=PACK_VMEM),
        name="finish",
    )(sides, sides_other, middle, middle_other)
    return (conv_out[None], feature_grad[None], weight_grad)


def passed_along(block, axis, distance):
    devices = range(lax.axis_size(axis))
    route = [(i - distance, i) for i in devices if i - distance in devices]
    return lax.ppermute(block, axis, route)


def slab_rows(block, side_recv, front_recv, width):
    widened = jnp.concatenate([side_recv[0], block, side_recv[1]], axis=1)
    slab = jnp.concatenate([front_recv[0][None], widened, front_recv[1][None]], axis=0)
    flat = slab.reshape(-1, width)
    return jnp.concatenate([flat, jnp.zeros((1, width), jnp.bfloat16)], axis=0)


def with_halo(block, tiles_y):
    width = block.shape[-1]
    side = TILE
    side_recv = tuple(passed_along(block[:, edge], "brick", by)[:, None] for by, edge in ((1, side - 1), (-1, 0)))
    wide = jnp.concatenate([side_recv[0], block, side_recv[1]], axis=1)
    front_recv = tuple(passed_along(wide[edge], "brick", by) for by, edge in ((tiles_y, side - 1), (-tiles_y, 0)))
    return slab_rows(block, side_recv, front_recv, width)


def halo_plan(features, cotangent, neighbours, timesteps, condition, w_time, w_conv, tiles_x, tiles_y):
    rows_here, width = features.shape[1:]
    here = lax.axis_index("brick")
    tile_x = here // tiles_y
    tile_y = here % tiles_y
    side = TILE
    layers = LAYERS
    wide = side + 2
    valid = neighbours >= 0
    safe = jnp.where(valid, neighbours, 0)
    owner = safe // rows_here
    inside = safe % rows_here
    column = inside // layers
    layer = inside % layers
    local_x = (owner // tiles_y - tile_x) * side + column // side + 1
    local_y = (owner % tiles_y - tile_y) * side + column % side + 1
    sentinel = wide * wide * layers
    ext_index = jnp.where(valid, (local_x * wide + local_y) * layers + layer, sentinel).T
    temb = time_embedding(timesteps, width)
    shift = jnp.dot(temb, w_time, preferred_element_type=jnp.float32) + condition.astype(jnp.float32)
    z_val = features[0].astype(jnp.float32) + shift[0][None, :]
    act = jax.nn.silu(z_val).astype(jnp.bfloat16)
    cot = cotangent[0]
    w_forward = w_conv.reshape(27 * width, width)
    w_backward = jnp.transpose(w_conv[::-1], (0, 2, 1)).reshape(27 * width, width)
    act_ext = with_halo(act.reshape(side, side, layers, width), tiles_y)
    gathered = act_ext[ext_index].reshape(rows_here, 27 * width)
    conv_out = jnp.dot(gathered, w_forward, preferred_element_type=jnp.float32).astype(jnp.bfloat16)
    partial_grad = lax.dot_general(
        gathered, cot, (((0,), (0,)), ((), ())), preferred_element_type=jnp.float32
    )
    both = ("brick", "batch")
    parts = tiles_x * tiles_y * lax.axis_size("batch")
    rows = 27 * width
    extra = -rows % (8 * parts)
    pieces = jnp.pad(partial_grad.astype(jnp.bfloat16), ((0, extra), (0, 0))).reshape(parts, -1, width)
    arrived = lax.all_to_all(pieces, both, 0, 0)
    summed = arrived.astype(jnp.float32).sum(0).astype(jnp.bfloat16)
    whole = lax.all_gather(summed, both, axis=0, tiled=True)
    weight_grad = whole[:rows].astype(jnp.float32).reshape(27, width, width)
    cot_ext = with_halo(cot.reshape(side, side, layers, width), tiles_y)
    cot_gathered = cot_ext[ext_index].reshape(rows_here, 27 * width)
    back = jnp.dot(cot_gathered, w_backward, preferred_element_type=jnp.float32)
    sig = jax.nn.sigmoid(z_val)
    feature_grad = (back * sig * (1.0 + z_val * (1.0 - sig))).astype(jnp.bfloat16)
    return (conv_out[None], feature_grad[None], weight_grad)


def shards(*arrays):
    peers = lax.axis_size("brick")
    bits = peers.bit_length() - 1
    tiles_x = 2 ** ((bits + 1) // 2)
    tiles_y = 2 ** (bits // 2)
    plan = whole_scene if (tiles_x, tiles_y) == (ROW_STAGES, 2) else halo_plan
    return plan(*arrays, tiles_x, tiles_y)


def solution(mesh):
    in_specs = (
        P(("groups", "batch"), "brick", None),
        P(("groups", "batch"), "brick", None),
        P(None, ("groups", "brick")),
        P(("groups", "batch")),
        P(("groups", "batch"), None),
        P(),
        P(),
    )
    out_specs = (
        P(("groups", "batch"), "brick", None),
        P(("groups", "batch"), "brick", None),
        P("groups", None, None),
    )
    return jax.shard_map(shards, mesh=mesh, in_specs=in_specs, out_specs=out_specs, check_vma=False)
```

```python
import functools

import jax
import jax.numpy as jnp
from jax import lax
from jax.experimental import pallas as pl
from jax.experimental.pallas import tpu as pltpu
from jax.sharding import PartitionSpec as P

LAYERS = 16
TILE = 4
STRIP = TILE * LAYERS
HALF = 13
CODE_ROWS = 16
ROW_STAGES = 4
FINISH_STEP = 3
PACK_VMEM = 8 * 1024 * 1024
KERNEL_VMEM = 24 * 1024 * 1024


def time_embedding(timesteps, width):
    half = width // 2
    freq = jnp.exp(-jnp.log(10000.0) * jnp.arange(half, dtype=jnp.float32) / half)
    angle = timesteps.astype(jnp.float32)[:, None] * freq[None, :]
    return jnp.concatenate([jnp.sin(angle), jnp.cos(angle)], axis=1).astype(jnp.bfloat16)


def strip_codes(neighbours, tiles_y):
    rows_here = TILE * STRIP
    code = (neighbours // rows_here) % tiles_y * STRIP + neighbours % STRIP
    return jnp.where(neighbours < 0, -1, code).astype(jnp.float32)


def in_hbm(array):
    return pltpu.with_memory_space_constraint(array, pltpu.HBM)


def pack_kernel(time_ref, feat_hbm, cot_hbm, near_hbm, cond_hbm, wt_hbm, pack_ref, z_ref, code_ref,
                feat_ref, near_ref, cond_ref, wt_ref, sems):
    rows, width = feat_ref.shape
    half = width // 2
    moves = (
        (wt_hbm, wt_ref),
        (cond_hbm, cond_ref),
        (feat_hbm.at[0], feat_ref),
        (near_hbm, near_ref),
        (cot_hbm.at[0], pack_ref.at[:rows, width:]),
    )
    copies = [pltpu.make_async_copy(source, to, sems.at[i]) for i, (source, to) in enumerate(moves)]
    for copy in copies:
        copy.start()
    lane = lax.broadcasted_iota(jnp.int32, (1, width), 1)
    freq = jnp.exp(-jnp.log(10000.0) * (lane % half).astype(jnp.float32) / half)
    angle = time_ref[0].astype(jnp.float32) * freq
    temb = jnp.where(lane < half, jnp.sin(angle), jnp.cos(angle)).astype(jnp.bfloat16)
    copies[0].wait()
    copies[1].wait()
    shift = jnp.dot(temb, wt_ref[...], preferred_element_type=jnp.float32)
    shift = shift + cond_ref[...].astype(jnp.float32)
    copies[2].wait()
    z_val = feat_ref[...].astype(jnp.float32) + shift
    z_ref[...] = z_val
    pack_ref[:rows, :width] = (z_val * jax.nn.sigmoid(z_val)).astype(jnp.bfloat16)
    copies[3].wait()
    code = strip_codes(near_ref[...], 2)
    code_ref[...] = code
    pack_ref[rows:, :] = code[:CODE_ROWS, :].astype(jnp.bfloat16)
    copies[4].wait()


def lay_strip(ground, to, tile_y, mine_ref, other_ref, u):
    span = 2 * STRIP
    for ref, place in ((mine_ref, tile_y), (other_ref, 1 - tile_y)):
        at = pl.multiple_of(to * span + place * STRIP, STRIP)
        ground[pl.ds(at, STRIP), :] = ref[u * STRIP:(u + 1) * STRIP, :]


def look_up(window, picks, places):
    ref, first, lanes = window
    width = ref.shape[0] // 2
    for i in range(0, len(picks), 2):
        pair = picks[i:i + 2]
        pick = jnp.concatenate(pair, axis=1) if len(pair) == 2 else pair[0]
        span = pair[0].shape[1]
        for side in range(2):
            near = jnp.dot(ref[side * width:(side + 1) * width, first:first + lanes], pick,
                           preferred_element_type=jnp.float32).astype(jnp.bfloat16)
            for j, (to, row, lane) in enumerate(places[i:i + 2]):
                to[side][row:row + width, lane:lane + span] = near[:, j * span:(j + 1) * span]


def row_kernel(first_stage, final, groups, strips, borders, *refs):
    refs = list(refs)
    where_ref = refs.pop(0)
    pairs = [(refs.pop(0), refs.pop(0)) for _ in range(1 + max(pair for pair, _ in strips))]
    before = [refs.pop(0) for _ in range(0 if first_stage else 3)]
    outs = [refs.pop(0) for _ in range(2 if final else 3)]
    ground, turned, codes, near_act, near_cot = refs
    width = ground.shape[1] // 2
    rows = TILE * STRIP
    span = 2 * STRIP
    tile_y = where_ref[0] % 2
    borders = [(u, u - 1) for u in range(1, TILE)] + borders
    targets = sorted({target for target, _ in borders})
    for i, (pair, u) in enumerate(strips):
        lay_strip(ground, i, tile_y, *pairs[pair], u)
        if i < TILE or i in targets:
            both = [ref[rows:, u * STRIP:(u + 1) * STRIP].astype(jnp.float32) for ref in pairs[pair]]
            first = jnp.where(tile_y == 0, both[0], both[1])
            second = jnp.where(tile_y == 0, both[1], both[0])
            codes[i] = jnp.concatenate([first, second], axis=1)
        if i < TILE or i in [source for _, source in borders]:
            turned[:, i * span:(i + 1) * span] = ground[i * span:(i + 1) * span, :].T
    place = lax.broadcasted_iota(jnp.int32, (span, span), 0).astype(jnp.float32)

    to = (near_act, near_cot)
    for source in range(TILE + 2):
        found = [(source, k) for k in range(9, HALF)] if 1 in groups and source < TILE else []
        if 0 in groups:
            found += [(target, k) for target, origin in borders if origin == source for k in range(9)]
        if found:
            picks = [(place == codes[target, k:k + 1, :]).astype(jnp.bfloat16) for target, k in found]
            look_up((turned, source * span, span), picks, [(to, k * width, target * span) for target, k in found])
    extents = ((0, 9, span * targets[0], span * (targets[-1] + 1)), (9, HALF, 0, TILE * span))
    for turn, near in ((0, near_act), (1, near_cot)):
        for group in groups:
            start, stop, first, last = extents[group]
            other = ground[first:last, (1 - turn) * width:(2 - turn) * width]
            value = jnp.dot(near[start * width:stop * width, first:last], other, preferred_element_type=jnp.float32)
            if not first_stage:
                value = value + before[turn][start * width:stop * width, :]
            if not final:
                outs[turn][start * width:stop * width, :] = value
                continue
            for k in range(start, stop):
                one = value[(k - start) * width:(k - start + 1) * width, :]
                to = 2 * HALF - k if turn else k
                if turn:
                    one = one.T
                to = to - 9 if group == 1 else to - 9 * turn
                outs[0][to] = one
                outs[1][to] = one.astype(jnp.bfloat16)
    if 1 in groups:
        centre = jnp.dot(turned[:width, :TILE * span], ground[:TILE * span, width:], preferred_element_type=jnp.float32)
        if not first_stage:
            centre = centre + before[2][...]
        if final:
            outs[0][HALF - 9] = centre
            outs[1][HALF - 9] = centre.astype(jnp.bfloat16)
        else:
            outs[2][...] = centre


def turn_kernel(w_ref, forward_ref, back_ref):
    width = w_ref.shape[1]
    for k in range(27):
        forward_ref[:, k * width:(k + 1) * width] = w_ref[k].T
        back_ref[:, k * width:(k + 1) * width] = w_ref[26 - k]


def own_kernel(where_ref, mine_ref, other_ref, code_ref, forward_ref, back_ref, conv_ref, grad_ref,
               ground, turned, codes, near_act, near_cot):
    width = conv_ref.shape[0]
    span = 2 * STRIP
    tile_y = where_ref[0] % 2
    for u in range(TILE):
        lay_strip(ground, u, tile_y, mine_ref, other_ref, u)
        turned[:, (u + 1) * span:(u + 2) * span] = ground[u * span:(u + 1) * span, :].T
    for i in (0, TILE + 1):
        turned[:, i * span:(i + 1) * span] = jnp.zeros((2 * width, span), jnp.bfloat16)
    code = code_ref[...]
    lane = lax.broadcasted_iota(jnp.int32, code.shape, 1)
    codes[...] = jnp.where((code >= 0) & (lane // STRIP % 2 == 1), code + span, code)
    place = lax.broadcasted_iota(jnp.int32, (2 * span, span), 0).astype(jnp.float32)
    for half in range(TILE // 2):
        at = half * span
        for side in range(3):
            source = (2 * half + side) * span
            ks = range(9 * side, 9 * side + 9)
            picks = [(place == codes[k:k + 1, at:at + span]).astype(jnp.bfloat16) for k in ks]
            look_up((turned, source, 2 * span), picks, [((near_act, near_cot), k * width, at) for k in ks])
    conv_ref[...] = jnp.dot(forward_ref[...], near_act[...], preferred_element_type=jnp.float32)
    grad_ref[...] = jnp.dot(back_ref[...], near_cot[...], preferred_element_type=jnp.float32)


def edge_kernel(where_ref, before_mine, before_other, after_mine, after_other, code_ref, forward_ref, back_ref,
                own_conv, own_grad, z_ref, conv_ref, grad_ref, ground, turned, near):
    width = z_ref.shape[1]
    span = 2 * STRIP
    tile_y = where_ref[0] % 2
    lay_strip(ground, 0, tile_y, before_mine, before_other, TILE - 1)
    lay_strip(ground, 1, tile_y, after_mine, after_other, 0)
    for i in range(2):
        turned[:, i * span:(i + 1) * span] = ground[i * span:(i + 1) * span, :].T
    first = code_ref[:9, :span]
    last = code_ref[18:, span:]
    lane = lax.broadcasted_iota(jnp.int32, first.shape, 1)
    code = jnp.where(lane < STRIP, first, jnp.where(last >= 0, last + span, last))
    place = lax.broadcasted_iota(jnp.int32, (2 * span, span), 0).astype(jnp.float32)
    picks = [(place == code[k:k + 1, :]).astype(jnp.bfloat16) for k in range(9)]
    look_up((turned, 0, 2 * span), picks, [((near.at[0], near.at[1]), k * width, 0) for k in range(9)])
    lane = lax.broadcasted_iota(jnp.int32, (width, span), 1)

    def total(own_ref, weights, side):
        low = jnp.dot(weights[:, :9 * width], near[side], preferred_element_type=jnp.float32)
        high = jnp.dot(weights[:, 18 * width:], near[side], preferred_element_type=jnp.float32)
        low = own_ref[:, :span] + jnp.where(lane < STRIP, low, 0.0)
        high = own_ref[:, span:] + jnp.where(lane < STRIP, 0.0, high)
        return jnp.concatenate([low, high], axis=1).T

    conv_ref[...] = total(own_conv, forward_ref, 0).astype(jnp.bfloat16)
    back = total(own_grad, back_ref, 1)
    z_val = z_ref[...]
    sig = jax.nn.sigmoid(z_val)
    grad_ref[...] = (back * sig * (1.0 + z_val * (1.0 - sig))).astype(jnp.bfloat16)


def finish_kernel(sides_ref, sides_sent, middle_ref, middle_sent, weight_hbm, weight, sems):
    copies = []
    for i, first in enumerate(range(0, 27, FINISH_STEP)):
        kept, sent, at = (middle_ref, middle_sent, first - 9) if first // 9 == 1 else (
            sides_ref, sides_sent, first if first < 9 else first - 9)
        part, taken = pl.ds(first, FINISH_STEP), pl.ds(at, FINISH_STEP)
        weight[part] = kept[taken] + sent[taken].astype(jnp.float32)
        copies.append(pltpu.make_async_copy(weight.at[part], weight_hbm.at[part], sems.at[i]))
        copies[-1].start()
    for copy in copies:
        copy.wait()


def whole_scene(features, cotangent, neighbours, timesteps, condition, w_time, w_conv, tiles_x, tiles_y):
    rows, width = features.shape[1:]
    peers = tiles_x * tiles_y
    span = 2 * STRIP
    vmem = pl.BlockSpec(memory_space=pltpu.VMEM)
    smem = pl.BlockSpec(memory_space=pltpu.SMEM)
    params = pltpu.CompilerParams(vmem_limit_bytes=KERNEL_VMEM)
    packed, z_val, code = pl.pallas_call(
        pack_kernel,
        out_shape=(
            jax.ShapeDtypeStruct((rows + CODE_ROWS, 2 * width), jnp.bfloat16),
            jax.ShapeDtypeStruct((rows, width), jnp.float32),
            jax.ShapeDtypeStruct(neighbours.shape, jnp.float32),
        ),
        in_specs=[smem] + [pl.BlockSpec(memory_space=pltpu.HBM)] * 5,
        out_specs=(vmem, vmem, vmem),
        scratch_shapes=[
            pltpu.VMEM((rows, width), jnp.bfloat16),
            pltpu.VMEM(neighbours.shape, jnp.int32),
            pltpu.VMEM((1, width), jnp.bfloat16),
            pltpu.VMEM((width, width), jnp.bfloat16),
            pltpu.SemaphoreType.DMA((5,)),
        ],
        compiler_params=pltpu.CompilerParams(vmem_limit_bytes=PACK_VMEM),
        name="pack_tile",
    )(timesteps, *[in_hbm(array) for array in (features, cotangent, neighbours, condition, w_time)])
    here = lax.axis_index("brick").astype(jnp.int32).reshape(1)

    def across(block):
        return lax.ppermute(block, "brick", [(i, i ^ 1) for i in range(peers)])

    def along(block, turn):
        return lax.ppermute(block, "brick", [(i, (i + turn * tiles_y) % peers) for i in range(peers)])

    w_conv, packed = lax.optimization_barrier((w_conv, packed))
    w_forward, w_back = pl.pallas_call(
        turn_kernel,
        out_shape=(jax.ShapeDtypeStruct((width, 27 * width), jnp.bfloat16),) * 2,
        in_specs=[vmem],
        out_specs=(vmem, vmem),
        compiler_params=params,
        cost_estimate=pl.CostEstimate(flops=2 * 10**8, bytes_accessed=3 * 10**6, transcendentals=0),
        name="turn_weights",
    )(w_conv)
    before, after = along(packed, 1), along(packed, -1)
    before, w_forward = lax.optimization_barrier((before, w_forward))
    far = along(before, 1)
    own_pair = (packed, across(packed))
    own_conv, own_grad = pl.pallas_call(
        own_kernel,
        out_shape=(jax.ShapeDtypeStruct((width, rows), jnp.float32),) * 2,
        in_specs=[smem] + [vmem] * 5,
        out_specs=(vmem, vmem),
        scratch_shapes=[
            pltpu.VMEM((TILE * span, 2 * width), jnp.bfloat16),
            pltpu.VMEM((2 * width, (TILE + 2) * span), jnp.bfloat16),
            pltpu.VMEM((27, rows), jnp.float32),
            pltpu.VMEM((27 * width, rows), jnp.bfloat16),
            pltpu.VMEM((27 * width, rows), jnp.bfloat16),
        ],
        compiler_params=params,
        cost_estimate=pl.CostEstimate(flops=2 * 10**9, bytes_accessed=4 * 10**6, transcendentals=0),
        name="voxels_own_row",
    )(here, *own_pair, code, w_forward, w_back)
    far, own_conv = lax.optimization_barrier((far, own_conv))
    before_pair = (before, across(before))
    after_pair = (after, across(after))
    far_pair = (far, across(far))
    def row_sums(name, pairs, strips, borders, sums, groups=(0, 1), final=0):
        blocks = [block for pair in pairs for block in pair]
        if final:
            out_shape = (
                jax.ShapeDtypeStruct((final, width, width), jnp.float32),
                jax.ShapeDtypeStruct((final, width, width), jnp.bfloat16),
            )
        else:
            out_shape = (
                jax.ShapeDtypeStruct((HALF * width, width), jnp.float32),
                jax.ShapeDtypeStruct((HALF * width, width), jnp.float32),
                jax.ShapeDtypeStruct((width, width), jnp.float32),
            )
        return pl.pallas_call(
            functools.partial(row_kernel, not sums, bool(final), groups, strips, borders),
            out_shape=out_shape,
            in_specs=[smem] + [vmem] * (len(blocks) + len(sums)),
            out_specs=(vmem,) * len(out_shape),
            scratch_shapes=[
                pltpu.VMEM(((TILE + 2) * span, 2 * width), jnp.bfloat16),
                pltpu.VMEM((2 * width, (TILE + 2) * span), jnp.bfloat16),
                pltpu.VMEM((TILE + 1, CODE_ROWS, span), jnp.float32),
                pltpu.VMEM((HALF * width, (TILE + 1) * span), jnp.bfloat16),
                pltpu.VMEM((HALF * width, (TILE + 1) * span), jnp.bfloat16),
            ],
            compiler_params=params,
            cost_estimate=pl.CostEstimate(flops=2 * 10**9, bytes_accessed=4 * 10**6, transcendentals=0),
            name=name,
        )(here, *blocks, *sums)

    def swapped(block):
        return lax.ppermute(block, "batch", [(0, 1), (1, 0)])

    line = [(0, u) for u in range(TILE)]
    sums = row_sums("weight_row_0", (own_pair,), line, [], ())
    sums = row_sums("weight_row_1", (before_pair, own_pair), line + [(1, 0)], [(TILE, TILE - 1)], sums)
    sums = row_sums("weight_row_2", (after_pair, own_pair), line + [(1, TILE - 1)], [(0, TILE)], sums)
    sides, sides_sent = row_sums("weight_row_3", (far_pair, before_pair, after_pair),
                                 line + [(1, 0), (2, TILE - 1)], [(TILE, TILE - 1), (0, TILE + 1)],
                                 sums, groups=(0,), final=18)
    sides_other = swapped(sides_sent)
    centre, sides = lax.optimization_barrier((sums[2], sides))
    middle, middle_sent = row_sums("weight_row_3_middle", (far_pair,), line, [], (sums[0], sums[1], centre),
                                   groups=(1,), final=9)
    middle_other = swapped(middle_sent)
    conv_out, feature_grad = pl.pallas_call(
        edge_kernel,
        out_shape=(jax.ShapeDtypeStruct((rows, width), jnp.bfloat16),) * 2,
        in_specs=[smem] + [vmem] * 10,
        out_specs=(vmem, vmem),
        scratch_shapes=[
            pltpu.VMEM((2 * span, 2 * width), jnp.bfloat16),
            pltpu.VMEM((2 * width, 2 * span), jnp.bfloat16),
            pltpu.VMEM((2, 9 * width, span), jnp.bfloat16),
        ],
        compiler_params=params,
        cost_estimate=pl.CostEstimate(flops=10**9, bytes_accessed=4 * 10**6, transcendentals=0),
        name="voxel_edges",
    )(here, *before_pair, *after_pair, code, w_forward, w_back, own_conv, own_grad, z_val)
    middle_other, conv_out = lax.optimization_barrier((middle_other, conv_out))
    weight_grad = pl.pallas_call(
        finish_kernel,
        out_shape=jax.ShapeDtypeStruct((27, width, width), jnp.float32),
        in_specs=[vmem] * 4,
        out_specs=pl.BlockSpec(memory_space=pltpu.HBM),
        scratch_shapes=[
            pltpu.VMEM((27, width, width), jnp.float32),
            pltpu.SemaphoreType.DMA((27 // FINISH_STEP,)),
        ],
        compiler_params=pltpu.CompilerParams(vmem_limit_bytes=PACK_VMEM),
        name="finish",
    )(sides, sides_other, middle, middle_other)
    return (conv_out[None], feature_grad[None], weight_grad)


def passed_along(block, axis, distance):
    devices = range(lax.axis_size(axis))
    route = [(i - distance, i) for i in devices if i - distance in devices]
    return lax.ppermute(block, axis, route)


def slab_rows(block, side_recv, front_recv, width):
    widened = jnp.concatenate([side_recv[0], block, side_recv[1]], axis=1)
    slab = jnp.concatenate([front_recv[0][None], widened, front_recv[1][None]], axis=0)
    flat = slab.reshape(-1, width)
    return jnp.concatenate([flat, jnp.zeros((1, width), jnp.bfloat16)], axis=0)


def with_halo(block, tiles_y):
    width = block.shape[-1]
    side = TILE
    side_recv = tuple(passed_along(block[:, edge], "brick", by)[:, None] for by, edge in ((1, side - 1), (-1, 0)))
    wide = jnp.concatenate([side_recv[0], block, side_recv[1]], axis=1)
    front_recv = tuple(passed_along(wide[edge], "brick", by) for by, edge in ((tiles_y, side - 1), (-tiles_y, 0)))
    return slab_rows(block, side_recv, front_recv, width)


def halo_plan(features, cotangent, neighbours, timesteps, condition, w_time, w_conv, tiles_x, tiles_y):
    rows_here, width = features.shape[1:]
    here = lax.axis_index("brick")
    tile_x = here // tiles_y
    tile_y = here % tiles_y
    side = TILE
    layers = LAYERS
    wide = side + 2
    valid = neighbours >= 0
    safe = jnp.where(valid, neighbours, 0)
    owner = safe // rows_here
    inside = safe % rows_here
    column = inside // layers
    layer = inside % layers
    local_x = (owner // tiles_y - tile_x) * side + column // side + 1
    local_y = (owner % tiles_y - tile_y) * side + column % side + 1
    sentinel = wide * wide * layers
    ext_index = jnp.where(valid, (local_x * wide + local_y) * layers + layer, sentinel).T
    temb = time_embedding(timesteps, width)
    shift = jnp.dot(temb, w_time, preferred_element_type=jnp.float32) + condition.astype(jnp.float32)
    z_val = features[0].astype(jnp.float32) + shift[0][None, :]
    act = jax.nn.silu(z_val).astype(jnp.bfloat16)
    cot = cotangent[0]
    w_forward = w_conv.reshape(27 * width, width)
    w_backward = jnp.transpose(w_conv[::-1], (0, 2, 1)).reshape(27 * width, width)
    act_ext = with_halo(act.reshape(side, side, layers, width), tiles_y)
    gathered = act_ext[ext_index].reshape(rows_here, 27 * width)
    conv_out = jnp.dot(gathered, w_forward, preferred_element_type=jnp.float32).astype(jnp.bfloat16)
    partial_grad = lax.dot_general(
        gathered, cot, (((0,), (0,)), ((), ())), preferred_element_type=jnp.float32
    )
    both = ("brick", "batch")
    parts = tiles_x * tiles_y * lax.axis_size("batch")
    rows = 27 * width
    extra = -rows % (8 * parts)
    pieces = jnp.pad(partial_grad.astype(jnp.bfloat16), ((0, extra), (0, 0))).reshape(parts, -1, width)
    arrived = lax.all_to_all(pieces, both, 0, 0)
    summed = arrived.astype(jnp.float32).sum(0).astype(jnp.bfloat16)
    whole = lax.all_gather(summed, both, axis=0, tiled=True)
    weight_grad = whole[:rows].astype(jnp.float32).reshape(27, width, width)
    cot_ext = with_halo(cot.reshape(side, side, layers, width), tiles_y)
    cot_gathered = cot_ext[ext_index].reshape(rows_here, 27 * width)
    back = jnp.dot(cot_gathered, w_backward, preferred_element_type=jnp.float32)
    sig = jax.nn.sigmoid(z_val)
    feature_grad = (back * sig * (1.0 + z_val * (1.0 - sig))).astype(jnp.bfloat16)
    return (conv_out[None], feature_grad[None], weight_grad)


def shards(*arrays):
    peers = lax.axis_size("brick")
    bits = peers.bit_length() - 1
    tiles_x = 2 ** ((bits + 1) // 2)
    tiles_y = 2 ** (bits // 2)
    plan = whole_scene if (tiles_x, tiles_y) == (ROW_STAGES, 2) else halo_plan
    return plan(*arrays, tiles_x, tiles_y)


def solution(mesh):
    in_specs = (
        P(("groups", "batch"), "brick", None),
        P(("groups", "batch"), "brick", None),
        P(None, ("groups", "brick")),
        P(("groups", "batch")),
        P(("groups", "batch"), None),
        P(),
        P(),
    )
    out_specs = (
        P(("groups", "batch"), "brick", None),
        P(("groups", "batch"), "brick", None),
        P("groups", None, None),
    )
    return jax.shard_map(shards, mesh=mesh, in_specs=in_specs, out_specs=out_specs, check_vma=False)
```

```python
import functools

import jax
import jax.numpy as jnp
from jax import lax
from jax.experimental import pallas as pl
from jax.experimental.pallas import tpu as pltpu
from jax.sharding import PartitionSpec as P

LAYERS = 16
TILE = 4
STRIP = TILE * LAYERS
HALF = 13
CODE_ROWS = 16
ROW_STAGES = 4
FINISH_STEP = 3
PACK_VMEM = 8 * 1024 * 1024
KERNEL_VMEM = 24 * 1024 * 1024


def time_embedding(timesteps, width):
    half = width // 2
    freq = jnp.exp(-jnp.log(10000.0) * jnp.arange(half, dtype=jnp.float32) / half)
    angle = timesteps.astype(jnp.float32)[:, None] * freq[None, :]
    return jnp.concatenate([jnp.sin(angle), jnp.cos(angle)], axis=1).astype(jnp.bfloat16)


def strip_codes(neighbours, tiles_y):
    rows_here = TILE * STRIP
    code = (neighbours // rows_here) % tiles_y * STRIP + neighbours % STRIP
    return jnp.where(neighbours < 0, -1, code).astype(jnp.float32)


def in_hbm(array):
    return pltpu.with_memory_space_constraint(array, pltpu.HBM)


def pack_kernel(time_ref, feat_hbm, cot_hbm, near_hbm, cond_hbm, wt_hbm, pack_ref, z_ref, code_ref,
                feat_ref, near_ref, cond_ref, wt_ref, sems):
    rows, width = feat_ref.shape
    half = width // 2
    moves = (
        (wt_hbm, wt_ref),
        (cond_hbm, cond_ref),
        (feat_hbm.at[0], feat_ref),
        (near_hbm, near_ref),
        (cot_hbm.at[0], pack_ref.at[:rows, width:]),
    )
    copies = [pltpu.make_async_copy(source, to, sems.at[i]) for i, (source, to) in enumerate(moves)]
    for copy in copies:
        copy.start()
    lane = lax.broadcasted_iota(jnp.int32, (1, width), 1)
    freq = jnp.exp(-jnp.log(10000.0) * (lane % half).astype(jnp.float32) / half)
    angle = time_ref[0].astype(jnp.float32) * freq
    temb = jnp.where(lane < half, jnp.sin(angle), jnp.cos(angle)).astype(jnp.bfloat16)
    copies[0].wait()
    copies[1].wait()
    shift = jnp.dot(temb, wt_ref[...], preferred_element_type=jnp.float32)
    shift = shift + cond_ref[...].astype(jnp.float32)
    copies[2].wait()
    z_val = feat_ref[...].astype(jnp.float32) + shift
    z_ref[...] = z_val
    pack_ref[:rows, :width] = (z_val * jax.nn.sigmoid(z_val)).astype(jnp.bfloat16)
    copies[3].wait()
    code = strip_codes(near_ref[...], 2)
    code_ref[...] = code
    pack_ref[rows:, :] = code[:CODE_ROWS, :].astype(jnp.bfloat16)
    copies[4].wait()


def lay_strip(ground, to, tile_y, mine_ref, other_ref, u):
    span = 2 * STRIP
    for ref, place in ((mine_ref, tile_y), (other_ref, 1 - tile_y)):
        at = pl.multiple_of(to * span + place * STRIP, STRIP)
        ground[pl.ds(at, STRIP), :] = ref[u * STRIP:(u + 1) * STRIP, :]


def look_up(window, picks, places):
    ref, first, lanes = window
    width = ref.shape[0] // 2
    for i in range(0, len(picks), 2):
        pair = picks[i:i + 2]
        pick = jnp.concatenate(pair, axis=1) if len(pair) == 2 else pair[0]
        span = pair[0].shape[1]
        for side in range(2):
            near = jnp.dot(ref[side * width:(side + 1) * width, first:first + lanes], pick,
                           preferred_element_type=jnp.float32).astype(jnp.bfloat16)
            for j, (to, row, lane) in enumerate(places[i:i + 2]):
                to[side][row:row + width, lane:lane + span] = near[:, j * span:(j + 1) * span]


def row_kernel(first_stage, final, groups, strips, borders, *refs):
    refs = list(refs)
    where_ref = refs.pop(0)
    pairs = [(refs.pop(0), refs.pop(0)) for _ in range(1 + max(pair for pair, _ in strips))]
    before = [refs.pop(0) for _ in range(0 if first_stage else 3)]
    outs = [refs.pop(0) for _ in range(2 if final else 3)]
    ground, turned, codes, near_act, near_cot = refs
    width = ground.shape[1] // 2
    rows = TILE * STRIP
    span = 2 * STRIP
    tile_y = where_ref[0] % 2
    borders = [(u, u - 1) for u in range(1, TILE)] + borders
    targets = sorted({target for target, _ in borders})
    for i, (pair, u) in enumerate(strips):
        lay_strip(ground, i, tile_y, *pairs[pair], u)
        if i < TILE or i in targets:
            both = [ref[rows:, u * STRIP:(u + 1) * STRIP].astype(jnp.float32) for ref in pairs[pair]]
            first = jnp.where(tile_y == 0, both[0], both[1])
            second = jnp.where(tile_y == 0, both[1], both[0])
            codes[i] = jnp.concatenate([first, second], axis=1)
        if i < TILE or i in [source for _, source in borders]:
            turned[:, i * span:(i + 1) * span] = ground[i * span:(i + 1) * span, :].T
    place = lax.broadcasted_iota(jnp.int32, (span, span), 0).astype(jnp.float32)

    to = (near_act, near_cot)
    for source in range(TILE + 2):
        found = [(source, k) for k in range(9, HALF)] if 1 in groups and source < TILE else []
        if 0 in groups:
            found += [(target, k) for target, origin in borders if origin == source for k in range(9)]
        if found:
            picks = [(place == codes[target, k:k + 1, :]).astype(jnp.bfloat16) for target, k in found]
            look_up((turned, source * span, span), picks, [(to, k * width, target * span) for target, k in found])
    extents = ((0, 9, span * targets[0], span * (targets[-1] + 1)), (9, HALF, 0, TILE * span))
    for turn, near in ((0, near_act), (1, near_cot)):
        for group in groups:
            start, stop, first, last = extents[group]
            other = ground[first:last, (1 - turn) * width:(2 - turn) * width]
            value = jnp.dot(near[start * width:stop * width, first:last], other, preferred_element_type=jnp.float32)
            if not first_stage:
                value = value + before[turn][start * width:stop * width, :]
            if not final:
                outs[turn][start * width:stop * width, :] = value
                continue
            for k in range(start, stop):
                one = value[(k - start) * width:(k - start + 1) * width, :]
                to = 2 * HALF - k if turn else k
                if turn:
                    one = one.T
                to = to - 9 if group == 1 else to - 9 * turn
                outs[0][to] = one
                outs[1][to] = one.astype(jnp.bfloat16)
    if 1 in groups:
        centre = jnp.dot(turned[:width, :TILE * span], ground[:TILE * span, width:], preferred_element_type=jnp.float32)
        if not first_stage:
            centre = centre + before[2][...]
        if final:
            outs[0][HALF - 9] = centre
            outs[1][HALF - 9] = centre.astype(jnp.bfloat16)
        else:
            outs[2][...] = centre


def turn_kernel(w_ref, forward_ref, back_ref):
    width = w_ref.shape[1]
    for k in range(27):
        forward_ref[:, k * width:(k + 1) * width] = w_ref[k].T
        back_ref[:, k * width:(k + 1) * width] = w_ref[26 - k]


def own_kernel(where_ref, mine_ref, other_ref, code_ref, forward_ref, back_ref, conv_ref, grad_ref,
               ground, turned, codes, near_act, near_cot):
    width = conv_ref.shape[0]
    span = 2 * STRIP
    tile_y = where_ref[0] % 2
    for u in range(TILE):
        lay_strip(ground, u, tile_y, mine_ref, other_ref, u)
        turned[:, (u + 1) * span:(u + 2) * span] = ground[u * span:(u + 1) * span, :].T
    for i in (0, TILE + 1):
        turned[:, i * span:(i + 1) * span] = jnp.zeros((2 * width, span), jnp.bfloat16)
    code = code_ref[...]
    lane = lax.broadcasted_iota(jnp.int32, code.shape, 1)
    codes[...] = jnp.where((code >= 0) & (lane // STRIP % 2 == 1), code + span, code)
    place = lax.broadcasted_iota(jnp.int32, (2 * span, span), 0).astype(jnp.float32)
    for half in range(TILE // 2):
        at = half * span
        for side in range(3):
            source = (2 * half + side) * span
            ks = range(9 * side, 9 * side + 9)
            picks = [(place == codes[k:k + 1, at:at + span]).astype(jnp.bfloat16) for k in ks]
            look_up((turned, source, 2 * span), picks, [((near_act, near_cot), k * width, at) for k in ks])
    conv_ref[...] = jnp.dot(forward_ref[...], near_act[...], preferred_element_type=jnp.float32)
    grad_ref[...] = jnp.dot(back_ref[...], near_cot[...], preferred_element_type=jnp.float32)


def edge_kernel(where_ref, before_mine, before_other, after_mine, after_other, code_ref, forward_ref, back_ref,
                own_conv, own_grad, z_ref, conv_ref, grad_ref, ground, turned, near):
    width = z_ref.shape[1]
    span = 2 * STRIP
    tile_y = where_ref[0] % 2
    lay_strip(ground, 0, tile_y, before_mine, before_other, TILE - 1)
    lay_strip(ground, 1, tile_y, after_mine, after_other, 0)
    for i in range(2):
        turned[:, i * span:(i + 1) * span] = ground[i * span:(i + 1) * span, :].T
    first = code_ref[:9, :span]
    last = code_ref[18:, span:]
    lane = lax.broadcasted_iota(jnp.int32, first.shape, 1)
    code = jnp.where(lane < STRIP, first, jnp.where(last >= 0, last + span, last))
    place = lax.broadcasted_iota(jnp.int32, (2 * span, span), 0).astype(jnp.float32)
    picks = [(place == code[k:k + 1, :]).astype(jnp.bfloat16) for k in range(9)]
    look_up((turned, 0, 2 * span), picks, [((near.at[0], near.at[1]), k * width, 0) for k in range(9)])
    lane = lax.broadcasted_iota(jnp.int32, (width, span), 1)

    def total(own_ref, weights, side):
        low = jnp.dot(weights[:, :9 * width], near[side], preferred_element_type=jnp.float32)
        high = jnp.dot(weights[:, 18 * width:], near[side], preferred_element_type=jnp.float32)
        low = own_ref[:, :span] + jnp.where(lane < STRIP, low, 0.0)
        high = own_ref[:, span:] + jnp.where(lane < STRIP, 0.0, high)
        return jnp.concatenate([low, high], axis=1).T

    conv_ref[...] = total(own_conv, forward_ref, 0).astype(jnp.bfloat16)
    back = total(own_grad, back_ref, 1)
    z_val = z_ref[...]
    sig = jax.nn.sigmoid(z_val)
    grad_ref[...] = (back * sig * (1.0 + z_val * (1.0 - sig))).astype(jnp.bfloat16)


def finish_kernel(sides_ref, sides_sent, middle_ref, middle_sent, weight_hbm, weight, sems):
    copies = []
    for i, first in enumerate(range(0, 27, FINISH_STEP)):
        kept, sent, at = (middle_ref, middle_sent, first - 9) if first // 9 == 1 else (
            sides_ref, sides_sent, first if first < 9 else first - 9)
        part, taken = pl.ds(first, FINISH_STEP), pl.ds(at, FINISH_STEP)
        weight[part] = kept[taken] + sent[taken].astype(jnp.float32)
        copies.append(pltpu.make_async_copy(weight.at[part], weight_hbm.at[part], sems.at[i]))
        copies[-1].start()
    for copy in copies:
        copy.wait()


def whole_scene(features, cotangent, neighbours, timesteps, condition, w_time, w_conv, tiles_x, tiles_y):
    rows, width = features.shape[1:]
    peers = tiles_x * tiles_y
    span = 2 * STRIP
    vmem = pl.BlockSpec(memory_space=pltpu.VMEM)
    smem = pl.BlockSpec(memory_space=pltpu.SMEM)
    params = pltpu.CompilerParams(vmem_limit_bytes=KERNEL_VMEM)
    packed, z_val, code = pl.pallas_call(
        pack_kernel,
        out_shape=(
            jax.ShapeDtypeStruct((rows + CODE_ROWS, 2 * width), jnp.bfloat16),
            jax.ShapeDtypeStruct((rows, width), jnp.float32),
            jax.ShapeDtypeStruct(neighbours.shape, jnp.float32),
        ),
        in_specs=[smem] + [pl.BlockSpec(memory_space=pltpu.HBM)] * 5,
        out_specs=(vmem, vmem, vmem),
        scratch_shapes=[
            pltpu.VMEM((rows, width), jnp.bfloat16),
            pltpu.VMEM(neighbours.shape, jnp.int32),
            pltpu.VMEM((1, width), jnp.bfloat16),
            pltpu.VMEM((width, width), jnp.bfloat16),
            pltpu.SemaphoreType.DMA((5,)),
        ],
        compiler_params=pltpu.CompilerParams(vmem_limit_bytes=PACK_VMEM),
        name="pack_tile",
    )(timesteps, *[in_hbm(array) for array in (features, cotangent, neighbours, condition, w_time)])
    here = lax.axis_index("brick").astype(jnp.int32).reshape(1)

    def across(block):
        return lax.ppermute(block, "brick", [(i, i ^ 1) for i in range(peers)])

    def along(block, turn):
        return lax.ppermute(block, "brick", [(i, (i + turn * tiles_y) % peers) for i in range(peers)])

    w_conv, packed = lax.optimization_barrier((w_conv, packed))
    w_forward, w_back = pl.pallas_call(
        turn_kernel,
        out_shape=(jax.ShapeDtypeStruct((width, 27 * width), jnp.bfloat16),) * 2,
        in_specs=[vmem],
        out_specs=(vmem, vmem),
        compiler_params=params,
        cost_estimate=pl.CostEstimate(flops=2 * 10**8, bytes_accessed=3 * 10**6, transcendentals=0),
        name="turn_weights",
    )(w_conv)
    before, own_other = along(packed, 1), across(packed)
    before, w_forward, packed = lax.optimization_barrier((before, w_forward, packed))
    after = along(packed, -1)
    far = along(before, 1)
    own_pair = (packed, own_other)
    own_conv, own_grad = pl.pallas_call(
        own_kernel,
        out_shape=(jax.ShapeDtypeStruct((width, rows), jnp.float32),) * 2,
        in_specs=[smem] + [vmem] * 5,
        out_specs=(vmem, vmem),
        scratch_shapes=[
            pltpu.VMEM((TILE * span, 2 * width), jnp.bfloat16),
            pltpu.VMEM((2 * width, (TILE + 2) * span), jnp.bfloat16),
            pltpu.VMEM((27, rows), jnp.float32),
            pltpu.VMEM((27 * width, rows), jnp.bfloat16),
            pltpu.VMEM((27 * width, rows), jnp.bfloat16),
        ],
        compiler_params=params,
        cost_estimate=pl.CostEstimate(flops=2 * 10**9, bytes_accessed=4 * 10**6, transcendentals=0),
        name="voxels_own_row",
    )(here, *own_pair, code, w_forward, w_back)
    far, own_conv = lax.optimization_barrier((far, own_conv))
    before_pair = (before, across(before))
    after_pair = (after, across(after))
    far_pair = (far, across(far))
    def row_sums(name, pairs, strips, borders, sums, groups=(0, 1), final=0):
        blocks = [block for pair in pairs for block in pair]
        if final:
            out_shape = (
                jax.ShapeDtypeStruct((final, width, width), jnp.float32),
                jax.ShapeDtypeStruct((final, width, width), jnp.bfloat16),
            )
        else:
            out_shape = (
                jax.ShapeDtypeStruct((HALF * width, width), jnp.float32),
                jax.ShapeDtypeStruct((HALF * width, width), jnp.float32),
                jax.ShapeDtypeStruct((width, width), jnp.float32),
            )
        return pl.pallas_call(
            functools.partial(row_kernel, not sums, bool(final), groups, strips, borders),
            out_shape=out_shape,
            in_specs=[smem] + [vmem] * (len(blocks) + len(sums)),
            out_specs=(vmem,) * len(out_shape),
            scratch_shapes=[
                pltpu.VMEM(((TILE + 2) * span, 2 * width), jnp.bfloat16),
                pltpu.VMEM((2 * width, (TILE + 2) * span), jnp.bfloat16),
                pltpu.VMEM((TILE + 1, CODE_ROWS, span), jnp.float32),
                pltpu.VMEM((HALF * width, (TILE + 1) * span), jnp.bfloat16),
                pltpu.VMEM((HALF * width, (TILE + 1) * span), jnp.bfloat16),
            ],
            compiler_params=params,
            cost_estimate=pl.CostEstimate(flops=2 * 10**9, bytes_accessed=4 * 10**6, transcendentals=0),
            name=name,
        )(here, *blocks, *sums)

    def swapped(block):
        return lax.ppermute(block, "batch", [(0, 1), (1, 0)])

    line = [(0, u) for u in range(TILE)]
    sums = row_sums("weight_row_0", (own_pair,), line, [], ())
    sums = row_sums("weight_row_before", (before_pair, own_pair), line + [(1, 0)], [(TILE, TILE - 1)], sums)
    sums = row_sums("weight_row_far", (far_pair, before_pair), line + [(1, 0)], [(TILE, TILE - 1)], sums)
    sides, sides_sent = row_sums("weight_row_after", (after_pair, own_pair, far_pair),
                                 line + [(2, 0), (1, TILE - 1)], [(0, TILE + 1), (TILE, TILE - 1)],
                                 sums, groups=(0,), final=18)
    sides_other = swapped(sides_sent)
    centre, sides = lax.optimization_barrier((sums[2], sides))
    middle, middle_sent = row_sums("weight_row_after_middle", (after_pair,), line, [], (sums[0], sums[1], centre),
                                   groups=(1,), final=9)
    middle_other = swapped(middle_sent)
    conv_out, feature_grad = pl.pallas_call(
        edge_kernel,
        out_shape=(jax.ShapeDtypeStruct((rows, width), jnp.bfloat16),) * 2,
        in_specs=[smem] + [vmem] * 10,
        out_specs=(vmem, vmem),
        scratch_shapes=[
            pltpu.VMEM((2 * span, 2 * width), jnp.bfloat16),
            pltpu.VMEM((2 * width, 2 * span), jnp.bfloat16),
            pltpu.VMEM((2, 9 * width, span), jnp.bfloat16),
        ],
        compiler_params=params,
        cost_estimate=pl.CostEstimate(flops=10**9, bytes_accessed=4 * 10**6, transcendentals=0),
        name="voxel_edges",
    )(here, *before_pair, *after_pair, code, w_forward, w_back, own_conv, own_grad, z_val)
    middle_other, conv_out = lax.optimization_barrier((middle_other, conv_out))
    weight_grad = pl.pallas_call(
        finish_kernel,
        out_shape=jax.ShapeDtypeStruct((27, width, width), jnp.float32),
        in_specs=[vmem] * 4,
        out_specs=pl.BlockSpec(memory_space=pltpu.HBM),
        scratch_shapes=[
            pltpu.VMEM((27, width, width), jnp.float32),
            pltpu.SemaphoreType.DMA((27 // FINISH_STEP,)),
        ],
        compiler_params=pltpu.CompilerParams(vmem_limit_bytes=PACK_VMEM),
        name="finish",
    )(sides, sides_other, middle, middle_other)
    return (conv_out[None], feature_grad[None], weight_grad)


def passed_along(block, axis, distance):
    devices = range(lax.axis_size(axis))
    route = [(i - distance, i) for i in devices if i - distance in devices]
    return lax.ppermute(block, axis, route)


def slab_rows(block, side_recv, front_recv, width):
    widened = jnp.concatenate([side_recv[0], block, side_recv[1]], axis=1)
    slab = jnp.concatenate([front_recv[0][None], widened, front_recv[1][None]], axis=0)
    flat = slab.reshape(-1, width)
    return jnp.concatenate([flat, jnp.zeros((1, width), jnp.bfloat16)], axis=0)


def with_halo(block, tiles_y):
    width = block.shape[-1]
    side = TILE
    side_recv = tuple(passed_along(block[:, edge], "brick", by)[:, None] for by, edge in ((1, side - 1), (-1, 0)))
    wide = jnp.concatenate([side_recv[0], block, side_recv[1]], axis=1)
    front_recv = tuple(passed_along(wide[edge], "brick", by) for by, edge in ((tiles_y, side - 1), (-tiles_y, 0)))
    return slab_rows(block, side_recv, front_recv, width)


def halo_plan(features, cotangent, neighbours, timesteps, condition, w_time, w_conv, tiles_x, tiles_y):
    rows_here, width = features.shape[1:]
    here = lax.axis_index("brick")
    tile_x = here // tiles_y
    tile_y = here % tiles_y
    side = TILE
    layers = LAYERS
    wide = side + 2
    valid = neighbours >= 0
    safe = jnp.where(valid, neighbours, 0)
    owner = safe // rows_here
    inside = safe % rows_here
    column = inside // layers
    layer = inside % layers
    local_x = (owner // tiles_y - tile_x) * side + column // side + 1
    local_y = (owner % tiles_y - tile_y) * side + column % side + 1
    sentinel = wide * wide * layers
    ext_index = jnp.where(valid, (local_x * wide + local_y) * layers + layer, sentinel).T
    temb = time_embedding(timesteps, width)
    shift = jnp.dot(temb, w_time, preferred_element_type=jnp.float32) + condition.astype(jnp.float32)
    z_val = features[0].astype(jnp.float32) + shift[0][None, :]
    act = jax.nn.silu(z_val).astype(jnp.bfloat16)
    cot = cotangent[0]
    w_forward = w_conv.reshape(27 * width, width)
    w_backward = jnp.transpose(w_conv[::-1], (0, 2, 1)).reshape(27 * width, width)
    act_ext = with_halo(act.reshape(side, side, layers, width), tiles_y)
    gathered = act_ext[ext_index].reshape(rows_here, 27 * width)
    conv_out = jnp.dot(gathered, w_forward, preferred_element_type=jnp.float32).astype(jnp.bfloat16)
    partial_grad = lax.dot_general(
        gathered, cot, (((0,), (0,)), ((), ())), preferred_element_type=jnp.float32
    )
    both = ("brick", "batch")
    parts = tiles_x * tiles_y * lax.axis_size("batch")
    rows = 27 * width
    extra = -rows % (8 * parts)
    pieces = jnp.pad(partial_grad.astype(jnp.bfloat16), ((0, extra), (0, 0))).reshape(parts, -1, width)
    arrived = lax.all_to_all(pieces, both, 0, 0)
    summed = arrived.astype(jnp.float32).sum(0).astype(jnp.bfloat16)
    whole = lax.all_gather(summed, both, axis=0, tiled=True)
    weight_grad = whole[:rows].astype(jnp.float32).reshape(27, width, width)
    cot_ext = with_halo(cot.reshape(side, side, layers, width), tiles_y)
    cot_gathered = cot_ext[ext_index].reshape(rows_here, 27 * width)
    back = jnp.dot(cot_gathered, w_backward, preferred_element_type=jnp.float32)
    sig = jax.nn.sigmoid(z_val)
    feature_grad = (back * sig * (1.0 + z_val * (1.0 - sig))).astype(jnp.bfloat16)
    return (conv_out[None], feature_grad[None], weight_grad)


def shards(*arrays):
    peers = lax.axis_size("brick")
    bits = peers.bit_length() - 1
    tiles_x = 2 ** ((bits + 1) // 2)
    tiles_y = 2 ** (bits // 2)
    plan = whole_scene if (tiles_x, tiles_y) == (ROW_STAGES, 2) else halo_plan
    return plan(*arrays, tiles_x, tiles_y)


def solution(mesh):
    in_specs = (
        P(("groups", "batch"), "brick", None),
        P(("groups", "batch"), "brick", None),
        P(None, ("groups", "brick")),
        P(("groups", "batch")),
        P(("groups", "batch"), None),
        P(),
        P(),
    )
    out_specs = (
        P(("groups", "batch"), "brick", None),
        P(("groups", "batch"), "brick", None),
        P("groups", None, None),
    )
    return jax.shard_map(shards, mesh=mesh, in_specs=in_specs, out_specs=out_specs, check_vma=False)
```

```python
import functools

import jax
import jax.numpy as jnp
from jax import lax
from jax.experimental import pallas as pl
from jax.experimental.pallas import tpu as pltpu
from jax.sharding import PartitionSpec as P

LAYERS = 16
TILE = 4
STRIP = TILE * LAYERS
HALF = 13
CODE_ROWS = 16
ROW_STAGES = 4
FINISH_STEP = 3
PACK_VMEM = 8 * 1024 * 1024
KERNEL_VMEM = 24 * 1024 * 1024


def time_embedding(timesteps, width):
    half = width // 2
    freq = jnp.exp(-jnp.log(10000.0) * jnp.arange(half, dtype=jnp.float32) / half)
    angle = timesteps.astype(jnp.float32)[:, None] * freq[None, :]
    return jnp.concatenate([jnp.sin(angle), jnp.cos(angle)], axis=1).astype(jnp.bfloat16)


def strip_codes(neighbours, tiles_y):
    rows_here = TILE * STRIP
    code = (neighbours // rows_here) % tiles_y * STRIP + neighbours % STRIP
    return jnp.where(neighbours < 0, -1, code).astype(jnp.float32)


def in_hbm(array):
    return pltpu.with_memory_space_constraint(array, pltpu.HBM)


def pack_kernel(time_ref, feat_hbm, cot_hbm, near_hbm, cond_hbm, wt_hbm, pack_ref, z_ref, code_ref,
                feat_ref, near_ref, cond_ref, wt_ref, sems):
    rows, width = feat_ref.shape
    half = width // 2
    moves = (
        (wt_hbm, wt_ref),
        (cond_hbm, cond_ref),
        (feat_hbm.at[0], feat_ref),
        (near_hbm, near_ref),
        (cot_hbm.at[0], pack_ref.at[:rows, width:]),
    )
    copies = [pltpu.make_async_copy(source, to, sems.at[i]) for i, (source, to) in enumerate(moves)]
    for copy in copies:
        copy.start()
    lane = lax.broadcasted_iota(jnp.int32, (1, width), 1)
    freq = jnp.exp(-jnp.log(10000.0) * (lane % half).astype(jnp.float32) / half)
    angle = time_ref[0].astype(jnp.float32) * freq
    temb = jnp.where(lane < half, jnp.sin(angle), jnp.cos(angle)).astype(jnp.bfloat16)
    copies[0].wait()
    copies[1].wait()
    shift = jnp.dot(temb, wt_ref[...], preferred_element_type=jnp.float32)
    shift = shift + cond_ref[...].astype(jnp.float32)
    copies[2].wait()
    z_val = feat_ref[...].astype(jnp.float32) + shift
    z_ref[...] = z_val
    pack_ref[:rows, :width] = (z_val * jax.nn.sigmoid(z_val)).astype(jnp.bfloat16)
    copies[3].wait()
    code = strip_codes(near_ref[...], 2)
    code_ref[...] = code
    pack_ref[rows:, :] = code[:CODE_ROWS, :].astype(jnp.bfloat16)
    copies[4].wait()


def lay_strip(ground, to, tile_y, mine_ref, other_ref, u):
    span = 2 * STRIP
    for ref, place in ((mine_ref, tile_y), (other_ref, 1 - tile_y)):
        at = pl.multiple_of(to * span + place * STRIP, STRIP)
        ground[pl.ds(at, STRIP), :] = ref[u * STRIP:(u + 1) * STRIP, :]


def look_up(window, picks, places):
    ref, first, lanes = window
    width = ref.shape[0] // 2
    for i in range(0, len(picks), 2):
        pair = picks[i:i + 2]
        pick = jnp.concatenate(pair, axis=1) if len(pair) == 2 else pair[0]
        span = pair[0].shape[1]
        for side in range(2):
            near = jnp.dot(ref[side * width:(side + 1) * width, first:first + lanes], pick,
                           preferred_element_type=jnp.float32).astype(jnp.bfloat16)
            for j, (to, row, lane) in enumerate(places[i:i + 2]):
                to[side][row:row + width, lane:lane + span] = near[:, j * span:(j + 1) * span]


def row_kernel(first_stage, final, groups, laid, strips, borders, *refs):
    refs = list(refs)
    where_ref = refs.pop(0)
    pairs = [] if laid else [(refs.pop(0), refs.pop(0)) for _ in range(1 + max(pair for pair, _ in strips))]
    given = [refs.pop(0) for _ in range(3)] if laid else []
    before = [refs.pop(0) for _ in range(0 if first_stage else 3)]
    outs = [refs.pop(0) for _ in range(2 if final else 3)]
    ground, turned, codes = given or [refs.pop(0) for _ in range(3)]
    near_act, near_cot = refs
    width = ground.shape[1] // 2
    rows = TILE * STRIP
    span = 2 * STRIP
    tile_y = where_ref[0] % 2
    borders = [(u, u - 1) for u in range(1, TILE)] + borders
    targets = sorted({target for target, _ in borders})
    for i, (pair, u) in enumerate([] if laid else strips):
        lay_strip(ground, i, tile_y, *pairs[pair], u)
        if i < TILE or i in targets:
            both = [ref[rows:, u * STRIP:(u + 1) * STRIP].astype(jnp.float32) for ref in pairs[pair]]
            first = jnp.where(tile_y == 0, both[0], both[1])
            second = jnp.where(tile_y == 0, both[1], both[0])
            codes[i] = jnp.concatenate([first, second], axis=1)
        if i < TILE or i in [source for _, source in borders]:
            turned[:, i * span:(i + 1) * span] = ground[i * span:(i + 1) * span, :].T
    place = lax.broadcasted_iota(jnp.int32, (span, span), 0).astype(jnp.float32)

    to = (near_act, near_cot)
    for source in range(TILE + 2):
        found = [(source, k) for k in range(9, HALF)] if 1 in groups and source < TILE else []
        if 0 in groups:
            found += [(target, k) for target, origin in borders if origin == source for k in range(9)]
        if found:
            picks = [(place == codes[target, k:k + 1, :]).astype(jnp.bfloat16) for target, k in found]
            look_up((turned, source * span, span), picks, [(to, k * width, target * span) for target, k in found])
    extents = ((0, 9, span * targets[0], span * (targets[-1] + 1)), (9, HALF, 0, TILE * span))
    for turn, near in ((0, near_act), (1, near_cot)):
        for group in groups:
            start, stop, first, last = extents[group]
            other = ground[first:last, (1 - turn) * width:(2 - turn) * width]
            value = jnp.dot(near[start * width:stop * width, first:last], other, preferred_element_type=jnp.float32)
            if not first_stage:
                value = value + before[turn][start * width:stop * width, :]
            if not final:
                outs[turn][start * width:stop * width, :] = value
                continue
            for k in range(start, stop):
                one = value[(k - start) * width:(k - start + 1) * width, :]
                to = 2 * HALF - k if turn else k
                if turn:
                    one = one.T
                to = to - 9 if group == 1 else to - 9 * turn
                outs[0][to] = one
                outs[1][to] = one.astype(jnp.bfloat16)
    if 1 in groups:
        centre = jnp.dot(turned[:width, :TILE * span], ground[:TILE * span, width:], preferred_element_type=jnp.float32)
        if not first_stage:
            centre = centre + before[2][...]
        if final:
            outs[0][HALF - 9] = centre
            outs[1][HALF - 9] = centre.astype(jnp.bfloat16)
        else:
            outs[2][...] = centre


def turn_kernel(w_ref, forward_ref, back_ref):
    width = w_ref.shape[1]
    for k in range(27):
        forward_ref[:, k * width:(k + 1) * width] = w_ref[k].T
        back_ref[:, k * width:(k + 1) * width] = w_ref[26 - k]


def own_kernel(where_ref, mine_ref, other_ref, code_ref, forward_ref, back_ref, conv_ref, grad_ref,
               ground, turned, codes, near_act, near_cot):
    width = conv_ref.shape[0]
    span = 2 * STRIP
    tile_y = where_ref[0] % 2
    for u in range(TILE):
        lay_strip(ground, u, tile_y, mine_ref, other_ref, u)
        turned[:, (u + 1) * span:(u + 2) * span] = ground[u * span:(u + 1) * span, :].T
    for i in (0, TILE + 1):
        turned[:, i * span:(i + 1) * span] = jnp.zeros((2 * width, span), jnp.bfloat16)
    code = code_ref[...]
    lane = lax.broadcasted_iota(jnp.int32, code.shape, 1)
    codes[...] = jnp.where((code >= 0) & (lane // STRIP % 2 == 1), code + span, code)
    place = lax.broadcasted_iota(jnp.int32, (2 * span, span), 0).astype(jnp.float32)
    for half in range(TILE // 2):
        at = half * span
        for side in range(3):
            source = (2 * half + side) * span
            ks = range(9 * side, 9 * side + 9)
            picks = [(place == codes[k:k + 1, at:at + span]).astype(jnp.bfloat16) for k in ks]
            look_up((turned, source, 2 * span), picks, [((near_act, near_cot), k * width, at) for k in ks])
    conv_ref[...] = jnp.dot(forward_ref[...], near_act[...], preferred_element_type=jnp.float32)
    grad_ref[...] = jnp.dot(back_ref[...], near_cot[...], preferred_element_type=jnp.float32)


def edge_kernel(where_ref, before_mine, before_other, after_mine, after_other, code_ref, forward_ref, back_ref,
                own_conv, own_grad, z_ref, conv_ref, grad_ref, ground, turned, near):
    width = z_ref.shape[1]
    span = 2 * STRIP
    tile_y = where_ref[0] % 2
    lay_strip(ground, 0, tile_y, before_mine, before_other, TILE - 1)
    lay_strip(ground, 1, tile_y, after_mine, after_other, 0)
    for i in range(2):
        turned[:, i * span:(i + 1) * span] = ground[i * span:(i + 1) * span, :].T
    first = code_ref[:9, :span]
    last = code_ref[18:, span:]
    lane = lax.broadcasted_iota(jnp.int32, first.shape, 1)
    code = jnp.where(lane < STRIP, first, jnp.where(last >= 0, last + span, last))
    place = lax.broadcasted_iota(jnp.int32, (2 * span, span), 0).astype(jnp.float32)
    picks = [(place == code[k:k + 1, :]).astype(jnp.bfloat16) for k in range(9)]
    look_up((turned, 0, 2 * span), picks, [((near.at[0], near.at[1]), k * width, 0) for k in range(9)])
    lane = lax.broadcasted_iota(jnp.int32, (width, span), 1)

    def total(own_ref, weights, side):
        low = jnp.dot(weights[:, :9 * width], near[side], preferred_element_type=jnp.float32)
        high = jnp.dot(weights[:, 18 * width:], near[side], preferred_element_type=jnp.float32)
        low = own_ref[:, :span] + jnp.where(lane < STRIP, low, 0.0)
        high = own_ref[:, span:] + jnp.where(lane < STRIP, 0.0, high)
        return jnp.concatenate([low, high], axis=1).T

    conv_ref[...] = total(own_conv, forward_ref, 0).astype(jnp.bfloat16)
    back = total(own_grad, back_ref, 1)
    z_val = z_ref[...]
    sig = jax.nn.sigmoid(z_val)
    grad_ref[...] = (back * sig * (1.0 + z_val * (1.0 - sig))).astype(jnp.bfloat16)


def finish_kernel(sides_ref, sides_sent, middle_ref, middle_sent, conv_ref, grad_ref,
                  weight_hbm, conv_hbm, grad_hbm, weight, sems):
    steps = 27 // FINISH_STEP
    copies = [
        pltpu.make_async_copy(conv_ref, conv_hbm, sems.at[steps]),
        pltpu.make_async_copy(grad_ref, grad_hbm, sems.at[steps + 1]),
    ]
    for copy in copies:
        copy.start()
    for i in range(steps):
        first = i * FINISH_STEP
        kept, sent, at = (middle_ref, middle_sent, first - 9) if first // 9 == 1 else (
            sides_ref, sides_sent, first if first < 9 else first - 9)
        part, taken = pl.ds(first, FINISH_STEP), pl.ds(at, FINISH_STEP)
        weight[part] = kept[taken] + sent[taken].astype(jnp.float32)
        copies.append(pltpu.make_async_copy(weight.at[part], weight_hbm.at[part], sems.at[i]))
        copies[-1].start()
    for copy in copies:
        copy.wait()


def whole_scene(features, cotangent, neighbours, timesteps, condition, w_time, w_conv, tiles_x, tiles_y):
    rows, width = features.shape[1:]
    peers = tiles_x * tiles_y
    span = 2 * STRIP
    vmem = pl.BlockSpec(memory_space=pltpu.VMEM)
    smem = pl.BlockSpec(memory_space=pltpu.SMEM)
    params = pltpu.CompilerParams(vmem_limit_bytes=KERNEL_VMEM)
    packed, z_val, code = pl.pallas_call(
        pack_kernel,
        out_shape=(
            jax.ShapeDtypeStruct((rows + CODE_ROWS, 2 * width), jnp.bfloat16),
            jax.ShapeDtypeStruct((rows, width), jnp.float32),
            jax.ShapeDtypeStruct(neighbours.shape, jnp.float32),
        ),
        in_specs=[smem] + [pl.BlockSpec(memory_space=pltpu.HBM)] * 5,
        out_specs=(vmem, vmem, vmem),
        scratch_shapes=[
            pltpu.VMEM((rows, width), jnp.bfloat16),
            pltpu.VMEM(neighbours.shape, jnp.int32),
            pltpu.VMEM((1, width), jnp.bfloat16),
            pltpu.VMEM((width, width), jnp.bfloat16),
            pltpu.SemaphoreType.DMA((5,)),
        ],
        compiler_params=pltpu.CompilerParams(vmem_limit_bytes=PACK_VMEM),
        name="pack_tile",
    )(timesteps, *[in_hbm(array) for array in (features, cotangent, neighbours, condition, w_time)])
    here = lax.axis_index("brick").astype(jnp.int32).reshape(1)

    def across(block):
        return lax.ppermute(block, "brick", [(i, i ^ 1) for i in range(peers)])

    def along(block, turn):
        return lax.ppermute(block, "brick", [(i, (i + turn * tiles_y) % peers) for i in range(peers)])

    w_conv, packed = lax.optimization_barrier((w_conv, packed))
    w_forward, w_back = pl.pallas_call(
        turn_kernel,
        out_shape=(jax.ShapeDtypeStruct((width, 27 * width), jnp.bfloat16),) * 2,
        in_specs=[vmem],
        out_specs=(vmem, vmem),
        compiler_params=params,
        cost_estimate=pl.CostEstimate(flops=2 * 10**8, bytes_accessed=3 * 10**6, transcendentals=0),
        name="turn_weights",
    )(w_conv)
    before, after = along(packed, 1), along(packed, -1)
    before, w_forward = lax.optimization_barrier((before, w_forward))
    far = along(before, 1)
    own_pair = (packed, across(packed))
    own_conv, own_grad = pl.pallas_call(
        own_kernel,
        out_shape=(jax.ShapeDtypeStruct((width, rows), jnp.float32),) * 2,
        in_specs=[smem] + [vmem] * 5,
        out_specs=(vmem, vmem),
        scratch_shapes=[
            pltpu.VMEM((TILE * span, 2 * width), jnp.bfloat16),
            pltpu.VMEM((2 * width, (TILE + 2) * span), jnp.bfloat16),
            pltpu.VMEM((27, rows), jnp.float32),
            pltpu.VMEM((27 * width, rows), jnp.bfloat16),
            pltpu.VMEM((27 * width, rows), jnp.bfloat16),
        ],
        compiler_params=params,
        cost_estimate=pl.CostEstimate(flops=2 * 10**9, bytes_accessed=4 * 10**6, transcendentals=0),
        name="voxels_own_row",
    )(here, *own_pair, code, w_forward, w_back)
    far, own_conv = lax.optimization_barrier((far, own_conv))
    before_pair = (before, across(before))
    after_pair = (after, across(after))
    far_pair = (far, across(far))
    def row_sums(name, pairs, strips, borders, sums, groups=(0, 1), final=0, keep=False, laid=()):
        blocks = [block for pair in pairs for block in pair]
        if final:
            out_shape = (
                jax.ShapeDtypeStruct((final, width, width), jnp.float32),
                jax.ShapeDtypeStruct((final, width, width), jnp.bfloat16),
            )
        else:
            out_shape = (
                jax.ShapeDtypeStruct((HALF * width, width), jnp.float32),
                jax.ShapeDtypeStruct((HALF * width, width), jnp.float32),
                jax.ShapeDtypeStruct((width, width), jnp.float32),
            )
        layout = (
            ((TILE + 2) * span, 2 * width, jnp.bfloat16),
            (2 * width, (TILE + 2) * span, jnp.bfloat16),
            (TILE + 1, CODE_ROWS, span, jnp.float32),
        )
        scratch = [] if laid or keep else [pltpu.VMEM(tuple(shape), kind) for *shape, kind in layout]
        if keep:
            out_shape += tuple(jax.ShapeDtypeStruct(tuple(shape), kind) for *shape, kind in layout)
        operands = (*blocks, *laid, *sums)
        return pl.pallas_call(
            functools.partial(row_kernel, not sums, bool(final), groups, bool(laid), strips, borders),
            out_shape=out_shape,
            in_specs=[smem] + [vmem] * len(operands),
            out_specs=(vmem,) * len(out_shape),
            scratch_shapes=scratch + [
                pltpu.VMEM((HALF * width, (TILE + 1) * span), jnp.bfloat16),
                pltpu.VMEM((HALF * width, (TILE + 1) * span), jnp.bfloat16),
            ],
            compiler_params=params,
            cost_estimate=pl.CostEstimate(flops=2 * 10**9, bytes_accessed=4 * 10**6, transcendentals=0),
            name=name,
        )(here, *operands)

    def swapped(block):
        return lax.ppermute(block, "batch", [(0, 1), (1, 0)])

    line = [(0, u) for u in range(TILE)]
    sums = row_sums("weight_row_0", (own_pair,), line, [], ())
    sums = row_sums("weight_row_1", (before_pair, own_pair), line + [(1, 0)], [(TILE, TILE - 1)], sums)
    sums = row_sums("weight_row_2", (after_pair, own_pair), line + [(1, TILE - 1)], [(0, TILE)], sums)
    sides, sides_sent, *laid = row_sums("weight_row_3", (far_pair, before_pair, after_pair),
                                 line + [(1, 0), (2, TILE - 1)], [(TILE, TILE - 1), (0, TILE + 1)],
                                 sums, groups=(0,), final=18, keep=True)
    sides_other = swapped(sides_sent)
    centre, sides = lax.optimization_barrier((sums[2], sides))
    middle, middle_sent = row_sums("weight_row_3_middle", (), line, [], (sums[0], sums[1], centre),
                                   groups=(1,), final=9, laid=laid)
    middle_other = swapped(middle_sent)
    conv_out, feature_grad = pl.pallas_call(
        edge_kernel,
        out_shape=(jax.ShapeDtypeStruct((rows, width), jnp.bfloat16),) * 2,
        in_specs=[smem] + [vmem] * 10,
        out_specs=(vmem, vmem),
        scratch_shapes=[
            pltpu.VMEM((2 * span, 2 * width), jnp.bfloat16),
            pltpu.VMEM((2 * width, 2 * span), jnp.bfloat16),
            pltpu.VMEM((2, 9 * width, span), jnp.bfloat16),
        ],
        compiler_params=params,
        cost_estimate=pl.CostEstimate(flops=10**9, bytes_accessed=4 * 10**6, transcendentals=0),
        name="voxel_edges",
    )(here, *before_pair, *after_pair, code, w_forward, w_back, own_conv, own_grad, z_val)
    hbm = pl.BlockSpec(memory_space=pltpu.HBM)
    weight_grad, conv_out, feature_grad = pl.pallas_call(
        finish_kernel,
        out_shape=(
            jax.ShapeDtypeStruct((27, width, width), jnp.float32),
            jax.ShapeDtypeStruct((rows, width), jnp.bfloat16),
            jax.ShapeDtypeStruct((rows, width), jnp.bfloat16),
        ),
        in_specs=[vmem] * 6,
        out_specs=(hbm, hbm, hbm),
        scratch_shapes=[
            pltpu.VMEM((27, width, width), jnp.float32),
            pltpu.SemaphoreType.DMA((27 // FINISH_STEP + 2,)),
        ],
        compiler_params=pltpu.CompilerParams(vmem_limit_bytes=PACK_VMEM),
        name="finish",
    )(sides, sides_other, middle, middle_other, conv_out, feature_grad)
    return (conv_out[None], feature_grad[None], weight_grad)


def passed_along(block, axis, distance):
    devices = range(lax.axis_size(axis))
    route = [(i - distance, i) for i in devices if i - distance in devices]
    return lax.ppermute(block, axis, route)


def slab_rows(block, side_recv, front_recv, width):
    widened = jnp.concatenate([side_recv[0], block, side_recv[1]], axis=1)
    slab = jnp.concatenate([front_recv[0][None], widened, front_recv[1][None]], axis=0)
    flat = slab.reshape(-1, width)
    return jnp.concatenate([flat, jnp.zeros((1, width), jnp.bfloat16)], axis=0)


def with_halo(block, tiles_y):
    width = block.shape[-1]
    side = TILE
    side_recv = tuple(passed_along(block[:, edge], "brick", by)[:, None] for by, edge in ((1, side - 1), (-1, 0)))
    wide = jnp.concatenate([side_recv[0], block, side_recv[1]], axis=1)
    front_recv = tuple(passed_along(wide[edge], "brick", by) for by, edge in ((tiles_y, side - 1), (-tiles_y, 0)))
    return slab_rows(block, side_recv, front_recv, width)


def halo_plan(features, cotangent, neighbours, timesteps, condition, w_time, w_conv, tiles_x, tiles_y):
    rows_here, width = features.shape[1:]
    here = lax.axis_index("brick")
    tile_x = here // tiles_y
    tile_y = here % tiles_y
    side = TILE
    layers = LAYERS
    wide = side + 2
    valid = neighbours >= 0
    safe = jnp.where(valid, neighbours, 0)
    owner = safe // rows_here
    inside = safe % rows_here
    column = inside // layers
    layer = inside % layers
    local_x = (owner // tiles_y - tile_x) * side + column // side + 1
    local_y = (owner % tiles_y - tile_y) * side + column % side + 1
    sentinel = wide * wide * layers
    ext_index = jnp.where(valid, (local_x * wide + local_y) * layers + layer, sentinel).T
    temb = time_embedding(timesteps, width)
    shift = jnp.dot(temb, w_time, preferred_element_type=jnp.float32) + condition.astype(jnp.float32)
    z_val = features[0].astype(jnp.float32) + shift[0][None, :]
    act = jax.nn.silu(z_val).astype(jnp.bfloat16)
    cot = cotangent[0]
    w_forward = w_conv.reshape(27 * width, width)
    w_backward = jnp.transpose(w_conv[::-1], (0, 2, 1)).reshape(27 * width, width)
    act_ext = with_halo(act.reshape(side, side, layers, width), tiles_y)
    gathered = act_ext[ext_index].reshape(rows_here, 27 * width)
    conv_out = jnp.dot(gathered, w_forward, preferred_element_type=jnp.float32).astype(jnp.bfloat16)
    partial_grad = lax.dot_general(
        gathered, cot, (((0,), (0,)), ((), ())), preferred_element_type=jnp.float32
    )
    both = ("brick", "batch")
    parts = tiles_x * tiles_y * lax.axis_size("batch")
    rows = 27 * width
    extra = -rows % (8 * parts)
    pieces = jnp.pad(partial_grad.astype(jnp.bfloat16), ((0, extra), (0, 0))).reshape(parts, -1, width)
    arrived = lax.all_to_all(pieces, both, 0, 0)
    summed = arrived.astype(jnp.float32).sum(0).astype(jnp.bfloat16)
    whole = lax.all_gather(summed, both, axis=0, tiled=True)
    weight_grad = whole[:rows].astype(jnp.float32).reshape(27, width, width)
    cot_ext = with_halo(cot.reshape(side, side, layers, width), tiles_y)
    cot_gathered = cot_ext[ext_index].reshape(rows_here, 27 * width)
    back = jnp.dot(cot_gathered, w_backward, preferred_element_type=jnp.float32)
    sig = jax.nn.sigmoid(z_val)
    feature_grad = (back * sig * (1.0 + z_val * (1.0 - sig))).astype(jnp.bfloat16)
    return (conv_out[None], feature_grad[None], weight_grad)


def shards(*arrays):
    peers = lax.axis_size("brick")
    bits = peers.bit_length() - 1
    tiles_x = 2 ** ((bits + 1) // 2)
    tiles_y = 2 ** (bits // 2)
    plan = whole_scene if (tiles_x, tiles_y) == (ROW_STAGES, 2) else halo_plan
    return plan(*arrays, tiles_x, tiles_y)


def solution(mesh):
    in_specs = (
        P(("groups", "batch"), "brick", None),
        P(("groups", "batch"), "brick", None),
        P(None, ("groups", "brick")),
        P(("groups", "batch")),
        P(("groups", "batch"), None),
        P(),
        P(),
    )
    out_specs = (
        P(("groups", "batch"), "brick", None),
        P(("groups", "batch"), "brick", None),
        P("groups", None, None),
    )
    return jax.shard_map(shards, mesh=mesh, in_specs=in_specs, out_specs=out_specs, check_vma=False)
```

```python
import functools
import operator

import jax
import jax.numpy as jnp
from jax import lax
from jax.experimental import pallas as pl
from jax.experimental.pallas import tpu as pltpu
from jax.sharding import PartitionSpec as P

LAYERS = 16
TILE = 4
STRIP = TILE * LAYERS
HALF = 13
CODE_ROWS = 16
ROW_STAGES = 4
FINISH_STEP = 3
PACK_VMEM = 8 * 1024 * 1024
KERNEL_VMEM = 24 * 1024 * 1024


def time_embedding(timesteps, width):
    half = width // 2
    freq = jnp.exp(-jnp.log(10000.0) * jnp.arange(half, dtype=jnp.float32) / half)
    angle = timesteps.astype(jnp.float32)[:, None] * freq[None, :]
    return jnp.concatenate([jnp.sin(angle), jnp.cos(angle)], axis=1).astype(jnp.bfloat16)


def strip_codes(neighbours, tiles_y):
    rows_here = TILE * STRIP
    code = (neighbours // rows_here) % tiles_y * STRIP + neighbours % STRIP
    return jnp.where(neighbours < 0, -1, code).astype(jnp.float32)


def in_hbm(array):
    return pltpu.with_memory_space_constraint(array, pltpu.HBM)


def pack_kernel(time_ref, feat_hbm, cot_hbm, near_hbm, cond_hbm, wt_hbm, pack_ref, z_ref, code_ref,
                feat_ref, near_ref, cond_ref, wt_ref, sems):
    rows, width = feat_ref.shape
    half = width // 2
    moves = (
        (wt_hbm, wt_ref),
        (cond_hbm, cond_ref),
        (feat_hbm.at[0], feat_ref),
        (near_hbm, near_ref),
        (cot_hbm.at[0], pack_ref.at[:rows, width:]),
    )
    copies = [pltpu.make_async_copy(source, to, sems.at[i]) for i, (source, to) in enumerate(moves)]
    for copy in copies:
        copy.start()
    lane = lax.broadcasted_iota(jnp.int32, (1, width), 1)
    freq = jnp.exp(-jnp.log(10000.0) * (lane % half).astype(jnp.float32) / half)
    angle = time_ref[0].astype(jnp.float32) * freq
    temb = jnp.where(lane < half, jnp.sin(angle), jnp.cos(angle)).astype(jnp.bfloat16)
    copies[0].wait()
    copies[1].wait()
    shift = jnp.dot(temb, wt_ref[...], preferred_element_type=jnp.float32)
    shift = shift + cond_ref[...].astype(jnp.float32)
    copies[2].wait()
    z_val = feat_ref[...].astype(jnp.float32) + shift
    z_ref[...] = z_val
    pack_ref[:rows, :width] = (z_val * jax.nn.sigmoid(z_val)).astype(jnp.bfloat16)
    copies[3].wait()
    code = strip_codes(near_ref[...], 2)
    code_ref[...] = code
    pack_ref[rows:, :] = code[:CODE_ROWS, :].astype(jnp.bfloat16)
    copies[4].wait()


def lay_strip(ground, to, tile_y, mine_ref, other_ref, u):
    span = 2 * STRIP
    for ref, place in ((mine_ref, tile_y), (other_ref, 1 - tile_y)):
        at = pl.multiple_of(to * span + place * STRIP, STRIP)
        ground[pl.ds(at, STRIP), :] = ref[u * STRIP:(u + 1) * STRIP, :]


def look_up(window, picks, places):
    ref, first, lanes = window
    width = ref.shape[0] // 2
    for i in range(0, len(picks), 2):
        pair = picks[i:i + 2]
        pick = jnp.concatenate(pair, axis=1) if len(pair) == 2 else pair[0]
        span = pair[0].shape[1]
        for side in range(2):
            near = jnp.dot(ref[side * width:(side + 1) * width, first:first + lanes], pick,
                           preferred_element_type=jnp.float32).astype(jnp.bfloat16)
            for j, (to, row, lane) in enumerate(places[i:i + 2]):
                to[side][row:row + width, lane:lane + span] = near[:, j * span:(j + 1) * span]


def added(terms):
    return functools.reduce(operator.add, terms)


def row_kernel(first_stage, final, groups, laid, lines, strips, borders, *refs):
    refs = list(refs)
    where_ref = refs.pop(0)
    pairs = [] if laid else [(refs.pop(0), refs.pop(0)) for _ in range(1 + max(pair for pair, _ in strips))]
    given = [refs.pop(0) for _ in range(3)] if laid else []
    before = [refs.pop(0) for _ in range(0 if first_stage else 3)]
    outs = [refs.pop(0) for _ in range(2 if final else 3)]
    ground, turned, codes = given or [refs.pop(0) for _ in range(3)]
    near_act, near_cot = refs
    width = ground.shape[1] // 2
    rows = TILE * STRIP
    span = 2 * STRIP
    tile_y = where_ref[0] % 2
    borders = [(at + u, at + u - 1) for at in lines for u in range(1, TILE)] + borders
    targets = sorted({target for target, _ in borders})
    line_strips = [at + u for at in lines for u in range(TILE)]
    spans = [(at * span, (at + TILE) * span) for at in lines]
    for i, (pair, u) in enumerate([] if laid else strips):
        lay_strip(ground, i, tile_y, *pairs[pair], u)
        if i in line_strips + targets:
            both = [ref[rows:, u * STRIP:(u + 1) * STRIP].astype(jnp.float32) for ref in pairs[pair]]
            first = jnp.where(tile_y == 0, both[0], both[1])
            second = jnp.where(tile_y == 0, both[1], both[0])
            codes[i] = jnp.concatenate([first, second], axis=1)
        if i in line_strips + [source for _, source in borders]:
            turned[:, i * span:(i + 1) * span] = ground[i * span:(i + 1) * span, :].T
    place = lax.broadcasted_iota(jnp.int32, (span, span), 0).astype(jnp.float32)

    to = (near_act, near_cot)
    for source in range(len(strips)):
        found = [(source, k) for k in range(9, HALF)] if 1 in groups and source in line_strips else []
        if 0 in groups:
            found += [(target, k) for target, origin in borders if origin == source for k in range(9)]
        if found:
            picks = [(place == codes[target, k:k + 1, :]).astype(jnp.bfloat16) for target, k in found]
            look_up((turned, source * span, span), picks, [(to, k * width, target * span) for target, k in found])
    extents = ((0, 9, [(span * targets[0], span * (targets[-1] + 1))] if targets else []), (9, HALF, spans))
    for turn, near in ((0, near_act), (1, near_cot)):
        for group in groups:
            start, stop, parts = extents[group]
            value = added(jnp.dot(near[start * width:stop * width, first:last],
                                ground[first:last, (1 - turn) * width:(2 - turn) * width],
                                preferred_element_type=jnp.float32) for first, last in parts)
            if not first_stage:
                value = value + before[turn][start * width:stop * width, :]
            if not final:
                outs[turn][start * width:stop * width, :] = value
                continue
            for k in range(start, stop):
                one = value[(k - start) * width:(k - start + 1) * width, :]
                to = 2 * HALF - k if turn else k
                if turn:
                    one = one.T
                to = to - 9 if group == 1 else to - 9 * turn
                outs[0][to] = one
                outs[1][to] = one.astype(jnp.bfloat16)
    if 1 in groups:
        centre = added(jnp.dot(turned[:width, first:last], ground[first:last, width:], preferred_element_type=jnp.float32)
                       for first, last in spans)
        if not first_stage:
            centre = centre + before[2][...]
        if final:
            outs[0][HALF - 9] = centre
            outs[1][HALF - 9] = centre.astype(jnp.bfloat16)
        else:
            outs[2][...] = centre


def turn_kernel(w_ref, forward_ref, back_ref):
    width = w_ref.shape[1]
    for k in range(27):
        forward_ref[:, k * width:(k + 1) * width] = w_ref[k].T
        back_ref[:, k * width:(k + 1) * width] = w_ref[26 - k]


def own_kernel(where_ref, mine_ref, other_ref, code_ref, forward_ref, back_ref, conv_ref, grad_ref,
               ground, turned, codes, near_act, near_cot):
    width = conv_ref.shape[0]
    span = 2 * STRIP
    tile_y = where_ref[0] % 2
    for u in range(TILE):
        lay_strip(ground, u, tile_y, mine_ref, other_ref, u)
        turned[:, (u + 1) * span:(u + 2) * span] = ground[u * span:(u + 1) * span, :].T
    for i in (0, TILE + 1):
        turned[:, i * span:(i + 1) * span] = jnp.zeros((2 * width, span), jnp.bfloat16)
    code = code_ref[...]
    lane = lax.broadcasted_iota(jnp.int32, code.shape, 1)
    codes[...] = jnp.where((code >= 0) & (lane // STRIP % 2 == 1), code + span, code)
    place = lax.broadcasted_iota(jnp.int32, (2 * span, span), 0).astype(jnp.float32)
    for half in range(TILE // 2):
        at = half * span
        for side in range(3):
            source = (2 * half + side) * span
            ks = range(9 * side, 9 * side + 9)
            picks = [(place == codes[k:k + 1, at:at + span]).astype(jnp.bfloat16) for k in ks]
            look_up((turned, source, 2 * span), picks, [((near_act, near_cot), k * width, at) for k in ks])
    conv_ref[...] = jnp.dot(forward_ref[...], near_act[...], preferred_element_type=jnp.float32)
    grad_ref[...] = jnp.dot(back_ref[...], near_cot[...], preferred_element_type=jnp.float32)


def edge_kernel(where_ref, before_mine, before_other, after_mine, after_other, code_ref, forward_ref, back_ref,
                own_conv, own_grad, z_ref, conv_ref, grad_ref, ground, turned, near):
    width = z_ref.shape[1]
    span = 2 * STRIP
    tile_y = where_ref[0] % 2
    lay_strip(ground, 0, tile_y, before_mine, before_other, TILE - 1)
    lay_strip(ground, 1, tile_y, after_mine, after_other, 0)
    for i in range(2):
        turned[:, i * span:(i + 1) * span] = ground[i * span:(i + 1) * span, :].T
    first = code_ref[:9, :span]
    last = code_ref[18:, span:]
    lane = lax.broadcasted_iota(jnp.int32, first.shape, 1)
    code = jnp.where(lane < STRIP, first, jnp.where(last >= 0, last + span, last))
    place = lax.broadcasted_iota(jnp.int32, (2 * span, span), 0).astype(jnp.float32)
    picks = [(place == code[k:k + 1, :]).astype(jnp.bfloat16) for k in range(9)]
    look_up((turned, 0, 2 * span), picks, [((near.at[0], near.at[1]), k * width, 0) for k in range(9)])
    lane = lax.broadcasted_iota(jnp.int32, (width, span), 1)

    def total(own_ref, weights, side):
        low = jnp.dot(weights[:, :9 * width], near[side], preferred_element_type=jnp.float32)
        high = jnp.dot(weights[:, 18 * width:], near[side], preferred_element_type=jnp.float32)
        low = own_ref[:, :span] + jnp.where(lane < STRIP, low, 0.0)
        high = own_ref[:, span:] + jnp.where(lane < STRIP, 0.0, high)
        return jnp.concatenate([low, high], axis=1).T

    conv_ref[...] = total(own_conv, forward_ref, 0).astype(jnp.bfloat16)
    back = total(own_grad, back_ref, 1)
    z_val = z_ref[...]
    sig = jax.nn.sigmoid(z_val)
    grad_ref[...] = (back * sig * (1.0 + z_val * (1.0 - sig))).astype(jnp.bfloat16)


def finish_kernel(sides_ref, sides_sent, middle_ref, middle_sent, conv_ref, grad_ref,
                  weight_hbm, conv_hbm, grad_hbm, weight, sems):
    steps = 27 // FINISH_STEP
    copies = [
        pltpu.make_async_copy(conv_ref, conv_hbm, sems.at[steps]),
        pltpu.make_async_copy(grad_ref, grad_hbm, sems.at[steps + 1]),
    ]
    for copy in copies:
        copy.start()
    for i in range(steps):
        first = i * FINISH_STEP
        kept, sent, at = (middle_ref, middle_sent, first - 9) if first // 9 == 1 else (
            sides_ref, sides_sent, first if first < 9 else first - 9)
        part, taken = pl.ds(first, FINISH_STEP), pl.ds(at, FINISH_STEP)
        weight[part] = kept[taken] + sent[taken].astype(jnp.float32)
        copies.append(pltpu.make_async_copy(weight.at[part], weight_hbm.at[part], sems.at[i]))
        copies[-1].start()
    for copy in copies:
        copy.wait()


def whole_scene(features, cotangent, neighbours, timesteps, condition, w_time, w_conv, tiles_x, tiles_y):
    rows, width = features.shape[1:]
    peers = tiles_x * tiles_y
    span = 2 * STRIP
    vmem = pl.BlockSpec(memory_space=pltpu.VMEM)
    smem = pl.BlockSpec(memory_space=pltpu.SMEM)
    params = pltpu.CompilerParams(vmem_limit_bytes=KERNEL_VMEM)
    packed, z_val, code = pl.pallas_call(
        pack_kernel,
        out_shape=(
            jax.ShapeDtypeStruct((rows + CODE_ROWS, 2 * width), jnp.bfloat16),
            jax.ShapeDtypeStruct((rows, width), jnp.float32),
            jax.ShapeDtypeStruct(neighbours.shape, jnp.float32),
        ),
        in_specs=[smem] + [pl.BlockSpec(memory_space=pltpu.HBM)] * 5,
        out_specs=(vmem, vmem, vmem),
        scratch_shapes=[
            pltpu.VMEM((rows, width), jnp.bfloat16),
            pltpu.VMEM(neighbours.shape, jnp.int32),
            pltpu.VMEM((1, width), jnp.bfloat16),
            pltpu.VMEM((width, width), jnp.bfloat16),
            pltpu.SemaphoreType.DMA((5,)),
        ],
        compiler_params=pltpu.CompilerParams(vmem_limit_bytes=PACK_VMEM),
        name="pack_tile",
    )(timesteps, *[in_hbm(array) for array in (features, cotangent, neighbours, condition, w_time)])
    here = lax.axis_index("brick").astype(jnp.int32).reshape(1)

    def across(block):
        return lax.ppermute(block, "brick", [(i, i ^ 1) for i in range(peers)])

    def along(block, turn):
        return lax.ppermute(block, "brick", [(i, (i + turn * tiles_y) % peers) for i in range(peers)])

    w_conv, packed = lax.optimization_barrier((w_conv, packed))
    w_forward, w_back = pl.pallas_call(
        turn_kernel,
        out_shape=(jax.ShapeDtypeStruct((width, 27 * width), jnp.bfloat16),) * 2,
        in_specs=[vmem],
        out_specs=(vmem, vmem),
        compiler_params=params,
        cost_estimate=pl.CostEstimate(flops=2 * 10**8, bytes_accessed=3 * 10**6, transcendentals=0),
        name="turn_weights",
    )(w_conv)
    before, after = along(packed, 1), along(packed, -1)
    before, w_forward = lax.optimization_barrier((before, w_forward))
    far = along(before, 1)
    own_pair = (packed, across(packed))
    own_conv, own_grad = pl.pallas_call(
        own_kernel,
        out_shape=(jax.ShapeDtypeStruct((width, rows), jnp.float32),) * 2,
        in_specs=[smem] + [vmem] * 5,
        out_specs=(vmem, vmem),
        scratch_shapes=[
            pltpu.VMEM((TILE * span, 2 * width), jnp.bfloat16),
            pltpu.VMEM((2 * width, (TILE + 2) * span), jnp.bfloat16),
            pltpu.VMEM((27, rows), jnp.float32),
            pltpu.VMEM((27 * width, rows), jnp.bfloat16),
            pltpu.VMEM((27 * width, rows), jnp.bfloat16),
        ],
        compiler_params=params,
        cost_estimate=pl.CostEstimate(flops=2 * 10**9, bytes_accessed=4 * 10**6, transcendentals=0),
        name="voxels_own_row",
    )(here, *own_pair, code, w_forward, w_back)
    far, own_conv = lax.optimization_barrier((far, own_conv))
    before_pair = (before, across(before))
    after_pair = (after, across(after))
    far_pair = (far, across(far))
    def row_sums(name, pairs, strips, borders, sums, groups=(0, 1), final=0, keep=False, laid=(), lines=(0,)):
        blocks = [block for pair in pairs for block in pair]
        if final:
            out_shape = (
                jax.ShapeDtypeStruct((final, width, width), jnp.float32),
                jax.ShapeDtypeStruct((final, width, width), jnp.bfloat16),
            )
        else:
            out_shape = (
                jax.ShapeDtypeStruct((HALF * width, width), jnp.float32),
                jax.ShapeDtypeStruct((HALF * width, width), jnp.float32),
                jax.ShapeDtypeStruct((width, width), jnp.float32),
            )
        room = max(len(strips), TILE + 2) if not laid else TILE + 2
        layout = (
            (room * span, 2 * width, jnp.bfloat16),
            (2 * width, room * span, jnp.bfloat16),
            (room, CODE_ROWS, span, jnp.float32),
        )
        scratch = [] if laid or keep else [pltpu.VMEM(tuple(shape), kind) for *shape, kind in layout]
        if keep:
            out_shape += tuple(jax.ShapeDtypeStruct(tuple(shape), kind) for *shape, kind in layout)
        operands = (*blocks, *laid, *sums)
        return pl.pallas_call(
            functools.partial(row_kernel, not sums, bool(final), groups, bool(laid), lines, strips, borders),
            out_shape=out_shape,
            in_specs=[smem] + [vmem] * len(operands),
            out_specs=(vmem,) * len(out_shape),
            scratch_shapes=scratch + [
                pltpu.VMEM((HALF * width, room * span), jnp.bfloat16),
                pltpu.VMEM((HALF * width, room * span), jnp.bfloat16),
            ],
            compiler_params=params,
            cost_estimate=pl.CostEstimate(flops=2 * 10**9, bytes_accessed=4 * 10**6, transcendentals=0),
            name=name,
        )(here, *operands)

    def swapped(block):
        return lax.ppermute(block, "batch", [(0, 1), (1, 0)])

    line = [(0, u) for u in range(TILE)]
    sums = row_sums("weight_row_0", (own_pair,), line, [], ())
    around = line + [(1, 0)] + [(2, u) for u in range(TILE)] + [(1, TILE - 1)]
    sums = row_sums("weight_rows_1_2", (before_pair, own_pair, after_pair), around,
                    [(TILE, TILE - 1), (TILE + 1, 2 * TILE + 1)], sums, lines=(0, TILE + 1))
    sides, sides_sent, *laid = row_sums("weight_row_3", (far_pair, before_pair, after_pair),
                                 line + [(1, 0), (2, TILE - 1)], [(TILE, TILE - 1), (0, TILE + 1)],
                                 sums, groups=(0,), final=18, keep=True)
    sides_other = swapped(sides_sent)
    centre, sides = lax.optimization_barrier((sums[2], sides))
    middle, middle_sent = row_sums("weight_row_3_middle", (), line, [], (sums[0], sums[1], centre),
                                   groups=(1,), final=9, laid=laid)
    middle_other = swapped(middle_sent)
    conv_out, feature_grad = pl.pallas_call(
        edge_kernel,
        out_shape=(jax.ShapeDtypeStruct((rows, width), jnp.bfloat16),) * 2,
        in_specs=[smem] + [vmem] * 10,
        out_specs=(vmem, vmem),
        scratch_shapes=[
            pltpu.VMEM((2 * span, 2 * width), jnp.bfloat16),
            pltpu.VMEM((2 * width, 2 * span), jnp.bfloat16),
            pltpu.VMEM((2, 9 * width, span), jnp.bfloat16),
        ],
        compiler_params=params,
        cost_estimate=pl.CostEstimate(flops=10**9, bytes_accessed=4 * 10**6, transcendentals=0),
        name="voxel_edges",
    )(here, *before_pair, *after_pair, code, w_forward, w_back, own_conv, own_grad, z_val)
    hbm = pl.BlockSpec(memory_space=pltpu.HBM)
    weight_grad, conv_out, feature_grad = pl.pallas_call(
        finish_kernel,
        out_shape=(
            jax.ShapeDtypeStruct((27, width, width), jnp.float32),
            jax.ShapeDtypeStruct((rows, width), jnp.bfloat16),
            jax.ShapeDtypeStruct((rows, width), jnp.bfloat16),
        ),
        in_specs=[vmem] * 6,
        out_specs=(hbm, hbm, hbm),
        scratch_shapes=[
            pltpu.VMEM((27, width, width), jnp.float32),
            pltpu.SemaphoreType.DMA((27 // FINISH_STEP + 2,)),
        ],
        compiler_params=pltpu.CompilerParams(vmem_limit_bytes=PACK_VMEM),
        name="finish",
    )(sides, sides_other, middle, middle_other, conv_out, feature_grad)
    return (conv_out[None], feature_grad[None], weight_grad)


def passed_along(block, axis, distance):
    devices = range(lax.axis_size(axis))
    route = [(i - distance, i) for i in devices if i - distance in devices]
    return lax.ppermute(block, axis, route)


def slab_rows(block, side_recv, front_recv, width):
    widened = jnp.concatenate([side_recv[0], block, side_recv[1]], axis=1)
    slab = jnp.concatenate([front_recv[0][None], widened, front_recv[1][None]], axis=0)
    flat = slab.reshape(-1, width)
    return jnp.concatenate([flat, jnp.zeros((1, width), jnp.bfloat16)], axis=0)


def with_halo(block, tiles_y):
    width = block.shape[-1]
    side = TILE
    side_recv = tuple(passed_along(block[:, edge], "brick", by)[:, None] for by, edge in ((1, side - 1), (-1, 0)))
    wide = jnp.concatenate([side_recv[0], block, side_recv[1]], axis=1)
    front_recv = tuple(passed_along(wide[edge], "brick", by) for by, edge in ((tiles_y, side - 1), (-tiles_y, 0)))
    return slab_rows(block, side_recv, front_recv, width)


def halo_plan(features, cotangent, neighbours, timesteps, condition, w_time, w_conv, tiles_x, tiles_y):
    rows_here, width = features.shape[1:]
    here = lax.axis_index("brick")
    tile_x = here // tiles_y
    tile_y = here % tiles_y
    side = TILE
    layers = LAYERS
    wide = side + 2
    valid = neighbours >= 0
    safe = jnp.where(valid, neighbours, 0)
    owner = safe // rows_here
    inside = safe % rows_here
    column = inside // layers
    layer = inside % layers
    local_x = (owner // tiles_y - tile_x) * side + column // side + 1
    local_y = (owner % tiles_y - tile_y) * side + column % side + 1
    sentinel = wide * wide * layers
    ext_index = jnp.where(valid, (local_x * wide + local_y) * layers + layer, sentinel).T
    temb = time_embedding(timesteps, width)
    shift = jnp.dot(temb, w_time, preferred_element_type=jnp.float32) + condition.astype(jnp.float32)
    z_val = features[0].astype(jnp.float32) + shift[0][None, :]
    act = jax.nn.silu(z_val).astype(jnp.bfloat16)
    cot = cotangent[0]
    w_forward = w_conv.reshape(27 * width, width)
    w_backward = jnp.transpose(w_conv[::-1], (0, 2, 1)).reshape(27 * width, width)
    act_ext = with_halo(act.reshape(side, side, layers, width), tiles_y)
    gathered = act_ext[ext_index].reshape(rows_here, 27 * width)
    conv_out = jnp.dot(gathered, w_forward, preferred_element_type=jnp.float32).astype(jnp.bfloat16)
    partial_grad = lax.dot_general(
        gathered, cot, (((0,), (0,)), ((), ())), preferred_element_type=jnp.float32
    )
    both = ("brick", "batch")
    parts = tiles_x * tiles_y * lax.axis_size("batch")
    rows = 27 * width
    extra = -rows % (8 * parts)
    pieces = jnp.pad(partial_grad.astype(jnp.bfloat16), ((0, extra), (0, 0))).reshape(parts, -1, width)
    arrived = lax.all_to_all(pieces, both, 0, 0)
    summed = arrived.astype(jnp.float32).sum(0).astype(jnp.bfloat16)
    whole = lax.all_gather(summed, both, axis=0, tiled=True)
    weight_grad = whole[:rows].astype(jnp.float32).reshape(27, width, width)
    cot_ext = with_halo(cot.reshape(side, side, layers, width), tiles_y)
    cot_gathered = cot_ext[ext_index].reshape(rows_here, 27 * width)
    back = jnp.dot(cot_gathered, w_backward, preferred_element_type=jnp.float32)
    sig = jax.nn.sigmoid(z_val)
    feature_grad = (back * sig * (1.0 + z_val * (1.0 - sig))).astype(jnp.bfloat16)
    return (conv_out[None], feature_grad[None], weight_grad)


def shards(*arrays):
    peers = lax.axis_size("brick")
    bits = peers.bit_length() - 1
    tiles_x = 2 ** ((bits + 1) // 2)
    tiles_y = 2 ** (bits // 2)
    plan = whole_scene if (tiles_x, tiles_y) == (ROW_STAGES, 2) else halo_plan
    return plan(*arrays, tiles_x, tiles_y)


def solution(mesh):
    in_specs = (
        P(("groups", "batch"), "brick", None),
        P(("groups", "batch"), "brick", None),
        P(None, ("groups", "brick")),
        P(("groups", "batch")),
        P(("groups", "batch"), None),
        P(),
        P(),
    )
    out_specs = (
        P(("groups", "batch"), "brick", None),
        P(("groups", "batch"), "brick", None),
        P("groups", None, None),
    )
    return jax.shard_map(shards, mesh=mesh, in_specs=in_specs, out_specs=out_specs, check_vma=False)
```

```python
import functools

import jax
import jax.numpy as jnp
from jax import lax
from jax.experimental import pallas as pl
from jax.experimental.pallas import tpu as pltpu
from jax.sharding import PartitionSpec as P

LAYERS = 16
TILE = 4
STRIP = TILE * LAYERS
HALF = 13
CODE_ROWS = 16
ROW_STAGES = 4
FINISH_STEP = 3
PACK_VMEM = 8 * 1024 * 1024
KERNEL_VMEM = 24 * 1024 * 1024


def time_embedding(timesteps, width):
    half = width // 2
    freq = jnp.exp(-jnp.log(10000.0) * jnp.arange(half, dtype=jnp.float32) / half)
    angle = timesteps.astype(jnp.float32)[:, None] * freq[None, :]
    return jnp.concatenate([jnp.sin(angle), jnp.cos(angle)], axis=1).astype(jnp.bfloat16)


def strip_codes(neighbours, tiles_y):
    rows_here = TILE * STRIP
    code = (neighbours // rows_here) % tiles_y * STRIP + neighbours % STRIP
    return jnp.where(neighbours < 0, -1, code).astype(jnp.float32)


def in_hbm(array):
    return pltpu.with_memory_space_constraint(array, pltpu.HBM)


def pack_kernel(time_ref, feat_hbm, cot_hbm, near_hbm, cond_hbm, wt_hbm, pack_ref, z_ref, code_ref,
                feat_ref, near_ref, cond_ref, wt_ref, sems):
    rows, width = feat_ref.shape
    half = width // 2
    moves = (
        (wt_hbm, wt_ref),
        (cond_hbm, cond_ref),
        (feat_hbm.at[0], feat_ref),
        (near_hbm, near_ref),
        (cot_hbm.at[0], pack_ref.at[:rows, width:]),
    )
    copies = [pltpu.make_async_copy(source, to, sems.at[i]) for i, (source, to) in enumerate(moves)]
    for copy in copies:
        copy.start()
    lane = lax.broadcasted_iota(jnp.int32, (1, width), 1)
    freq = jnp.exp(-jnp.log(10000.0) * (lane % half).astype(jnp.float32) / half)
    angle = time_ref[0].astype(jnp.float32) * freq
    temb = jnp.where(lane < half, jnp.sin(angle), jnp.cos(angle)).astype(jnp.bfloat16)
    copies[0].wait()
    copies[1].wait()
    shift = jnp.dot(temb, wt_ref[...], preferred_element_type=jnp.float32)
    shift = shift + cond_ref[...].astype(jnp.float32)
    copies[2].wait()
    z_val = feat_ref[...].astype(jnp.float32) + shift
    z_ref[...] = z_val
    pack_ref[:rows, :width] = (z_val * jax.nn.sigmoid(z_val)).astype(jnp.bfloat16)
    copies[3].wait()
    code = strip_codes(near_ref[...], 2)
    code_ref[...] = code
    pack_ref[rows:, :] = code[:CODE_ROWS, :].astype(jnp.bfloat16)
    copies[4].wait()


def lay_strip(ground, to, tile_y, mine_ref, other_ref, u):
    span = 2 * STRIP
    for ref, place in ((mine_ref, tile_y), (other_ref, 1 - tile_y)):
        at = pl.multiple_of(to * span + place * STRIP, STRIP)
        ground[pl.ds(at, STRIP), :] = ref[u * STRIP:(u + 1) * STRIP, :]


def look_up(window, picks, places):
    ref, first, lanes = window
    width = ref.shape[0] // 2
    for i in range(0, len(picks), 2):
        pair = picks[i:i + 2]
        pick = jnp.concatenate(pair, axis=1) if len(pair) == 2 else pair[0]
        span = pair[0].shape[1]
        for side in range(2):
            near = jnp.dot(ref[side * width:(side + 1) * width, first:first + lanes], pick,
                           preferred_element_type=jnp.float32).astype(jnp.bfloat16)
            for j, (to, row, lane) in enumerate(places[i:i + 2]):
                to[side][row:row + width, lane:lane + span] = near[:, j * span:(j + 1) * span]


def row_kernel(first_stage, final, groups, laid, strips, borders, *refs):
    refs = list(refs)
    where_ref = refs.pop(0)
    pairs = [] if laid else [(refs.pop(0), refs.pop(0)) for _ in range(1 + max(pair for pair, _ in strips))]
    given = [refs.pop(0) for _ in range(3)] if laid else []
    before = [refs.pop(0) for _ in range(0 if first_stage else 3)]
    outs = [refs.pop(0) for _ in range(2 if final else 3)]
    ground, turned, codes = given or [refs.pop(0) for _ in range(3)]
    near_act, near_cot = refs
    width = ground.shape[1] // 2
    rows = TILE * STRIP
    span = 2 * STRIP
    tile_y = where_ref[0] % 2
    borders = [(u, u - 1) for u in range(1, TILE)] + borders
    targets = sorted({target for target, _ in borders})
    for i, (pair, u) in enumerate([] if laid else strips):
        lay_strip(ground, i, tile_y, *pairs[pair], u)
        if i < TILE or i in targets:
            both = [ref[rows:, u * STRIP:(u + 1) * STRIP].astype(jnp.float32) for ref in pairs[pair]]
            first = jnp.where(tile_y == 0, both[0], both[1])
            second = jnp.where(tile_y == 0, both[1], both[0])
            codes[i] = jnp.concatenate([first, second], axis=1)
        if i < TILE or i in [source for _, source in borders]:
            turned[:, i * span:(i + 1) * span] = ground[i * span:(i + 1) * span, :].T
    place = lax.broadcasted_iota(jnp.int32, (span, span), 0).astype(jnp.float32)

    to = (near_act, near_cot)
    for source in range(TILE + 2):
        found = [(source, k) for k in range(9, HALF)] if 1 in groups and source < TILE else []
        if 0 in groups:
            found += [(target, k) for target, origin in borders if origin == source for k in range(9)]
        if found:
            picks = [(place == codes[target, k:k + 1, :]).astype(jnp.bfloat16) for target, k in found]
            look_up((turned, source * span, span), picks, [(to, k * width, target * span) for target, k in found])
    extents = ((0, 9, span * targets[0], span * (targets[-1] + 1)), (9, HALF, 0, TILE * span))
    for turn, near in ((0, near_act), (1, near_cot)):
        for group in groups:
            start, stop, first, last = extents[group]
            other = ground[first:last, (1 - turn) * width:(2 - turn) * width]
            value = jnp.dot(near[start * width:stop * width, first:last], other, preferred_element_type=jnp.float32)
            if not first_stage:
                value = value + before[turn][start * width:stop * width, :]
            if not final:
                outs[turn][start * width:stop * width, :] = value
                continue
            for k in range(start, stop):
                one = value[(k - start) * width:(k - start + 1) * width, :]
                to = 2 * HALF - k if turn else k
                if turn:
                    one = one.T
                to = to - 9 if group == 1 else to - 9 * turn
                outs[0][to] = one
                outs[1][to] = one.astype(jnp.bfloat16)
    if 1 in groups:
        centre = jnp.dot(turned[:width, :TILE * span], ground[:TILE * span, width:], preferred_element_type=jnp.float32)
        if not first_stage:
            centre = centre + before[2][...]
        if final:
            outs[0][HALF - 9] = centre
            outs[1][HALF - 9] = centre.astype(jnp.bfloat16)
        else:
            outs[2][...] = centre


def turn_kernel(w_ref, forward_ref, back_ref):
    width = w_ref.shape[1]
    for k in range(27):
        forward_ref[:, k * width:(k + 1) * width] = w_ref[k].T
        back_ref[:, k * width:(k + 1) * width] = w_ref[26 - k]


def own_kernel(where_ref, mine_ref, other_ref, code_ref, forward_ref, back_ref, conv_ref, grad_ref,
               ground, turned, codes, near_act, near_cot):
    width = conv_ref.shape[0]
    span = 2 * STRIP
    tile_y = where_ref[0] % 2
    for u in range(TILE):
        lay_strip(ground, u, tile_y, mine_ref, other_ref, u)
        turned[:, (u + 1) * span:(u + 2) * span] = ground[u * span:(u + 1) * span, :].T
    for i in (0, TILE + 1):
        turned[:, i * span:(i + 1) * span] = jnp.zeros((2 * width, span), jnp.bfloat16)
    code = code_ref[...]
    lane = lax.broadcasted_iota(jnp.int32, code.shape, 1)
    codes[...] = jnp.where((code >= 0) & (lane // STRIP % 2 == 1), code + span, code)
    place = lax.broadcasted_iota(jnp.int32, (2 * span, span), 0).astype(jnp.float32)
    for half in range(TILE // 2):
        at = half * span
        for side in range(3):
            source = (2 * half + side) * span
            ks = range(9 * side, 9 * side + 9)
            picks = [(place == codes[k:k + 1, at:at + span]).astype(jnp.bfloat16) for k in ks]
            look_up((turned, source, 2 * span), picks, [((near_act, near_cot), k * width, at) for k in ks])
    conv_ref[...] = jnp.dot(forward_ref[...], near_act[...], preferred_element_type=jnp.float32)
    grad_ref[...] = jnp.dot(back_ref[...], near_cot[...], preferred_element_type=jnp.float32)


def edge_kernel(where_ref, before_mine, before_other, after_mine, after_other, code_ref, forward_ref, back_ref,
                own_conv, own_grad, z_ref, conv_ref, grad_ref, ground, turned, near):
    width = z_ref.shape[1]
    span = 2 * STRIP
    tile_y = where_ref[0] % 2
    lay_strip(ground, 0, tile_y, before_mine, before_other, TILE - 1)
    lay_strip(ground, 1, tile_y, after_mine, after_other, 0)
    for i in range(2):
        turned[:, i * span:(i + 1) * span] = ground[i * span:(i + 1) * span, :].T
    first = code_ref[:9, :span]
    last = code_ref[18:, span:]
    lane = lax.broadcasted_iota(jnp.int32, first.shape, 1)
    code = jnp.where(lane < STRIP, first, jnp.where(last >= 0, last + span, last))
    place = lax.broadcasted_iota(jnp.int32, (2 * span, span), 0).astype(jnp.float32)
    picks = [(place == code[k:k + 1, :]).astype(jnp.bfloat16) for k in range(9)]
    look_up((turned, 0, 2 * span), picks, [((near.at[0], near.at[1]), k * width, 0) for k in range(9)])
    lane = lax.broadcasted_iota(jnp.int32, (width, span), 1)

    def total(own_ref, weights, side):
        low = jnp.dot(weights[:, :9 * width], near[side], preferred_element_type=jnp.float32)
        high = jnp.dot(weights[:, 18 * width:], near[side], preferred_element_type=jnp.float32)
        low = own_ref[:, :span] + jnp.where(lane < STRIP, low, 0.0)
        high = own_ref[:, span:] + jnp.where(lane < STRIP, 0.0, high)
        return jnp.concatenate([low, high], axis=1).T

    conv_ref[...] = total(own_conv, forward_ref, 0).astype(jnp.bfloat16)
    back = total(own_grad, back_ref, 1)
    z_val = z_ref[...]
    sig = jax.nn.sigmoid(z_val)
    grad_ref[...] = (back * sig * (1.0 + z_val * (1.0 - sig))).astype(jnp.bfloat16)


def finish_kernel(sides_ref, sides_sent, middle_ref, middle_sent, conv_ref, grad_ref,
                  weight_hbm, conv_hbm, grad_hbm, weight, sems):
    steps = 27 // FINISH_STEP
    copies = [
        pltpu.make_async_copy(conv_ref, conv_hbm, sems.at[steps]),
        pltpu.make_async_copy(grad_ref, grad_hbm, sems.at[steps + 1]),
    ]
    for copy in copies:
        copy.start()
    for i in range(steps):
        first = i * FINISH_STEP
        kept, sent, at = (middle_ref, middle_sent, first - 9) if first // 9 == 1 else (
            sides_ref, sides_sent, first if first < 9 else first - 9)
        part, taken = pl.ds(first, FINISH_STEP), pl.ds(at, FINISH_STEP)
        weight[part] = kept[taken] + sent[taken].astype(jnp.float32)
        copies.append(pltpu.make_async_copy(weight.at[part], weight_hbm.at[part], sems.at[i]))
        copies[-1].start()
    for copy in copies:
        copy.wait()


def whole_scene(features, cotangent, neighbours, timesteps, condition, w_time, w_conv, tiles_x, tiles_y):
    rows, width = features.shape[1:]
    peers = tiles_x * tiles_y
    span = 2 * STRIP
    vmem = pl.BlockSpec(memory_space=pltpu.VMEM)
    smem = pl.BlockSpec(memory_space=pltpu.SMEM)
    params = pltpu.CompilerParams(vmem_limit_bytes=KERNEL_VMEM)
    packed, z_val, code = pl.pallas_call(
        pack_kernel,
        out_shape=(
            jax.ShapeDtypeStruct((rows + CODE_ROWS, 2 * width), jnp.bfloat16),
            jax.ShapeDtypeStruct((rows, width), jnp.float32),
            jax.ShapeDtypeStruct(neighbours.shape, jnp.float32),
        ),
        in_specs=[smem] + [pl.BlockSpec(memory_space=pltpu.HBM)] * 5,
        out_specs=(vmem, vmem, vmem),
        scratch_shapes=[
            pltpu.VMEM((rows, width), jnp.bfloat16),
            pltpu.VMEM(neighbours.shape, jnp.int32),
            pltpu.VMEM((1, width), jnp.bfloat16),
            pltpu.VMEM((width, width), jnp.bfloat16),
            pltpu.SemaphoreType.DMA((5,)),
        ],
        compiler_params=pltpu.CompilerParams(vmem_limit_bytes=PACK_VMEM),
        name="pack_tile",
    )(timesteps, *[in_hbm(array) for array in (features, cotangent, neighbours, condition, w_time)])
    here = lax.axis_index("brick").astype(jnp.int32).reshape(1)

    def across(block):
        return lax.ppermute(block, "brick", [(i, i ^ 1) for i in range(peers)])

    def along(block, turn):
        return lax.ppermute(block, "brick", [(i, (i + turn * tiles_y) % peers) for i in range(peers)])

    w_conv, packed = lax.optimization_barrier((w_conv, packed))
    w_forward, w_back = pl.pallas_call(
        turn_kernel,
        out_shape=(jax.ShapeDtypeStruct((width, 27 * width), jnp.bfloat16),) * 2,
        in_specs=[vmem],
        out_specs=(vmem, vmem),
        compiler_params=params,
        cost_estimate=pl.CostEstimate(flops=2 * 10**8, bytes_accessed=3 * 10**6, transcendentals=0),
        name="turn_weights",
    )(w_conv)
    before, after = along(packed, 1), along(packed, -1)
    before, w_forward = lax.optimization_barrier((before, w_forward))
    far = along(before, 1)
    own_pair = (packed, across(packed))
    own_conv, own_grad = pl.pallas_call(
        own_kernel,
        out_shape=(jax.ShapeDtypeStruct((width, rows), jnp.float32),) * 2,
        in_specs=[smem] + [vmem] * 5,
        out_specs=(vmem, vmem),
        scratch_shapes=[
            pltpu.VMEM((TILE * span, 2 * width), jnp.bfloat16),
            pltpu.VMEM((2 * width, (TILE + 2) * span), jnp.bfloat16),
            pltpu.VMEM((27, rows), jnp.float32),
            pltpu.VMEM((27 * width, rows), jnp.bfloat16),
            pltpu.VMEM((27 * width, rows), jnp.bfloat16),
        ],
        compiler_params=params,
        cost_estimate=pl.CostEstimate(flops=2 * 10**9, bytes_accessed=4 * 10**6, transcendentals=0),
        name="voxels_own_row",
    )(here, *own_pair, code, w_forward, w_back)
    far, own_conv = lax.optimization_barrier((far, own_conv))
    before_pair = (before, across(before))
    far_pair = (far, across(far))
    def row_sums(name, pairs, strips, borders, sums, groups=(0, 1), final=0, keep=False, laid=()):
        blocks = [block for pair in pairs for block in pair]
        if final:
            out_shape = (
                jax.ShapeDtypeStruct((final, width, width), jnp.float32),
                jax.ShapeDtypeStruct((final, width, width), jnp.bfloat16),
            )
        else:
            out_shape = (
                jax.ShapeDtypeStruct((HALF * width, width), jnp.float32),
                jax.ShapeDtypeStruct((HALF * width, width), jnp.float32),
                jax.ShapeDtypeStruct((width, width), jnp.float32),
            )
        layout = (
            ((TILE + 2) * span, 2 * width, jnp.bfloat16),
            (2 * width, (TILE + 2) * span, jnp.bfloat16),
            (TILE + 1, CODE_ROWS, span, jnp.float32),
        )
        scratch = [] if laid or keep else [pltpu.VMEM(tuple(shape), kind) for *shape, kind in layout]
        if keep:
            out_shape += tuple(jax.ShapeDtypeStruct(tuple(shape), kind) for *shape, kind in layout)
        operands = (*blocks, *laid, *sums)
        return pl.pallas_call(
            functools.partial(row_kernel, not sums, bool(final), groups, bool(laid), strips, borders),
            out_shape=out_shape,
            in_specs=[smem] + [vmem] * len(operands),
            out_specs=(vmem,) * len(out_shape),
            scratch_shapes=scratch + [
                pltpu.VMEM((HALF * width, (TILE + 1) * span), jnp.bfloat16),
                pltpu.VMEM((HALF * width, (TILE + 1) * span), jnp.bfloat16),
            ],
            compiler_params=params,
            cost_estimate=pl.CostEstimate(flops=2 * 10**9, bytes_accessed=4 * 10**6, transcendentals=0),
            name=name,
        )(here, *operands)

    def swapped(block):
        return lax.ppermute(block, "batch", [(0, 1), (1, 0)])

    line = [(0, u) for u in range(TILE)]
    sums = row_sums("weight_row_0", (own_pair,), line, [], ())
    after, centre = lax.optimization_barrier((after, sums[2]))
    sums = (sums[0], sums[1], centre)
    after_pair = (after, across(after))
    sums = row_sums("weight_row_1", (before_pair, own_pair), line + [(1, 0)], [(TILE, TILE - 1)], sums)
    sums = row_sums("weight_row_2", (after_pair, own_pair), line + [(1, TILE - 1)], [(0, TILE)], sums)
    sides, sides_sent, *laid = row_sums("weight_row_3", (far_pair, before_pair, after_pair),
                                 line + [(1, 0), (2, TILE - 1)], [(TILE, TILE - 1), (0, TILE + 1)],
                                 sums, groups=(0,), final=18, keep=True)
    sides_other = swapped(sides_sent)
    centre, sides = lax.optimization_barrier((sums[2], sides))
    middle, middle_sent = row_sums("weight_row_3_middle", (), line, [], (sums[0], sums[1], centre),
                                   groups=(1,), final=9, laid=laid)
    middle_other = swapped(middle_sent)
    conv_out, feature_grad = pl.pallas_call(
        edge_kernel,
        out_shape=(jax.ShapeDtypeStruct((rows, width), jnp.bfloat16),) * 2,
        in_specs=[smem] + [vmem] * 10,
        out_specs=(vmem, vmem),
        scratch_shapes=[
            pltpu.VMEM((2 * span, 2 * width), jnp.bfloat16),
            pltpu.VMEM((2 * width, 2 * span), jnp.bfloat16),
            pltpu.VMEM((2, 9 * width, span), jnp.bfloat16),
        ],
        compiler_params=params,
        cost_estimate=pl.CostEstimate(flops=10**9, bytes_accessed=4 * 10**6, transcendentals=0),
        name="voxel_edges",
    )(here, *before_pair, *after_pair, code, w_forward, w_back, own_conv, own_grad, z_val)
    hbm = pl.BlockSpec(memory_space=pltpu.HBM)
    weight_grad, conv_out, feature_grad = pl.pallas_call(
        finish_kernel,
        out_shape=(
            jax.ShapeDtypeStruct((27, width, width), jnp.float32),
            jax.ShapeDtypeStruct((rows, width), jnp.bfloat16),
            jax.ShapeDtypeStruct((rows, width), jnp.bfloat16),
        ),
        in_specs=[vmem] * 6,
        out_specs=(hbm, hbm, hbm),
        scratch_shapes=[
            pltpu.VMEM((27, width, width), jnp.float32),
            pltpu.SemaphoreType.DMA((27 // FINISH_STEP + 2,)),
        ],
        compiler_params=pltpu.CompilerParams(vmem_limit_bytes=PACK_VMEM),
        name="finish",
    )(sides, sides_other, middle, middle_other, conv_out, feature_grad)
    return (conv_out[None], feature_grad[None], weight_grad)


def passed_along(block, axis, distance):
    devices = range(lax.axis_size(axis))
    route = [(i - distance, i) for i in devices if i - distance in devices]
    return lax.ppermute(block, axis, route)


def slab_rows(block, side_recv, front_recv, width):
    widened = jnp.concatenate([side_recv[0], block, side_recv[1]], axis=1)
    slab = jnp.concatenate([front_recv[0][None], widened, front_recv[1][None]], axis=0)
    flat = slab.reshape(-1, width)
    return jnp.concatenate([flat, jnp.zeros((1, width), jnp.bfloat16)], axis=0)


def with_halo(block, tiles_y):
    width = block.shape[-1]
    side = TILE
    side_recv = tuple(passed_along(block[:, edge], "brick", by)[:, None] for by, edge in ((1, side - 1), (-1, 0)))
    wide = jnp.concatenate([side_recv[0], block, side_recv[1]], axis=1)
    front_recv = tuple(passed_along(wide[edge], "brick", by) for by, edge in ((tiles_y, side - 1), (-tiles_y, 0)))
    return slab_rows(block, side_recv, front_recv, width)


def halo_plan(features, cotangent, neighbours, timesteps, condition, w_time, w_conv, tiles_x, tiles_y):
    rows_here, width = features.shape[1:]
    here = lax.axis_index("brick")
    tile_x = here // tiles_y
    tile_y = here % tiles_y
    side = TILE
    layers = LAYERS
    wide = side + 2
    valid = neighbours >= 0
    safe = jnp.where(valid, neighbours, 0)
    owner = safe // rows_here
    inside = safe % rows_here
    column = inside // layers
    layer = inside % layers
    local_x = (owner // tiles_y - tile_x) * side + column // side + 1
    local_y = (owner % tiles_y - tile_y) * side + column % side + 1
    sentinel = wide * wide * layers
    ext_index = jnp.where(valid, (local_x * wide + local_y) * layers + layer, sentinel).T
    temb = time_embedding(timesteps, width)
    shift = jnp.dot(temb, w_time, preferred_element_type=jnp.float32) + condition.astype(jnp.float32)
    z_val = features[0].astype(jnp.float32) + shift[0][None, :]
    act = jax.nn.silu(z_val).astype(jnp.bfloat16)
    cot = cotangent[0]
    w_forward = w_conv.reshape(27 * width, width)
    w_backward = jnp.transpose(w_conv[::-1], (0, 2, 1)).reshape(27 * width, width)
    act_ext = with_halo(act.reshape(side, side, layers, width), tiles_y)
    gathered = act_ext[ext_index].reshape(rows_here, 27 * width)
    conv_out = jnp.dot(gathered, w_forward, preferred_element_type=jnp.float32).astype(jnp.bfloat16)
    partial_grad = lax.dot_general(
        gathered, cot, (((0,), (0,)), ((), ())), preferred_element_type=jnp.float32
    )
    both = ("brick", "batch")
    parts = tiles_x * tiles_y * lax.axis_size("batch")
    rows = 27 * width
    extra = -rows % (8 * parts)
    pieces = jnp.pad(partial_grad.astype(jnp.bfloat16), ((0, extra), (0, 0))).reshape(parts, -1, width)
    arrived = lax.all_to_all(pieces, both, 0, 0)
    summed = arrived.astype(jnp.float32).sum(0).astype(jnp.bfloat16)
    whole = lax.all_gather(summed, both, axis=0, tiled=True)
    weight_grad = whole[:rows].astype(jnp.float32).reshape(27, width, width)
    cot_ext = with_halo(cot.reshape(side, side, layers, width), tiles_y)
    cot_gathered = cot_ext[ext_index].reshape(rows_here, 27 * width)
    back = jnp.dot(cot_gathered, w_backward, preferred_element_type=jnp.float32)
    sig = jax.nn.sigmoid(z_val)
    feature_grad = (back * sig * (1.0 + z_val * (1.0 - sig))).astype(jnp.bfloat16)
    return (conv_out[None], feature_grad[None], weight_grad)


def shards(*arrays):
    peers = lax.axis_size("brick")
    bits = peers.bit_length() - 1
    tiles_x = 2 ** ((bits + 1) // 2)
    tiles_y = 2 ** (bits // 2)
    plan = whole_scene if (tiles_x, tiles_y) == (ROW_STAGES, 2) else halo_plan
    return plan(*arrays, tiles_x, tiles_y)


def solution(mesh):
    in_specs = (
        P(("groups", "batch"), "brick", None),
        P(("groups", "batch"), "brick", None),
        P(None, ("groups", "brick")),
        P(("groups", "batch")),
        P(("groups", "batch"), None),
        P(),
        P(),
    )
    out_specs = (
        P(("groups", "batch"), "brick", None),
        P(("groups", "batch"), "brick", None),
        P("groups", None, None),
    )
    return jax.shard_map(shards, mesh=mesh, in_specs=in_specs, out_specs=out_specs, check_vma=False)
```

```python
import functools

import jax
import jax.numpy as jnp
from jax import lax
from jax.experimental import pallas as pl
from jax.experimental.pallas import tpu as pltpu
from jax.sharding import PartitionSpec as P

LAYERS = 16
TILE = 4
STRIP = TILE * LAYERS
HALF = 13
CODE_ROWS = 16
ROW_STAGES = 4
FINISH_STEP = 3
PACK_VMEM = 8 * 1024 * 1024
KERNEL_VMEM = 24 * 1024 * 1024


def time_embedding(timesteps, width):
    half = width // 2
    freq = jnp.exp(-jnp.log(10000.0) * jnp.arange(half, dtype=jnp.float32) / half)
    angle = timesteps.astype(jnp.float32)[:, None] * freq[None, :]
    return jnp.concatenate([jnp.sin(angle), jnp.cos(angle)], axis=1).astype(jnp.bfloat16)


def strip_codes(neighbours, tiles_y):
    rows_here = TILE * STRIP
    code = (neighbours // rows_here) % tiles_y * STRIP + neighbours % STRIP
    return jnp.where(neighbours < 0, -1, code).astype(jnp.float32)


def in_hbm(array):
    return pltpu.with_memory_space_constraint(array, pltpu.HBM)


def pack_kernel(time_ref, feat_hbm, cot_hbm, near_hbm, cond_hbm, wt_hbm, pack_ref, z_ref, code_ref,
                feat_ref, near_ref, cond_ref, wt_ref, sems):
    rows, width = feat_ref.shape
    half = width // 2
    moves = (
        (wt_hbm, wt_ref),
        (cond_hbm, cond_ref),
        (feat_hbm.at[0], feat_ref),
        (near_hbm, near_ref),
        (cot_hbm.at[0], pack_ref.at[:rows, width:]),
    )
    copies = [pltpu.make_async_copy(source, to, sems.at[i]) for i, (source, to) in enumerate(moves)]
    for copy in copies:
        copy.start()
    lane = lax.broadcasted_iota(jnp.int32, (1, width), 1)
    freq = jnp.exp(-jnp.log(10000.0) * (lane % half).astype(jnp.float32) / half)
    angle = time_ref[0].astype(jnp.float32) * freq
    temb = jnp.where(lane < half, jnp.sin(angle), jnp.cos(angle)).astype(jnp.bfloat16)
    copies[0].wait()
    copies[1].wait()
    shift = jnp.dot(temb, wt_ref[...], preferred_element_type=jnp.float32)
    shift = shift + cond_ref[...].astype(jnp.float32)
    copies[2].wait()
    z_val = feat_ref[...].astype(jnp.float32) + shift
    z_ref[...] = z_val
    pack_ref[:rows, :width] = (z_val * jax.nn.sigmoid(z_val)).astype(jnp.bfloat16)
    copies[3].wait()
    code = strip_codes(near_ref[...], 2)
    code_ref[...] = code
    pack_ref[rows:, :] = code[:CODE_ROWS, :].astype(jnp.bfloat16)
    copies[4].wait()


def lay_strip(ground, to, tile_y, mine_ref, other_ref, u):
    span = 2 * STRIP
    for ref, place in ((mine_ref, tile_y), (other_ref, 1 - tile_y)):
        at = pl.multiple_of(to * span + place * STRIP, STRIP)
        ground[pl.ds(at, STRIP), :] = ref[u * STRIP:(u + 1) * STRIP, :]


def look_up(window, picks, places):
    ref, first, lanes = window
    width = ref.shape[0] // 2
    for i in range(0, len(picks), 2):
        pair = picks[i:i + 2]
        pick = jnp.concatenate(pair, axis=1) if len(pair) == 2 else pair[0]
        span = pair[0].shape[1]
        for side in range(2):
            near = jnp.dot(ref[side * width:(side + 1) * width, first:first + lanes], pick,
                           preferred_element_type=jnp.float32).astype(jnp.bfloat16)
            for j, (to, row, lane) in enumerate(places[i:i + 2]):
                to[side][row:row + width, lane:lane + span] = near[:, j * span:(j + 1) * span]


def row_kernel(first_stage, final, groups, laid, strips, borders, *refs):
    refs = list(refs)
    where_ref = refs.pop(0)
    pairs = [] if laid else [(refs.pop(0), refs.pop(0)) for _ in range(1 + max(pair for pair, _ in strips))]
    given = [refs.pop(0) for _ in range(3)] if laid else []
    before = [refs.pop(0) for _ in range(0 if first_stage else 3)]
    outs = [refs.pop(0) for _ in range(2 if final else 3)]
    ground, turned, codes = given or [refs.pop(0) for _ in range(3)]
    near_act, near_cot = refs
    width = ground.shape[1] // 2
    rows = TILE * STRIP
    span = 2 * STRIP
    tile_y = where_ref[0] % 2
    borders = [(u, u - 1) for u in range(1, TILE)] + borders
    targets = sorted({target for target, _ in borders})
    for i, (pair, u) in enumerate([] if laid else strips):
        lay_strip(ground, i, tile_y, *pairs[pair], u)
        if i < TILE or i in targets:
            both = [ref[rows:, u * STRIP:(u + 1) * STRIP].astype(jnp.float32) for ref in pairs[pair]]
            first = jnp.where(tile_y == 0, both[0], both[1])
            second = jnp.where(tile_y == 0, both[1], both[0])
            codes[i] = jnp.concatenate([first, second], axis=1)
        if i < TILE or i in [source for _, source in borders]:
            turned[:, i * span:(i + 1) * span] = ground[i * span:(i + 1) * span, :].T
    place = lax.broadcasted_iota(jnp.int32, (span, span), 0).astype(jnp.float32)

    to = (near_act, near_cot)
    for source in range(TILE + 2):
        found = [(source, k) for k in range(9, HALF)] if 1 in groups and source < TILE else []
        if 0 in groups:
            found += [(target, k) for target, origin in borders if origin == source for k in range(9)]
        if found:
            picks = [(place == codes[target, k:k + 1, :]).astype(jnp.bfloat16) for target, k in found]
            look_up((turned, source * span, span), picks, [(to, k * width, target * span) for target, k in found])
    extents = ((0, 9, span * targets[0], span * (targets[-1] + 1)), (9, HALF, 0, TILE * span))
    for turn, near in ((0, near_act), (1, near_cot)):
        for group in groups:
            start, stop, first, last = extents[group]
            other = ground[first:last, (1 - turn) * width:(2 - turn) * width]
            value = jnp.dot(near[start * width:stop * width, first:last], other, preferred_element_type=jnp.float32)
            if not first_stage:
                value = value + before[turn][start * width:stop * width, :]
            if not final:
                outs[turn][start * width:stop * width, :] = value
                continue
            for k in range(start, stop):
                one = value[(k - start) * width:(k - start + 1) * width, :]
                to = 2 * HALF - k if turn else k
                if turn:
                    one = one.T
                to = to - 9 if group == 1 else to - 9 * turn
                outs[0][to] = one
                outs[1][to] = one.astype(jnp.bfloat16)
    if 1 in groups:
        centre = jnp.dot(turned[:width, :TILE * span], ground[:TILE * span, width:], preferred_element_type=jnp.float32)
        if not first_stage:
            centre = centre + before[2][...]
        if final:
            outs[0][HALF - 9] = centre
            outs[1][HALF - 9] = centre.astype(jnp.bfloat16)
        else:
            outs[2][...] = centre


def turn_kernel(w_ref, forward_ref, back_ref):
    width = w_ref.shape[1]
    for k in range(27):
        forward_ref[:, k * width:(k + 1) * width] = w_ref[k].T
        back_ref[:, k * width:(k + 1) * width] = w_ref[26 - k]


def own_kernel(where_ref, mine_ref, other_ref, code_ref, forward_ref, back_ref, conv_ref, grad_ref,
               ground, turned, codes, near_act, near_cot):
    width = conv_ref.shape[0]
    span = 2 * STRIP
    tile_y = where_ref[0] % 2
    for u in range(TILE):
        lay_strip(ground, u, tile_y, mine_ref, other_ref, u)
        turned[:, (u + 1) * span:(u + 2) * span] = ground[u * span:(u + 1) * span, :].T
    for i in (0, TILE + 1):
        turned[:, i * span:(i + 1) * span] = jnp.zeros((2 * width, span), jnp.bfloat16)
    code = code_ref[...]
    lane = lax.broadcasted_iota(jnp.int32, code.shape, 1)
    codes[...] = jnp.where((code >= 0) & (lane // STRIP % 2 == 1), code + span, code)
    place = lax.broadcasted_iota(jnp.int32, (2 * span, span), 0).astype(jnp.float32)
    for half in range(TILE // 2):
        at = half * span
        for side in range(3):
            source = (2 * half + side) * span
            ks = range(9 * side, 9 * side + 9)
            picks = [(place == codes[k:k + 1, at:at + span]).astype(jnp.bfloat16) for k in ks]
            look_up((turned, source, 2 * span), picks, [((near_act, near_cot), k * width, at) for k in ks])
    conv_ref[...] = jnp.dot(forward_ref[...], near_act[...], preferred_element_type=jnp.float32)
    grad_ref[...] = jnp.dot(back_ref[...], near_cot[...], preferred_element_type=jnp.float32)


def edge_kernel(where_ref, before_mine, before_other, after_mine, after_other, code_ref, forward_ref, back_ref,
                own_conv, own_grad, z_ref, conv_ref, grad_ref, ground, turned, near):
    width = z_ref.shape[1]
    span = 2 * STRIP
    tile_y = where_ref[0] % 2
    lay_strip(ground, 0, tile_y, before_mine, before_other, TILE - 1)
    lay_strip(ground, 1, tile_y, after_mine, after_other, 0)
    for i in range(2):
        turned[:, i * span:(i + 1) * span] = ground[i * span:(i + 1) * span, :].T
    first = code_ref[:9, :span]
    last = code_ref[18:, span:]
    lane = lax.broadcasted_iota(jnp.int32, first.shape, 1)
    code = jnp.where(lane < STRIP, first, jnp.where(last >= 0, last + span, last))
    place = lax.broadcasted_iota(jnp.int32, (2 * span, span), 0).astype(jnp.float32)
    picks = [(place == code[k:k + 1, :]).astype(jnp.bfloat16) for k in range(9)]
    look_up((turned, 0, 2 * span), picks, [((near.at[0], near.at[1]), k * width, 0) for k in range(9)])
    lane = lax.broadcasted_iota(jnp.int32, (width, span), 1)

    def total(own_ref, weights, side):
        low = jnp.dot(weights[:, :9 * width], near[side], preferred_element_type=jnp.float32)
        high = jnp.dot(weights[:, 18 * width:], near[side], preferred_element_type=jnp.float32)
        low = own_ref[:, :span] + jnp.where(lane < STRIP, low, 0.0)
        high = own_ref[:, span:] + jnp.where(lane < STRIP, 0.0, high)
        return jnp.concatenate([low, high], axis=1).T

    conv_ref[...] = total(own_conv, forward_ref, 0).astype(jnp.bfloat16)
    back = total(own_grad, back_ref, 1)
    z_val = z_ref[...]
    sig = jax.nn.sigmoid(z_val)
    grad_ref[...] = (back * sig * (1.0 + z_val * (1.0 - sig))).astype(jnp.bfloat16)


def finish_kernel(sides_ref, sides_sent, middle_ref, middle_sent, conv_ref, grad_ref,
                  weight_hbm, conv_hbm, grad_hbm, weight, sems):
    steps = 27 // FINISH_STEP
    copies = [
        pltpu.make_async_copy(conv_ref, conv_hbm, sems.at[steps]),
        pltpu.make_async_copy(grad_ref, grad_hbm, sems.at[steps + 1]),
    ]
    for copy in copies:
        copy.start()
    for i in range(steps):
        first = i * FINISH_STEP
        kept, sent, at = (middle_ref, middle_sent, first - 9) if first // 9 == 1 else (
            sides_ref, sides_sent, first if first < 9 else first - 9)
        part, taken = pl.ds(first, FINISH_STEP), pl.ds(at, FINISH_STEP)
        weight[part] = kept[taken] + sent[taken].astype(jnp.float32)
        copies.append(pltpu.make_async_copy(weight.at[part], weight_hbm.at[part], sems.at[i]))
        copies[-1].start()
    for copy in copies:
        copy.wait()


def whole_scene(features, cotangent, neighbours, timesteps, condition, w_time, w_conv, tiles_x, tiles_y):
    rows, width = features.shape[1:]
    peers = tiles_x * tiles_y
    span = 2 * STRIP
    vmem = pl.BlockSpec(memory_space=pltpu.VMEM)
    smem = pl.BlockSpec(memory_space=pltpu.SMEM)
    params = pltpu.CompilerParams(vmem_limit_bytes=KERNEL_VMEM)
    packed, z_val, code = pl.pallas_call(
        pack_kernel,
        out_shape=(
            jax.ShapeDtypeStruct((rows + CODE_ROWS, 2 * width), jnp.bfloat16),
            jax.ShapeDtypeStruct((rows, width), jnp.float32),
            jax.ShapeDtypeStruct(neighbours.shape, jnp.float32),
        ),
        in_specs=[smem] + [pl.BlockSpec(memory_space=pltpu.HBM)] * 5,
        out_specs=(vmem, vmem, vmem),
        scratch_shapes=[
            pltpu.VMEM((rows, width), jnp.bfloat16),
            pltpu.VMEM(neighbours.shape, jnp.int32),
            pltpu.VMEM((1, width), jnp.bfloat16),
            pltpu.VMEM((width, width), jnp.bfloat16),
            pltpu.SemaphoreType.DMA((5,)),
        ],
        compiler_params=pltpu.CompilerParams(vmem_limit_bytes=PACK_VMEM),
        name="pack_tile",
    )(timesteps, *[in_hbm(array) for array in (features, cotangent, neighbours, condition, w_time)])
    here = lax.axis_index("brick").astype(jnp.int32).reshape(1)

    def across(block):
        return lax.ppermute(block, "brick", [(i, i ^ 1) for i in range(peers)])

    def along(block, turn):
        return lax.ppermute(block, "brick", [(i, (i + turn * tiles_y) % peers) for i in range(peers)])

    w_conv, packed = lax.optimization_barrier((w_conv, packed))
    w_forward, w_back = pl.pallas_call(
        turn_kernel,
        out_shape=(jax.ShapeDtypeStruct((width, 27 * width), jnp.bfloat16),) * 2,
        in_specs=[vmem],
        out_specs=(vmem, vmem),
        compiler_params=params,
        cost_estimate=pl.CostEstimate(flops=2 * 10**8, bytes_accessed=3 * 10**6, transcendentals=0),
        name="turn_weights",
    )(w_conv)
    before = along(packed, 1)
    w_back, later = lax.optimization_barrier((w_back, packed))
    after = along(later, -1)
    before, w_forward = lax.optimization_barrier((before, w_forward))
    far = along(before, 1)
    own_pair = (packed, across(packed))
    own_conv, own_grad = pl.pallas_call(
        own_kernel,
        out_shape=(jax.ShapeDtypeStruct((width, rows), jnp.float32),) * 2,
        in_specs=[smem] + [vmem] * 5,
        out_specs=(vmem, vmem),
        scratch_shapes=[
            pltpu.VMEM((TILE * span, 2 * width), jnp.bfloat16),
            pltpu.VMEM((2 * width, (TILE + 2) * span), jnp.bfloat16),
            pltpu.VMEM((27, rows), jnp.float32),
            pltpu.VMEM((27 * width, rows), jnp.bfloat16),
            pltpu.VMEM((27 * width, rows), jnp.bfloat16),
        ],
        compiler_params=params,
        cost_estimate=pl.CostEstimate(flops=2 * 10**9, bytes_accessed=4 * 10**6, transcendentals=0),
        name="voxels_own_row",
    )(here, *own_pair, code, w_forward, w_back)
    far, own_conv = lax.optimization_barrier((far, own_conv))
    before_pair = (before, across(before))
    far_pair = (far, across(far))
    def row_sums(name, pairs, strips, borders, sums, groups=(0, 1), final=0, keep=False, laid=()):
        blocks = [block for pair in pairs for block in pair]
        if final:
            out_shape = (
                jax.ShapeDtypeStruct((final, width, width), jnp.float32),
                jax.ShapeDtypeStruct((final, width, width), jnp.bfloat16),
            )
        else:
            out_shape = (
                jax.ShapeDtypeStruct((HALF * width, width), jnp.float32),
                jax.ShapeDtypeStruct((HALF * width, width), jnp.float32),
                jax.ShapeDtypeStruct((width, width), jnp.float32),
            )
        layout = (
            ((TILE + 2) * span, 2 * width, jnp.bfloat16),
            (2 * width, (TILE + 2) * span, jnp.bfloat16),
            (TILE + 1, CODE_ROWS, span, jnp.float32),
        )
        scratch = [] if laid or keep else [pltpu.VMEM(tuple(shape), kind) for *shape, kind in layout]
        if keep:
            out_shape += tuple(jax.ShapeDtypeStruct(tuple(shape), kind) for *shape, kind in layout)
        operands = (*blocks, *laid, *sums)
        return pl.pallas_call(
            functools.partial(row_kernel, not sums, bool(final), groups, bool(laid), strips, borders),
            out_shape=out_shape,
            in_specs=[smem] + [vmem] * len(operands),
            out_specs=(vmem,) * len(out_shape),
            scratch_shapes=scratch + [
                pltpu.VMEM((HALF * width, (TILE + 1) * span), jnp.bfloat16),
                pltpu.VMEM((HALF * width, (TILE + 1) * span), jnp.bfloat16),
            ],
            compiler_params=params,
            cost_estimate=pl.CostEstimate(flops=2 * 10**9, bytes_accessed=4 * 10**6, transcendentals=0),
            name=name,
        )(here, *operands)

    def swapped(block):
        return lax.ppermute(block, "batch", [(0, 1), (1, 0)])

    line = [(0, u) for u in range(TILE)]
    sums = row_sums("weight_row_0", (own_pair,), line, [], ())
    after, centre = lax.optimization_barrier((after, sums[2]))
    sums = (sums[0], sums[1], centre)
    after_pair = (after, across(after))
    sums = row_sums("weight_row_1", (before_pair, own_pair), line + [(1, 0)], [(TILE, TILE - 1)], sums)
    sums = row_sums("weight_row_2", (after_pair, own_pair), line + [(1, TILE - 1)], [(0, TILE)], sums)
    sides, sides_sent, *laid = row_sums("weight_row_3", (far_pair, before_pair, after_pair),
                                 line + [(1, 0), (2, TILE - 1)], [(TILE, TILE - 1), (0, TILE + 1)],
                                 sums, groups=(0,), final=18, keep=True)
    sides_other = swapped(sides_sent)
    centre, sides = lax.optimization_barrier((sums[2], sides))
    middle, middle_sent = row_sums("weight_row_3_middle", (), line, [], (sums[0], sums[1], centre),
                                   groups=(1,), final=9, laid=laid)
    middle_other = swapped(middle_sent)
    conv_out, feature_grad = pl.pallas_call(
        edge_kernel,
        out_shape=(jax.ShapeDtypeStruct((rows, width), jnp.bfloat16),) * 2,
        in_specs=[smem] + [vmem] * 10,
        out_specs=(vmem, vmem),
        scratch_shapes=[
            pltpu.VMEM((2 * span, 2 * width), jnp.bfloat16),
            pltpu.VMEM((2 * width, 2 * span), jnp.bfloat16),
            pltpu.VMEM((2, 9 * width, span), jnp.bfloat16),
        ],
        compiler_params=params,
        cost_estimate=pl.CostEstimate(flops=10**9, bytes_accessed=4 * 10**6, transcendentals=0),
        name="voxel_edges",
    )(here, *before_pair, *after_pair, code, w_forward, w_back, own_conv, own_grad, z_val)
    hbm = pl.BlockSpec(memory_space=pltpu.HBM)
    weight_grad, conv_out, feature_grad = pl.pallas_call(
        finish_kernel,
        out_shape=(
            jax.ShapeDtypeStruct((27, width, width), jnp.float32),
            jax.ShapeDtypeStruct((rows, width), jnp.bfloat16),
            jax.ShapeDtypeStruct((rows, width), jnp.bfloat16),
        ),
        in_specs=[vmem] * 6,
        out_specs=(hbm, hbm, hbm),
        scratch_shapes=[
            pltpu.VMEM((27, width, width), jnp.float32),
            pltpu.SemaphoreType.DMA((27 // FINISH_STEP + 2,)),
        ],
        compiler_params=pltpu.CompilerParams(vmem_limit_bytes=PACK_VMEM),
        name="finish",
    )(sides, sides_other, middle, middle_other, conv_out, feature_grad)
    return (conv_out[None], feature_grad[None], weight_grad)


def passed_along(block, axis, distance):
    devices = range(lax.axis_size(axis))
    route = [(i - distance, i) for i in devices if i - distance in devices]
    return lax.ppermute(block, axis, route)


def slab_rows(block, side_recv, front_recv, width):
    widened = jnp.concatenate([side_recv[0], block, side_recv[1]], axis=1)
    slab = jnp.concatenate([front_recv[0][None], widened, front_recv[1][None]], axis=0)
    flat = slab.reshape(-1, width)
    return jnp.concatenate([flat, jnp.zeros((1, width), jnp.bfloat16)], axis=0)


def with_halo(block, tiles_y):
    width = block.shape[-1]
    side = TILE
    side_recv = tuple(passed_along(block[:, edge], "brick", by)[:, None] for by, edge in ((1, side - 1), (-1, 0)))
    wide = jnp.concatenate([side_recv[0], block, side_recv[1]], axis=1)
    front_recv = tuple(passed_along(wide[edge], "brick", by) for by, edge in ((tiles_y, side - 1), (-tiles_y, 0)))
    return slab_rows(block, side_recv, front_recv, width)


def halo_plan(features, cotangent, neighbours, timesteps, condition, w_time, w_conv, tiles_x, tiles_y):
    rows_here, width = features.shape[1:]
    here = lax.axis_index("brick")
    tile_x = here // tiles_y
    tile_y = here % tiles_y
    side = TILE
    layers = LAYERS
    wide = side + 2
    valid = neighbours >= 0
    safe = jnp.where(valid, neighbours, 0)
    owner = safe // rows_here
    inside = safe % rows_here
    column = inside // layers
    layer = inside % layers
    local_x = (owner // tiles_y - tile_x) * side + column // side + 1
    local_y = (owner % tiles_y - tile_y) * side + column % side + 1
    sentinel = wide * wide * layers
    ext_index = jnp.where(valid, (local_x * wide + local_y) * layers + layer, sentinel).T
    temb = time_embedding(timesteps, width)
    shift = jnp.dot(temb, w_time, preferred_element_type=jnp.float32) + condition.astype(jnp.float32)
    z_val = features[0].astype(jnp.float32) + shift[0][None, :]
    act = jax.nn.silu(z_val).astype(jnp.bfloat16)
    cot = cotangent[0]
    w_forward = w_conv.reshape(27 * width, width)
    w_backward = jnp.transpose(w_conv[::-1], (0, 2, 1)).reshape(27 * width, width)
    act_ext = with_halo(act.reshape(side, side, layers, width), tiles_y)
    gathered = act_ext[ext_index].reshape(rows_here, 27 * width)
    conv_out = jnp.dot(gathered, w_forward, preferred_element_type=jnp.float32).astype(jnp.bfloat16)
    partial_grad = lax.dot_general(
        gathered, cot, (((0,), (0,)), ((), ())), preferred_element_type=jnp.float32
    )
    both = ("brick", "batch")
    parts = tiles_x * tiles_y * lax.axis_size("batch")
    rows = 27 * width
    extra = -rows % (8 * parts)
    pieces = jnp.pad(partial_grad.astype(jnp.bfloat16), ((0, extra), (0, 0))).reshape(parts, -1, width)
    arrived = lax.all_to_all(pieces, both, 0, 0)
    summed = arrived.astype(jnp.float32).sum(0).astype(jnp.bfloat16)
    whole = lax.all_gather(summed, both, axis=0, tiled=True)
    weight_grad = whole[:rows].astype(jnp.float32).reshape(27, width, width)
    cot_ext = with_halo(cot.reshape(side, side, layers, width), tiles_y)
    cot_gathered = cot_ext[ext_index].reshape(rows_here, 27 * width)
    back = jnp.dot(cot_gathered, w_backward, preferred_element_type=jnp.float32)
    sig = jax.nn.sigmoid(z_val)
    feature_grad = (back * sig * (1.0 + z_val * (1.0 - sig))).astype(jnp.bfloat16)
    return (conv_out[None], feature_grad[None], weight_grad)


def shards(*arrays):
    peers = lax.axis_size("brick")
    bits = peers.bit_length() - 1
    tiles_x = 2 ** ((bits + 1) // 2)
    tiles_y = 2 ** (bits // 2)
    plan = whole_scene if (tiles_x, tiles_y) == (ROW_STAGES, 2) else halo_plan
    return plan(*arrays, tiles_x, tiles_y)


def solution(mesh):
    in_specs = (
        P(("groups", "batch"), "brick", None),
        P(("groups", "batch"), "brick", None),
        P(None, ("groups", "brick")),
        P(("groups", "batch")),
        P(("groups", "batch"), None),
        P(),
        P(),
    )
    out_specs = (
        P(("groups", "batch"), "brick", None),
        P(("groups", "batch"), "brick", None),
        P("groups", None, None),
    )
    return jax.shard_map(shards, mesh=mesh, in_specs=in_specs, out_specs=out_specs, check_vma=False)
```

```python
import functools

import jax
import jax.numpy as jnp
from jax import lax
from jax.experimental import pallas as pl
from jax.experimental.pallas import tpu as pltpu
from jax.sharding import PartitionSpec as P

LAYERS = 16
TILE = 4
STRIP = TILE * LAYERS
HALF = 13
CODE_ROWS = 16
ROW_STAGES = 4
FINISH_STEP = 3
PACK_VMEM = 8 * 1024 * 1024
KERNEL_VMEM = 24 * 1024 * 1024


def time_embedding(timesteps, width):
    half = width // 2
    freq = jnp.exp(-jnp.log(10000.0) * jnp.arange(half, dtype=jnp.float32) / half)
    angle = timesteps.astype(jnp.float32)[:, None] * freq[None, :]
    return jnp.concatenate([jnp.sin(angle), jnp.cos(angle)], axis=1).astype(jnp.bfloat16)


def strip_codes(neighbours, tiles_y):
    rows_here = TILE * STRIP
    code = (neighbours // rows_here) % tiles_y * STRIP + neighbours % STRIP
    return jnp.where(neighbours < 0, -1, code).astype(jnp.float32)


def in_hbm(array):
    return pltpu.with_memory_space_constraint(array, pltpu.HBM)


def pack_kernel(time_ref, feat_hbm, cot_hbm, near_hbm, cond_hbm, wt_hbm, pack_ref, z_ref, code_ref,
                feat_ref, near_ref, cond_ref, wt_ref, sems):
    rows, width = feat_ref.shape
    half = width // 2
    moves = (
        (wt_hbm, wt_ref),
        (cond_hbm, cond_ref),
        (feat_hbm.at[0], feat_ref),
        (near_hbm, near_ref),
        (cot_hbm.at[0], pack_ref.at[:rows, width:]),
    )
    copies = [pltpu.make_async_copy(source, to, sems.at[i]) for i, (source, to) in enumerate(moves)]
    for copy in copies:
        copy.start()
    lane = lax.broadcasted_iota(jnp.int32, (1, width), 1)
    freq = jnp.exp(-jnp.log(10000.0) * (lane % half).astype(jnp.float32) / half)
    angle = time_ref[0].astype(jnp.float32) * freq
    temb = jnp.where(lane < half, jnp.sin(angle), jnp.cos(angle)).astype(jnp.bfloat16)
    copies[0].wait()
    copies[1].wait()
    shift = jnp.dot(temb, wt_ref[...], preferred_element_type=jnp.float32)
    shift = shift + cond_ref[...].astype(jnp.float32)
    copies[2].wait()
    z_val = feat_ref[...].astype(jnp.float32) + shift
    z_ref[...] = z_val
    pack_ref[:rows, :width] = (z_val * jax.nn.sigmoid(z_val)).astype(jnp.bfloat16)
    copies[3].wait()
    code = strip_codes(near_ref[...], 2)
    code_ref[...] = code
    pack_ref[rows:, :] = code[:CODE_ROWS, :].astype(jnp.bfloat16)
    copies[4].wait()


def lay_strip(ground, to, tile_y, mine_ref, other_ref, u):
    span = 2 * STRIP
    for ref, place in ((mine_ref, tile_y), (other_ref, 1 - tile_y)):
        at = pl.multiple_of(to * span + place * STRIP, STRIP)
        ground[pl.ds(at, STRIP), :] = ref[u * STRIP:(u + 1) * STRIP, :]


def look_up(window, picks, places):
    ref, first, lanes = window
    width = ref.shape[0] // 2
    for i in range(0, len(picks), 2):
        pair = picks[i:i + 2]
        pick = jnp.concatenate(pair, axis=1) if len(pair) == 2 else pair[0]
        span = pair[0].shape[1]
        for side in range(2):
            near = jnp.dot(ref[side * width:(side + 1) * width, first:first + lanes], pick,
                           preferred_element_type=jnp.float32).astype(jnp.bfloat16)
            for j, (to, row, lane) in enumerate(places[i:i + 2]):
                to[side][row:row + width, lane:lane + span] = near[:, j * span:(j + 1) * span]


def row_kernel(first_stage, final, groups, laid, skip_target, strips, borders, *refs):
    refs = list(refs)
    where_ref = refs.pop(0)
    pairs = [] if laid else [(refs.pop(0), refs.pop(0)) for _ in range(1 + max(pair for pair, _ in strips))]
    given = [refs.pop(0) for _ in range(3)] if laid else []
    before = [refs.pop(0) for _ in range(0 if first_stage else 3)]
    outs = [refs.pop(0) for _ in range(2 if final else 3)]
    ground, turned, codes = given or [refs.pop(0) for _ in range(3)]
    near_act, near_cot = refs
    width = ground.shape[1] // 2
    rows = TILE * STRIP
    span = 2 * STRIP
    tile_y = where_ref[0] % 2
    borders = [(u, u - 1) for u in range(1, TILE)] + borders
    targets = sorted({target for target, _ in borders})
    for i, (pair, u) in enumerate([] if laid else strips):
        lay_strip(ground, i, tile_y, *pairs[pair], u)
        if i < TILE or i in targets:
            both = [ref[rows:, u * STRIP:(u + 1) * STRIP].astype(jnp.float32) for ref in pairs[pair]]
            first = jnp.where(tile_y == 0, both[0], both[1])
            second = jnp.where(tile_y == 0, both[1], both[0])
            codes[i] = jnp.concatenate([first, second], axis=1)
        if i < TILE or i in [source for _, source in borders]:
            turned[:, i * span:(i + 1) * span] = ground[i * span:(i + 1) * span, :].T
    place = lax.broadcasted_iota(jnp.int32, (span, span), 0).astype(jnp.float32)

    to = (near_act, near_cot)
    for source in range(TILE + 2):
        found = [(source, k) for k in range(9, HALF)] if 1 in groups and source < TILE else []
        if 0 in groups:
            found += [(target, k) for target, origin in borders if origin == source for k in range(9)]
        outer = [(target, k) for target, k in found if target == skip_target]
        found = [(target, k) for target, k in found if target != skip_target]
        if found:
            picks = [(place == codes[target, k:k + 1, :]).astype(jnp.bfloat16) for target, k in found]
            look_up((turned, source * span, span), picks, [(to, k * width, target * span) for target, k in found])
        if outer:
            first = skip_target * span

            @pl.when(where_ref[0] < 2)
            def _(first=first):
                for near in to:
                    near[:9 * width, first:first + span] = jnp.zeros((9 * width, span), jnp.bfloat16)

            @pl.when(where_ref[0] >= 2)
            def _(outer=outer, source=source):
                picks = [(place == codes[target, k:k + 1, :]).astype(jnp.bfloat16) for target, k in outer]
                look_up((turned, source * span, span), picks, [(to, k * width, target * span) for target, k in outer])
    extents = ((0, 9, span * targets[0], span * (targets[-1] + 1)), (9, HALF, 0, TILE * span))
    for turn, near in ((0, near_act), (1, near_cot)):
        for group in groups:
            start, stop, first, last = extents[group]
            other = ground[first:last, (1 - turn) * width:(2 - turn) * width]
            value = jnp.dot(near[start * width:stop * width, first:last], other, preferred_element_type=jnp.float32)
            if not first_stage:
                value = value + before[turn][start * width:stop * width, :]
            if not final:
                outs[turn][start * width:stop * width, :] = value
                continue
            for k in range(start, stop):
                one = value[(k - start) * width:(k - start + 1) * width, :]
                to = 2 * HALF - k if turn else k
                if turn:
                    one = one.T
                to = to - 9 if group == 1 else to - 9 * turn
                outs[0][to] = one
                outs[1][to] = one.astype(jnp.bfloat16)
    if 1 in groups:
        centre = jnp.dot(turned[:width, :TILE * span], ground[:TILE * span, width:], preferred_element_type=jnp.float32)
        if not first_stage:
            centre = centre + before[2][...]
        if final:
            outs[0][HALF - 9] = centre
            outs[1][HALF - 9] = centre.astype(jnp.bfloat16)
        else:
            outs[2][...] = centre


def turn_kernel(w_ref, forward_ref, back_ref):
    width = w_ref.shape[1]
    for k in range(27):
        forward_ref[:, k * width:(k + 1) * width] = w_ref[k].T
        back_ref[:, k * width:(k + 1) * width] = w_ref[26 - k]


def own_kernel(where_ref, mine_ref, other_ref, code_ref, forward_ref, back_ref, conv_ref, grad_ref,
               ground, turned, codes, near_act, near_cot):
    width = conv_ref.shape[0]
    span = 2 * STRIP
    tile_y = where_ref[0] % 2
    for u in range(TILE):
        lay_strip(ground, u, tile_y, mine_ref, other_ref, u)
        turned[:, (u + 1) * span:(u + 2) * span] = ground[u * span:(u + 1) * span, :].T
    for i in (0, TILE + 1):
        turned[:, i * span:(i + 1) * span] = jnp.zeros((2 * width, span), jnp.bfloat16)
    code = code_ref[...]
    lane = lax.broadcasted_iota(jnp.int32, code.shape, 1)
    codes[...] = jnp.where((code >= 0) & (lane // STRIP % 2 == 1), code + span, code)
    place = lax.broadcasted_iota(jnp.int32, (2 * span, span), 0).astype(jnp.float32)
    for half in range(TILE // 2):
        at = half * span
        for side in range(3):
            source = (2 * half + side) * span
            ks = range(9 * side, 9 * side + 9)
            picks = [(place == codes[k:k + 1, at:at + span]).astype(jnp.bfloat16) for k in ks]
            look_up((turned, source, 2 * span), picks, [((near_act, near_cot), k * width, at) for k in ks])
    conv_ref[...] = jnp.dot(forward_ref[...], near_act[...], preferred_element_type=jnp.float32)
    grad_ref[...] = jnp.dot(back_ref[...], near_cot[...], preferred_element_type=jnp.float32)


def edge_kernel(where_ref, before_mine, before_other, after_mine, after_other, code_ref, forward_ref, back_ref,
                own_conv, own_grad, z_ref, conv_ref, grad_ref, ground, turned, near):
    width = z_ref.shape[1]
    span = 2 * STRIP
    tile_y = where_ref[0] % 2
    lay_strip(ground, 0, tile_y, before_mine, before_other, TILE - 1)
    lay_strip(ground, 1, tile_y, after_mine, after_other, 0)
    for i in range(2):
        turned[:, i * span:(i + 1) * span] = ground[i * span:(i + 1) * span, :].T
    first = code_ref[:9, :span]
    last = code_ref[18:, span:]
    lane = lax.broadcasted_iota(jnp.int32, first.shape, 1)
    code = jnp.where(lane < STRIP, first, jnp.where(last >= 0, last + span, last))
    place = lax.broadcasted_iota(jnp.int32, (2 * span, span), 0).astype(jnp.float32)
    picks = [(place == code[k:k + 1, :]).astype(jnp.bfloat16) for k in range(9)]
    look_up((turned, 0, 2 * span), picks, [((near.at[0], near.at[1]), k * width, 0) for k in range(9)])
    lane = lax.broadcasted_iota(jnp.int32, (width, span), 1)

    def total(own_ref, weights, side):
        low = jnp.dot(weights[:, :9 * width], near[side], preferred_element_type=jnp.float32)
        high = jnp.dot(weights[:, 18 * width:], near[side], preferred_element_type=jnp.float32)
        low = own_ref[:, :span] + jnp.where(lane < STRIP, low, 0.0)
        high = own_ref[:, span:] + jnp.where(lane < STRIP, 0.0, high)
        return jnp.concatenate([low, high], axis=1).T

    conv_ref[...] = total(own_conv, forward_ref, 0).astype(jnp.bfloat16)
    back = total(own_grad, back_ref, 1)
    z_val = z_ref[...]
    sig = jax.nn.sigmoid(z_val)
    grad_ref[...] = (back * sig * (1.0 + z_val * (1.0 - sig))).astype(jnp.bfloat16)


def finish_kernel(sides_ref, sides_sent, middle_ref, middle_sent, conv_ref, grad_ref,
                  weight_hbm, conv_hbm, grad_hbm, weight, sems):
    steps = 27 // FINISH_STEP
    copies = [
        pltpu.make_async_copy(conv_ref, conv_hbm, sems.at[steps]),
        pltpu.make_async_copy(grad_ref, grad_hbm, sems.at[steps + 1]),
    ]
    for copy in copies:
        copy.start()
    for i in range(steps):
        first = i * FINISH_STEP
        kept, sent, at = (middle_ref, middle_sent, first - 9) if first // 9 == 1 else (
            sides_ref, sides_sent, first if first < 9 else first - 9)
        part, taken = pl.ds(first, FINISH_STEP), pl.ds(at, FINISH_STEP)
        weight[part] = kept[taken] + sent[taken].astype(jnp.float32)
        copies.append(pltpu.make_async_copy(weight.at[part], weight_hbm.at[part], sems.at[i]))
        copies[-1].start()
    for copy in copies:
        copy.wait()


def whole_scene(features, cotangent, neighbours, timesteps, condition, w_time, w_conv, tiles_x, tiles_y):
    rows, width = features.shape[1:]
    peers = tiles_x * tiles_y
    span = 2 * STRIP
    vmem = pl.BlockSpec(memory_space=pltpu.VMEM)
    smem = pl.BlockSpec(memory_space=pltpu.SMEM)
    params = pltpu.CompilerParams(vmem_limit_bytes=KERNEL_VMEM)
    packed, z_val, code = pl.pallas_call(
        pack_kernel,
        out_shape=(
            jax.ShapeDtypeStruct((rows + CODE_ROWS, 2 * width), jnp.bfloat16),
            jax.ShapeDtypeStruct((rows, width), jnp.float32),
            jax.ShapeDtypeStruct(neighbours.shape, jnp.float32),
        ),
        in_specs=[smem] + [pl.BlockSpec(memory_space=pltpu.HBM)] * 5,
        out_specs=(vmem, vmem, vmem),
        scratch_shapes=[
            pltpu.VMEM((rows, width), jnp.bfloat16),
            pltpu.VMEM(neighbours.shape, jnp.int32),
            pltpu.VMEM((1, width), jnp.bfloat16),
            pltpu.VMEM((width, width), jnp.bfloat16),
            pltpu.SemaphoreType.DMA((5,)),
        ],
        compiler_params=pltpu.CompilerParams(vmem_limit_bytes=PACK_VMEM),
        name="pack_tile",
    )(timesteps, *[in_hbm(array) for array in (features, cotangent, neighbours, condition, w_time)])
    here = lax.axis_index("brick").astype(jnp.int32).reshape(1)

    def across(block):
        return lax.ppermute(block, "brick", [(i, i ^ 1) for i in range(peers)])

    def along(block, turn):
        return lax.ppermute(block, "brick", [(i, (i + turn * tiles_y) % peers) for i in range(peers)])

    w_conv, packed = lax.optimization_barrier((w_conv, packed))
    w_forward, w_back = pl.pallas_call(
        turn_kernel,
        out_shape=(jax.ShapeDtypeStruct((width, 27 * width), jnp.bfloat16),) * 2,
        in_specs=[vmem],
        out_specs=(vmem, vmem),
        compiler_params=params,
        cost_estimate=pl.CostEstimate(flops=2 * 10**8, bytes_accessed=3 * 10**6, transcendentals=0),
        name="turn_weights",
    )(w_conv)
    before = along(packed, 1)
    w_back, later = lax.optimization_barrier((w_back, packed))
    after = along(later, -1)
    before, w_forward = lax.optimization_barrier((before, w_forward))
    far = along(before, 1)
    own_pair = (packed, across(packed))
    own_conv, own_grad = pl.pallas_call(
        own_kernel,
        out_shape=(jax.ShapeDtypeStruct((width, rows), jnp.float32),) * 2,
        in_specs=[smem] + [vmem] * 5,
        out_specs=(vmem, vmem),
        scratch_shapes=[
            pltpu.VMEM((TILE * span, 2 * width), jnp.bfloat16),
            pltpu.VMEM((2 * width, (TILE + 2) * span), jnp.bfloat16),
            pltpu.VMEM((27, rows), jnp.float32),
            pltpu.VMEM((27 * width, rows), jnp.bfloat16),
            pltpu.VMEM((27 * width, rows), jnp.bfloat16),
        ],
        compiler_params=params,
        cost_estimate=pl.CostEstimate(flops=2 * 10**9, bytes_accessed=4 * 10**6, transcendentals=0),
        name="voxels_own_row",
    )(here, *own_pair, code, w_forward, w_back)
    far, own_conv = lax.optimization_barrier((far, own_conv))
    before_pair = (before, across(before))
    far_pair = (far, across(far))
    def row_sums(name, pairs, strips, borders, sums, groups=(0, 1), final=0, keep=False, laid=(), skip_target=-1):
        blocks = [block for pair in pairs for block in pair]
        if final:
            out_shape = (
                jax.ShapeDtypeStruct((final, width, width), jnp.float32),
                jax.ShapeDtypeStruct((final, width, width), jnp.bfloat16),
            )
        else:
            out_shape = (
                jax.ShapeDtypeStruct((HALF * width, width), jnp.float32),
                jax.ShapeDtypeStruct((HALF * width, width), jnp.float32),
                jax.ShapeDtypeStruct((width, width), jnp.float32),
            )
        layout = (
            ((TILE + 2) * span, 2 * width, jnp.bfloat16),
            (2 * width, (TILE + 2) * span, jnp.bfloat16),
            (TILE + 1, CODE_ROWS, span, jnp.float32),
        )
        scratch = [] if laid or keep else [pltpu.VMEM(tuple(shape), kind) for *shape, kind in layout]
        if keep:
            out_shape += tuple(jax.ShapeDtypeStruct(tuple(shape), kind) for *shape, kind in layout)
        operands = (*blocks, *laid, *sums)
        return pl.pallas_call(
            functools.partial(row_kernel, not sums, bool(final), groups, bool(laid), skip_target, strips, borders),
            out_shape=out_shape,
            in_specs=[smem] + [vmem] * len(operands),
            out_specs=(vmem,) * len(out_shape),
            scratch_shapes=scratch + [
                pltpu.VMEM((HALF * width, (TILE + 1) * span), jnp.bfloat16),
                pltpu.VMEM((HALF * width, (TILE + 1) * span), jnp.bfloat16),
            ],
            compiler_params=params,
            cost_estimate=pl.CostEstimate(flops=2 * 10**9, bytes_accessed=4 * 10**6, transcendentals=0),
            name=name,
        )(here, *operands)

    def swapped(block):
        return lax.ppermute(block, "batch", [(0, 1), (1, 0)])

    line = [(0, u) for u in range(TILE)]
    sums = row_sums("weight_row_0", (own_pair,), line, [], ())
    after, centre = lax.optimization_barrier((after, sums[2]))
    sums = (sums[0], sums[1], centre)
    after_pair = (after, across(after))
    sums = row_sums("weight_row_1", (before_pair, own_pair), line + [(1, 0)], [(TILE, TILE - 1)], sums,
                    skip_target=TILE)
    sums = row_sums("weight_row_2", (after_pair, own_pair), line + [(1, TILE - 1)], [(0, TILE)], sums)
    sides, sides_sent, *laid = row_sums("weight_row_3", (far_pair, before_pair, after_pair),
                                 line + [(1, 0), (2, TILE - 1)], [(TILE, TILE - 1), (0, TILE + 1)],
                                 sums, groups=(0,), final=18, keep=True)
    sides_other = swapped(sides_sent)
    centre, sides = lax.optimization_barrier((sums[2], sides))
    middle, middle_sent = row_sums("weight_row_3_middle", (), line, [], (sums[0], sums[1], centre),
                                   groups=(1,), final=9, laid=laid)
    middle_other = swapped(middle_sent)
    conv_out, feature_grad = pl.pallas_call(
        edge_kernel,
        out_shape=(jax.ShapeDtypeStruct((rows, width), jnp.bfloat16),) * 2,
        in_specs=[smem] + [vmem] * 10,
        out_specs=(vmem, vmem),
        scratch_shapes=[
            pltpu.VMEM((2 * span, 2 * width), jnp.bfloat16),
            pltpu.VMEM((2 * width, 2 * span), jnp.bfloat16),
            pltpu.VMEM((2, 9 * width, span), jnp.bfloat16),
        ],
        compiler_params=params,
        cost_estimate=pl.CostEstimate(flops=10**9, bytes_accessed=4 * 10**6, transcendentals=0),
        name="voxel_edges",
    )(here, *before_pair, *after_pair, code, w_forward, w_back, own_conv, own_grad, z_val)
    hbm = pl.BlockSpec(memory_space=pltpu.HBM)
    weight_grad, conv_out, feature_grad = pl.pallas_call(
        finish_kernel,
        out_shape=(
            jax.ShapeDtypeStruct((27, width, width), jnp.float32),
            jax.ShapeDtypeStruct((rows, width), jnp.bfloat16),
            jax.ShapeDtypeStruct((rows, width), jnp.bfloat16),
        ),
        in_specs=[vmem] * 6,
        out_specs=(hbm, hbm, hbm),
        scratch_shapes=[
            pltpu.VMEM((27, width, width), jnp.float32),
            pltpu.SemaphoreType.DMA((27 // FINISH_STEP + 2,)),
        ],
        compiler_params=pltpu.CompilerParams(vmem_limit_bytes=PACK_VMEM),
        name="finish",
    )(sides, sides_other, middle, middle_other, conv_out, feature_grad)
    return (conv_out[None], feature_grad[None], weight_grad)


def passed_along(block, axis, distance):
    devices = range(lax.axis_size(axis))
    route = [(i - distance, i) for i in devices if i - distance in devices]
    return lax.ppermute(block, axis, route)


def slab_rows(block, side_recv, front_recv, width):
    widened = jnp.concatenate([side_recv[0], block, side_recv[1]], axis=1)
    slab = jnp.concatenate([front_recv[0][None], widened, front_recv[1][None]], axis=0)
    flat = slab.reshape(-1, width)
    return jnp.concatenate([flat, jnp.zeros((1, width), jnp.bfloat16)], axis=0)


def with_halo(block, tiles_y):
    width = block.shape[-1]
    side = TILE
    side_recv = tuple(passed_along(block[:, edge], "brick", by)[:, None] for by, edge in ((1, side - 1), (-1, 0)))
    wide = jnp.concatenate([side_recv[0], block, side_recv[1]], axis=1)
    front_recv = tuple(passed_along(wide[edge], "brick", by) for by, edge in ((tiles_y, side - 1), (-tiles_y, 0)))
    return slab_rows(block, side_recv, front_recv, width)


def halo_plan(features, cotangent, neighbours, timesteps, condition, w_time, w_conv, tiles_x, tiles_y):
    rows_here, width = features.shape[1:]
    here = lax.axis_index("brick")
    tile_x = here // tiles_y
    tile_y = here % tiles_y
    side = TILE
    layers = LAYERS
    wide = side + 2
    valid = neighbours >= 0
    safe = jnp.where(valid, neighbours, 0)
    owner = safe // rows_here
    inside = safe % rows_here
    column = inside // layers
    layer = inside % layers
    local_x = (owner // tiles_y - tile_x) * side + column // side + 1
    local_y = (owner % tiles_y - tile_y) * side + column % side + 1
    sentinel = wide * wide * layers
    ext_index = jnp.where(valid, (local_x * wide + local_y) * layers + layer, sentinel).T
    temb = time_embedding(timesteps, width)
    shift = jnp.dot(temb, w_time, preferred_element_type=jnp.float32) + condition.astype(jnp.float32)
    z_val = features[0].astype(jnp.float32) + shift[0][None, :]
    act = jax.nn.silu(z_val).astype(jnp.bfloat16)
    cot = cotangent[0]
    w_forward = w_conv.reshape(27 * width, width)
    w_backward = jnp.transpose(w_conv[::-1], (0, 2, 1)).reshape(27 * width, width)
    act_ext = with_halo(act.reshape(side, side, layers, width), tiles_y)
    gathered = act_ext[ext_index].reshape(rows_here, 27 * width)
    conv_out = jnp.dot(gathered, w_forward, preferred_element_type=jnp.float32).astype(jnp.bfloat16)
    partial_grad = lax.dot_general(
        gathered, cot, (((0,), (0,)), ((), ())), preferred_element_type=jnp.float32
    )
    both = ("brick", "batch")
    parts = tiles_x * tiles_y * lax.axis_size("batch")
    rows = 27 * width
    extra = -rows % (8 * parts)
    pieces = jnp.pad(partial_grad.astype(jnp.bfloat16), ((0, extra), (0, 0))).reshape(parts, -1, width)
    arrived = lax.all_to_all(pieces, both, 0, 0)
    summed = arrived.astype(jnp.float32).sum(0).astype(jnp.bfloat16)
    whole = lax.all_gather(summed, both, axis=0, tiled=True)
    weight_grad = whole[:rows].astype(jnp.float32).reshape(27, width, width)
    cot_ext = with_halo(cot.reshape(side, side, layers, width), tiles_y)
    cot_gathered = cot_ext[ext_index].reshape(rows_here, 27 * width)
    back = jnp.dot(cot_gathered, w_backward, preferred_element_type=jnp.float32)
    sig = jax.nn.sigmoid(z_val)
    feature_grad = (back * sig * (1.0 + z_val * (1.0 - sig))).astype(jnp.bfloat16)
    return (conv_out[None], feature_grad[None], weight_grad)


def shards(*arrays):
    peers = lax.axis_size("brick")
    bits = peers.bit_length() - 1
    tiles_x = 2 ** ((bits + 1) // 2)
    tiles_y = 2 ** (bits // 2)
    plan = whole_scene if (tiles_x, tiles_y) == (ROW_STAGES, 2) else halo_plan
    return plan(*arrays, tiles_x, tiles_y)


def solution(mesh):
    in_specs = (
        P(("groups", "batch"), "brick", None),
        P(("groups", "batch"), "brick", None),
        P(None, ("groups", "brick")),
        P(("groups", "batch")),
        P(("groups", "batch"), None),
        P(),
        P(),
    )
    out_specs = (
        P(("groups", "batch"), "brick", None),
        P(("groups", "batch"), "brick", None),
        P("groups", None, None),
    )
    return jax.shard_map(shards, mesh=mesh, in_specs=in_specs, out_specs=out_specs, check_vma=False)
```

```python
import functools

import jax
import jax.numpy as jnp
from jax import lax
from jax.experimental import pallas as pl
from jax.experimental.pallas import tpu as pltpu
from jax.sharding import PartitionSpec as P

LAYERS = 16
TILE = 4
STRIP = TILE * LAYERS
HALF = 13
CODE_ROWS = 16
ROW_STAGES = 4
FINISH_STEP = 3
PACK_VMEM = 8 * 1024 * 1024
KERNEL_VMEM = 24 * 1024 * 1024


def time_embedding(timesteps, width):
    half = width // 2
    freq = jnp.exp(-jnp.log(10000.0) * jnp.arange(half, dtype=jnp.float32) / half)
    angle = timesteps.astype(jnp.float32)[:, None] * freq[None, :]
    return jnp.concatenate([jnp.sin(angle), jnp.cos(angle)], axis=1).astype(jnp.bfloat16)


def strip_codes(neighbours, tiles_y):
    rows_here = TILE * STRIP
    code = (neighbours // rows_here) % tiles_y * STRIP + neighbours % STRIP
    return jnp.where(neighbours < 0, -1, code).astype(jnp.float32)


def in_hbm(array):
    return pltpu.with_memory_space_constraint(array, pltpu.HBM)


def pack_kernel(time_ref, feat_hbm, cot_hbm, near_hbm, cond_hbm, wt_hbm, pack_ref, z_ref, code_ref,
                feat_ref, near_ref, cond_ref, wt_ref, sems):
    rows, width = feat_ref.shape
    half = width // 2
    moves = (
        (wt_hbm, wt_ref),
        (cond_hbm, cond_ref),
        (feat_hbm.at[0], feat_ref),
        (near_hbm, near_ref),
        (cot_hbm.at[0], pack_ref.at[:rows, width:]),
    )
    copies = [pltpu.make_async_copy(source, to, sems.at[i]) for i, (source, to) in enumerate(moves)]
    for copy in copies:
        copy.start()
    lane = lax.broadcasted_iota(jnp.int32, (1, width), 1)
    freq = jnp.exp(-jnp.log(10000.0) * (lane % half).astype(jnp.float32) / half)
    angle = time_ref[0].astype(jnp.float32) * freq
    temb = jnp.where(lane < half, jnp.sin(angle), jnp.cos(angle)).astype(jnp.bfloat16)
    copies[0].wait()
    copies[1].wait()
    shift = jnp.dot(temb, wt_ref[...], preferred_element_type=jnp.float32)
    shift = shift + cond_ref[...].astype(jnp.float32)
    copies[2].wait()
    z_val = feat_ref[...].astype(jnp.float32) + shift
    z_ref[...] = z_val
    pack_ref[:rows, :width] = (z_val * jax.nn.sigmoid(z_val)).astype(jnp.bfloat16)
    copies[3].wait()
    code = strip_codes(near_ref[...], 2)
    code_ref[...] = code
    pack_ref[rows:, :] = code[:CODE_ROWS, :].astype(jnp.bfloat16)
    copies[4].wait()


def lay_strip(ground, to, tile_y, mine_ref, other_ref, u):
    span = 2 * STRIP
    for ref, place in ((mine_ref, tile_y), (other_ref, 1 - tile_y)):
        at = pl.multiple_of(to * span + place * STRIP, STRIP)
        ground[pl.ds(at, STRIP), :] = ref[u * STRIP:(u + 1) * STRIP, :]


def look_up(window, picks, places):
    ref, first, lanes = window
    width = ref.shape[0] // 2
    for i in range(0, len(picks), 2):
        pair = picks[i:i + 2]
        pick = jnp.concatenate(pair, axis=1) if len(pair) == 2 else pair[0]
        span = pair[0].shape[1]
        for side in range(2):
            near = jnp.dot(ref[side * width:(side + 1) * width, first:first + lanes], pick,
                           preferred_element_type=jnp.float32).astype(jnp.bfloat16)
            for j, (to, row, lane) in enumerate(places[i:i + 2]):
                to[side][row:row + width, lane:lane + span] = near[:, j * span:(j + 1) * span]


def row_kernel(first_stage, final, groups, laid, strips, borders, *refs):
    refs = list(refs)
    where_ref = refs.pop(0)
    pairs = [] if laid else [(refs.pop(0), refs.pop(0)) for _ in range(1 + max(pair for pair, _ in strips))]
    given = [refs.pop(0) for _ in range(3)] if laid else []
    before = {} if first_stage else {group: [refs.pop(0) for _ in range(2 + group)] for group in groups}
    outs = [refs.pop(0) for _ in range(2)] if final else {
        group: [refs.pop(0) for _ in range(2 + group)] for group in groups}
    ground, turned, codes = given or [refs.pop(0) for _ in range(3)]
    near_act, near_cot = refs
    width = ground.shape[1] // 2
    rows = TILE * STRIP
    span = 2 * STRIP
    tile_y = where_ref[0] % 2
    borders = [(u, u - 1) for u in range(1, TILE)] + borders
    targets = sorted({target for target, _ in borders})
    for i, (pair, u) in enumerate([] if laid else strips):
        lay_strip(ground, i, tile_y, *pairs[pair], u)
        if i < TILE or i in targets:
            both = [ref[rows:, u * STRIP:(u + 1) * STRIP].astype(jnp.float32) for ref in pairs[pair]]
            first = jnp.where(tile_y == 0, both[0], both[1])
            second = jnp.where(tile_y == 0, both[1], both[0])
            codes[i] = jnp.concatenate([first, second], axis=1)
        if i < TILE or i in [source for _, source in borders]:
            turned[:, i * span:(i + 1) * span] = ground[i * span:(i + 1) * span, :].T
    place = lax.broadcasted_iota(jnp.int32, (span, span), 0).astype(jnp.float32)

    to = (near_act, near_cot)
    for source in range(TILE + 2):
        found = [(source, k) for k in range(9, HALF)] if 1 in groups and source < TILE else []
        if 0 in groups:
            found += [(target, k) for target, origin in borders if origin == source for k in range(9)]
        if found:
            picks = [(place == codes[target, k:k + 1, :]).astype(jnp.bfloat16) for target, k in found]
            look_up((turned, source * span, span), picks, [(to, k * width, target * span) for target, k in found])
    extents = ((0, 9, span * targets[0], span * (targets[-1] + 1)), (9, HALF, 0, TILE * span))
    for turn, near in ((0, near_act), (1, near_cot)):
        for group in groups:
            start, stop, first, last = extents[group]
            other = ground[first:last, (1 - turn) * width:(2 - turn) * width]
            value = jnp.dot(near[start * width:stop * width, first:last], other, preferred_element_type=jnp.float32)
            if not first_stage:
                value = value + before[group][turn][...]
            if not final:
                outs[group][turn][...] = value
                continue
            for k in range(start, stop):
                one = value[(k - start) * width:(k - start + 1) * width, :]
                to = 2 * HALF - k if turn else k
                if turn:
                    one = one.T
                to = to - 9 if group == 1 else to - 9 * turn
                outs[0][to] = one
                outs[1][to] = one.astype(jnp.bfloat16)
    if 1 in groups:
        centre = jnp.dot(turned[:width, :TILE * span], ground[:TILE * span, width:], preferred_element_type=jnp.float32)
        if not first_stage:
            centre = centre + before[1][2][...]
        if final:
            outs[0][HALF - 9] = centre
            outs[1][HALF - 9] = centre.astype(jnp.bfloat16)
        else:
            outs[1][2][...] = centre


def turn_kernel(w_ref, forward_ref, back_ref):
    width = w_ref.shape[1]
    for k in range(27):
        forward_ref[:, k * width:(k + 1) * width] = w_ref[k].T
        back_ref[:, k * width:(k + 1) * width] = w_ref[26 - k]


def own_kernel(where_ref, mine_ref, other_ref, code_ref, forward_ref, back_ref, conv_ref, grad_ref,
               ground, turned, codes, near_act, near_cot):
    width = conv_ref.shape[0]
    span = 2 * STRIP
    tile_y = where_ref[0] % 2
    for u in range(TILE):
        lay_strip(ground, u, tile_y, mine_ref, other_ref, u)
        turned[:, (u + 1) * span:(u + 2) * span] = ground[u * span:(u + 1) * span, :].T
    for i in (0, TILE + 1):
        turned[:, i * span:(i + 1) * span] = jnp.zeros((2 * width, span), jnp.bfloat16)
    code = code_ref[...]
    lane = lax.broadcasted_iota(jnp.int32, code.shape, 1)
    codes[...] = jnp.where((code >= 0) & (lane // STRIP % 2 == 1), code + span, code)
    place = lax.broadcasted_iota(jnp.int32, (2 * span, span), 0).astype(jnp.float32)
    for half in range(TILE // 2):
        at = half * span
        for side in range(3):
            source = (2 * half + side) * span
            ks = range(9 * side, 9 * side + 9)
            picks = [(place == codes[k:k + 1, at:at + span]).astype(jnp.bfloat16) for k in ks]
            look_up((turned, source, 2 * span), picks, [((near_act, near_cot), k * width, at) for k in ks])
    conv_ref[...] = jnp.dot(forward_ref[...], near_act[...], preferred_element_type=jnp.float32)
    grad_ref[...] = jnp.dot(back_ref[...], near_cot[...], preferred_element_type=jnp.float32)


def edge_kernel(where_ref, before_mine, before_other, after_mine, after_other, code_ref, forward_ref, back_ref,
                own_conv, own_grad, z_ref, conv_ref, grad_ref, ground, turned, near):
    width = z_ref.shape[1]
    span = 2 * STRIP
    tile_y = where_ref[0] % 2
    lay_strip(ground, 0, tile_y, before_mine, before_other, TILE - 1)
    lay_strip(ground, 1, tile_y, after_mine, after_other, 0)
    for i in range(2):
        turned[:, i * span:(i + 1) * span] = ground[i * span:(i + 1) * span, :].T
    first = code_ref[:9, :span]
    last = code_ref[18:, span:]
    lane = lax.broadcasted_iota(jnp.int32, first.shape, 1)
    code = jnp.where(lane < STRIP, first, jnp.where(last >= 0, last + span, last))
    place = lax.broadcasted_iota(jnp.int32, (2 * span, span), 0).astype(jnp.float32)
    picks = [(place == code[k:k + 1, :]).astype(jnp.bfloat16) for k in range(9)]
    look_up((turned, 0, 2 * span), picks, [((near.at[0], near.at[1]), k * width, 0) for k in range(9)])
    lane = lax.broadcasted_iota(jnp.int32, (width, span), 1)

    def total(own_ref, weights, side):
        low = jnp.dot(weights[:, :9 * width], near[side], preferred_element_type=jnp.float32)
        high = jnp.dot(weights[:, 18 * width:], near[side], preferred_element_type=jnp.float32)
        low = own_ref[:, :span] + jnp.where(lane < STRIP, low, 0.0)
        high = own_ref[:, span:] + jnp.where(lane < STRIP, 0.0, high)
        return jnp.concatenate([low, high], axis=1).T

    conv_ref[...] = total(own_conv, forward_ref, 0).astype(jnp.bfloat16)
    back = total(own_grad, back_ref, 1)
    z_val = z_ref[...]
    sig = jax.nn.sigmoid(z_val)
    grad_ref[...] = (back * sig * (1.0 + z_val * (1.0 - sig))).astype(jnp.bfloat16)


def finish_kernel(sides_ref, sides_sent, middle_ref, middle_sent, conv_ref, grad_ref,
                  weight_hbm, conv_hbm, grad_hbm, weight, sems):
    steps = 27 // FINISH_STEP
    copies = [
        pltpu.make_async_copy(conv_ref, conv_hbm, sems.at[steps]),
        pltpu.make_async_copy(grad_ref, grad_hbm, sems.at[steps + 1]),
    ]
    for copy in copies:
        copy.start()
    for i in range(steps):
        first = i * FINISH_STEP
        kept, sent, at = (middle_ref, middle_sent, first - 9) if first // 9 == 1 else (
            sides_ref, sides_sent, first if first < 9 else first - 9)
        part, taken = pl.ds(first, FINISH_STEP), pl.ds(at, FINISH_STEP)
        weight[part] = kept[taken] + sent[taken].astype(jnp.float32)
        copies.append(pltpu.make_async_copy(weight.at[part], weight_hbm.at[part], sems.at[i]))
        copies[-1].start()
    for copy in copies:
        copy.wait()


def whole_scene(features, cotangent, neighbours, timesteps, condition, w_time, w_conv, tiles_x, tiles_y):
    rows, width = features.shape[1:]
    peers = tiles_x * tiles_y
    span = 2 * STRIP
    vmem = pl.BlockSpec(memory_space=pltpu.VMEM)
    smem = pl.BlockSpec(memory_space=pltpu.SMEM)
    params = pltpu.CompilerParams(vmem_limit_bytes=KERNEL_VMEM)
    packed, z_val, code = pl.pallas_call(
        pack_kernel,
        out_shape=(
            jax.ShapeDtypeStruct((rows + CODE_ROWS, 2 * width), jnp.bfloat16),
            jax.ShapeDtypeStruct((rows, width), jnp.float32),
            jax.ShapeDtypeStruct(neighbours.shape, jnp.float32),
        ),
        in_specs=[smem] + [pl.BlockSpec(memory_space=pltpu.HBM)] * 5,
        out_specs=(vmem, vmem, vmem),
        scratch_shapes=[
            pltpu.VMEM((rows, width), jnp.bfloat16),
            pltpu.VMEM(neighbours.shape, jnp.int32),
            pltpu.VMEM((1, width), jnp.bfloat16),
            pltpu.VMEM((width, width), jnp.bfloat16),
            pltpu.SemaphoreType.DMA((5,)),
        ],
        compiler_params=pltpu.CompilerParams(vmem_limit_bytes=PACK_VMEM),
        name="pack_tile",
    )(timesteps, *[in_hbm(array) for array in (features, cotangent, neighbours, condition, w_time)])
    here = lax.axis_index("brick").astype(jnp.int32).reshape(1)

    def across(block):
        return lax.ppermute(block, "brick", [(i, i ^ 1) for i in range(peers)])

    def along(block, turn):
        return lax.ppermute(block, "brick", [(i, (i + turn * tiles_y) % peers) for i in range(peers)])

    w_conv, packed = lax.optimization_barrier((w_conv, packed))
    w_forward, w_back = pl.pallas_call(
        turn_kernel,
        out_shape=(jax.ShapeDtypeStruct((width, 27 * width), jnp.bfloat16),) * 2,
        in_specs=[vmem],
        out_specs=(vmem, vmem),
        compiler_params=params,
        cost_estimate=pl.CostEstimate(flops=2 * 10**8, bytes_accessed=3 * 10**6, transcendentals=0),
        name="turn_weights",
    )(w_conv)
    before = along(packed, 1)
    w_back, later = lax.optimization_barrier((w_back, packed))
    after = along(later, -1)
    before, w_forward = lax.optimization_barrier((before, w_forward))
    far = along(before, 1)
    own_pair = (packed, across(packed))
    own_conv, own_grad = pl.pallas_call(
        own_kernel,
        out_shape=(jax.ShapeDtypeStruct((width, rows), jnp.float32),) * 2,
        in_specs=[smem] + [vmem] * 5,
        out_specs=(vmem, vmem),
        scratch_shapes=[
            pltpu.VMEM((TILE * span, 2 * width), jnp.bfloat16),
            pltpu.VMEM((2 * width, (TILE + 2) * span), jnp.bfloat16),
            pltpu.VMEM((27, rows), jnp.float32),
            pltpu.VMEM((27 * width, rows), jnp.bfloat16),
            pltpu.VMEM((27 * width, rows), jnp.bfloat16),
        ],
        compiler_params=params,
        cost_estimate=pl.CostEstimate(flops=2 * 10**9, bytes_accessed=4 * 10**6, transcendentals=0),
        name="voxels_own_row",
    )(here, *own_pair, code, w_forward, w_back)
    before_pair = (before, across(before))
    def row_sums(name, pairs, strips, borders, sums, groups=(0, 1), final=0, keep=False, laid=()):
        blocks = [block for pair in pairs for block in pair]
        if final:
            out_shape = [
                jax.ShapeDtypeStruct((final, width, width), jnp.float32),
                jax.ShapeDtypeStruct((final, width, width), jnp.bfloat16),
            ]
        else:
            lengths = {0: (9, 9), 1: (HALF - 9, HALF - 9, 1)}
            out_shape = [jax.ShapeDtypeStruct((length * width, width), jnp.float32)
                         for group in groups for length in lengths[group]]
        layout = (
            ((TILE + 2) * span, 2 * width, jnp.bfloat16),
            (2 * width, (TILE + 2) * span, jnp.bfloat16),
            (TILE + 1, CODE_ROWS, span, jnp.float32),
        )
        scratch = [] if laid or keep else [pltpu.VMEM(tuple(shape), kind) for *shape, kind in layout]
        results = len(out_shape)
        if keep:
            out_shape += [jax.ShapeDtypeStruct(tuple(shape), kind) for *shape, kind in layout]
        earlier = [part for group in groups for part in sums[group]] if sums else []
        operands = (*blocks, *laid, *earlier)
        out = pl.pallas_call(
            functools.partial(row_kernel, not sums, bool(final), groups, bool(laid), strips, borders),
            out_shape=out_shape,
            in_specs=[smem] + [vmem] * len(operands),
            out_specs=[vmem] * len(out_shape),
            scratch_shapes=scratch + [
                pltpu.VMEM((HALF * width, (TILE + 1) * span), jnp.bfloat16),
                pltpu.VMEM((HALF * width, (TILE + 1) * span), jnp.bfloat16),
            ],
            compiler_params=params,
            cost_estimate=pl.CostEstimate(flops=2 * 10**9, bytes_accessed=4 * 10**6, transcendentals=0),
            name=name,
        )(here, *operands)
        if final:
            return out
        totals, parts = dict(sums), list(out[:results])
        for group in groups:
            totals[group] = tuple(parts.pop(0) for _ in range(2 + group))
        return totals, out[results:]

    def swapped(block):
        return lax.ppermute(block, "batch", [(0, 1), (1, 0)])

    line = [(0, u) for u in range(TILE)]
    sums, _ = row_sums("weight_row_0", (own_pair,), line, [], {})
    low, high, centre = sums[1]
    after, centre = lax.optimization_barrier((after, centre))
    sums[1] = (low, high, centre)
    after_pair = (after, across(after))
    border = [(TILE, TILE - 1)]
    sums, laid = row_sums("weight_row_1_middle", (before_pair, own_pair), line + [(1, 0)], border, sums,
                          groups=(1,), keep=True)
    low, high, centre = sums[1]
    far, own_conv, centre = lax.optimization_barrier((far, own_conv, centre))
    sums[1] = (low, high, centre)
    far_pair = (far, across(far))
    sums, _ = row_sums("weight_row_1", (), line + [(1, 0)], border, sums, groups=(0,), laid=laid)
    sums, _ = row_sums("weight_row_2", (after_pair, own_pair), line + [(1, TILE - 1)], [(0, TILE)], sums)
    sides, sides_sent, *laid = row_sums("weight_row_3", (far_pair, before_pair, after_pair),
                                        line + [(1, 0), (2, TILE - 1)], [(TILE, TILE - 1), (0, TILE + 1)],
                                        sums, groups=(0,), final=18, keep=True)
    sides_other = swapped(sides_sent)
    low, high, centre = sums[1]
    centre, sides = lax.optimization_barrier((centre, sides))
    sums[1] = (low, high, centre)
    middle, middle_sent = row_sums("weight_row_3_middle", (), line, [], sums, groups=(1,), final=9, laid=laid)
    middle_other = swapped(middle_sent)
    conv_out, feature_grad = pl.pallas_call(
        edge_kernel,
        out_shape=(jax.ShapeDtypeStruct((rows, width), jnp.bfloat16),) * 2,
        in_specs=[smem] + [vmem] * 10,
        out_specs=(vmem, vmem),
        scratch_shapes=[
            pltpu.VMEM((2 * span, 2 * width), jnp.bfloat16),
            pltpu.VMEM((2 * width, 2 * span), jnp.bfloat16),
            pltpu.VMEM((2, 9 * width, span), jnp.bfloat16),
        ],
        compiler_params=params,
        cost_estimate=pl.CostEstimate(flops=10**9, bytes_accessed=4 * 10**6, transcendentals=0),
        name="voxel_edges",
    )(here, *before_pair, *after_pair, code, w_forward, w_back, own_conv, own_grad, z_val)
    hbm = pl.BlockSpec(memory_space=pltpu.HBM)
    weight_grad, conv_out, feature_grad = pl.pallas_call(
        finish_kernel,
        out_shape=(
            jax.ShapeDtypeStruct((27, width, width), jnp.float32),
            jax.ShapeDtypeStruct((rows, width), jnp.bfloat16),
            jax.ShapeDtypeStruct((rows, width), jnp.bfloat16),
        ),
        in_specs=[vmem] * 6,
        out_specs=(hbm, hbm, hbm),
        scratch_shapes=[
            pltpu.VMEM((27, width, width), jnp.float32),
            pltpu.SemaphoreType.DMA((27 // FINISH_STEP + 2,)),
        ],
        compiler_params=pltpu.CompilerParams(vmem_limit_bytes=PACK_VMEM),
        name="finish",
    )(sides, sides_other, middle, middle_other, conv_out, feature_grad)
    return (conv_out[None], feature_grad[None], weight_grad)


def passed_along(block, axis, distance):
    devices = range(lax.axis_size(axis))
    route = [(i - distance, i) for i in devices if i - distance in devices]
    return lax.ppermute(block, axis, route)


def slab_rows(block, side_recv, front_recv, width):
    widened = jnp.concatenate([side_recv[0], block, side_recv[1]], axis=1)
    slab = jnp.concatenate([front_recv[0][None], widened, front_recv[1][None]], axis=0)
    flat = slab.reshape(-1, width)
    return jnp.concatenate([flat, jnp.zeros((1, width), jnp.bfloat16)], axis=0)


def with_halo(block, tiles_y):
    width = block.shape[-1]
    side = TILE
    side_recv = tuple(passed_along(block[:, edge], "brick", by)[:, None] for by, edge in ((1, side - 1), (-1, 0)))
    wide = jnp.concatenate([side_recv[0], block, side_recv[1]], axis=1)
    front_recv = tuple(passed_along(wide[edge], "brick", by) for by, edge in ((tiles_y, side - 1), (-tiles_y, 0)))
    return slab_rows(block, side_recv, front_recv, width)


def halo_plan(features, cotangent, neighbours, timesteps, condition, w_time, w_conv, tiles_x, tiles_y):
    rows_here, width = features.shape[1:]
    here = lax.axis_index("brick")
    tile_x = here // tiles_y
    tile_y = here % tiles_y
    side = TILE
    layers = LAYERS
    wide = side + 2
    valid = neighbours >= 0
    safe = jnp.where(valid, neighbours, 0)
    owner = safe // rows_here
    inside = safe % rows_here
    column = inside // layers
    layer = inside % layers
    local_x = (owner // tiles_y - tile_x) * side + column // side + 1
    local_y = (owner % tiles_y - tile_y) * side + column % side + 1
    sentinel = wide * wide * layers
    ext_index = jnp.where(valid, (local_x * wide + local_y) * layers + layer, sentinel).T
    temb = time_embedding(timesteps, width)
    shift = jnp.dot(temb, w_time, preferred_element_type=jnp.float32) + condition.astype(jnp.float32)
    z_val = features[0].astype(jnp.float32) + shift[0][None, :]
    act = jax.nn.silu(z_val).astype(jnp.bfloat16)
    cot = cotangent[0]
    w_forward = w_conv.reshape(27 * width, width)
    w_backward = jnp.transpose(w_conv[::-1], (0, 2, 1)).reshape(27 * width, width)
    act_ext = with_halo(act.reshape(side, side, layers, width), tiles_y)
    gathered = act_ext[ext_index].reshape(rows_here, 27 * width)
    conv_out = jnp.dot(gathered, w_forward, preferred_element_type=jnp.float32).astype(jnp.bfloat16)
    partial_grad = lax.dot_general(
        gathered, cot, (((0,), (0,)), ((), ())), preferred_element_type=jnp.float32
    )
    both = ("brick", "batch")
    parts = tiles_x * tiles_y * lax.axis_size("batch")
    rows = 27 * width
    extra = -rows % (8 * parts)
    pieces = jnp.pad(partial_grad.astype(jnp.bfloat16), ((0, extra), (0, 0))).reshape(parts, -1, width)
    arrived = lax.all_to_all(pieces, both, 0, 0)
    summed = arrived.astype(jnp.float32).sum(0).astype(jnp.bfloat16)
    whole = lax.all_gather(summed, both, axis=0, tiled=True)
    weight_grad = whole[:rows].astype(jnp.float32).reshape(27, width, width)
    cot_ext = with_halo(cot.reshape(side, side, layers, width), tiles_y)
    cot_gathered = cot_ext[ext_index].reshape(rows_here, 27 * width)
    back = jnp.dot(cot_gathered, w_backward, preferred_element_type=jnp.float32)
    sig = jax.nn.sigmoid(z_val)
    feature_grad = (back * sig * (1.0 + z_val * (1.0 - sig))).astype(jnp.bfloat16)
    return (conv_out[None], feature_grad[None], weight_grad)


def shards(*arrays):
    peers = lax.axis_size("brick")
    bits = peers.bit_length() - 1
    tiles_x = 2 ** ((bits + 1) // 2)
    tiles_y = 2 ** (bits // 2)
    plan = whole_scene if (tiles_x, tiles_y) == (ROW_STAGES, 2) else halo_plan
    return plan(*arrays, tiles_x, tiles_y)


def solution(mesh):
    in_specs = (
        P(("groups", "batch"), "brick", None),
        P(("groups", "batch"), "brick", None),
        P(None, ("groups", "brick")),
        P(("groups", "batch")),
        P(("groups", "batch"), None),
        P(),
        P(),
    )
    out_specs = (
        P(("groups", "batch"), "brick", None),
        P(("groups", "batch"), "brick", None),
        P("groups", None, None),
    )
    return jax.shard_map(shards, mesh=mesh, in_specs=in_specs, out_specs=out_specs, check_vma=False)
```

```python
import functools

import jax
import jax.numpy as jnp
from jax import lax
from jax.experimental import pallas as pl
from jax.experimental.pallas import tpu as pltpu
from jax.sharding import PartitionSpec as P

LAYERS = 16
TILE = 4
STRIP = TILE * LAYERS
HALF = 13
CODE_ROWS = 16
ROW_STAGES = 4
FINISH_STEP = 9
PACK_VMEM = 8 * 1024 * 1024
KERNEL_VMEM = 24 * 1024 * 1024


def time_embedding(timesteps, width):
    half = width // 2
    freq = jnp.exp(-jnp.log(10000.0) * jnp.arange(half, dtype=jnp.float32) / half)
    angle = timesteps.astype(jnp.float32)[:, None] * freq[None, :]
    return jnp.concatenate([jnp.sin(angle), jnp.cos(angle)], axis=1).astype(jnp.bfloat16)


def strip_codes(neighbours, tiles_y):
    rows_here = TILE * STRIP
    code = (neighbours // rows_here) % tiles_y * STRIP + neighbours % STRIP
    return jnp.where(neighbours < 0, -1, code).astype(jnp.float32)


def in_hbm(array):
    return pltpu.with_memory_space_constraint(array, pltpu.HBM)


def pack_kernel(time_ref, feat_hbm, cot_hbm, near_hbm, cond_hbm, wt_hbm, pack_ref, z_ref, code_ref,
                feat_ref, near_ref, cond_ref, wt_ref, sems):
    rows, width = feat_ref.shape
    half = width // 2
    moves = (
        (wt_hbm, wt_ref),
        (cond_hbm, cond_ref),
        (feat_hbm.at[0], feat_ref),
        (near_hbm, near_ref),
        (cot_hbm.at[0], pack_ref.at[:rows, width:]),
    )
    copies = [pltpu.make_async_copy(source, to, sems.at[i]) for i, (source, to) in enumerate(moves)]
    for copy in copies:
        copy.start()
    lane = lax.broadcasted_iota(jnp.int32, (1, width), 1)
    freq = jnp.exp(-jnp.log(10000.0) * (lane % half).astype(jnp.float32) / half)
    angle = time_ref[0].astype(jnp.float32) * freq
    temb = jnp.where(lane < half, jnp.sin(angle), jnp.cos(angle)).astype(jnp.bfloat16)
    copies[0].wait()
    copies[1].wait()
    shift = jnp.dot(temb, wt_ref[...], preferred_element_type=jnp.float32)
    shift = shift + cond_ref[...].astype(jnp.float32)
    copies[2].wait()
    z_val = feat_ref[...].astype(jnp.float32) + shift
    z_ref[...] = z_val
    pack_ref[:rows, :width] = (z_val * jax.nn.sigmoid(z_val)).astype(jnp.bfloat16)
    copies[3].wait()
    code = strip_codes(near_ref[...], 2)
    code_ref[...] = code
    pack_ref[rows:, :] = code[:CODE_ROWS, :].astype(jnp.bfloat16)
    copies[4].wait()


def lay_strip(ground, to, tile_y, mine_ref, other_ref, u):
    span = 2 * STRIP
    for ref, place in ((mine_ref, tile_y), (other_ref, 1 - tile_y)):
        at = pl.multiple_of(to * span + place * STRIP, STRIP)
        ground[pl.ds(at, STRIP), :] = ref[u * STRIP:(u + 1) * STRIP, :]


def look_up(window, picks, places):
    ref, first, lanes = window
    width = ref.shape[0] // 2
    for i in range(0, len(picks), 2):
        pair = picks[i:i + 2]
        pick = jnp.concatenate(pair, axis=1) if len(pair) == 2 else pair[0]
        span = pair[0].shape[1]
        for side in range(2):
            near = jnp.dot(ref[side * width:(side + 1) * width, first:first + lanes], pick,
                           preferred_element_type=jnp.float32).astype(jnp.bfloat16)
            for j, (to, row, lane) in enumerate(places[i:i + 2]):
                to[side][row:row + width, lane:lane + span] = near[:, j * span:(j + 1) * span]


def row_kernel(first_stage, final, groups, laid, strips, borders, *refs):
    refs = list(refs)
    where_ref = refs.pop(0)
    pairs = [] if laid else [(refs.pop(0), refs.pop(0)) for _ in range(1 + max(pair for pair, _ in strips))]
    given = [refs.pop(0) for _ in range(3)] if laid else []
    before = [refs.pop(0) for _ in range(0 if first_stage else 3)]
    outs = [refs.pop(0) for _ in range(2 if final else 3)]
    ground, turned, codes = given or [refs.pop(0) for _ in range(3)]
    near_act, near_cot = refs
    width = ground.shape[1] // 2
    rows = TILE * STRIP
    span = 2 * STRIP
    tile_y = where_ref[0] % 2
    borders = [(u, u - 1) for u in range(1, TILE)] + borders
    targets = sorted({target for target, _ in borders})
    for i, (pair, u) in enumerate([] if laid else strips):
        lay_strip(ground, i, tile_y, *pairs[pair], u)
        if i < TILE or i in targets:
            both = [ref[rows:, u * STRIP:(u + 1) * STRIP].astype(jnp.float32) for ref in pairs[pair]]
            first = jnp.where(tile_y == 0, both[0], both[1])
            second = jnp.where(tile_y == 0, both[1], both[0])
            codes[i] = jnp.concatenate([first, second], axis=1)
        if i < TILE or i in [source for _, source in borders]:
            turned[:, i * span:(i + 1) * span] = ground[i * span:(i + 1) * span, :].T
    place = lax.broadcasted_iota(jnp.int32, (span, span), 0).astype(jnp.float32)

    to = (near_act, near_cot)
    for source in range(TILE + 2):
        found = [(source, k) for k in range(9, HALF)] if 1 in groups and source < TILE else []
        if 0 in groups:
            found += [(target, k) for target, origin in borders if origin == source for k in range(9)]
        if found:
            picks = [(place == codes[target, k:k + 1, :]).astype(jnp.bfloat16) for target, k in found]
            look_up((turned, source * span, span), picks, [(to, k * width, target * span) for target, k in found])
    extents = ((0, 9, span * targets[0], span * (targets[-1] + 1)), (9, HALF, 0, TILE * span))
    for turn, near in ((0, near_act), (1, near_cot)):
        for group in groups:
            start, stop, first, last = extents[group]
            other = ground[first:last, (1 - turn) * width:(2 - turn) * width]
            value = jnp.dot(near[start * width:stop * width, first:last], other, preferred_element_type=jnp.float32)
            if not first_stage:
                value = value + before[turn][start * width:stop * width, :]
            if not final:
                outs[turn][start * width:stop * width, :] = value
                continue
            for k in range(start, stop):
                one = value[(k - start) * width:(k - start + 1) * width, :]
                to = 2 * HALF - k if turn else k
                if turn:
                    one = one.T
                to = to - 9 if group == 1 else to - 9 * turn
                outs[0][to] = one
                outs[1][to] = one.astype(jnp.bfloat16)
    if 1 in groups:
        centre = jnp.dot(turned[:width, :TILE * span], ground[:TILE * span, width:], preferred_element_type=jnp.float32)
        if not first_stage:
            centre = centre + before[2][...]
        if final:
            outs[0][HALF - 9] = centre
            outs[1][HALF - 9] = centre.astype(jnp.bfloat16)
        else:
            outs[2][...] = centre


def turn_kernel(w_ref, forward_ref, back_ref):
    width = w_ref.shape[1]
    for k in range(27):
        forward_ref[:, k * width:(k + 1) * width] = w_ref[k].T
        back_ref[:, k * width:(k + 1) * width] = w_ref[26 - k]


def own_kernel(where_ref, mine_ref, other_ref, code_ref, forward_ref, back_ref, conv_ref, grad_ref,
               ground, turned, codes, near_act, near_cot):
    width = conv_ref.shape[0]
    span = 2 * STRIP
    tile_y = where_ref[0] % 2
    for u in range(TILE):
        lay_strip(ground, u, tile_y, mine_ref, other_ref, u)
        turned[:, (u + 1) * span:(u + 2) * span] = ground[u * span:(u + 1) * span, :].T
    for i in (0, TILE + 1):
        turned[:, i * span:(i + 1) * span] = jnp.zeros((2 * width, span), jnp.bfloat16)
    code = code_ref[...]
    lane = lax.broadcasted_iota(jnp.int32, code.shape, 1)
    codes[...] = jnp.where((code >= 0) & (lane // STRIP % 2 == 1), code + span, code)
    place = lax.broadcasted_iota(jnp.int32, (2 * span, span), 0).astype(jnp.float32)
    for half in range(TILE // 2):
        at = half * span
        for side in range(3):
            source = (2 * half + side) * span
            ks = range(9 * side, 9 * side + 9)
            picks = [(place == codes[k:k + 1, at:at + span]).astype(jnp.bfloat16) for k in ks]
            look_up((turned, source, 2 * span), picks, [((near_act, near_cot), k * width, at) for k in ks])
    conv_ref[...] = jnp.dot(forward_ref[...], near_act[...], preferred_element_type=jnp.float32)
    grad_ref[...] = jnp.dot(back_ref[...], near_cot[...], preferred_element_type=jnp.float32)


def edge_kernel(where_ref, before_mine, before_other, after_mine, after_other, code_ref, forward_ref, back_ref,
                own_conv, own_grad, z_ref, conv_ref, grad_ref, ground, turned, near):
    width = z_ref.shape[1]
    span = 2 * STRIP
    tile_y = where_ref[0] % 2
    lay_strip(ground, 0, tile_y, before_mine, before_other, TILE - 1)
    lay_strip(ground, 1, tile_y, after_mine, after_other, 0)
    for i in range(2):
        turned[:, i * span:(i + 1) * span] = ground[i * span:(i + 1) * span, :].T
    first = code_ref[:9, :span]
    last = code_ref[18:, span:]
    lane = lax.broadcasted_iota(jnp.int32, first.shape, 1)
    code = jnp.where(lane < STRIP, first, jnp.where(last >= 0, last + span, last))
    place = lax.broadcasted_iota(jnp.int32, (2 * span, span), 0).astype(jnp.float32)
    picks = [(place == code[k:k + 1, :]).astype(jnp.bfloat16) for k in range(9)]
    look_up((turned, 0, 2 * span), picks, [((near.at[0], near.at[1]), k * width, 0) for k in range(9)])
    lane = lax.broadcasted_iota(jnp.int32, (width, span), 1)

    def total(own_ref, weights, side):
        low = jnp.dot(weights[:, :9 * width], near[side], preferred_element_type=jnp.float32)
        high = jnp.dot(weights[:, 18 * width:], near[side], preferred_element_type=jnp.float32)
        low = own_ref[:, :span] + jnp.where(lane < STRIP, low, 0.0)
        high = own_ref[:, span:] + jnp.where(lane < STRIP, 0.0, high)
        return jnp.concatenate([low, high], axis=1).T

    conv_ref[...] = total(own_conv, forward_ref, 0).astype(jnp.bfloat16)
    back = total(own_grad, back_ref, 1)
    z_val = z_ref[...]
    sig = jax.nn.sigmoid(z_val)
    grad_ref[...] = (back * sig * (1.0 + z_val * (1.0 - sig))).astype(jnp.bfloat16)


def finish_kernel(sides_ref, sides_sent, middle_ref, middle_sent, conv_ref, grad_ref,
                  weight_hbm, conv_hbm, grad_hbm, weight, sems):
    steps = 27 // FINISH_STEP
    copies = [
        pltpu.make_async_copy(conv_ref, conv_hbm, sems.at[steps]),
        pltpu.make_async_copy(grad_ref, grad_hbm, sems.at[steps + 1]),
    ]
    for copy in copies:
        copy.start()
    for i in range(steps):
        first = i * FINISH_STEP
        kept, sent, at = (middle_ref, middle_sent, first - 9) if first // 9 == 1 else (
            sides_ref, sides_sent, first if first < 9 else first - 9)
        part, taken = pl.ds(first, FINISH_STEP), pl.ds(at, FINISH_STEP)
        weight[part] = kept[taken] + sent[taken].astype(jnp.float32)
        copies.append(pltpu.make_async_copy(weight.at[part], weight_hbm.at[part], sems.at[i]))
        copies[-1].start()
    for copy in copies:
        copy.wait()


def whole_scene(features, cotangent, neighbours, timesteps, condition, w_time, w_conv, tiles_x, tiles_y):
    rows, width = features.shape[1:]
    peers = tiles_x * tiles_y
    span = 2 * STRIP
    vmem = pl.BlockSpec(memory_space=pltpu.VMEM)
    smem = pl.BlockSpec(memory_space=pltpu.SMEM)
    params = pltpu.CompilerParams(vmem_limit_bytes=KERNEL_VMEM)
    packed, z_val, code = pl.pallas_call(
        pack_kernel,
        out_shape=(
            jax.ShapeDtypeStruct((rows + CODE_ROWS, 2 * width), jnp.bfloat16),
            jax.ShapeDtypeStruct((rows, width), jnp.float32),
            jax.ShapeDtypeStruct(neighbours.shape, jnp.float32),
        ),
        in_specs=[smem] + [pl.BlockSpec(memory_space=pltpu.HBM)] * 5,
        out_specs=(vmem, vmem, vmem),
        scratch_shapes=[
            pltpu.VMEM((rows, width), jnp.bfloat16),
            pltpu.VMEM(neighbours.shape, jnp.int32),
            pltpu.VMEM((1, width), jnp.bfloat16),
            pltpu.VMEM((width, width), jnp.bfloat16),
            pltpu.SemaphoreType.DMA((5,)),
        ],
        compiler_params=pltpu.CompilerParams(vmem_limit_bytes=PACK_VMEM),
        name="pack_tile",
    )(timesteps, *[in_hbm(array) for array in (features, cotangent, neighbours, condition, w_time)])
    here = lax.axis_index("brick").astype(jnp.int32).reshape(1)

    def across(block):
        return lax.ppermute(block, "brick", [(i, i ^ 1) for i in range(peers)])

    def along(block, turn):
        return lax.ppermute(block, "brick", [(i, (i + turn * tiles_y) % peers) for i in range(peers)])

    w_conv, packed = lax.optimization_barrier((w_conv, packed))
    w_forward, w_back = pl.pallas_call(
        turn_kernel,
        out_shape=(jax.ShapeDtypeStruct((width, 27 * width), jnp.bfloat16),) * 2,
        in_specs=[vmem],
        out_specs=(vmem, vmem),
        compiler_params=params,
        cost_estimate=pl.CostEstimate(flops=2 * 10**8, bytes_accessed=3 * 10**6, transcendentals=0),
        name="turn_weights",
    )(w_conv)
    before = along(packed, 1)
    w_back, later = lax.optimization_barrier((w_back, packed))
    after = along(later, -1)
    before, w_forward = lax.optimization_barrier((before, w_forward))
    far = along(before, 1)
    own_pair = (packed, across(packed))
    own_conv, own_grad = pl.pallas_call(
        own_kernel,
        out_shape=(jax.ShapeDtypeStruct((width, rows), jnp.float32),) * 2,
        in_specs=[smem] + [vmem] * 5,
        out_specs=(vmem, vmem),
        scratch_shapes=[
            pltpu.VMEM((TILE * span, 2 * width), jnp.bfloat16),
            pltpu.VMEM((2 * width, (TILE + 2) * span), jnp.bfloat16),
            pltpu.VMEM((27, rows), jnp.float32),
            pltpu.VMEM((27 * width, rows), jnp.bfloat16),
            pltpu.VMEM((27 * width, rows), jnp.bfloat16),
        ],
        compiler_params=params,
        cost_estimate=pl.CostEstimate(flops=2 * 10**9, bytes_accessed=4 * 10**6, transcendentals=0),
        name="voxels_own_row",
    )(here, *own_pair, code, w_forward, w_back)
    far, own_conv = lax.optimization_barrier((far, own_conv))
    before_pair = (before, across(before))
    far_pair = (far, across(far))
    def row_sums(name, pairs, strips, borders, sums, groups=(0, 1), final=0, keep=False, laid=()):
        blocks = [block for pair in pairs for block in pair]
        if final:
            out_shape = (
                jax.ShapeDtypeStruct((final, width, width), jnp.float32),
                jax.ShapeDtypeStruct((final, width, width), jnp.bfloat16),
            )
        else:
            out_shape = (
                jax.ShapeDtypeStruct((HALF * width, width), jnp.float32),
                jax.ShapeDtypeStruct((HALF * width, width), jnp.float32),
                jax.ShapeDtypeStruct((width, width), jnp.float32),
            )
        layout = (
            ((TILE + 2) * span, 2 * width, jnp.bfloat16),
            (2 * width, (TILE + 2) * span, jnp.bfloat16),
            (TILE + 1, CODE_ROWS, span, jnp.float32),
        )
        scratch = [] if laid or keep else [pltpu.VMEM(tuple(shape), kind) for *shape, kind in layout]
        if keep:
            out_shape += tuple(jax.ShapeDtypeStruct(tuple(shape), kind) for *shape, kind in layout)
        operands = (*blocks, *laid, *sums)
        return pl.pallas_call(
            functools.partial(row_kernel, not sums, bool(final), groups, bool(laid), strips, borders),
            out_shape=out_shape,
            in_specs=[smem] + [vmem] * len(operands),
            out_specs=(vmem,) * len(out_shape),
            scratch_shapes=scratch + [
                pltpu.VMEM((HALF * width, (TILE + 1) * span), jnp.bfloat16),
                pltpu.VMEM((HALF * width, (TILE + 1) * span), jnp.bfloat16),
            ],
            compiler_params=params,
            cost_estimate=pl.CostEstimate(flops=2 * 10**9, bytes_accessed=4 * 10**6, transcendentals=0),
            name=name,
        )(here, *operands)

    def swapped(block):
        return lax.ppermute(block, "batch", [(0, 1), (1, 0)])

    line = [(0, u) for u in range(TILE)]
    sums = row_sums("weight_row_0", (own_pair,), line, [], ())
    after, centre = lax.optimization_barrier((after, sums[2]))
    sums = (sums[0], sums[1], centre)
    after_pair = (after, across(after))
    sums = row_sums("weight_row_1", (before_pair, own_pair), line + [(1, 0)], [(TILE, TILE - 1)], sums)
    sums = row_sums("weight_row_2", (after_pair, own_pair), line + [(1, TILE - 1)], [(0, TILE)], sums)
    sides, sides_sent, *laid = row_sums("weight_row_3", (far_pair, before_pair, after_pair),
                                 line + [(1, 0), (2, TILE - 1)], [(TILE, TILE - 1), (0, TILE + 1)],
                                 sums, groups=(0,), final=18, keep=True)
    sides_other = swapped(sides_sent)
    centre, sides = lax.optimization_barrier((sums[2], sides))
    middle, middle_sent = row_sums("weight_row_3_middle", (), line, [], (sums[0], sums[1], centre),
                                   groups=(1,), final=9, laid=laid)
    middle_other = swapped(middle_sent)
    conv_out, feature_grad = pl.pallas_call(
        edge_kernel,
        out_shape=(jax.ShapeDtypeStruct((rows, width), jnp.bfloat16),) * 2,
        in_specs=[smem] + [vmem] * 10,
        out_specs=(vmem, vmem),
        scratch_shapes=[
            pltpu.VMEM((2 * span, 2 * width), jnp.bfloat16),
            pltpu.VMEM((2 * width, 2 * span), jnp.bfloat16),
            pltpu.VMEM((2, 9 * width, span), jnp.bfloat16),
        ],
        compiler_params=params,
        cost_estimate=pl.CostEstimate(flops=10**9, bytes_accessed=4 * 10**6, transcendentals=0),
        name="voxel_edges",
    )(here, *before_pair, *after_pair, code, w_forward, w_back, own_conv, own_grad, z_val)
    hbm = pl.BlockSpec(memory_space=pltpu.HBM)
    weight_grad, conv_out, feature_grad = pl.pallas_call(
        finish_kernel,
        out_shape=(
            jax.ShapeDtypeStruct((27, width, width), jnp.float32),
            jax.ShapeDtypeStruct((rows, width), jnp.bfloat16),
            jax.ShapeDtypeStruct((rows, width), jnp.bfloat16),
        ),
        in_specs=[vmem] * 6,
        out_specs=(hbm, hbm, hbm),
        scratch_shapes=[
            pltpu.VMEM((27, width, width), jnp.float32),
            pltpu.SemaphoreType.DMA((27 // FINISH_STEP + 2,)),
        ],
        compiler_params=pltpu.CompilerParams(vmem_limit_bytes=PACK_VMEM),
        name="finish",
    )(sides, sides_other, middle, middle_other, conv_out, feature_grad)
    return (conv_out[None], feature_grad[None], weight_grad)


def passed_along(block, axis, distance):
    devices = range(lax.axis_size(axis))
    route = [(i - distance, i) for i in devices if i - distance in devices]
    return lax.ppermute(block, axis, route)


def slab_rows(block, side_recv, front_recv, width):
    widened = jnp.concatenate([side_recv[0], block, side_recv[1]], axis=1)
    slab = jnp.concatenate([front_recv[0][None], widened, front_recv[1][None]], axis=0)
    flat = slab.reshape(-1, width)
    return jnp.concatenate([flat, jnp.zeros((1, width), jnp.bfloat16)], axis=0)


def with_halo(block, tiles_y):
    width = block.shape[-1]
    side = TILE
    side_recv = tuple(passed_along(block[:, edge], "brick", by)[:, None] for by, edge in ((1, side - 1), (-1, 0)))
    wide = jnp.concatenate([side_recv[0], block, side_recv[1]], axis=1)
    front_recv = tuple(passed_along(wide[edge], "brick", by) for by, edge in ((tiles_y, side - 1), (-tiles_y, 0)))
    return slab_rows(block, side_recv, front_recv, width)


def halo_plan(features, cotangent, neighbours, timesteps, condition, w_time, w_conv, tiles_x, tiles_y):
    rows_here, width = features.shape[1:]
    here = lax.axis_index("brick")
    tile_x = here // tiles_y
    tile_y = here % tiles_y
    side = TILE
    layers = LAYERS
    wide = side + 2
    valid = neighbours >= 0
    safe = jnp.where(valid, neighbours, 0)
    owner = safe // rows_here
    inside = safe % rows_here
    column = inside // layers
    layer = inside % layers
    local_x = (owner // tiles_y - tile_x) * side + column // side + 1
    local_y = (owner % tiles_y - tile_y) * side + column % side + 1
    sentinel = wide * wide * layers
    ext_index = jnp.where(valid, (local_x * wide + local_y) * layers + layer, sentinel).T
    temb = time_embedding(timesteps, width)
    shift = jnp.dot(temb, w_time, preferred_element_type=jnp.float32) + condition.astype(jnp.float32)
    z_val = features[0].astype(jnp.float32) + shift[0][None, :]
    act = jax.nn.silu(z_val).astype(jnp.bfloat16)
    cot = cotangent[0]
    w_forward = w_conv.reshape(27 * width, width)
    w_backward = jnp.transpose(w_conv[::-1], (0, 2, 1)).reshape(27 * width, width)
    act_ext = with_halo(act.reshape(side, side, layers, width), tiles_y)
    gathered = act_ext[ext_index].reshape(rows_here, 27 * width)
    conv_out = jnp.dot(gathered, w_forward, preferred_element_type=jnp.float32).astype(jnp.bfloat16)
    partial_grad = lax.dot_general(
        gathered, cot, (((0,), (0,)), ((), ())), preferred_element_type=jnp.float32
    )
    both = ("brick", "batch")
    parts = tiles_x * tiles_y * lax.axis_size("batch")
    rows = 27 * width
    extra = -rows % (8 * parts)
    pieces = jnp.pad(partial_grad.astype(jnp.bfloat16), ((0, extra), (0, 0))).reshape(parts, -1, width)
    arrived = lax.all_to_all(pieces, both, 0, 0)
    summed = arrived.astype(jnp.float32).sum(0).astype(jnp.bfloat16)
    whole = lax.all_gather(summed, both, axis=0, tiled=True)
    weight_grad = whole[:rows].astype(jnp.float32).reshape(27, width, width)
    cot_ext = with_halo(cot.reshape(side, side, layers, width), tiles_y)
    cot_gathered = cot_ext[ext_index].reshape(rows_here, 27 * width)
    back = jnp.dot(cot_gathered, w_backward, preferred_element_type=jnp.float32)
    sig = jax.nn.sigmoid(z_val)
    feature_grad = (back * sig * (1.0 + z_val * (1.0 - sig))).astype(jnp.bfloat16)
    return (conv_out[None], feature_grad[None], weight_grad)


def shards(*arrays):
    peers = lax.axis_size("brick")
    bits = peers.bit_length() - 1
    tiles_x = 2 ** ((bits + 1) // 2)
    tiles_y = 2 ** (bits // 2)
    plan = whole_scene if (tiles_x, tiles_y) == (ROW_STAGES, 2) else halo_plan
    return plan(*arrays, tiles_x, tiles_y)


def solution(mesh):
    in_specs = (
        P(("groups", "batch"), "brick", None),
        P(("groups", "batch"), "brick", None),
        P(None, ("groups", "brick")),
        P(("groups", "batch")),
        P(("groups", "batch"), None),
        P(),
        P(),
    )
    out_specs = (
        P(("groups", "batch"), "brick", None),
        P(("groups", "batch"), "brick", None),
        P("groups", None, None),
    )
    return jax.shard_map(shards, mesh=mesh, in_specs=in_specs, out_specs=out_specs, check_vma=False)
```

```python
import functools

import jax
import jax.numpy as jnp
from jax import lax
from jax.experimental import pallas as pl
from jax.experimental.pallas import tpu as pltpu
from jax.sharding import PartitionSpec as P

LAYERS = 16
TILE = 4
STRIP = TILE * LAYERS
HALF = 13
CODE_ROWS = 16
ROW_STAGES = 4
FINISH_STEP = 9
PACK_VMEM = 8 * 1024 * 1024
KERNEL_VMEM = 24 * 1024 * 1024


def time_embedding(timesteps, width):
    half = width // 2
    freq = jnp.exp(-jnp.log(10000.0) * jnp.arange(half, dtype=jnp.float32) / half)
    angle = timesteps.astype(jnp.float32)[:, None] * freq[None, :]
    return jnp.concatenate([jnp.sin(angle), jnp.cos(angle)], axis=1).astype(jnp.bfloat16)


def strip_codes(neighbours, tiles_y):
    rows_here = TILE * STRIP
    code = (neighbours // rows_here) % tiles_y * STRIP + neighbours % STRIP
    return jnp.where(neighbours < 0, -1, code).astype(jnp.float32)


def in_hbm(array):
    return pltpu.with_memory_space_constraint(array, pltpu.HBM)


def pack_kernel(time_ref, feat_hbm, cot_hbm, near_hbm, cond_hbm, wt_hbm, pack_ref, z_ref, code_ref,
                feat_ref, near_ref, cond_ref, wt_ref, sems):
    rows, width = feat_ref.shape
    half = width // 2
    moves = (
        (wt_hbm, wt_ref),
        (cond_hbm, cond_ref),
        (feat_hbm.at[0], feat_ref),
        (near_hbm, near_ref),
        (cot_hbm.at[0], pack_ref.at[:rows, width:]),
    )
    copies = [pltpu.make_async_copy(source, to, sems.at[i]) for i, (source, to) in enumerate(moves)]
    for copy in copies:
        copy.start()
    lane = lax.broadcasted_iota(jnp.int32, (1, width), 1)
    freq = jnp.exp(-jnp.log(10000.0) * (lane % half).astype(jnp.float32) / half)
    angle = time_ref[0].astype(jnp.float32) * freq
    temb = jnp.where(lane < half, jnp.sin(angle), jnp.cos(angle)).astype(jnp.bfloat16)
    copies[0].wait()
    copies[1].wait()
    shift = jnp.dot(temb, wt_ref[...], preferred_element_type=jnp.float32)
    shift = shift + cond_ref[...].astype(jnp.float32)
    copies[2].wait()
    z_val = feat_ref[...].astype(jnp.float32) + shift
    z_ref[...] = z_val
    pack_ref[:rows, :width] = (z_val * jax.nn.sigmoid(z_val)).astype(jnp.bfloat16)
    copies[3].wait()
    code = strip_codes(near_ref[...], 2)
    code_ref[...] = code
    pack_ref[rows:, :] = code[:CODE_ROWS, :].astype(jnp.bfloat16)
    copies[4].wait()


def lay_strip(ground, to, tile_y, mine_ref, other_ref, u):
    span = 2 * STRIP
    for ref, place in ((mine_ref, tile_y), (other_ref, 1 - tile_y)):
        at = pl.multiple_of(to * span + place * STRIP, STRIP)
        ground[pl.ds(at, STRIP), :] = ref[u * STRIP:(u + 1) * STRIP, :]


def look_up(window, picks, places):
    ref, first, lanes = window
    width = ref.shape[0] // 2
    for i in range(0, len(picks), 2):
        pair = picks[i:i + 2]
        pick = jnp.concatenate(pair, axis=1) if len(pair) == 2 else pair[0]
        span = pair[0].shape[1]
        for side in range(2):
            near = jnp.dot(ref[side * width:(side + 1) * width, first:first + lanes], pick,
                           preferred_element_type=jnp.float32).astype(jnp.bfloat16)
            for j, (to, row, lane) in enumerate(places[i:i + 2]):
                to[side][row:row + width, lane:lane + span] = near[:, j * span:(j + 1) * span]


def row_kernel(first_stage, final, groups, laid, strips, borders, *refs):
    refs = list(refs)
    where_ref = refs.pop(0)
    pairs = [] if laid else [(refs.pop(0), refs.pop(0)) for _ in range(1 + max(pair for pair, _ in strips))]
    given = [refs.pop(0) for _ in range(3)] if laid else []
    before = [refs.pop(0) for _ in range(0 if first_stage else 3)]
    outs = [refs.pop(0) for _ in range(1 if final else 3)]
    ground, turned, codes = given or [refs.pop(0) for _ in range(3)]
    near_act, near_cot = refs
    width = ground.shape[1] // 2
    rows = TILE * STRIP
    span = 2 * STRIP
    tile_y = where_ref[0] % 2
    borders = [(u, u - 1) for u in range(1, TILE)] + borders
    targets = sorted({target for target, _ in borders})
    for i, (pair, u) in enumerate([] if laid else strips):
        lay_strip(ground, i, tile_y, *pairs[pair], u)
        if i < TILE or i in targets:
            both = [ref[rows:, u * STRIP:(u + 1) * STRIP].astype(jnp.float32) for ref in pairs[pair]]
            first = jnp.where(tile_y == 0, both[0], both[1])
            second = jnp.where(tile_y == 0, both[1], both[0])
            codes[i] = jnp.concatenate([first, second], axis=1)
        if i < TILE or i in [source for _, source in borders]:
            turned[:, i * span:(i + 1) * span] = ground[i * span:(i + 1) * span, :].T
    place = lax.broadcasted_iota(jnp.int32, (span, span), 0).astype(jnp.float32)

    to = (near_act, near_cot)
    for source in range(TILE + 2):
        found = [(source, k) for k in range(9, HALF)] if 1 in groups and source < TILE else []
        if 0 in groups:
            found += [(target, k) for target, origin in borders if origin == source for k in range(9)]
        if found:
            picks = [(place == codes[target, k:k + 1, :]).astype(jnp.bfloat16) for target, k in found]
            look_up((turned, source * span, span), picks, [(to, k * width, target * span) for target, k in found])
    extents = ((0, 9, span * targets[0], span * (targets[-1] + 1)), (9, HALF, 0, TILE * span))
    for turn, near in ((0, near_act), (1, near_cot)):
        for group in groups:
            start, stop, first, last = extents[group]
            other = ground[first:last, (1 - turn) * width:(2 - turn) * width]
            value = jnp.dot(near[start * width:stop * width, first:last], other, preferred_element_type=jnp.float32)
            if not first_stage:
                value = value + before[turn][start * width:stop * width, :]
            if not final:
                outs[turn][start * width:stop * width, :] = value
                continue
            for k in range(start, stop):
                one = value[(k - start) * width:(k - start + 1) * width, :]
                to = 2 * HALF - k if turn else k
                if turn:
                    one = one.T
                to = to - 9 if group == 1 else to - 9 * turn
                outs[0][to] = one.astype(jnp.bfloat16)
    if 1 in groups:
        centre = jnp.dot(turned[:width, :TILE * span], ground[:TILE * span, width:], preferred_element_type=jnp.float32)
        if not first_stage:
            centre = centre + before[2][...]
        if final:
            outs[0][HALF - 9] = centre.astype(jnp.bfloat16)
        else:
            outs[2][...] = centre


def turn_kernel(w_ref, forward_ref, back_ref):
    width = w_ref.shape[1]
    for k in range(27):
        forward_ref[:, k * width:(k + 1) * width] = w_ref[k].T
        back_ref[:, k * width:(k + 1) * width] = w_ref[26 - k]


def own_kernel(where_ref, mine_ref, other_ref, code_ref, forward_ref, back_ref, conv_ref, grad_ref,
               ground, turned, codes, near_act, near_cot):
    width = conv_ref.shape[0]
    span = 2 * STRIP
    tile_y = where_ref[0] % 2
    for u in range(TILE):
        lay_strip(ground, u, tile_y, mine_ref, other_ref, u)
        turned[:, (u + 1) * span:(u + 2) * span] = ground[u * span:(u + 1) * span, :].T
    for i in (0, TILE + 1):
        turned[:, i * span:(i + 1) * span] = jnp.zeros((2 * width, span), jnp.bfloat16)
    code = code_ref[...]
    lane = lax.broadcasted_iota(jnp.int32, code.shape, 1)
    codes[...] = jnp.where((code >= 0) & (lane // STRIP % 2 == 1), code + span, code)
    place = lax.broadcasted_iota(jnp.int32, (2 * span, span), 0).astype(jnp.float32)
    for half in range(TILE // 2):
        at = half * span
        for side in range(3):
            source = (2 * half + side) * span
            ks = range(9 * side, 9 * side + 9)
            picks = [(place == codes[k:k + 1, at:at + span]).astype(jnp.bfloat16) for k in ks]
            look_up((turned, source, 2 * span), picks, [((near_act, near_cot), k * width, at) for k in ks])
    conv_ref[...] = jnp.dot(forward_ref[...], near_act[...], preferred_element_type=jnp.float32)
    grad_ref[...] = jnp.dot(back_ref[...], near_cot[...], preferred_element_type=jnp.float32)


def edge_kernel(where_ref, before_mine, before_other, after_mine, after_other, code_ref, forward_ref, back_ref,
                own_conv, own_grad, z_ref, conv_ref, grad_ref, ground, turned, near):
    width = z_ref.shape[1]
    span = 2 * STRIP
    tile_y = where_ref[0] % 2
    lay_strip(ground, 0, tile_y, before_mine, before_other, TILE - 1)
    lay_strip(ground, 1, tile_y, after_mine, after_other, 0)
    for i in range(2):
        turned[:, i * span:(i + 1) * span] = ground[i * span:(i + 1) * span, :].T
    first = code_ref[:9, :span]
    last = code_ref[18:, span:]
    lane = lax.broadcasted_iota(jnp.int32, first.shape, 1)
    code = jnp.where(lane < STRIP, first, jnp.where(last >= 0, last + span, last))
    place = lax.broadcasted_iota(jnp.int32, (2 * span, span), 0).astype(jnp.float32)
    picks = [(place == code[k:k + 1, :]).astype(jnp.bfloat16) for k in range(9)]
    look_up((turned, 0, 2 * span), picks, [((near.at[0], near.at[1]), k * width, 0) for k in range(9)])
    lane = lax.broadcasted_iota(jnp.int32, (width, span), 1)

    def total(own_ref, weights, side):
        low = jnp.dot(weights[:, :9 * width], near[side], preferred_element_type=jnp.float32)
        high = jnp.dot(weights[:, 18 * width:], near[side], preferred_element_type=jnp.float32)
        low = own_ref[:, :span] + jnp.where(lane < STRIP, low, 0.0)
        high = own_ref[:, span:] + jnp.where(lane < STRIP, 0.0, high)
        return jnp.concatenate([low, high], axis=1).T

    conv_ref[...] = total(own_conv, forward_ref, 0).astype(jnp.bfloat16)
    back = total(own_grad, back_ref, 1)
    z_val = z_ref[...]
    sig = jax.nn.sigmoid(z_val)
    grad_ref[...] = (back * sig * (1.0 + z_val * (1.0 - sig))).astype(jnp.bfloat16)


def finish_kernel(sides_ref, sides_sent, middle_ref, middle_sent, conv_ref, grad_ref,
                  weight_hbm, conv_hbm, grad_hbm, weight, sems):
    steps = 27 // FINISH_STEP
    copies = [
        pltpu.make_async_copy(conv_ref, conv_hbm, sems.at[steps]),
        pltpu.make_async_copy(grad_ref, grad_hbm, sems.at[steps + 1]),
    ]
    for copy in copies:
        copy.start()
    for i in range(steps):
        first = i * FINISH_STEP
        kept, sent, at = (middle_ref, middle_sent, first - 9) if first // 9 == 1 else (
            sides_ref, sides_sent, first if first < 9 else first - 9)
        part, taken = pl.ds(first, FINISH_STEP), pl.ds(at, FINISH_STEP)
        weight[part] = kept[taken].astype(jnp.float32) + sent[taken].astype(jnp.float32)
        copies.append(pltpu.make_async_copy(weight.at[part], weight_hbm.at[part], sems.at[i]))
        copies[-1].start()
    for copy in copies:
        copy.wait()


def whole_scene(features, cotangent, neighbours, timesteps, condition, w_time, w_conv, tiles_x, tiles_y):
    rows, width = features.shape[1:]
    peers = tiles_x * tiles_y
    span = 2 * STRIP
    vmem = pl.BlockSpec(memory_space=pltpu.VMEM)
    smem = pl.BlockSpec(memory_space=pltpu.SMEM)
    params = pltpu.CompilerParams(vmem_limit_bytes=KERNEL_VMEM)
    packed, z_val, code = pl.pallas_call(
        pack_kernel,
        out_shape=(
            jax.ShapeDtypeStruct((rows + CODE_ROWS, 2 * width), jnp.bfloat16),
            jax.ShapeDtypeStruct((rows, width), jnp.float32),
            jax.ShapeDtypeStruct(neighbours.shape, jnp.float32),
        ),
        in_specs=[smem] + [pl.BlockSpec(memory_space=pltpu.HBM)] * 5,
        out_specs=(vmem, vmem, vmem),
        scratch_shapes=[
            pltpu.VMEM((rows, width), jnp.bfloat16),
            pltpu.VMEM(neighbours.shape, jnp.int32),
            pltpu.VMEM((1, width), jnp.bfloat16),
            pltpu.VMEM((width, width), jnp.bfloat16),
            pltpu.SemaphoreType.DMA((5,)),
        ],
        compiler_params=pltpu.CompilerParams(vmem_limit_bytes=PACK_VMEM),
        name="pack_tile",
    )(timesteps, *[in_hbm(array) for array in (features, cotangent, neighbours, condition, w_time)])
    here = lax.axis_index("brick").astype(jnp.int32).reshape(1)

    def across(block):
        return lax.ppermute(block, "brick", [(i, i ^ 1) for i in range(peers)])

    def along(block, turn):
        return lax.ppermute(block, "brick", [(i, (i + turn * tiles_y) % peers) for i in range(peers)])

    w_conv, packed = lax.optimization_barrier((w_conv, packed))
    w_forward, w_back = pl.pallas_call(
        turn_kernel,
        out_shape=(jax.ShapeDtypeStruct((width, 27 * width), jnp.bfloat16),) * 2,
        in_specs=[vmem],
        out_specs=(vmem, vmem),
        compiler_params=params,
        cost_estimate=pl.CostEstimate(flops=2 * 10**8, bytes_accessed=3 * 10**6, transcendentals=0),
        name="turn_weights",
    )(w_conv)
    before = along(packed, 1)
    w_back, later = lax.optimization_barrier((w_back, packed))
    after = along(later, -1)
    before, w_forward = lax.optimization_barrier((before, w_forward))
    far = along(before, 1)
    own_pair = (packed, across(packed))
    own_conv, own_grad = pl.pallas_call(
        own_kernel,
        out_shape=(jax.ShapeDtypeStruct((width, rows), jnp.float32),) * 2,
        in_specs=[smem] + [vmem] * 5,
        out_specs=(vmem, vmem),
        scratch_shapes=[
            pltpu.VMEM((TILE * span, 2 * width), jnp.bfloat16),
            pltpu.VMEM((2 * width, (TILE + 2) * span), jnp.bfloat16),
            pltpu.VMEM((27, rows), jnp.float32),
            pltpu.VMEM((27 * width, rows), jnp.bfloat16),
            pltpu.VMEM((27 * width, rows), jnp.bfloat16),
        ],
        compiler_params=params,
        cost_estimate=pl.CostEstimate(flops=2 * 10**9, bytes_accessed=4 * 10**6, transcendentals=0),
        name="voxels_own_row",
    )(here, *own_pair, code, w_forward, w_back)
    far, own_conv = lax.optimization_barrier((far, own_conv))
    before_pair = (before, across(before))
    far_pair = (far, across(far))
    def row_sums(name, pairs, strips, borders, sums, groups=(0, 1), final=0, keep=False, laid=()):
        blocks = [block for pair in pairs for block in pair]
        if final:
            out_shape = (jax.ShapeDtypeStruct((final, width, width), jnp.bfloat16),)
        else:
            out_shape = (
                jax.ShapeDtypeStruct((HALF * width, width), jnp.float32),
                jax.ShapeDtypeStruct((HALF * width, width), jnp.float32),
                jax.ShapeDtypeStruct((width, width), jnp.float32),
            )
        layout = (
            ((TILE + 2) * span, 2 * width, jnp.bfloat16),
            (2 * width, (TILE + 2) * span, jnp.bfloat16),
            (TILE + 1, CODE_ROWS, span, jnp.float32),
        )
        scratch = [] if laid or keep else [pltpu.VMEM(tuple(shape), kind) for *shape, kind in layout]
        if keep:
            out_shape += tuple(jax.ShapeDtypeStruct(tuple(shape), kind) for *shape, kind in layout)
        operands = (*blocks, *laid, *sums)
        return pl.pallas_call(
            functools.partial(row_kernel, not sums, bool(final), groups, bool(laid), strips, borders),
            out_shape=out_shape,
            in_specs=[smem] + [vmem] * len(operands),
            out_specs=(vmem,) * len(out_shape),
            scratch_shapes=scratch + [
                pltpu.VMEM((HALF * width, (TILE + 1) * span), jnp.bfloat16),
                pltpu.VMEM((HALF * width, (TILE + 1) * span), jnp.bfloat16),
            ],
            compiler_params=params,
            cost_estimate=pl.CostEstimate(flops=2 * 10**9, bytes_accessed=4 * 10**6, transcendentals=0),
            name=name,
        )(here, *operands)

    def swapped(block):
        return lax.ppermute(block, "batch", [(0, 1), (1, 0)])

    line = [(0, u) for u in range(TILE)]
    sums = row_sums("weight_row_0", (own_pair,), line, [], ())
    after, centre = lax.optimization_barrier((after, sums[2]))
    sums = (sums[0], sums[1], centre)
    after_pair = (after, across(after))
    sums = row_sums("weight_row_1", (before_pair, own_pair), line + [(1, 0)], [(TILE, TILE - 1)], sums)
    sums = row_sums("weight_row_2", (after_pair, own_pair), line + [(1, TILE - 1)], [(0, TILE)], sums)
    sides, *laid = row_sums("weight_row_3", (far_pair, before_pair, after_pair),
                                 line + [(1, 0), (2, TILE - 1)], [(TILE, TILE - 1), (0, TILE + 1)],
                                 sums, groups=(0,), final=18, keep=True)
    sides_other = swapped(sides)
    centre, sides = lax.optimization_barrier((sums[2], sides))
    middle, = row_sums("weight_row_3_middle", (), line, [], (sums[0], sums[1], centre),
                                   groups=(1,), final=9, laid=laid)
    middle_other = swapped(middle)
    conv_out, feature_grad = pl.pallas_call(
        edge_kernel,
        out_shape=(jax.ShapeDtypeStruct((rows, width), jnp.bfloat16),) * 2,
        in_specs=[smem] + [vmem] * 10,
        out_specs=(vmem, vmem),
        scratch_shapes=[
            pltpu.VMEM((2 * span, 2 * width), jnp.bfloat16),
            pltpu.VMEM((2 * width, 2 * span), jnp.bfloat16),
            pltpu.VMEM((2, 9 * width, span), jnp.bfloat16),
        ],
        compiler_params=params,
        cost_estimate=pl.CostEstimate(flops=10**9, bytes_accessed=4 * 10**6, transcendentals=0),
        name="voxel_edges",
    )(here, *before_pair, *after_pair, code, w_forward, w_back, own_conv, own_grad, z_val)
    hbm = pl.BlockSpec(memory_space=pltpu.HBM)
    weight_grad, conv_out, feature_grad = pl.pallas_call(
        finish_kernel,
        out_shape=(
            jax.ShapeDtypeStruct((27, width, width), jnp.float32),
            jax.ShapeDtypeStruct((rows, width), jnp.bfloat16),
            jax.ShapeDtypeStruct((rows, width), jnp.bfloat16),
        ),
        in_specs=[vmem] * 6,
        out_specs=(hbm, hbm, hbm),
        scratch_shapes=[
            pltpu.VMEM((27, width, width), jnp.float32),
            pltpu.SemaphoreType.DMA((27 // FINISH_STEP + 2,)),
        ],
        compiler_params=pltpu.CompilerParams(vmem_limit_bytes=PACK_VMEM),
        name="finish",
    )(sides, sides_other, middle, middle_other, conv_out, feature_grad)
    return (conv_out[None], feature_grad[None], weight_grad)


def passed_along(block, axis, distance):
    devices = range(lax.axis_size(axis))
    route = [(i - distance, i) for i in devices if i - distance in devices]
    return lax.ppermute(block, axis, route)


def slab_rows(block, side_recv, front_recv, width):
    widened = jnp.concatenate([side_recv[0], block, side_recv[1]], axis=1)
    slab = jnp.concatenate([front_recv[0][None], widened, front_recv[1][None]], axis=0)
    flat = slab.reshape(-1, width)
    return jnp.concatenate([flat, jnp.zeros((1, width), jnp.bfloat16)], axis=0)


def with_halo(block, tiles_y):
    width = block.shape[-1]
    side = TILE
    side_recv = tuple(passed_along(block[:, edge], "brick", by)[:, None] for by, edge in ((1, side - 1), (-1, 0)))
    wide = jnp.concatenate([side_recv[0], block, side_recv[1]], axis=1)
    front_recv = tuple(passed_along(wide[edge], "brick", by) for by, edge in ((tiles_y, side - 1), (-tiles_y, 0)))
    return slab_rows(block, side_recv, front_recv, width)


def halo_plan(features, cotangent, neighbours, timesteps, condition, w_time, w_conv, tiles_x, tiles_y):
    rows_here, width = features.shape[1:]
    here = lax.axis_index("brick")
    tile_x = here // tiles_y
    tile_y = here % tiles_y
    side = TILE
    layers = LAYERS
    wide = side + 2
    valid = neighbours >= 0
    safe = jnp.where(valid, neighbours, 0)
    owner = safe // rows_here
    inside = safe % rows_here
    column = inside // layers
    layer = inside % layers
    local_x = (owner // tiles_y - tile_x) * side + column // side + 1
    local_y = (owner % tiles_y - tile_y) * side + column % side + 1
    sentinel = wide * wide * layers
    ext_index = jnp.where(valid, (local_x * wide + local_y) * layers + layer, sentinel).T
    temb = time_embedding(timesteps, width)
    shift = jnp.dot(temb, w_time, preferred_element_type=jnp.float32) + condition.astype(jnp.float32)
    z_val = features[0].astype(jnp.float32) + shift[0][None, :]
    act = jax.nn.silu(z_val).astype(jnp.bfloat16)
    cot = cotangent[0]
    w_forward = w_conv.reshape(27 * width, width)
    w_backward = jnp.transpose(w_conv[::-1], (0, 2, 1)).reshape(27 * width, width)
    act_ext = with_halo(act.reshape(side, side, layers, width), tiles_y)
    gathered = act_ext[ext_index].reshape(rows_here, 27 * width)
    conv_out = jnp.dot(gathered, w_forward, preferred_element_type=jnp.float32).astype(jnp.bfloat16)
    partial_grad = lax.dot_general(
        gathered, cot, (((0,), (0,)), ((), ())), preferred_element_type=jnp.float32
    )
    both = ("brick", "batch")
    parts = tiles_x * tiles_y * lax.axis_size("batch")
    rows = 27 * width
    extra = -rows % (8 * parts)
    pieces = jnp.pad(partial_grad.astype(jnp.bfloat16), ((0, extra), (0, 0))).reshape(parts, -1, width)
    arrived = lax.all_to_all(pieces, both, 0, 0)
    summed = arrived.astype(jnp.float32).sum(0).astype(jnp.bfloat16)
    whole = lax.all_gather(summed, both, axis=0, tiled=True)
    weight_grad = whole[:rows].astype(jnp.float32).reshape(27, width, width)
    cot_ext = with_halo(cot.reshape(side, side, layers, width), tiles_y)
    cot_gathered = cot_ext[ext_index].reshape(rows_here, 27 * width)
    back = jnp.dot(cot_gathered, w_backward, preferred_element_type=jnp.float32)
    sig = jax.nn.sigmoid(z_val)
    feature_grad = (back * sig * (1.0 + z_val * (1.0 - sig))).astype(jnp.bfloat16)
    return (conv_out[None], feature_grad[None], weight_grad)


def shards(*arrays):
    peers = lax.axis_size("brick")
    bits = peers.bit_length() - 1
    tiles_x = 2 ** ((bits + 1) // 2)
    tiles_y = 2 ** (bits // 2)
    plan = whole_scene if (tiles_x, tiles_y) == (ROW_STAGES, 2) else halo_plan
    return plan(*arrays, tiles_x, tiles_y)


def solution(mesh):
    in_specs = (
        P(("groups", "batch"), "brick", None),
        P(("groups", "batch"), "brick", None),
        P(None, ("groups", "brick")),
        P(("groups", "batch")),
        P(("groups", "batch"), None),
        P(),
        P(),
    )
    out_specs = (
        P(("groups", "batch"), "brick", None),
        P(("groups", "batch"), "brick", None),
        P("groups", None, None),
    )
    return jax.shard_map(shards, mesh=mesh, in_specs=in_specs, out_specs=out_specs, check_vma=False)
```
